128 devices in a mesh: dp: 32 (over y, x_hi, z), mp: 4 (over x_lo, core).
Axes of the slice: x: 4 (x_hi: 2, x_lo: 2; x = x_hi * 2 + x_lo), y: 4, z: 4, core: 2. Of those that a mesh axis runs over, the one named last changes fastest.
Arguments:
- layer_inputs: bfloat16 [4096, 1, 4096], P(('dp', 'mp')), may hold values from -6 to 6
- output_grads: bfloat16 [4096, 1, 4096], P('dp', None, 'mp'), may hold values from -0.09375 to 0.09375
- feature_order: int32 [1, 4096], replicated, may hold values from 0 to 4095, each once within a row
- block_slot: int32 [4], replicated, may hold values from 0 to 3, each once
- layer_owner: int32 [32], replicated, may hold values from 0 to 31, each once
- in_basis: float32 [4096, 1024], P('dp'), may hold values from -0.1875 to 0.1875
- in_values: float32 [4096], P('dp'), may hold values from 0.1 to 10
- out_basis: float32 [32, 4096, 1024], P('dp', 'mp'), may hold values from -0.1875 to 0.1875
- out_values: float32 [32, 4096], P('dp', 'mp'), may hold values from 0.1 to 10
Outputs:
- preconditioned: float32 [4096, 4096], P('dp', 'mp')
The draws below stay inside these ranges and needn't reach their ends.
Inputs may be any that keep to these rules, and one draw needn't show every extreme that they name: `feature_order`: each layer's features are split into 4 blocks of 1024. `block_slot`: every slot holds exactly one input block. `layer_owner`: distinct dp indices.
All inputs are finite; a program needn't handle non-finite values.
Results may differ from the reference program's by a relative error of at most 0.0003.
Values may be sent and summed in bfloat16 or wider, within the bound.
No kernel may reach another device: no remote copies, remote signals or barrier semaphores. Data moves between devices by JAX's collectives and lax.ppermute only.
A program may use at most 128 MiB of HBM per device.

```python
import math
import jax
import jax.numpy as jnp
from jax import lax

DIN = 4096
DOUT = 4096
BLK = 1024
LAYERS = 1
TOK_GRP = 128
PAIRS = 4
TOKENS = 4096
N_DP = 32


def level_of(stream_key, shape, shards, low, high):
    level = 1.0
    for position, blocks in shards:
        heights = jax.random.uniform(jax.random.fold_in(jax.random.fold_in(stream_key, 6), position), (blocks,), jnp.float32, low / len(shards), high / len(shards))
        level = level * jnp.repeat(jnp.exp(heights), shape[position] // blocks).reshape((-1,) + (1,) * (len(shape) - 1 - position))
    return level


def noise(stream_key, extent, deviation, most, pieces=(), kind=jnp.bfloat16):
    array = jax.random.normal(stream_key, extent, jnp.float32) * deviation
    if len(pieces) > 0:
        array = level_of(stream_key, extent, pieces, -0.22, 0.18) * array
    return jnp.clip(array, min=-most, max=most).astype(kind)


def setup_inputs(seed: int = 0) -> dict:
    keys = jax.random.split(jax.random.key(seed), 10)
    return {
        "layer_inputs": noise(keys[0], (TOKENS, LAYERS, DIN), 1.0, 6.0, ((0, 128),)),
        "output_grads": noise(keys[1], (TOKENS, LAYERS, DOUT), TOKENS ** -0.5, 0.09375, ((0, 32), (2, 4))),
        "feature_order": jax.vmap(lambda own: jax.random.permutation(own, DIN))(jax.random.split(keys[2], LAYERS)).reshape((LAYERS, DIN)).astype(jnp.int32),
        "block_slot": jax.random.permutation(keys[3], PAIRS).astype(jnp.int32),
        "layer_owner": jax.random.permutation(keys[4], N_DP).astype(jnp.int32),
        "in_basis": noise(keys[5], (PAIRS * BLK, BLK), BLK ** -0.5, 0.1875, ((0, 32),), jnp.float32),
        "in_values": jnp.clip(jnp.exp(math.log(10.0) - 4.6051702 * jax.random.uniform(keys[6], (PAIRS * BLK,), jnp.float32) ** level_of(keys[6], (PAIRS * BLK,), ((0, 32),), -0.2, 0.2)), 0.1, 10.0),
        "out_basis": noise(keys[7], (N_DP, DOUT, BLK), BLK ** -0.5, 0.1875, ((0, 32), (1, 4)), jnp.float32),
        "out_values": jnp.clip(jnp.exp(math.log(10.0) - 4.6051702 * jax.random.uniform(keys[8], (N_DP, DOUT), jnp.float32) ** level_of(keys[8], (N_DP, DOUT), ((0, 32), (1, 4)), -0.2, 0.2)), 0.1, 10.0),
    }


DAMPING = 0.1
HIGHEST_MODE = lax.Precision.HIGHEST


def kronecker_solve(grad_block, basis_in, vals_in, basis_out, vals_out):
    out_blocks = basis_out.shape[0]
    width = basis_in.shape[0]
    projected = jnp.dot(basis_in.T, grad_block, precision=HIGHEST_MODE).reshape(width, out_blocks, width)
    rotated = jnp.einsum('ajb,jbc->ajc', projected, basis_out, precision=HIGHEST_MODE)
    scaled = rotated / (vals_in[:, None, None] * vals_out[None, :, :] + DAMPING)
    restored = jnp.einsum('ajc,jbc->ajb', scaled, basis_out, precision=HIGHEST_MODE)
    return restored.reshape(width, out_blocks * width)


def reference(layer_inputs, output_grads, feature_order, block_slot, layer_owner, in_basis, in_values, out_basis, out_values):
    in_blocks = DIN // BLK
    pair_count = LAYERS * in_blocks
    inputs_all = layer_inputs.reshape(N_DP, TOK_GRP, LAYERS, DIN)
    grads_all = output_grads.reshape(N_DP, TOK_GRP, LAYERS, DOUT)

    def add_group(running, members):
        inputs_group = members[0].astype(jnp.float32)
        grads_group = members[1].astype(jnp.float32)
        partial_sum = jnp.einsum('tli,tlo->lio', inputs_group, grads_group)
        return running + partial_sum, None

    gradient, _ = lax.scan(add_group, jnp.zeros((LAYERS, DIN, DOUT), jnp.float32), (inputs_all, grads_all))
    pair_at_slot = jnp.zeros((pair_count,), jnp.int32).at[block_slot].set(jnp.arange(pair_count, dtype=jnp.int32))
    layer_of_slot = pair_at_slot // in_blocks
    permuted = jax.vmap(lambda matrix, picks: jnp.take(matrix, picks, axis=0))(gradient, feature_order)
    stacked = jnp.take(permuted.reshape(pair_count, BLK, DOUT), pair_at_slot, axis=0)
    owners = layer_owner[:LAYERS]
    owner_basis = jnp.take(out_basis, owners, axis=0)
    owner_values = jnp.take(out_values, owners, axis=0)
    out_blocks = DOUT // BLK

    def per_slot(members):
        grad_block, basis_in, vals_in, layer_id = members
        basis_out = jnp.take(owner_basis, layer_id, axis=0).reshape(out_blocks, BLK, BLK)
        vals_out = jnp.take(owner_values, layer_id, axis=0).reshape(out_blocks, BLK)
        restored = kronecker_solve(grad_block, basis_in, vals_in, basis_out, vals_out)
        return jnp.dot(basis_in, restored, precision=HIGHEST_MODE)

    result = lax.map(per_slot, (stacked, in_basis.reshape(pair_count, BLK, BLK), in_values.reshape(pair_count, BLK), layer_of_slot))
    return result.reshape(pair_count * BLK, DOUT)
```

```python
import jax
import jax.numpy as jnp
from jax import lax
from jax.sharding import Mesh, PartitionSpec as P

DIN = 4096
BLK = 1024
LANES = 128
GROUP = 256
DAMPING = 0.1
TOP = 32767.0
LOG_UNIT = 65536.0
VALUE_UNIT = 134217728.0
PAIR = ("h", "z")
ALL_DP = ("y", "h", "z")
PREC = lax.Precision.HIGH


def dot(a, b, dims):
    return lax.dot_general(a, b, (dims, ((), ())), precision=PREC, preferred_element_type=jnp.float32)


def pack_basis(basis, values):
    groups = BLK // GROUP
    most = jnp.max(jnp.abs(basis.reshape(BLK, groups, GROUP)), axis=2)
    code = jnp.ceil(jnp.log2(jnp.maximum(most, 1e-30)) * LOG_UNIT).astype(jnp.int32) + 1
    scale = jnp.exp2(code.astype(jnp.float32) / LOG_UNIT) / TOP
    inv = jnp.repeat(1.0 / scale, GROUP, axis=1)
    q = jnp.clip(jnp.round(basis * inv), -TOP, TOP).astype(jnp.int32)
    half = BLK // 2
    packed = jnp.bitwise_or(jnp.left_shift(q[:, half:], 16), jnp.bitwise_and(q[:, :half], 65535))
    packed = packed.reshape(32, 32, 4, LANES).transpose(0, 2, 1, 3).reshape(32, 128, LANES)
    coded = (values * VALUE_UNIT).astype(jnp.int32)
    side = jnp.concatenate([code.T.reshape(groups, 32, 32), coded.reshape(1, 32, 32)], 0)
    side = jnp.pad(side.transpose(1, 0, 2), ((0, 0), (0, 3), (0, LANES - 32)))
    return jnp.concatenate([packed, side], 1)


def unpack_basis(got):
    packed = got[:, :128].reshape(32, 4, 32, LANES).transpose(0, 2, 1, 3).reshape(BLK, BLK // 2)
    low = jnp.right_shift(jnp.left_shift(packed, 16), 16)
    high = jnp.right_shift(packed, 16)
    q = jnp.concatenate([low, high], 1).astype(jnp.float32)
    side = got[:, 128:133, :32]
    code = side[:, :4].transpose(1, 0, 2).reshape(4, BLK).T
    scale = jnp.exp2(code.astype(jnp.float32) / LOG_UNIT) / TOP
    basis = q * jnp.repeat(scale, GROUP, axis=1)
    values = side[:, 4].reshape(BLK).astype(jnp.float32) / VALUE_UNIT
    return basis, values


def body(
    layer_inputs,
    output_grads,
    feature_order,
    block_slot,
    layer_owner,
    in_basis,
    in_values,
    out_basis,
    out_values,
):
    side_rows = jnp.pad(in_values.reshape(1, LANES), ((0, 7), (0, BLK - LANES)))
    in_all = lax.all_gather(jnp.concatenate([in_basis, side_rows], 0), PAIR)
    basis_in = in_all[:, :128].reshape(BLK, BLK)
    vals_in = in_all[:, 128, :LANES].reshape(BLK)

    pair_at_slot = jnp.zeros((4,), jnp.int32).at[block_slot].set(jnp.arange(4, dtype=jnp.int32))
    order = jnp.take(feature_order.reshape(4, BLK), pair_at_slot, axis=0).reshape(-1)
    mine = layer_inputs.reshape(32, DIN)
    columns = jnp.take(mine, order, axis=1)
    chunks = columns.reshape(32, 8, 512).transpose(1, 0, 2)
    chunks = lax.all_to_all(chunks, ("y", "h"), 0, 0, tiled=True)
    tokens = lax.all_to_all(jnp.broadcast_to(chunks[None], (4, 8, 32, 512)), ("l", "c"), 0, 0, tiled=True)
    tokens = tokens.transpose(1, 0, 2, 3).reshape(1024, 512)

    grads = output_grads.reshape(128, BLK)
    grads = lax.all_to_all(jnp.broadcast_to(grads[None], (8, 128, BLK)), ("y", "h"), 0, 0, tiled=True)
    grads = grads.reshape(1024, BLK)

    part = lax.dot_general(tokens, grads, (((0,), (0,)), ((), ())), preferred_element_type=jnp.float32)
    parts = lax.all_to_all(part.reshape(4, 128, BLK), "z", 0, 0, tiled=True)
    grad_rows = parts.sum(0)

    spread = lax.all_to_all(pack_basis(out_basis[0], out_values[0]), ALL_DP, 0, 0, tiled=True)
    piece = lax.dynamic_index_in_dim(spread, layer_owner[0], 0, keepdims=True)
    got = lax.all_to_all(jnp.broadcast_to(piece, spread.shape), ALL_DP, 0, 0, tiled=True)
    basis_out, vals_out = unpack_basis(got)

    v = dot(grad_rows, basis_out, ((1,), (0,)))
    v = v.reshape(128, 8, LANES).transpose(1, 0, 2)
    v = lax.all_to_all(v, PAIR, 0, 0, tiled=True).reshape(BLK, LANES)
    r = dot(basis_in, v, ((0,), (0,)))
    me = lax.axis_index(PAIR)
    lb = lax.dynamic_slice(vals_out, (me * LANES,), (LANES,))
    s = r / (vals_in[:, None] * lb[None, :] + DAMPING)
    u = dot(basis_in, s, ((1,), (0,)))
    u = lax.all_to_all(u.reshape(8, 128, LANES), PAIR, 0, 0, tiled=True)
    u = u.transpose(1, 0, 2).reshape(128, BLK)
    return dot(u, basis_out, ((1,), (1,)))


def solution(mesh):
    fine = Mesh(mesh.devices.reshape(4, 2, 4, 2, 2), ("y", "h", "z", "l", "c"))
    dp, mp = ("y", "h", "z"), ("l", "c")
    in_specs = (
        P(dp + mp, None, None),
        P(dp, None, mp),
        P(),
        P(),
        P(),
        P(dp, None),
        P(dp),
        P(dp, mp, None),
        P(dp, mp),
    )
    return jax.shard_map(body, mesh=fine, in_specs=in_specs, out_specs=P(dp, mp), check_vma=False)
```

```python
import functools
import jax
import jax.numpy as jnp
from jax import lax
from jax.experimental import pallas as pl
from jax.experimental.pallas import tpu as pltpu
from jax.sharding import Mesh, PartitionSpec as P

DIN = 4096
BLK = 1024
LANES = 128
GROUP = 256
ROWS = 136
DAMPING = 0.1
TOP = 32767.0
LOG_UNIT = 65536.0
VALUE_UNIT = 134217728.0
PAIR = ("h", "z")
ALL_DP = ("y", "h", "z")
VMEM = 48 * 1024 * 1024
f32, bf16, i32 = jnp.float32, jnp.bfloat16, jnp.int32


def params(*semantics):
    return pltpu.CompilerParams(vmem_limit_bytes=VMEM, dimension_semantics=semantics or None)


def mul(a, b, ca=1, cb=0):
    return lax.dot_general(a, b, (((ca,), (cb,)), ((), ())), preferred_element_type=f32)


def halves(a):
    high = a.astype(bf16)
    return high, (a - high.astype(f32)).astype(bf16)


def gather_kernel(order_ref, x_ref, out_ref):
    x = x_ref[...].astype(f32)
    for b in range(4):
        idx = order_ref[:, b * LANES:(b + 1) * LANES]
        lane = jnp.broadcast_to(jnp.bitwise_and(idx, LANES - 1), (32, LANES))
        src = jnp.broadcast_to(jnp.right_shift(idx, 7), (32, LANES))
        acc = jnp.zeros((32, LANES), f32)
        for k in range(DIN // LANES):
            got = jnp.take_along_axis(x[:, k * LANES:(k + 1) * LANES], lane, axis=1)
            acc = jnp.where(src == k, got, acc)
        out_ref[0, :, b * LANES:(b + 1) * LANES] = acc.astype(bf16)


def gather_columns(order, x):
    return pl.pallas_call(
        gather_kernel,
        grid=(8,),
        in_specs=[pl.BlockSpec((1, 512), lambda i: (0, i)), pl.BlockSpec((32, DIN), lambda i: (0, 0))],
        out_specs=pl.BlockSpec((1, 32, 512), lambda i: (i, 0, 0)),
        out_shape=jax.ShapeDtypeStruct((8, 32, 512), bf16),
        compiler_params=params("arbitrary"),
        cost_estimate=pl.CostEstimate(flops=10**6, bytes_accessed=10**6, transcendentals=0),
    )(order, x)


def pack_kernel(basis_ref, values_ref, out_ref):
    eye = lax.broadcasted_iota(i32, (LANES, LANES), 0) == lax.broadcasted_iota(i32, (LANES, LANES), 1)
    coded = (values_ref[...] * VALUE_UNIT).astype(i32)
    for d in range(4):
        codes = []
        for g in range(4):
            part = basis_ref[d * 32:(d + 1) * 32, g * GROUP:(g + 1) * GROUP]
            most = jnp.maximum(jnp.max(jnp.abs(part), axis=1, keepdims=True), 1e-30)
            code = jnp.ceil(jnp.log2(most) * LOG_UNIT) + 1.0
            scale = jnp.exp2(code / LOG_UNIT) / TOP
            q = jnp.clip(jnp.round(part / scale), -TOP, TOP).astype(i32)
            word = jnp.bitwise_or(jnp.left_shift(q[:, LANES:], 16), jnp.bitwise_and(q[:, :LANES], 65535))
            out_ref[d, g * 32:(g + 1) * 32, :] = word
            codes.append(code.astype(i32))
        column = jnp.concatenate(codes, axis=0)
        row = jnp.sum(jnp.where(eye, column, 0), axis=0, keepdims=True)
        out_ref[d, LANES:ROWS, :] = jnp.concatenate([row, coded, jnp.zeros((6, LANES), i32)], axis=0)


def pack_basis(basis, values):
    return pl.pallas_call(
        pack_kernel,
        grid=(8,),
        in_specs=[pl.BlockSpec((LANES, BLK), lambda i: (i, 0)), pl.BlockSpec((1, LANES), lambda i: (0, i))],
        out_specs=pl.BlockSpec((4, ROWS, LANES), lambda i: (i, 0, 0)),
        out_shape=jax.ShapeDtypeStruct((32, ROWS, LANES), i32),
        compiler_params=params("arbitrary"),
        cost_estimate=pl.CostEstimate(flops=10**7, bytes_accessed=6 * 10**6, transcendentals=0),
    )(basis, values)


def front_kernel(got_ref, parts_ref, v_ref, high_ref, low_ref):
    step = pl.program_id(0)
    eye = lax.broadcasted_iota(i32, (LANES, LANES), 0) == lax.broadcasted_iota(i32, (LANES, LANES), 1)
    for d in range(4):
        row = got_ref[d, LANES:LANES + 1, :]
        column = jnp.sum(jnp.where(eye, row, 0), axis=1, keepdims=True)
        scale = jnp.exp2(column.astype(f32) / LOG_UNIT) / TOP
        for g in range(4):
            word = got_ref[d, g * 32:(g + 1) * 32, :]
            unit = scale[g * 32:(g + 1) * 32]
            first = jnp.right_shift(jnp.left_shift(word, 16), 16).astype(f32) * unit
            second = jnp.right_shift(word, 16).astype(f32) * unit
            for k, value in ((0, first), (1, second)):
                high, low = halves(value)
                where = (slice(d * 32, (d + 1) * 32), slice(g * GROUP + k * LANES, g * GROUP + (k + 1) * LANES))
                high_ref[where] = high
                low_ref[where] = low
    grad = parts_ref[0] + parts_ref[1] + parts_ref[2] + parts_ref[3]
    grad_high, grad_low = halves(grad)
    both = mul(jnp.concatenate([grad_high, grad_low], axis=0), high_ref[...])
    v = both[:LANES] + both[LANES:] + mul(grad_high, low_ref[...])
    for c in range(8):
        piece = v[:, c * LANES:(c + 1) * LANES]
        v_ref[c] = jnp.where(step == 0, piece, v_ref[c] + piece)


def front(got, parts):
    return pl.pallas_call(
        front_kernel,
        grid=(8,),
        in_specs=[
            pl.BlockSpec((4, ROWS, LANES), lambda i: (i, 0, 0)),
            pl.BlockSpec((4, LANES, LANES), lambda i: (0, 0, i)),
        ],
        out_specs=[
            pl.BlockSpec((8, LANES, LANES), lambda i: (0, 0, 0)),
            pl.BlockSpec((LANES, BLK), lambda i: (i, 0)),
            pl.BlockSpec((LANES, BLK), lambda i: (i, 0)),
        ],
        out_shape=[
            jax.ShapeDtypeStruct((8, LANES, LANES), f32),
            jax.ShapeDtypeStruct((BLK, BLK), bf16),
            jax.ShapeDtypeStruct((BLK, BLK), bf16),
        ],
        compiler_params=params("arbitrary"),
        cost_estimate=pl.CostEstimate(flops=8 * 10**8, bytes_accessed=9 * 10**6, transcendentals=0),
    )(got, parts)


def middle_kernel(v_ref, high_ref, low_ref, la_ref, lb_ref, u_ref):
    v = v_ref[...].reshape(BLK, LANES)
    v_high, v_low = halves(v)
    qh, ql = high_ref[...], low_ref[...]
    both = mul(jnp.concatenate([v_high, v_low], axis=1), qh, 0, 0)
    rt = both[:LANES] + both[LANES:] + mul(v_high, ql, 0, 0)
    st = rt / (lb_ref[...] * la_ref[...] + DAMPING)
    s_high, s_low = halves(st)
    both = mul(jnp.concatenate([s_high, s_low], axis=0), qh, 1, 1)
    ut = both[:LANES] + both[LANES:] + mul(s_high, ql, 1, 1)
    for c in range(8):
        u_ref[c] = ut[:, c * LANES:(c + 1) * LANES]


def middle(v, high, low, la, lb):
    return pl.pallas_call(
        middle_kernel,
        out_shape=jax.ShapeDtypeStruct((8, LANES, LANES), f32),
        compiler_params=params(),
        cost_estimate=pl.CostEstimate(flops=16 * 10**8, bytes_accessed=6 * 10**6, transcendentals=0),
    )(v, high, low, la, lb)


def back_kernel(u_ref, high_ref, low_ref, out_ref):
    u_high, u_low = halves(u_ref[...].reshape(BLK, LANES).T)
    both = mul(jnp.concatenate([u_high, u_low], axis=0), high_ref[...], 1, 1)
    out_ref[...] = both[:LANES] + both[LANES:] + mul(u_high, low_ref[...], 1, 1)


def back(u, high, low):
    return pl.pallas_call(
        back_kernel,
        grid=(4,),
        in_specs=[
            pl.BlockSpec((8, LANES, LANES), lambda i: (0, 0, 0)),
            pl.BlockSpec((GROUP, BLK), lambda i: (i, 0)),
            pl.BlockSpec((GROUP, BLK), lambda i: (i, 0)),
        ],
        out_specs=pl.BlockSpec((LANES, GROUP), lambda i: (0, i)),
        out_shape=jax.ShapeDtypeStruct((LANES, BLK), f32),
        compiler_params=params("arbitrary"),
        cost_estimate=pl.CostEstimate(flops=8 * 10**8, bytes_accessed=5 * 10**6, transcendentals=0),
    )(u, high, low)


def body(
    layer_inputs,
    output_grads,
    feature_order,
    block_slot,
    layer_owner,
    in_basis,
    in_values,
    out_basis,
    out_values,
):
    packed = pack_basis(out_basis[0], out_values)
    spread = lax.all_to_all(packed, ALL_DP, 0, 0, tiled=True)

    side_rows = jnp.pad(in_values.reshape(1, LANES), ((0, 7), (0, BLK - LANES)))
    in_all = lax.all_gather(jnp.concatenate([in_basis, side_rows], 0), PAIR)
    basis_in = in_all[:, :LANES].reshape(BLK, BLK)
    rounded = lax.reduce_precision(basis_in, 8, 7)
    in_high, in_low = rounded.astype(bf16), (basis_in - rounded).astype(bf16)
    la = in_all[:, LANES, :LANES].reshape(1, BLK)

    grads = output_grads.reshape(LANES, BLK)
    grads = lax.all_to_all(jnp.broadcast_to(grads[None], (8, LANES, BLK)), ("y", "h"), 0, 0, tiled=True)
    grads = grads.reshape(BLK, BLK)

    pair_at_slot = jnp.zeros((4,), i32).at[block_slot].set(jnp.arange(4, dtype=i32))
    order = jnp.take(feature_order.reshape(4, BLK), pair_at_slot, axis=0).reshape(1, DIN)
    chunks = gather_columns(order, layer_inputs.reshape(32, DIN))
    chunks = jnp.broadcast_to(chunks[:, None], (8, 4, 32, 512)).reshape(32, 32, 512)
    tokens = lax.all_to_all(chunks, ("y", "h", "l", "c"), 0, 0, tiled=True).reshape(BLK, 512)

    part = lax.dot_general(tokens, grads, (((0,), (0,)), ((), ())), preferred_element_type=f32)
    parts = lax.all_to_all(part.reshape(4, LANES, BLK), "z", 0, 0, tiled=True)

    piece = lax.dynamic_index_in_dim(spread, layer_owner[0], 0, keepdims=True)
    got = lax.all_to_all(jnp.broadcast_to(piece, spread.shape), ALL_DP, 0, 0, tiled=True)

    v, out_high, out_low = front(got, parts)
    v = lax.all_to_all(v, PAIR, 0, 0, tiled=True)
    me = lax.axis_index(PAIR)
    lb = lax.dynamic_index_in_dim(got[::4, LANES + 1], me, 0, keepdims=False).astype(f32) / VALUE_UNIT
    u = middle(v, in_high, in_low, la, lb.reshape(LANES, 1))
    u = lax.all_to_all(u, PAIR, 0, 0, tiled=True)
    return back(u, out_high, out_low)


def solution(mesh):
    fine = Mesh(mesh.devices.reshape(4, 2, 4, 2, 2), ("y", "h", "z", "l", "c"))
    dp, mp = ("y", "h", "z"), ("l", "c")
    in_specs = (
        P(dp + mp, None, None),
        P(dp, None, mp),
        P(),
        P(),
        P(),
        P(dp, None),
        P(dp),
        P(dp, mp, None),
        P(dp, mp),
    )
    return jax.shard_map(body, mesh=fine, in_specs=in_specs, out_specs=P(dp, mp), check_vma=False)
```

```python
import jax
import jax.numpy as jnp
from jax import lax
from jax.experimental import pallas as pl
from jax.experimental.pallas import tpu as pltpu
from jax.sharding import Mesh, PartitionSpec as P

DIN = 4096
BLK = 1024
LANES = 128
GROUP = 256
ROWS = 136
DAMPING = 0.1
TOP = 32767.0
LOG_UNIT = 65536.0
VALUE_UNIT = 134217728.0
PAIR = ("h", "z")
ALL_DP = ("y", "h", "z")
VMEM = 48 * 1024 * 1024
f32, bf16, i32 = jnp.float32, jnp.bfloat16, jnp.int32


def params(*semantics):
    return pltpu.CompilerParams(vmem_limit_bytes=VMEM, dimension_semantics=semantics or None)


def mul(a, b, ca=1, cb=0):
    return lax.dot_general(a, b, (((ca,), (cb,)), ((), ())), preferred_element_type=f32)


def halves(a):
    high = a.astype(bf16)
    return high, (a - high.astype(f32)).astype(bf16)


def gather_kernel(me_ref, order_ref, x_ref, out_ref):
    i = pl.program_id(0)
    slot = lax.rem(me_ref[0] + i // 2, 4)
    half = lax.rem(me_ref[1] + lax.rem(i, 2), 2)
    pair = sum(jnp.where(me_ref[4 + j] == slot, j, 0) for j in range(4))
    start = pair * BLK + half * 512
    for b in range(4):
        idx = order_ref[:, pl.ds(pl.multiple_of(start + b * LANES, LANES), LANES)]
        lane = jnp.broadcast_to(jnp.bitwise_and(idx, LANES - 1), (32, LANES))
        src = jnp.broadcast_to(jnp.right_shift(idx, 7), (32, LANES))
        acc = jnp.zeros((32, LANES), f32)
        for k in range(DIN // LANES):
            x = x_ref[:, k * LANES:(k + 1) * LANES].astype(f32)
            acc = jnp.where(src == k, jnp.take_along_axis(x, lane, axis=1), acc)
        out_ref[0, :, b * LANES:(b + 1) * LANES] = acc.astype(bf16)


def gather_columns(me, order, x):
    return pl.pallas_call(
        gather_kernel,
        grid=(8,),
        in_specs=[
            pl.BlockSpec(memory_space=pltpu.SMEM),
            pl.BlockSpec((1, DIN), lambda i: (0, 0)),
            pl.BlockSpec((32, DIN), lambda i: (0, 0)),
        ],
        out_specs=pl.BlockSpec((1, 32, 512), lambda i: (i, 0, 0)),
        out_shape=jax.ShapeDtypeStruct((8, 32, 512), bf16),
        compiler_params=params("arbitrary"),
        cost_estimate=pl.CostEstimate(flops=10**6, bytes_accessed=10**6, transcendentals=0),
    )(me, order, x)


def diagonal():
    return lax.broadcasted_iota(i32, (LANES, LANES), 0) == lax.broadcasted_iota(i32, (LANES, LANES), 1)


def encode(part):
    most = jnp.maximum(jnp.max(jnp.abs(part), axis=1, keepdims=True), 1e-30)
    code = jnp.ceil(jnp.log2(most) * LOG_UNIT) + 1.0
    q = jnp.round(part * (TOP * jnp.exp2(-code / LOG_UNIT)))
    q = jnp.clip(q, -TOP, TOP).astype(i32)
    word = jnp.bitwise_or(jnp.left_shift(q[:, LANES:], 16), jnp.bitwise_and(q[:, :LANES], 65535))
    return word, code.astype(i32)


def decode(word, unit):
    first = jnp.right_shift(jnp.left_shift(word, 16), 16).astype(f32) * unit
    return first, jnp.right_shift(word, 16).astype(f32) * unit


def to_row(column, eye):
    return jnp.sum(jnp.where(eye, column, 0), axis=0, keepdims=True)


def to_unit(row, eye):
    return jnp.exp2(jnp.sum(jnp.where(eye, row, 0), axis=1, keepdims=True).astype(f32) / LOG_UNIT) / TOP


def pack_kernel(basis_ref, values_ref, out_ref):
    eye = diagonal()
    coded = (values_ref[...] * VALUE_UNIT).astype(i32)
    for d in range(4):
        codes = []
        for g in range(4):
            word, code = encode(basis_ref[d * 32:(d + 1) * 32, g * GROUP:(g + 1) * GROUP])
            out_ref[d, g * 32:(g + 1) * 32, :] = word
            codes.append(code)
        row = to_row(jnp.concatenate(codes, axis=0), eye)
        out_ref[d, LANES:ROWS, :] = jnp.concatenate([row, coded, jnp.zeros((6, LANES), i32)], axis=0)


def pack_basis(basis, values):
    steps = basis.shape[0] // LANES
    return pl.pallas_call(
        pack_kernel,
        grid=(steps,),
        in_specs=[pl.BlockSpec((LANES, BLK), lambda i: (i, 0)), pl.BlockSpec((1, LANES), lambda i: (0, i))],
        out_specs=pl.BlockSpec((4, ROWS, LANES), lambda i: (i, 0, 0)),
        out_shape=jax.ShapeDtypeStruct((steps * 4, ROWS, LANES), i32),
        compiler_params=params("arbitrary"),
        cost_estimate=pl.CostEstimate(flops=steps * 10**6, bytes_accessed=steps * 800000, transcendentals=0),
    )(basis, values)


def decode_chunks(got_ref, count, high_ref, low_ref, eye):
    for d in range(count):
        unit = to_unit(got_ref[d, LANES:LANES + 1, :], eye)
        for g in range(4):
            pair = decode(got_ref[d, g * 32:(g + 1) * 32, :], unit[g * 32:(g + 1) * 32])
            for k in range(2):
                high, low = halves(pair[k])
                where = (slice(d * 32, (d + 1) * 32), slice(g * GROUP + k * LANES, g * GROUP + (k + 1) * LANES))
                high_ref[where] = high
                low_ref[where] = low


def unpack_kernel(got_ref, high_ref, low_ref):
    decode_chunks(got_ref, 8, high_ref, low_ref, diagonal())


def unpack_basis(got):
    return pl.pallas_call(
        unpack_kernel,
        grid=(4,),
        in_specs=[pl.BlockSpec((8, ROWS, LANES), lambda i: (i, 0, 0))],
        out_specs=[pl.BlockSpec((GROUP, BLK), lambda i: (i, 0))] * 2,
        out_shape=[jax.ShapeDtypeStruct((BLK, BLK), bf16)] * 2,
        compiler_params=params("arbitrary"),
        cost_estimate=pl.CostEstimate(flops=10**7, bytes_accessed=6 * 10**6, transcendentals=0),
    )(got)


def partial_kernel(me_ref, *refs):
    x_refs, g_refs = refs[:4], refs[4:12]
    own_ref, word_refs, tokens, total = refs[12], refs[13:16], refs[16], refs[17]
    for j in range(4):
        place = jnp.bitwise_xor(me_ref[3], j)
        for r in range(8):
            tokens[pl.ds(pl.multiple_of(r * LANES + place * 32, 32), 32), :] = x_refs[j][r]
    for r in range(4):
        grads = jnp.concatenate([g_refs[2 * r][...], g_refs[2 * r + 1][...]], axis=0)
        part = mul(tokens[r * GROUP:(r + 1) * GROUP, :], grads, 0, 0)
        total[...] = part if r == 0 else total[...] + part
    eye = diagonal()
    for k in range(4):
        start = pl.multiple_of(lax.rem(me_ref[2] + k, 4) * LANES, LANES)
        if k == 0:
            own_ref[...] = total[pl.ds(start, LANES), :]
            continue
        rows = []
        for g in range(4):
            word, code = encode(total[pl.ds(start, LANES), g * GROUP:(g + 1) * GROUP])
            word_refs[k - 1][g * LANES:(g + 1) * LANES, :] = word
            rows.append(to_row(code, eye))
        word_refs[k - 1][4 * LANES:, :] = jnp.concatenate(rows + [jnp.zeros((4, LANES), i32)], axis=0)


def partial_rows(me, tokens, grads):
    vmem = pl.BlockSpec(memory_space=pltpu.VMEM)
    return pl.pallas_call(
        partial_kernel,
        in_specs=[pl.BlockSpec(memory_space=pltpu.SMEM)] + [vmem] * 12,
        out_specs=[vmem] * 4,
        out_shape=[jax.ShapeDtypeStruct((LANES, BLK), f32)] + [jax.ShapeDtypeStruct((520, LANES), i32)] * 3,
        scratch_shapes=[pltpu.VMEM((BLK, 512), bf16), pltpu.VMEM((512, BLK), f32)],
        compiler_params=params(),
        cost_estimate=pl.CostEstimate(flops=10**9, bytes_accessed=5 * 10**6, transcendentals=0),
    )(me, *tokens, *grads)


def front_kernel(got_ref, own_ref, w1_ref, w2_ref, w3_ref, v_ref, high_ref, low_ref, grad):
    step = pl.program_id(0)
    eye = diagonal()
    decode_chunks(got_ref, 8, high_ref, low_ref, eye)

    @pl.when(step == 0)
    def _():
        for g in range(4):
            sums = [own_ref[:, g * GROUP:g * GROUP + LANES], own_ref[:, g * GROUP + LANES:(g + 1) * GROUP]]
            for ref in (w1_ref, w2_ref, w3_ref):
                unit = to_unit(ref[4 * LANES + g:4 * LANES + g + 1, :], eye)
                pair = decode(ref[g * LANES:(g + 1) * LANES, :], unit)
                sums = [sums[0] + pair[0], sums[1] + pair[1]]
            grad[g] = jnp.concatenate(sums, axis=1)

    grad_high, grad_low = halves(grad[step])
    both = mul(jnp.concatenate([grad_high, grad_low], axis=0), high_ref[...])
    v = both[:LANES] + both[LANES:] + mul(grad_high, low_ref[...])
    for c in range(8):
        piece = v[:, c * LANES:(c + 1) * LANES]
        v_ref[c] = jnp.where(step == 0, piece, v_ref[c] + piece)


def front(got, own, words):
    whole = lambda i: (0, 0)
    return pl.pallas_call(
        front_kernel,
        grid=(4,),
        in_specs=[pl.BlockSpec((8, ROWS, LANES), lambda i: (i, 0, 0)), pl.BlockSpec((LANES, BLK), whole)]
        + [pl.BlockSpec((520, LANES), whole)] * 3,
        out_specs=[pl.BlockSpec((8, LANES, LANES), lambda i: (0, 0, 0))]
        + [pl.BlockSpec((GROUP, BLK), lambda i: (i, 0))] * 2,
        out_shape=[jax.ShapeDtypeStruct((8, LANES, LANES), f32)] + [jax.ShapeDtypeStruct((BLK, BLK), bf16)] * 2,
        scratch_shapes=[pltpu.VMEM((4, LANES, GROUP), f32)],
        compiler_params=params("arbitrary"),
        cost_estimate=pl.CostEstimate(flops=8 * 10**8, bytes_accessed=8 * 10**6, transcendentals=0),
    )(got, own, *words)


def middle_kernel(v_ref, high_ref, low_ref, la_ref, lb_ref, u_ref):
    v = v_ref[...].reshape(BLK, LANES)
    v_high, v_low = halves(v)
    qh, ql = high_ref[...], low_ref[...]
    both = mul(jnp.concatenate([v_high, v_low], axis=1), qh, 0, 0)
    rt = both[:LANES] + both[LANES:] + mul(v_high, ql, 0, 0)
    st = rt / (lb_ref[...] * la_ref[...] + DAMPING)
    s_high, s_low = halves(st)
    both = mul(jnp.concatenate([s_high, s_low], axis=0), qh, 1, 1)
    ut = both[:LANES] + both[LANES:] + mul(s_high, ql, 1, 1)
    for c in range(8):
        u_ref[c] = ut[:, c * LANES:(c + 1) * LANES]


def middle(v, high, low, la, lb):
    return pl.pallas_call(
        middle_kernel,
        out_shape=jax.ShapeDtypeStruct((8, LANES, LANES), f32),
        compiler_params=params(),
        cost_estimate=pl.CostEstimate(flops=16 * 10**8, bytes_accessed=6 * 10**6, transcendentals=0),
    )(v, high, low, la, lb)


def back_kernel(u_ref, high_ref, low_ref, out_ref):
    u_high, u_low = halves(u_ref[...].reshape(BLK, LANES).T)
    both = mul(jnp.concatenate([u_high, u_low], axis=0), high_ref[...], 1, 1)
    out_ref[...] = both[:LANES] + both[LANES:] + mul(u_high, low_ref[...], 1, 1)


def back(u, high, low):
    return pl.pallas_call(
        back_kernel,
        grid=(4,),
        in_specs=[
            pl.BlockSpec((8, LANES, LANES), lambda i: (0, 0, 0)),
            pl.BlockSpec((GROUP, BLK), lambda i: (i, 0)),
            pl.BlockSpec((GROUP, BLK), lambda i: (i, 0)),
        ],
        out_specs=pl.BlockSpec((LANES, GROUP), lambda i: (0, i)),
        out_shape=jax.ShapeDtypeStruct((LANES, BLK), f32),
        compiler_params=params("arbitrary"),
        cost_estimate=pl.CostEstimate(flops=8 * 10**8, bytes_accessed=5 * 10**6, transcendentals=0),
    )(u, high, low)


def body(
    layer_inputs,
    output_grads,
    feature_order,
    block_slot,
    layer_owner,
    in_basis,
    in_values,
    out_basis,
    out_values,
):
    me = jnp.stack([lax.axis_index("y"), lax.axis_index("h"), lax.axis_index("z"), lax.axis_index(("l", "c"))])
    me = jnp.concatenate([me.astype(i32), block_slot])

    packed = pack_basis(out_basis[0], out_values)
    spread = lax.all_to_all(packed, ALL_DP, 0, 0, tiled=True)

    grads = [output_grads.reshape(LANES, BLK)]
    grads.append(across(grads[0]))
    grads = [along(g, "y", k) for k in range(4) for g in grads]

    chunks = gather_columns(me, feature_order, layer_inputs.reshape(32, DIN))
    moved = [chunks[0]]
    for i in range(1, 8):
        route = [(y * 2 + h, (y + i // 2) % 4 * 2 + (h + i) % 2) for y in range(4) for h in range(2)]
        moved.append(lax.ppermute(chunks[i], ("y", "h"), route))
    moved = jnp.stack(moved)
    tokens = [moved] + [lax.ppermute(moved, ("l", "c"), [(m, m ^ j) for m in range(4)]) for j in range(1, 4)]

    in_all = lax.all_gather(pack_basis(in_basis, in_values.reshape(1, LANES)), PAIR, tiled=True)

    own, *words = partial_rows(me, tokens, grads)
    words = [along(w, "z", k + 1) for k, w in enumerate(words)]

    piece = lax.dynamic_index_in_dim(spread, layer_owner[0], 0, keepdims=True)
    got = lax.all_to_all(jnp.broadcast_to(piece, spread.shape), ALL_DP, 0, 0, tiled=True)

    v, out_high, out_low = front(got, own, words)
    v = lax.all_to_all(v, PAIR, 0, 0, tiled=True)
    in_high, in_low = unpack_basis(in_all)
    la = (in_all[::4, LANES + 1].astype(f32) / VALUE_UNIT).reshape(1, BLK)
    lb = lax.dynamic_index_in_dim(got[::4, LANES + 1], lax.axis_index(PAIR), 0, keepdims=False)
    u = middle(v, in_high, in_low, la, lb.astype(f32).reshape(LANES, 1) / VALUE_UNIT)
    u = lax.all_to_all(u, PAIR, 0, 0, tiled=True)
    return back(u, out_high, out_low)


def along(block, axis, shift):
    if shift == 0:
        return block
    return lax.ppermute(block, axis, [(i, (i + shift) % 4) for i in range(4)])


def across(block):
    return lax.ppermute(block, "h", [(0, 1), (1, 0)])


def solution(mesh):
    fine = Mesh(mesh.devices.reshape(4, 2, 4, 2, 2), ("y", "h", "z", "l", "c"))
    dp, mp = ("y", "h", "z"), ("l", "c")
    in_specs = (
        P(dp + mp, None, None),
        P(dp, None, mp),
        P(),
        P(),
        P(),
        P(dp, None),
        P(dp),
        P(dp, mp, None),
        P(dp, mp),
    )
    return jax.shard_map(body, mesh=fine, in_specs=in_specs, out_specs=P(dp, mp), check_vma=False)
```

```python
import jax
import jax.numpy as jnp
from jax import lax
from jax.experimental import pallas as pl
from jax.experimental.pallas import tpu as pltpu
from jax.sharding import Mesh, PartitionSpec as P

DIN = 4096
BLK = 1024
LANES = 128
GROUP = 256
ROWS = 136
DAMPING = 0.1
TOP = 32767.0
LOG_UNIT = 65536.0
VALUE_UNIT = 134217728.0
PAIR = ("h", "z")
ALL_DP = ("y", "h", "z")
VMEM = 48 * 1024 * 1024
f32, bf16, i32 = jnp.float32, jnp.bfloat16, jnp.int32


def params(*semantics):
    return pltpu.CompilerParams(vmem_limit_bytes=VMEM, dimension_semantics=semantics or None)


def mul(a, b, ca=1, cb=0):
    return lax.dot_general(a, b, (((ca,), (cb,)), ((), ())), preferred_element_type=f32)


def halves(a):
    high = a.astype(bf16)
    return high, (a - high.astype(f32)).astype(bf16)


def gather_kernel(me_ref, order_ref, x_ref, out_ref):
    i = pl.program_id(0)
    slot = lax.rem(me_ref[0] + i // 2, 4)
    half = lax.rem(me_ref[1] + lax.rem(i, 2), 2)
    pair = sum(jnp.where(me_ref[4 + j] == slot, j, 0) for j in range(4))
    start = pair * BLK + half * 512
    for b in range(4):
        idx = order_ref[:, pl.ds(pl.multiple_of(start + b * LANES, LANES), LANES)]
        lane = jnp.broadcast_to(jnp.bitwise_and(idx, LANES - 1), (32, LANES))
        src = jnp.broadcast_to(jnp.right_shift(idx, 7), (32, LANES))
        acc = jnp.zeros((32, LANES), f32)
        for k in range(DIN // LANES):
            x = x_ref[:, k * LANES:(k + 1) * LANES].astype(f32)
            acc = jnp.where(src == k, jnp.take_along_axis(x, lane, axis=1), acc)
        out_ref[0, :, b * LANES:(b + 1) * LANES] = acc.astype(bf16)


def gather_columns(me, order, x):
    return pl.pallas_call(
        gather_kernel,
        grid=(8,),
        in_specs=[
            pl.BlockSpec(memory_space=pltpu.SMEM),
            pl.BlockSpec((1, DIN), lambda i: (0, 0)),
            pl.BlockSpec((32, DIN), lambda i: (0, 0)),
        ],
        out_specs=pl.BlockSpec((1, 32, 512), lambda i: (i, 0, 0)),
        out_shape=jax.ShapeDtypeStruct((8, 32, 512), bf16),
        compiler_params=params("arbitrary"),
        cost_estimate=pl.CostEstimate(flops=10**6, bytes_accessed=10**6, transcendentals=0),
    )(me, order, x)


def diagonal():
    return lax.broadcasted_iota(i32, (LANES, LANES), 0) == lax.broadcasted_iota(i32, (LANES, LANES), 1)


def encode(part):
    most = jnp.maximum(jnp.max(jnp.abs(part), axis=1, keepdims=True), 1e-30)
    code = jnp.ceil(jnp.log2(most) * LOG_UNIT) + 4.0
    q = jnp.round(part * (TOP * jnp.exp2(-code / LOG_UNIT))).astype(i32)
    word = jnp.bitwise_or(jnp.left_shift(q[:, LANES:], 16), jnp.bitwise_and(q[:, :LANES], 65535))
    return word, code.astype(i32)


def decode(word, unit):
    first = jnp.right_shift(jnp.left_shift(word, 16), 16).astype(f32) * unit
    return first, jnp.right_shift(word, 16).astype(f32) * unit


def to_row(column, eye):
    return jnp.sum(jnp.where(eye, column, 0), axis=0, keepdims=True)


def to_unit(row, eye):
    return jnp.exp2(jnp.sum(jnp.where(eye, row, 0), axis=1, keepdims=True).astype(f32) / LOG_UNIT) / TOP


def pack_kernel(basis_ref, values_ref, out_ref):
    eye = diagonal()
    coded = (values_ref[...] * VALUE_UNIT).astype(i32)
    codes = [[] for _ in range(4)]
    for g in range(4):
        word, code = encode(basis_ref[:, g * GROUP:(g + 1) * GROUP])
        for d in range(4):
            out_ref[d, g * 32:(g + 1) * 32, :] = word[d * 32:(d + 1) * 32]
            codes[d].append(code[d * 32:(d + 1) * 32])
    for d in range(4):
        row = to_row(jnp.concatenate(codes[d], axis=0), eye)
        out_ref[d, LANES:ROWS, :] = jnp.concatenate([row, coded, jnp.zeros((6, LANES), i32)], axis=0)


def pack_basis(basis, values):
    steps = basis.shape[0] // LANES
    return pl.pallas_call(
        pack_kernel,
        grid=(steps,),
        in_specs=[pl.BlockSpec((LANES, BLK), lambda i: (i, 0)), pl.BlockSpec((1, LANES), lambda i: (0, i))],
        out_specs=pl.BlockSpec((4, ROWS, LANES), lambda i: (i, 0, 0)),
        out_shape=jax.ShapeDtypeStruct((steps * 4, ROWS, LANES), i32),
        compiler_params=params("arbitrary"),
        cost_estimate=pl.CostEstimate(flops=steps * 10**6, bytes_accessed=steps * 800000, transcendentals=0),
    )(basis, values)


def decode_chunks(got_ref, count, high_ref, low_ref, eye):
    for d in range(count):
        unit = to_unit(got_ref[d, LANES:LANES + 1, :], eye)
        for g in range(4):
            pair = decode(got_ref[d, g * 32:(g + 1) * 32, :], unit[g * 32:(g + 1) * 32])
            for k in range(2):
                high, low = halves(pair[k])
                where = (slice(d * 32, (d + 1) * 32), slice(g * GROUP + k * LANES, g * GROUP + (k + 1) * LANES))
                high_ref[where] = high
                low_ref[where] = low


def unpack_kernel(got_ref, high_ref, low_ref):
    decode_chunks(got_ref, 8, high_ref, low_ref, diagonal())


def unpack_basis(got):
    return pl.pallas_call(
        unpack_kernel,
        grid=(4,),
        in_specs=[pl.BlockSpec((8, ROWS, LANES), lambda i: (i, 0, 0))],
        out_specs=[pl.BlockSpec((GROUP, BLK), lambda i: (i, 0))] * 2,
        out_shape=[jax.ShapeDtypeStruct((BLK, BLK), bf16)] * 2,
        compiler_params=params("arbitrary"),
        cost_estimate=pl.CostEstimate(flops=10**7, bytes_accessed=6 * 10**6, transcendentals=0),
    )(got)


def partial_kernel(me_ref, *refs):
    x_refs, g_refs = refs[:4], refs[4:6]
    own_ref, word_refs, tokens, total = refs[6], refs[7:10], refs[10], refs[11]
    for j in range(4):
        place = jnp.bitwise_xor(me_ref[3], j)
        for r in range(8):
            tokens[pl.ds(pl.multiple_of(r * LANES + place * 32, 32), 32), :] = x_refs[j][r]
    for r in range(4):
        place = lax.rem(me_ref[0] + 4 - r, 4)
        grads = jnp.concatenate([g_refs[0][place], g_refs[1][place]], axis=0)
        part = mul(tokens[r * GROUP:(r + 1) * GROUP, :], grads, 0, 0)
        total[...] = part if r == 0 else total[...] + part
    eye = diagonal()
    for k in range(4):
        start = pl.multiple_of(lax.rem(me_ref[2] + k, 4) * LANES, LANES)
        if k == 0:
            own_ref[...] = total[pl.ds(start, LANES), :]
            continue
        rows = []
        for g in range(4):
            word, code = encode(total[pl.ds(start, LANES), g * GROUP:(g + 1) * GROUP])
            word_refs[k - 1][g * LANES:(g + 1) * LANES, :] = word
            rows.append(to_row(code, eye))
        word_refs[k - 1][4 * LANES:, :] = jnp.concatenate(rows + [jnp.zeros((4, LANES), i32)], axis=0)


def partial_rows(me, tokens, grads):
    vmem = pl.BlockSpec(memory_space=pltpu.VMEM)
    return pl.pallas_call(
        partial_kernel,
        in_specs=[pl.BlockSpec(memory_space=pltpu.SMEM)] + [vmem] * 6,
        out_specs=[vmem] * 4,
        out_shape=[jax.ShapeDtypeStruct((LANES, BLK), f32)] + [jax.ShapeDtypeStruct((520, LANES), i32)] * 3,
        scratch_shapes=[pltpu.VMEM((BLK, 512), bf16), pltpu.VMEM((512, BLK), f32)],
        compiler_params=params(),
        cost_estimate=pl.CostEstimate(flops=10**9, bytes_accessed=5 * 10**6, transcendentals=0),
    )(me, *tokens, *grads)


def front_kernel(got_ref, own_ref, w1_ref, w2_ref, w3_ref, v_ref, high_ref, low_ref, grad):
    step = pl.program_id(0)
    eye = diagonal()
    decode_chunks(got_ref, 8, high_ref, low_ref, eye)

    @pl.when(step == 0)
    def _():
        for g in range(4):
            sums = [own_ref[:, g * GROUP:g * GROUP + LANES], own_ref[:, g * GROUP + LANES:(g + 1) * GROUP]]
            for ref in (w1_ref, w2_ref, w3_ref):
                unit = to_unit(ref[4 * LANES + g:4 * LANES + g + 1, :], eye)
                pair = decode(ref[g * LANES:(g + 1) * LANES, :], unit)
                sums = [sums[0] + pair[0], sums[1] + pair[1]]
            grad[g] = jnp.concatenate(sums, axis=1)

    grad_high, grad_low = halves(grad[step])
    both = mul(jnp.concatenate([grad_high, grad_low], axis=0), high_ref[...])
    v = both[:LANES] + both[LANES:] + mul(grad_high, low_ref[...])
    for c in range(8):
        piece = v[:, c * LANES:(c + 1) * LANES]
        v_ref[c] = jnp.where(step == 0, piece, v_ref[c] + piece)


def front(got, own, words):
    whole = lambda i: (0, 0)
    return pl.pallas_call(
        front_kernel,
        grid=(4,),
        in_specs=[pl.BlockSpec((8, ROWS, LANES), lambda i: (i, 0, 0)), pl.BlockSpec((LANES, BLK), whole)]
        + [pl.BlockSpec((520, LANES), whole)] * 3,
        out_specs=[pl.BlockSpec((8, LANES, LANES), lambda i: (0, 0, 0))]
        + [pl.BlockSpec((GROUP, BLK), lambda i: (i, 0))] * 2,
        out_shape=[jax.ShapeDtypeStruct((8, LANES, LANES), f32)] + [jax.ShapeDtypeStruct((BLK, BLK), bf16)] * 2,
        scratch_shapes=[pltpu.VMEM((4, LANES, GROUP), f32)],
        compiler_params=params("arbitrary"),
        cost_estimate=pl.CostEstimate(flops=8 * 10**8, bytes_accessed=8 * 10**6, transcendentals=0),
    )(got, own, *words)


def middle_kernel(me_ref, v_ref, high_ref, low_ref, in_side_ref, out_side_ref, u_ref):
    v = v_ref[...].reshape(BLK, LANES)
    v_high, v_low = halves(v)
    qh, ql = high_ref[...], low_ref[...]
    both = mul(jnp.concatenate([v_high, v_low], axis=1), qh, 0, 0)
    rt = both[:LANES] + both[LANES:] + mul(v_high, ql, 0, 0)
    la = jnp.concatenate([in_side_ref[4 * c, 1:2, :] for c in range(8)], axis=1).astype(f32) / VALUE_UNIT
    lb = jnp.sum(jnp.where(diagonal(), out_side_ref[0, 1:2, :], 0), axis=1, keepdims=True).astype(f32) / VALUE_UNIT
    st = rt / (lb * la + DAMPING)
    s_high, s_low = halves(st)
    both = mul(jnp.concatenate([s_high, s_low], axis=0), qh, 1, 1)
    ut = both[:LANES] + both[LANES:] + mul(s_high, ql, 1, 1)
    for c in range(8):
        u_ref[c] = ut[:, c * LANES:(c + 1) * LANES]


def middle(me, v, high, low, in_all, got):
    whole = lambda i, m: (0, 0)
    return pl.pallas_call(
        middle_kernel,
        grid_spec=pltpu.PrefetchScalarGridSpec(
            num_scalar_prefetch=1,
            grid=(1,),
            in_specs=[
                pl.BlockSpec((8, LANES, LANES), lambda i, m: (0, 0, 0)),
                pl.BlockSpec((BLK, BLK), whole),
                pl.BlockSpec((BLK, BLK), whole),
                pl.BlockSpec((32, 8, LANES), lambda i, m: (0, 16, 0)),
                pl.BlockSpec((1, 8, LANES), lambda i, m: (4 * (m[1] * 4 + m[2]), 16, 0)),
            ],
            out_specs=pl.BlockSpec((8, LANES, LANES), lambda i, m: (0, 0, 0)),
        ),
        out_shape=jax.ShapeDtypeStruct((8, LANES, LANES), f32),
        compiler_params=params("arbitrary"),
        cost_estimate=pl.CostEstimate(flops=16 * 10**8, bytes_accessed=6 * 10**6, transcendentals=0),
    )(me, v, high, low, in_all, got)


def back_kernel(u_ref, high_ref, low_ref, out_ref):
    u_high, u_low = halves(u_ref[...].reshape(BLK, LANES).T)
    both = mul(jnp.concatenate([u_high, u_low], axis=0), high_ref[...], 1, 1)
    out_ref[...] = both[:LANES] + both[LANES:] + mul(u_high, low_ref[...], 1, 1)


def back(u, high, low):
    return pl.pallas_call(
        back_kernel,
        grid=(4,),
        in_specs=[
            pl.BlockSpec((8, LANES, LANES), lambda i: (0, 0, 0)),
            pl.BlockSpec((GROUP, BLK), lambda i: (i, 0)),
            pl.BlockSpec((GROUP, BLK), lambda i: (i, 0)),
        ],
        out_specs=pl.BlockSpec((LANES, GROUP), lambda i: (0, i)),
        out_shape=jax.ShapeDtypeStruct((LANES, BLK), f32),
        compiler_params=params("arbitrary"),
        cost_estimate=pl.CostEstimate(flops=8 * 10**8, bytes_accessed=5 * 10**6, transcendentals=0),
    )(u, high, low)


def body(
    layer_inputs,
    output_grads,
    feature_order,
    block_slot,
    layer_owner,
    in_basis,
    in_values,
    out_basis,
    out_values,
):
    me = jnp.stack([lax.axis_index("y"), lax.axis_index("h"), lax.axis_index("z"), lax.axis_index(("l", "c"))])
    me = jnp.concatenate([me.astype(i32), block_slot])

    packed = pack_basis(out_basis[0], out_values)
    spread = lax.all_to_all(packed, ALL_DP, 0, 0, tiled=True)

    grads = [lax.all_gather(output_grads.reshape(LANES, BLK), "y")]
    grads.append(across(grads[0]))

    chunks = gather_columns(me, feature_order, layer_inputs.reshape(32, DIN))
    moved = [chunks[0]]
    for i in range(1, 8):
        route = [(y * 2 + h, (y + i // 2) % 4 * 2 + (h + i) % 2) for y in range(4) for h in range(2)]
        moved.append(lax.ppermute(chunks[i], ("y", "h"), route))
    moved = jnp.stack(moved)
    tokens = [moved] + [lax.ppermute(moved, ("l", "c"), [(m, m ^ j) for m in range(4)]) for j in range(1, 4)]

    in_all = lax.all_gather(pack_basis(in_basis, in_values.reshape(1, LANES)), PAIR, tiled=True)
    in_high, in_low = unpack_basis(in_all)

    piece = lax.dynamic_index_in_dim(spread, layer_owner[0], 0, keepdims=True)
    piece, *tokens = lax.optimization_barrier((piece, *tokens))
    got = lax.all_to_all(jnp.broadcast_to(piece, spread.shape), ALL_DP, 0, 0, tiled=True)

    own, *words = partial_rows(me, tokens, grads)
    words = [along(w, "z", k + 1) for k, w in enumerate(words)]

    own, in_high, in_low = lax.optimization_barrier((own, in_high, in_low))
    v, out_high, out_low = front(got, own, words)
    v = lax.all_to_all(v, PAIR, 0, 0, tiled=True)
    u = middle(me, v, in_high, in_low, in_all, got)
    u = lax.all_to_all(u, PAIR, 0, 0, tiled=True)
    return back(u, out_high, out_low)


def along(block, axis, shift):
    if shift == 0:
        return block
    return lax.ppermute(block, axis, [(i, (i + shift) % 4) for i in range(4)])


def across(block):
    return lax.ppermute(block, "h", [(0, 1), (1, 0)])


def solution(mesh):
    fine = Mesh(mesh.devices.reshape(4, 2, 4, 2, 2), ("y", "h", "z", "l", "c"))
    dp, mp = ("y", "h", "z"), ("l", "c")
    in_specs = (
        P(dp + mp, None, None),
        P(dp, None, mp),
        P(),
        P(),
        P(),
        P(dp, None),
        P(dp),
        P(dp, mp, None),
        P(dp, mp),
    )
    return jax.shard_map(body, mesh=fine, in_specs=in_specs, out_specs=P(dp, mp), check_vma=False)
```

```python
import jax
import jax.numpy as jnp
from jax import lax
from jax.experimental import pallas as pl
from jax.experimental.pallas import tpu as pltpu
from jax.sharding import Mesh, PartitionSpec as P

DIN = 4096
BLK = 1024
LANES = 128
GROUP = 256
ROWS = 136
DAMPING = 0.1
TOP = 32767.0
LOG_UNIT = 65536.0
VALUE_UNIT = 134217728.0
PAIR = ("h", "z")
ALL_DP = ("y", "h", "z")
VMEM = 48 * 1024 * 1024
f32, bf16, i32 = jnp.float32, jnp.bfloat16, jnp.int32


def params(*semantics):
    return pltpu.CompilerParams(vmem_limit_bytes=VMEM, dimension_semantics=semantics or None)


def mul(a, b, ca=1, cb=0):
    return lax.dot_general(a, b, (((ca,), (cb,)), ((), ())), preferred_element_type=f32)


def halves(a):
    high = a.astype(bf16)
    return high, (a - high.astype(f32)).astype(bf16)


def gather_kernel(me_ref, order_ref, x_ref, out_ref):
    i = pl.program_id(0)
    pair = sum(jnp.where(me_ref[4 + j] == i // 2, j, 0) for j in range(4))
    start = pair * BLK + lax.rem(i, 2) * 512
    for b in range(4):
        idx = order_ref[:, pl.ds(pl.multiple_of(start + b * LANES, LANES), LANES)]
        lane = jnp.broadcast_to(jnp.bitwise_and(idx, LANES - 1), (32, LANES))
        src = jnp.broadcast_to(jnp.right_shift(idx, 7), (32, LANES))
        acc = jnp.zeros((32, LANES), f32)
        for k in range(DIN // LANES):
            x = x_ref[:, k * LANES:(k + 1) * LANES].astype(f32)
            acc = jnp.where(src == k, jnp.take_along_axis(x, lane, axis=1), acc)
        for m in range(4):
            out_ref[m, :, b * LANES:(b + 1) * LANES] = acc.astype(bf16)


def gather_columns(me, order, x):
    return pl.pallas_call(
        gather_kernel,
        grid=(8,),
        in_specs=[
            pl.BlockSpec(memory_space=pltpu.SMEM),
            pl.BlockSpec((1, DIN), lambda i: (0, 0)),
            pl.BlockSpec((32, DIN), lambda i: (0, 0)),
        ],
        out_specs=pl.BlockSpec((4, 32, 512), lambda i: (i, 0, 0)),
        out_shape=jax.ShapeDtypeStruct((32, 32, 512), bf16),
        compiler_params=params("arbitrary"),
        cost_estimate=pl.CostEstimate(flops=10**6, bytes_accessed=10**6, transcendentals=0),
    )(me, order, x)


def diagonal():
    return lax.broadcasted_iota(i32, (LANES, LANES), 0) == lax.broadcasted_iota(i32, (LANES, LANES), 1)


def encode(part):
    most = jnp.maximum(jnp.max(jnp.abs(part), axis=1, keepdims=True), 1e-30)
    code = jnp.ceil(jnp.log2(most) * LOG_UNIT) + 4.0
    q = jnp.round(part * (TOP * jnp.exp2(-code / LOG_UNIT))).astype(i32)
    word = jnp.bitwise_or(jnp.left_shift(q[:, LANES:], 16), jnp.bitwise_and(q[:, :LANES], 65535))
    return word, code.astype(i32)


def decode(word, unit):
    first = jnp.right_shift(jnp.left_shift(word, 16), 16).astype(f32) * unit
    return first, jnp.right_shift(word, 16).astype(f32) * unit


def to_row(column, eye):
    return jnp.sum(jnp.where(eye, column, 0), axis=0, keepdims=True)


def to_unit(row, eye):
    return jnp.exp2(jnp.sum(jnp.where(eye, row, 0), axis=1, keepdims=True).astype(f32) / LOG_UNIT) / TOP


def pack_kernel(basis_ref, values_ref, out_ref):
    eye = diagonal()
    blocks = values_ref.shape[1] // LANES
    codes = [[] for _ in range(4)]
    for g in range(4):
        word, code = encode(basis_ref[:, g * GROUP:(g + 1) * GROUP])
        for d in range(4):
            out_ref[d, g * 32:(g + 1) * 32, :] = word[d * 32:(d + 1) * 32]
            codes[d].append(code[d * 32:(d + 1) * 32])
    for d in range(4):
        row = to_row(jnp.concatenate(codes[d], axis=0), eye)
        block = lax.rem(pl.program_id(0) * 4 + d, blocks)
        coded = (values_ref[:, pl.ds(pl.multiple_of(block * LANES, LANES), LANES)] * VALUE_UNIT).astype(i32)
        out_ref[d, LANES:ROWS, :] = jnp.concatenate([row, coded, jnp.zeros((6, LANES), i32)], axis=0)


def pack_basis(basis, values):
    steps = basis.shape[0] // LANES
    return pl.pallas_call(
        pack_kernel,
        grid=(steps,),
        in_specs=[pl.BlockSpec((LANES, BLK), lambda i: (i, 0)), pl.BlockSpec(values.shape, lambda i: (0, 0))],
        out_specs=pl.BlockSpec((4, ROWS, LANES), lambda i: (i, 0, 0)),
        out_shape=jax.ShapeDtypeStruct((steps * 4, ROWS, LANES), i32),
        compiler_params=params("arbitrary"),
        cost_estimate=pl.CostEstimate(flops=steps * 10**6, bytes_accessed=steps * 800000, transcendentals=0),
    )(basis, values)


def decode_chunks(got_ref, count, high_ref, low_ref, eye):
    for d in range(count):
        unit = to_unit(got_ref[d, LANES:LANES + 1, :], eye)
        for g in range(4):
            pair = decode(got_ref[d, g * 32:(g + 1) * 32, :], unit[g * 32:(g + 1) * 32])
            for k in range(2):
                high, low = halves(pair[k])
                where = (slice(d * 32, (d + 1) * 32), slice(g * GROUP + k * LANES, g * GROUP + (k + 1) * LANES))
                high_ref[where] = high
                low_ref[where] = low


def unpack_kernel(got_ref, high_ref, low_ref):
    decode_chunks(got_ref, 8, high_ref, low_ref, diagonal())


def unpack_basis(got):
    return pl.pallas_call(
        unpack_kernel,
        grid=(4,),
        in_specs=[pl.BlockSpec((8, ROWS, LANES), lambda i: (i, 0, 0))],
        out_specs=[pl.BlockSpec((GROUP, BLK), lambda i: (i, 0))] * 2,
        out_shape=[jax.ShapeDtypeStruct((BLK, BLK), bf16)] * 2,
        compiler_params=params("arbitrary"),
        cost_estimate=pl.CostEstimate(flops=10**7, bytes_accessed=6 * 10**6, transcendentals=0),
    )(got)


def partial_kernel(me_ref, tokens_ref, grads_ref, *refs):
    own_ref, word_refs, total = refs[0], refs[1:4], refs[4]
    for r in range(4):
        grads = jnp.concatenate([grads_ref[r, me_ref[1]], grads_ref[r, 1 - me_ref[1]]], axis=0)
        part = mul(tokens_ref[r * GROUP:(r + 1) * GROUP, :], grads, 0, 0)
        total[...] = part if r == 0 else total[...] + part
    eye = diagonal()
    for k in range(4):
        start = pl.multiple_of(lax.rem(me_ref[2] + k, 4) * LANES, LANES)
        if k == 0:
            own_ref[...] = total[pl.ds(start, LANES), :]
            continue
        rows = []
        for g in range(4):
            word, code = encode(total[pl.ds(start, LANES), g * GROUP:(g + 1) * GROUP])
            word_refs[k - 1][g * LANES:(g + 1) * LANES, :] = word
            rows.append(to_row(code, eye))
        word_refs[k - 1][4 * LANES:, :] = jnp.concatenate(rows + [jnp.zeros((4, LANES), i32)], axis=0)


def partial_rows(me, tokens, grads):
    vmem = pl.BlockSpec(memory_space=pltpu.VMEM)
    return pl.pallas_call(
        partial_kernel,
        in_specs=[pl.BlockSpec(memory_space=pltpu.SMEM)] + [vmem] * 2,
        out_specs=[vmem] * 4,
        out_shape=[jax.ShapeDtypeStruct((LANES, BLK), f32)] + [jax.ShapeDtypeStruct((520, LANES), i32)] * 3,
        scratch_shapes=[pltpu.VMEM((512, BLK), f32)],
        compiler_params=params(),
        cost_estimate=pl.CostEstimate(flops=10**9, bytes_accessed=5 * 10**6, transcendentals=0),
    )(me, tokens, grads)


def front_kernel(me_ref, p0_ref, p1_ref, p2_ref, p3_ref, own_ref, w1_ref, w2_ref, w3_ref, v_ref, high_ref, low_ref, grad):
    step = pl.program_id(0)
    eye = diagonal()
    for j, piece_ref in enumerate((p0_ref, p1_ref, p2_ref, p3_ref)):
        pl.when(step == j)(lambda ref=piece_ref: decode_chunks(ref, 8, high_ref, low_ref, eye))

    @pl.when(step == 0)
    def _():
        for g in range(4):
            sums = [own_ref[:, g * GROUP:g * GROUP + LANES], own_ref[:, g * GROUP + LANES:(g + 1) * GROUP]]
            for ref in (w1_ref, w2_ref, w3_ref):
                unit = to_unit(ref[4 * LANES + g:4 * LANES + g + 1, :], eye)
                pair = decode(ref[g * LANES:(g + 1) * LANES, :], unit)
                sums = [sums[0] + pair[0], sums[1] + pair[1]]
            grad[g] = jnp.concatenate(sums, axis=1)

    grad_high, grad_low = halves(grad[lax.rem(me_ref[0] + 4 - step, 4)])
    both = mul(jnp.concatenate([grad_high, grad_low], axis=0), high_ref[...])
    v = both[:LANES] + both[LANES:] + mul(grad_high, low_ref[...])
    for c in range(8):
        part = v[:, c * LANES:(c + 1) * LANES]
        v_ref[c] = jnp.where(step == 0, part, v_ref[c] + part)


def front(me, pieces, own, words):
    whole = lambda i, m: (0, 0)
    rows = lambda i, m: (lax.rem(m[0] + 4 - i, 4), 0)
    return pl.pallas_call(
        front_kernel,
        grid_spec=pltpu.PrefetchScalarGridSpec(
            num_scalar_prefetch=1,
            grid=(4,),
            in_specs=[pl.BlockSpec((8, ROWS, LANES), lambda i, m: (0, 0, 0))] * 4
            + [pl.BlockSpec((LANES, BLK), whole)]
            + [pl.BlockSpec((520, LANES), whole)] * 3,
            out_specs=[pl.BlockSpec((8, LANES, LANES), lambda i, m: (0, 0, 0))] + [pl.BlockSpec((GROUP, BLK), rows)] * 2,
            scratch_shapes=[pltpu.VMEM((4, LANES, GROUP), f32)],
        ),
        out_shape=[jax.ShapeDtypeStruct((8, LANES, LANES), f32)] + [jax.ShapeDtypeStruct((BLK, BLK), bf16)] * 2,
        compiler_params=params("arbitrary"),
        cost_estimate=pl.CostEstimate(flops=8 * 10**8, bytes_accessed=8 * 10**6, transcendentals=0),
    )(me, *pieces, own, *words)


def middle_kernel(v_ref, high_ref, low_ref, in_side_ref, out_side_ref, u_ref):
    v = v_ref[...].reshape(BLK, LANES)
    v_high, v_low = halves(v)
    qh, ql = high_ref[...], low_ref[...]
    both = mul(jnp.concatenate([v_high, v_low], axis=1), qh, 0, 0)
    rt = both[:LANES] + both[LANES:] + mul(v_high, ql, 0, 0)
    la = jnp.concatenate([in_side_ref[4 * c, 1:2, :] for c in range(8)], axis=1).astype(f32) / VALUE_UNIT
    lb = jnp.sum(jnp.where(diagonal(), out_side_ref[0, 1:2, :], 0), axis=1, keepdims=True).astype(f32) / VALUE_UNIT
    st = rt / (lb * la + DAMPING)
    s_high, s_low = halves(st)
    both = mul(jnp.concatenate([s_high, s_low], axis=0), qh, 1, 1)
    ut = both[:LANES] + both[LANES:] + mul(s_high, ql, 1, 1)
    for c in range(8):
        u_ref[c] = ut[:, c * LANES:(c + 1) * LANES]


def middle(v, high, low, in_all, piece):
    whole = lambda i: (0, 0)
    return pl.pallas_call(
        middle_kernel,
        grid=(1,),
        in_specs=[
            pl.BlockSpec((8, LANES, LANES), lambda i: (0, 0, 0)),
            pl.BlockSpec((BLK, BLK), whole),
            pl.BlockSpec((BLK, BLK), whole),
            pl.BlockSpec((32, 8, LANES), lambda i: (0, 16, 0)),
            pl.BlockSpec((1, 8, LANES), lambda i: (0, 16, 0)),
        ],
        out_specs=pl.BlockSpec((8, LANES, LANES), lambda i: (0, 0, 0)),
        out_shape=jax.ShapeDtypeStruct((8, LANES, LANES), f32),
        compiler_params=params("arbitrary"),
        cost_estimate=pl.CostEstimate(flops=16 * 10**8, bytes_accessed=6 * 10**6, transcendentals=0),
    )(v, high, low, in_all, piece)


def back_kernel(u_ref, high_ref, low_ref, out_ref):
    u_high, u_low = halves(u_ref[...].reshape(BLK, LANES).T)
    both = mul(jnp.concatenate([u_high, u_low], axis=0), high_ref[...], 1, 1)
    out_ref[...] = both[:LANES] + both[LANES:] + mul(u_high, low_ref[...], 1, 1)


def back(u, high, low):
    return pl.pallas_call(
        back_kernel,
        grid=(4,),
        in_specs=[
            pl.BlockSpec((8, LANES, LANES), lambda i: (0, 0, 0)),
            pl.BlockSpec((GROUP, BLK), lambda i: (i, 0)),
            pl.BlockSpec((GROUP, BLK), lambda i: (i, 0)),
        ],
        out_specs=pl.BlockSpec((LANES, GROUP), lambda i: (0, i)),
        out_shape=jax.ShapeDtypeStruct((LANES, BLK), f32),
        compiler_params=params("arbitrary"),
        cost_estimate=pl.CostEstimate(flops=8 * 10**8, bytes_accessed=5 * 10**6, transcendentals=0),
    )(u, high, low)


def body(
    layer_inputs,
    output_grads,
    feature_order,
    block_slot,
    layer_owner,
    in_basis,
    in_values,
    out_basis,
    out_values,
):
    me = jnp.stack([lax.axis_index("y"), lax.axis_index("h"), lax.axis_index("z"), lax.axis_index(("l", "c"))])
    me = jnp.concatenate([me.astype(i32), block_slot])

    packed = pack_basis(out_basis[0], out_values).reshape(8, 4, ROWS, LANES)
    my_z = lax.axis_index("z")
    owner = layer_owner[0]
    back_z = (my_z + 4 - owner % 4) % 4
    stage = [lax.dynamic_index_in_dim(packed, (my_z + k) % 4, 1, keepdims=False) for k in range(4)]
    stage = lax.select_n(back_z, *[along(part, "z", k) for k, part in enumerate(stage)])
    stage = lax.all_to_all(stage, ("y", "h"), 0, 0, tiled=True)
    piece = lax.dynamic_index_in_dim(stage, owner // 4, 0, keepdims=True)

    grads = output_grads.reshape(LANES, BLK)
    grads = lax.all_gather(jnp.stack([grads, across(grads)]), "y")

    chunks = gather_columns(me, feature_order, layer_inputs.reshape(32, DIN))
    tokens = lax.all_to_all(chunks, ("y", "h", "l", "c"), 0, 0, tiled=True).reshape(BLK, 512)

    in_all = lax.all_gather(pack_basis(in_basis, in_values.reshape(1, LANES)), PAIR, tiled=True)
    in_high, in_low = unpack_basis(in_all)

    own, *words = partial_rows(me, tokens, grads)
    words = [along(w, "z", k + 1) for k, w in enumerate(words)]

    pieces = lax.all_to_all(jnp.broadcast_to(piece, (8, ROWS, LANES)), PAIR, 0, 0, tiled=True)
    pieces = [along(pieces, "y", k) for k in range(4)]

    own, in_high, in_low = lax.optimization_barrier((own, in_high, in_low))
    v, out_high, out_low = front(me, pieces, own, words)
    v = lax.all_to_all(v, PAIR, 0, 0, tiled=True)
    u = middle(v, in_high, in_low, in_all, piece)
    u = lax.all_to_all(u, PAIR, 0, 0, tiled=True)
    return back(u, out_high, out_low)


def along(block, axis, shift):
    if shift == 0:
        return block
    return lax.ppermute(block, axis, [(i, (i + shift) % 4) for i in range(4)])


def across(block):
    return lax.ppermute(block, "h", [(0, 1), (1, 0)])


def solution(mesh):
    fine = Mesh(mesh.devices.reshape(4, 2, 4, 2, 2), ("y", "h", "z", "l", "c"))
    dp, mp = ("y", "h", "z"), ("l", "c")
    in_specs = (
        P(dp + mp, None, None),
        P(dp, None, mp),
        P(),
        P(),
        P(),
        P(dp, None),
        P(dp),
        P(dp, mp, None),
        P(dp, mp),
    )
    return jax.shard_map(body, mesh=fine, in_specs=in_specs, out_specs=P(dp, mp), check_vma=False)
```

```python
import jax
import jax.numpy as jnp
from jax import lax
from jax.experimental import pallas as pl
from jax.experimental.pallas import tpu as pltpu
from jax.sharding import Mesh, PartitionSpec as P

DIN = 4096
BLK = 1024
LANES = 128
GROUP = 256
ROWS = 136
DAMPING = 0.1
TOP = 32767.0
LOG_UNIT = 65536.0
VALUE_UNIT = 134217728.0
PAIR = ("h", "z")
ALL_DP = ("y", "h", "z")
VMEM = 60 * 1024 * 1024
f32, bf16, i32 = jnp.float32, jnp.bfloat16, jnp.int32


def params(*semantics):
    return pltpu.CompilerParams(vmem_limit_bytes=VMEM, dimension_semantics=semantics or None)


def mul(a, b, ca=1, cb=0):
    return lax.dot_general(a, b, (((ca,), (cb,)), ((), ())), preferred_element_type=f32)


def halves(a):
    high = a.astype(bf16)
    return high, (a - high.astype(f32)).astype(bf16)


def gather_kernel(me_ref, order_ref, x_ref, out_ref):
    i = pl.program_id(0)
    pair = sum(jnp.where(me_ref[4 + j] == i // 2, j, 0) for j in range(4))
    start = pair * BLK + lax.rem(i, 2) * 512
    for b in range(4):
        idx = order_ref[:, pl.ds(pl.multiple_of(start + b * LANES, LANES), LANES)]
        lane = jnp.broadcast_to(jnp.bitwise_and(idx, LANES - 1), (32, LANES))
        src = jnp.broadcast_to(jnp.right_shift(idx, 7), (32, LANES))
        acc = jnp.zeros((32, LANES), f32)
        for k in range(DIN // LANES):
            x = x_ref[:, k * LANES:(k + 1) * LANES].astype(f32)
            acc = jnp.where(src == k, jnp.take_along_axis(x, lane, axis=1), acc)
        out_ref[0, :, b * LANES:(b + 1) * LANES] = acc.astype(bf16)


def gather_columns(me, order, x):
    return pl.pallas_call(
        gather_kernel,
        grid=(8,),
        in_specs=[
            pl.BlockSpec(memory_space=pltpu.SMEM),
            pl.BlockSpec((1, DIN), lambda i: (0, 0)),
            pl.BlockSpec((32, DIN), lambda i: (0, 0)),
        ],
        out_specs=pl.BlockSpec((1, 32, 512), lambda i: (i, 0, 0)),
        out_shape=jax.ShapeDtypeStruct((8, 32, 512), bf16),
        compiler_params=params("arbitrary"),
        cost_estimate=pl.CostEstimate(flops=10**6, bytes_accessed=10**6, transcendentals=0),
    )(me, order, x)


def diagonal():
    return lax.broadcasted_iota(i32, (LANES, LANES), 0) == lax.broadcasted_iota(i32, (LANES, LANES), 1)


def encode(part):
    most = jnp.maximum(jnp.max(jnp.abs(part), axis=1, keepdims=True), 1e-30)
    code = jnp.ceil(jnp.log2(most) * LOG_UNIT) + 4.0
    q = jnp.round(part * (TOP * jnp.exp2(-code / LOG_UNIT))).astype(i32)
    word = jnp.bitwise_or(jnp.left_shift(q[:, LANES:], 16), jnp.bitwise_and(q[:, :LANES], 65535))
    return word, code.astype(i32)


def decode(word, unit):
    first = jnp.right_shift(jnp.left_shift(word, 16), 16).astype(f32) * unit
    return first, jnp.right_shift(word, 16).astype(f32) * unit


def to_row(column, eye):
    return jnp.sum(jnp.where(eye, column, 0), axis=0, keepdims=True)


def to_unit(row, eye):
    return jnp.exp2(jnp.sum(jnp.where(eye, row, 0), axis=1, keepdims=True).astype(f32) / LOG_UNIT) / TOP


def pack_kernel(basis_ref, values_ref, out_ref):
    eye = diagonal()
    blocks = values_ref.shape[1] // LANES
    codes = [[] for _ in range(4)]
    for g in range(4):
        word, code = encode(basis_ref[:, g * GROUP:(g + 1) * GROUP])
        for d in range(4):
            out_ref[d, g * 32:(g + 1) * 32, :] = word[d * 32:(d + 1) * 32]
            codes[d].append(code[d * 32:(d + 1) * 32])
    for d in range(4):
        row = to_row(jnp.concatenate(codes[d], axis=0), eye)
        block = lax.rem(pl.program_id(0) * 4 + d, blocks)
        coded = (values_ref[:, pl.ds(pl.multiple_of(block * LANES, LANES), LANES)] * VALUE_UNIT).astype(i32)
        out_ref[d, LANES:ROWS, :] = jnp.concatenate([row, coded, jnp.zeros((6, LANES), i32)], axis=0)


def pack_basis(basis, values):
    steps = basis.shape[0] // LANES
    return pl.pallas_call(
        pack_kernel,
        grid=(steps,),
        in_specs=[pl.BlockSpec((LANES, BLK), lambda i: (i, 0)), pl.BlockSpec(values.shape, lambda i: (0, 0))],
        out_specs=pl.BlockSpec((4, ROWS, LANES), lambda i: (i, 0, 0)),
        out_shape=jax.ShapeDtypeStruct((steps * 4, ROWS, LANES), i32),
        compiler_params=params("arbitrary"),
        cost_estimate=pl.CostEstimate(flops=steps * 10**6, bytes_accessed=steps * 800000, transcendentals=0),
    )(basis, values)


def decode_chunks(got_ref, count, high_ref, low_ref, eye):
    for d in range(count):
        unit = to_unit(got_ref[d, LANES:LANES + 1, :], eye)
        for g in range(4):
            pair = decode(got_ref[d, g * 32:(g + 1) * 32, :], unit[g * 32:(g + 1) * 32])
            for k in range(2):
                high, low = halves(pair[k])
                where = (slice(d * 32, (d + 1) * 32), slice(g * GROUP + k * LANES, g * GROUP + (k + 1) * LANES))
                high_ref[where] = high
                low_ref[where] = low


def unpack_kernel(me_ref, got_ref, high_ref, low_ref, side_ref):
    decode_chunks(got_ref.at[0, 0], 4, high_ref, low_ref, diagonal())
    side_ref[0] = got_ref[0, 0, 0, LANES:ROWS, :]


def unpack_basis(me, got):
    rows = lambda i, m: (i, 0)
    return pl.pallas_call(
        unpack_kernel,
        grid_spec=pltpu.PrefetchScalarGridSpec(
            num_scalar_prefetch=1,
            grid=(8,),
            in_specs=[
                pl.BlockSpec((1, 1, 4, ROWS, LANES), lambda i, m: (lax.rem(i, 4), lax.rem(i // 4 + m[1], 2), 0, 0, 0))
            ],
            out_specs=[pl.BlockSpec((LANES, BLK), rows)] * 2 + [pl.BlockSpec((1, 8, LANES), lambda i, m: (i, 0, 0))],
        ),
        out_shape=[jax.ShapeDtypeStruct((BLK, BLK), bf16)] * 2 + [jax.ShapeDtypeStruct((8, 8, LANES), i32)],
        compiler_params=params("arbitrary"),
        cost_estimate=pl.CostEstimate(flops=10**7, bytes_accessed=6 * 10**6, transcendentals=0),
    )(me, got)


def partial_kernel(me_ref, x0_ref, x1_ref, x2_ref, x3_ref, grads_ref, *refs):
    own_ref, word_refs, tokens, total = refs[0], refs[1:4], refs[4], refs[5]
    for j, x_ref in enumerate((x0_ref, x1_ref, x2_ref, x3_ref)):
        place = jnp.bitwise_xor(me_ref[3], j)
        for r in range(8):
            tokens[pl.ds(pl.multiple_of(r * LANES + place * 32, 32), 32), :] = x_ref[r]
    for r in range(4):
        grads = jnp.concatenate([grads_ref[r, me_ref[1]], grads_ref[r, 1 - me_ref[1]]], axis=0)
        part = mul(tokens[r * GROUP:(r + 1) * GROUP, :], grads, 0, 0)
        total[...] = part if r == 0 else total[...] + part
    eye = diagonal()
    for k in range(4):
        start = pl.multiple_of(lax.rem(me_ref[2] + k, 4) * LANES, LANES)
        if k == 0:
            own_ref[...] = total[pl.ds(start, LANES), :]
            continue
        rows = []
        for g in range(4):
            word, code = encode(total[pl.ds(start, LANES), g * GROUP:(g + 1) * GROUP])
            word_refs[k - 1][g * LANES:(g + 1) * LANES, :] = word
            rows.append(to_row(code, eye))
        word_refs[k - 1][4 * LANES:, :] = jnp.concatenate(rows + [jnp.zeros((4, LANES), i32)], axis=0)


def partial_rows(me, tokens, grads):
    vmem = pl.BlockSpec(memory_space=pltpu.VMEM)
    return pl.pallas_call(
        partial_kernel,
        in_specs=[pl.BlockSpec(memory_space=pltpu.SMEM)] + [vmem] * 5,
        out_specs=[vmem] * 4,
        out_shape=[jax.ShapeDtypeStruct((LANES, BLK), f32)] + [jax.ShapeDtypeStruct((520, LANES), i32)] * 3,
        scratch_shapes=[pltpu.VMEM((BLK, 512), bf16), pltpu.VMEM((512, BLK), f32)],
        compiler_params=params(),
        cost_estimate=pl.CostEstimate(flops=10**9, bytes_accessed=5 * 10**6, transcendentals=0),
    )(me, *tokens, grads)


def front_kernel(got_ref, own_ref, w1_ref, w2_ref, w3_ref, v_ref, high_ref, low_ref, grad):
    step = pl.program_id(0)
    eye = diagonal()
    decode_chunks(got_ref, 8, high_ref, low_ref, eye)

    @pl.when(step == 0)
    def _():
        for g in range(4):
            sums = [own_ref[:, g * GROUP:g * GROUP + LANES], own_ref[:, g * GROUP + LANES:(g + 1) * GROUP]]
            for ref in (w1_ref, w2_ref, w3_ref):
                unit = to_unit(ref[4 * LANES + g:4 * LANES + g + 1, :], eye)
                pair = decode(ref[g * LANES:(g + 1) * LANES, :], unit)
                sums = [sums[0] + pair[0], sums[1] + pair[1]]
            grad[g] = jnp.concatenate(sums, axis=1)

    grad_high, grad_low = halves(grad[step])
    both = mul(jnp.concatenate([grad_high, grad_low], axis=0), high_ref[...])
    v = both[:LANES] + both[LANES:] + mul(grad_high, low_ref[...])
    for c in range(8):
        part = v[:, c * LANES:(c + 1) * LANES]
        v_ref[c] = jnp.where(step == 0, part, v_ref[c] + part)


def front(got, own, words):
    whole = lambda i: (0, 0)
    return pl.pallas_call(
        front_kernel,
        grid=(4,),
        in_specs=[pl.BlockSpec((8, ROWS, LANES), lambda i: (i, 0, 0)), pl.BlockSpec((LANES, BLK), whole)]
        + [pl.BlockSpec((520, LANES), whole)] * 3,
        out_specs=[pl.BlockSpec((8, LANES, LANES), lambda i: (0, 0, 0))]
        + [pl.BlockSpec((GROUP, BLK), lambda i: (i, 0))] * 2,
        out_shape=[jax.ShapeDtypeStruct((8, LANES, LANES), f32)] + [jax.ShapeDtypeStruct((BLK, BLK), bf16)] * 2,
        scratch_shapes=[pltpu.VMEM((4, LANES, GROUP), f32)],
        compiler_params=params("arbitrary"),
        cost_estimate=pl.CostEstimate(flops=8 * 10**8, bytes_accessed=8 * 10**6, transcendentals=0),
    )(got, own, *words)


def middle_kernel(v_ref, high_ref, low_ref, in_side_ref, out_side_ref, u_ref):
    v = v_ref[...].reshape(BLK, LANES)
    v_high, v_low = halves(v)
    qh, ql = high_ref[...], low_ref[...]
    both = mul(jnp.concatenate([v_high, v_low], axis=1), qh, 0, 0)
    rt = both[:LANES] + both[LANES:] + mul(v_high, ql, 0, 0)
    la = jnp.concatenate([in_side_ref[c, 1:2, :] for c in range(8)], axis=1).astype(f32) / VALUE_UNIT
    lb = jnp.sum(jnp.where(diagonal(), out_side_ref[0, 1:2, :], 0), axis=1, keepdims=True).astype(f32) / VALUE_UNIT
    st = rt / (lb * la + DAMPING)
    s_high, s_low = halves(st)
    both = mul(jnp.concatenate([s_high, s_low], axis=0), qh, 1, 1)
    ut = both[:LANES] + both[LANES:] + mul(s_high, ql, 1, 1)
    for c in range(8):
        u_ref[c] = ut[:, c * LANES:(c + 1) * LANES]


def middle(v, high, low, in_side, piece):
    whole = lambda i: (0, 0)
    return pl.pallas_call(
        middle_kernel,
        grid=(1,),
        in_specs=[
            pl.BlockSpec((8, LANES, LANES), lambda i: (0, 0, 0)),
            pl.BlockSpec((BLK, BLK), whole),
            pl.BlockSpec((BLK, BLK), whole),
            pl.BlockSpec((8, 8, LANES), lambda i: (0, 0, 0)),
            pl.BlockSpec((1, 8, LANES), lambda i: (0, 16, 0)),
        ],
        out_specs=pl.BlockSpec((8, LANES, LANES), lambda i: (0, 0, 0)),
        out_shape=jax.ShapeDtypeStruct((8, LANES, LANES), f32),
        compiler_params=params("arbitrary"),
        cost_estimate=pl.CostEstimate(flops=16 * 10**8, bytes_accessed=6 * 10**6, transcendentals=0),
    )(v, high, low, in_side, piece)


def back_kernel(u_ref, high_ref, low_ref, out_ref):
    u_high, u_low = halves(u_ref[...].reshape(BLK, LANES).T)
    both = mul(jnp.concatenate([u_high, u_low], axis=0), high_ref[...], 1, 1)
    out_ref[...] = both[:LANES] + both[LANES:] + mul(u_high, low_ref[...], 1, 1)


def back(u, high, low):
    return pl.pallas_call(
        back_kernel,
        grid=(4,),
        in_specs=[
            pl.BlockSpec((8, LANES, LANES), lambda i: (0, 0, 0)),
            pl.BlockSpec((GROUP, BLK), lambda i: (i, 0)),
            pl.BlockSpec((GROUP, BLK), lambda i: (i, 0)),
        ],
        out_specs=pl.BlockSpec((LANES, GROUP), lambda i: (0, i)),
        out_shape=jax.ShapeDtypeStruct((LANES, BLK), f32),
        compiler_params=params("arbitrary"),
        cost_estimate=pl.CostEstimate(flops=8 * 10**8, bytes_accessed=5 * 10**6, transcendentals=0),
    )(u, high, low)


def body(
    layer_inputs,
    output_grads,
    feature_order,
    block_slot,
    layer_owner,
    in_basis,
    in_values,
    out_basis,
    out_values,
):
    me = jnp.stack([lax.axis_index("y"), lax.axis_index("h"), lax.axis_index("z"), lax.axis_index(("l", "c"))])
    me = jnp.concatenate([me.astype(i32), block_slot])

    chunks = gather_columns(me, feature_order, layer_inputs.reshape(32, DIN))
    moved = lax.all_to_all(chunks, ("y", "h"), 0, 0, tiled=True)
    tokens = [moved] + [lax.ppermute(moved, ("l", "c"), [(m, m ^ j) for m in range(4)]) for j in range(1, 4)]

    packed = pack_basis(out_basis[0], out_values)
    grads = output_grads.reshape(LANES, BLK)
    packed, crossed, in_basis = lax.optimization_barrier((packed, across(grads), in_basis))
    spread = lax.all_to_all(packed, ALL_DP, 0, 0, tiled=True)
    piece = lax.dynamic_index_in_dim(spread, layer_owner[0], 0, keepdims=True)

    grads = lax.all_gather(jnp.stack([grads, crossed]), "y")

    in_part = pack_basis(in_basis, in_values.reshape(1, LANES))
    in_pair = jnp.stack([in_part, lax.ppermute(in_part, ("h", "l"), [(i, 3 - i) for i in range(4)])])
    in_high, in_low, in_side = unpack_basis(me, lax.all_gather(in_pair, "z"))

    own, *words = partial_rows(me, tokens, grads)
    words = [along(w, "z", k + 1) for k, w in enumerate(words)]

    got = lax.all_to_all(jnp.broadcast_to(piece, spread.shape), ALL_DP, 0, 0, tiled=True)
    v, out_high, out_low = front(got, own, words)
    v = lax.all_to_all(v, PAIR, 0, 0, tiled=True)
    u = middle(v, in_high, in_low, in_side, piece)
    u = lax.all_to_all(u, PAIR, 0, 0, tiled=True)
    return back(u, out_high, out_low)


def along(block, axis, shift):
    if shift == 0:
        return block
    return lax.ppermute(block, axis, [(i, (i + shift) % 4) for i in range(4)])


def across(block):
    return lax.ppermute(block, "h", [(0, 1), (1, 0)])


def solution(mesh):
    fine = Mesh(mesh.devices.reshape(4, 2, 4, 2, 2), ("y", "h", "z", "l", "c"))
    dp, mp = ("y", "h", "z"), ("l", "c")
    in_specs = (
        P(dp + mp, None, None),
        P(dp, None, mp),
        P(),
        P(),
        P(),
        P(dp, None),
        P(dp),
        P(dp, mp, None),
        P(dp, mp),
    )
    return jax.shard_map(body, mesh=fine, in_specs=in_specs, out_specs=P(dp, mp), check_vma=False)
```

```python
import jax
import jax.numpy as jnp
from jax import lax
from jax.experimental import pallas as pl
from jax.experimental.pallas import tpu as pltpu
from jax.sharding import Mesh, PartitionSpec as P

DIN = 4096
BLK = 1024
LANES = 128
GROUP = 256
ROWS = 136
DAMPING = 0.1
TOP = 32767.0
LOG_UNIT = 65536.0
VALUE_UNIT = 134217728.0
PAIR = ("h", "z")
ALL_DP = ("y", "h", "z")
VMEM = 48 * 1024 * 1024
f32, bf16, i32 = jnp.float32, jnp.bfloat16, jnp.int32


def params(*semantics):
    return pltpu.CompilerParams(vmem_limit_bytes=VMEM, dimension_semantics=semantics or None)


def mul(a, b, ca=1, cb=0):
    return lax.dot_general(a, b, (((ca,), (cb,)), ((), ())), preferred_element_type=f32)


def halves(a):
    high = a.astype(bf16)
    return high, (a - high.astype(f32)).astype(bf16)


def gather_kernel(me_ref, order_ref, x_ref, out_ref):
    x = [x_ref[:, k * LANES:(k + 1) * LANES].astype(f32) for k in range(DIN // LANES)]
    for n in range(4):
        pair = sum(jnp.where(me_ref[4 + j] == pl.program_id(0) * 2 + n // 2, j, 0) for j in range(4))
        start = pair * BLK + n % 2 * 512
        for b in range(4):
            idx = order_ref[:, pl.ds(pl.multiple_of(start + b * LANES, LANES), LANES)]
            lane = jnp.broadcast_to(jnp.bitwise_and(idx, LANES - 1), (32, LANES))
            src = jnp.broadcast_to(jnp.right_shift(idx, 7), (32, LANES))
            acc = jnp.zeros((32, LANES), f32)
            for k in range(DIN // LANES):
                acc = jnp.where(src == k, jnp.take_along_axis(x[k], lane, axis=1), acc)
            out_ref[n, :, b * LANES:(b + 1) * LANES] = acc.astype(bf16)


def gather_columns(me, order, x):
    return pl.pallas_call(
        gather_kernel,
        grid=(2,),
        in_specs=[
            pl.BlockSpec(memory_space=pltpu.SMEM),
            pl.BlockSpec((1, DIN), lambda i: (0, 0)),
            pl.BlockSpec((32, DIN), lambda i: (0, 0)),
        ],
        out_specs=pl.BlockSpec((4, 32, 512), lambda i: (i, 0, 0)),
        out_shape=jax.ShapeDtypeStruct((8, 32, 512), bf16),
        compiler_params=params("arbitrary"),
        cost_estimate=pl.CostEstimate(flops=10**6, bytes_accessed=10**6, transcendentals=0),
    )(me, order, x)


def diagonal():
    return lax.broadcasted_iota(i32, (LANES, LANES), 0) == lax.broadcasted_iota(i32, (LANES, LANES), 1)


def encode(part):
    most = jnp.maximum(jnp.max(jnp.abs(part), axis=1, keepdims=True), 1e-30)
    code = jnp.ceil(jnp.log2(most) * LOG_UNIT) + 4.0
    q = jnp.round(part * (TOP * jnp.exp2(-code / LOG_UNIT))).astype(i32)
    word = jnp.bitwise_or(jnp.left_shift(q[:, LANES:], 16), jnp.bitwise_and(q[:, :LANES], 65535))
    return word, code.astype(i32)


def decode(word, unit):
    first = jnp.right_shift(jnp.left_shift(word, 16), 16).astype(f32) * unit
    return first, jnp.right_shift(word, 16).astype(f32) * unit


def to_row(column, eye):
    return jnp.sum(jnp.where(eye, column, 0), axis=0, keepdims=True)


def to_unit(row, eye):
    return jnp.exp2(jnp.sum(jnp.where(eye, row, 0), axis=1, keepdims=True).astype(f32) / LOG_UNIT) / TOP


def pack_kernel(basis_ref, values_ref, out_ref):
    eye = diagonal()
    blocks = values_ref.shape[1] // LANES
    count = out_ref.shape[0]
    for n in range(count // 4):
        codes = [[] for _ in range(4)]
        for g in range(4):
            word, code = encode(basis_ref[n * LANES:(n + 1) * LANES, g * GROUP:(g + 1) * GROUP])
            for d in range(4):
                out_ref[n * 4 + d, g * 32:(g + 1) * 32, :] = word[d * 32:(d + 1) * 32]
                codes[d].append(code[d * 32:(d + 1) * 32])
        for d in range(4):
            row = to_row(jnp.concatenate(codes[d], axis=0), eye)
            block = (n * 4 + d) % blocks
            coded = (values_ref[:, block * LANES:(block + 1) * LANES] * VALUE_UNIT).astype(i32)
            out_ref[n * 4 + d, LANES:ROWS, :] = jnp.concatenate([row, coded, jnp.zeros((6, LANES), i32)], axis=0)


def pack_basis(basis, values):
    rows = basis.shape[0]
    size = min(rows, 512)
    return pl.pallas_call(
        pack_kernel,
        grid=(rows // size,),
        in_specs=[pl.BlockSpec((size, BLK), lambda i: (i, 0)), pl.BlockSpec(values.shape, lambda i: (0, 0))],
        out_specs=pl.BlockSpec((size // 32, ROWS, LANES), lambda i: (i, 0, 0)),
        out_shape=jax.ShapeDtypeStruct((rows // 32, ROWS, LANES), i32),
        compiler_params=params("arbitrary"),
        cost_estimate=pl.CostEstimate(flops=rows * 10**4, bytes_accessed=rows * 6000, transcendentals=0),
    )(basis, values)


def decode_chunks(get, first, count, high_ref, low_ref, eye):
    for d in range(count):
        unit = to_unit(get(d, LANES, 1), eye)
        for g in range(4):
            pair = decode(get(d, g * 32, 32), unit[g * 32:(g + 1) * 32])
            for k in range(2):
                high, low = halves(pair[k])
                start = (first + d) * 32
                where = (slice(start, start + 32), slice(g * GROUP + k * LANES, g * GROUP + (k + 1) * LANES))
                high_ref[where] = high
                low_ref[where] = low


def unpack_kernel(me_ref, own_ref, other_ref, high_ref, low_ref, side_ref):
    core = lax.rem(me_ref[3], 2)
    eye = diagonal()
    for z in range(4):
        def get(d, start, size):
            rows = slice(start, start + size)
            return jnp.where(core == d // 2, own_ref[z, 0, d % 2, rows, :], other_ref[z, 0, d % 2, rows, :])
        decode_chunks(get, z * 4, 4, high_ref, low_ref, eye)
        side_ref[z] = get(0, LANES, 8)


def unpack_basis(me, own, other):
    rows = lambda i, m: (i, 0)
    half = pl.BlockSpec((4, 1, 2, ROWS, LANES), lambda i, m: (0, lax.rem(i + m[1], 2), 0, 0, 0))
    return pl.pallas_call(
        unpack_kernel,
        grid_spec=pltpu.PrefetchScalarGridSpec(
            num_scalar_prefetch=1,
            grid=(2,),
            in_specs=[half, half],
            out_specs=[pl.BlockSpec((512, BLK), rows)] * 2 + [pl.BlockSpec((4, 8, LANES), lambda i, m: (i, 0, 0))],
        ),
        out_shape=[jax.ShapeDtypeStruct((BLK, BLK), bf16)] * 2 + [jax.ShapeDtypeStruct((8, 8, LANES), i32)],
        compiler_params=params("arbitrary"),
        cost_estimate=pl.CostEstimate(flops=10**7, bytes_accessed=6 * 10**6, transcendentals=0),
    )(me, own, other)


def partial_kernel(me_ref, x0_ref, x1_ref, x2_ref, x3_ref, grads_ref, *refs):
    own_ref, word_refs, tokens, total = refs[0], refs[1:4], refs[4], refs[5]
    for j, x_ref in enumerate((x0_ref, x2_ref, x1_ref, x3_ref)):
        place = jnp.bitwise_xor(me_ref[3], j)
        for r in range(8):
            tokens[pl.ds(pl.multiple_of(r * LANES + place * 32, 32), 32), :] = x_ref[r]
    for r in range(4):
        grads = jnp.concatenate([grads_ref[r, me_ref[1]], grads_ref[r, 1 - me_ref[1]]], axis=0)
        part = mul(tokens[r * GROUP:(r + 1) * GROUP, :], grads, 0, 0)
        total[...] = part if r == 0 else total[...] + part
    eye = diagonal()
    for k in range(4):
        start = pl.multiple_of(lax.rem(me_ref[2] + k, 4) * LANES, LANES)
        if k == 0:
            own_ref[...] = total[pl.ds(start, LANES), :]
            continue
        rows = []
        for g in range(4):
            word, code = encode(total[pl.ds(start, LANES), g * GROUP:(g + 1) * GROUP])
            word_refs[k - 1][g * LANES:(g + 1) * LANES, :] = word
            rows.append(to_row(code, eye))
        word_refs[k - 1][4 * LANES:, :] = jnp.concatenate(rows + [jnp.zeros((4, LANES), i32)], axis=0)


def partial_rows(me, tokens, grads):
    vmem = pl.BlockSpec(memory_space=pltpu.VMEM)
    return pl.pallas_call(
        partial_kernel,
        in_specs=[pl.BlockSpec(memory_space=pltpu.SMEM)] + [vmem] * 5,
        out_specs=[vmem] * 4,
        out_shape=[jax.ShapeDtypeStruct((LANES, BLK), f32)] + [jax.ShapeDtypeStruct((520, LANES), i32)] * 3,
        scratch_shapes=[pltpu.VMEM((BLK, 512), bf16), pltpu.VMEM((512, BLK), f32)],
        compiler_params=params(),
        cost_estimate=pl.CostEstimate(flops=10**9, bytes_accessed=5 * 10**6, transcendentals=0),
    )(me, *tokens, grads)


def front_kernel(got_ref, own_ref, w1_ref, w2_ref, w3_ref, v_ref, high_ref, low_ref, grad):
    step = pl.program_id(0)
    eye = diagonal()
    decode_chunks(lambda d, start, size: got_ref[d, start:start + size, :], 0, 16, high_ref, low_ref, eye)

    @pl.when(step == 0)
    def _():
        for g in range(4):
            sums = [own_ref[:, g * GROUP:g * GROUP + LANES], own_ref[:, g * GROUP + LANES:(g + 1) * GROUP]]
            for ref in (w1_ref, w2_ref, w3_ref):
                unit = to_unit(ref[4 * LANES + g:4 * LANES + g + 1, :], eye)
                pair = decode(ref[g * LANES:(g + 1) * LANES, :], unit)
                sums = [sums[0] + pair[0], sums[1] + pair[1]]
            grad[g // 2, :, g % 2 * GROUP:(g % 2 + 1) * GROUP] = jnp.concatenate(sums, axis=1)

    grad_high, grad_low = halves(grad[step])
    both = mul(jnp.concatenate([grad_high, grad_low], axis=0), high_ref[...])
    v = both[:LANES] + both[LANES:] + mul(grad_high, low_ref[...])
    for c in range(8):
        part = v[:, c * LANES:(c + 1) * LANES]
        v_ref[c] = jnp.where(step == 0, part, v_ref[c] + part)


def front(got, own, words):
    whole = lambda i: (0, 0)
    return pl.pallas_call(
        front_kernel,
        grid=(2,),
        in_specs=[pl.BlockSpec((16, ROWS, LANES), lambda i: (i, 0, 0)), pl.BlockSpec((LANES, BLK), whole)]
        + [pl.BlockSpec((520, LANES), whole)] * 3,
        out_specs=[pl.BlockSpec((8, LANES, LANES), lambda i: (0, 0, 0))]
        + [pl.BlockSpec((512, BLK), lambda i: (i, 0))] * 2,
        out_shape=[jax.ShapeDtypeStruct((8, LANES, LANES), f32)] + [jax.ShapeDtypeStruct((BLK, BLK), bf16)] * 2,
        scratch_shapes=[pltpu.VMEM((2, LANES, 512), f32)],
        compiler_params=params("arbitrary"),
        cost_estimate=pl.CostEstimate(flops=8 * 10**8, bytes_accessed=8 * 10**6, transcendentals=0),
    )(got, own, *words)


def middle_kernel(v_ref, high_ref, low_ref, in_side_ref, out_side_ref, u_ref):
    v = v_ref[...].reshape(BLK, LANES)
    v_high, v_low = halves(v)
    qh, ql = high_ref[...], low_ref[...]
    both = mul(jnp.concatenate([v_high, v_low], axis=1), qh, 0, 0)
    rt = both[:LANES] + both[LANES:] + mul(v_high, ql, 0, 0)
    la = jnp.concatenate([in_side_ref[c, 1:2, :] for c in range(8)], axis=1).astype(f32) / VALUE_UNIT
    lb = jnp.sum(jnp.where(diagonal(), out_side_ref[0, 1:2, :], 0), axis=1, keepdims=True).astype(f32) / VALUE_UNIT
    st = rt / (lb * la + DAMPING)
    s_high, s_low = halves(st)
    both = mul(jnp.concatenate([s_high, s_low], axis=0), qh, 1, 1)
    ut = both[:LANES] + both[LANES:] + mul(s_high, ql, 1, 1)
    for c in range(8):
        u_ref[c] = ut[:, c * LANES:(c + 1) * LANES]


def middle(v, high, low, in_side, piece):
    whole = lambda i: (0, 0)
    return pl.pallas_call(
        middle_kernel,
        grid=(1,),
        in_specs=[
            pl.BlockSpec((8, LANES, LANES), lambda i: (0, 0, 0)),
            pl.BlockSpec((BLK, BLK), whole),
            pl.BlockSpec((BLK, BLK), whole),
            pl.BlockSpec((8, 8, LANES), lambda i: (0, 0, 0)),
            pl.BlockSpec((1, 8, LANES), lambda i: (0, 16, 0)),
        ],
        out_specs=pl.BlockSpec((8, LANES, LANES), lambda i: (0, 0, 0)),
        out_shape=jax.ShapeDtypeStruct((8, LANES, LANES), f32),
        compiler_params=params("arbitrary"),
        cost_estimate=pl.CostEstimate(flops=16 * 10**8, bytes_accessed=6 * 10**6, transcendentals=0),
    )(v, high, low, in_side, piece)


def back_kernel(u_ref, high_ref, low_ref, out_ref):
    u_high, u_low = halves(u_ref[...].reshape(BLK, LANES).T)
    both = mul(jnp.concatenate([u_high, u_low], axis=0), high_ref[...], 1, 1)
    out_ref[...] = both[:LANES] + both[LANES:] + mul(u_high, low_ref[...], 1, 1)


def back(u, high, low):
    return pl.pallas_call(
        back_kernel,
        grid=(2,),
        in_specs=[
            pl.BlockSpec((8, LANES, LANES), lambda i: (0, 0, 0)),
            pl.BlockSpec((512, BLK), lambda i: (i, 0)),
            pl.BlockSpec((512, BLK), lambda i: (i, 0)),
        ],
        out_specs=pl.BlockSpec((LANES, 512), lambda i: (0, i)),
        out_shape=jax.ShapeDtypeStruct((LANES, BLK), f32),
        compiler_params=params("arbitrary"),
        cost_estimate=pl.CostEstimate(flops=8 * 10**8, bytes_accessed=5 * 10**6, transcendentals=0),
    )(u, high, low)


def body(
    layer_inputs,
    output_grads,
    feature_order,
    block_slot,
    layer_owner,
    in_basis,
    in_values,
    out_basis,
    out_values,
):
    me = jnp.stack([lax.axis_index("y"), lax.axis_index("h"), lax.axis_index("z"), lax.axis_index(("l", "c"))])
    me = jnp.concatenate([me.astype(i32), block_slot])

    chunks = gather_columns(me, feature_order, layer_inputs.reshape(32, DIN))
    chunks, out_part = lax.optimization_barrier((chunks, out_basis[0]))
    moved = lax.all_to_all(chunks, ("y", "h"), 0, 0, tiled=True)

    packed = pack_basis(out_part, out_values)
    grads = output_grads.reshape(LANES, BLK)
    packed, moved, crossed, in_part = lax.optimization_barrier((packed, moved, flip(grads, "h"), in_basis))
    spread = lax.all_to_all(packed, ALL_DP, 0, 0, tiled=True)
    piece = lax.dynamic_index_in_dim(spread, layer_owner[0], 0, keepdims=True)

    tokens = [moved, flip(moved, "l")]
    tokens += [flip(t, "c") for t in tokens]

    grads = lax.all_gather(jnp.stack([grads, crossed]), "y")

    in_part = pack_basis(in_part, in_values.reshape(1, LANES))
    in_part = lax.dynamic_slice_in_dim(in_part, lax.axis_index("c") * 2, 2, 0)
    in_cross = lax.ppermute(in_part, ("h", "l"), [(i, 3 - i) for i in range(4)])

    piece, *tokens, in_part, in_cross = lax.optimization_barrier((piece, *tokens, in_part, in_cross))
    got = lax.all_to_all(jnp.broadcast_to(piece, spread.shape), ALL_DP, 0, 0, tiled=True)

    own, *words = partial_rows(me, tokens, grads)
    words = [along(w, "z", k + 1) for k, w in enumerate(words)]

    in_own = lax.all_gather(jnp.stack([in_part, in_cross]), "z")
    in_high, in_low, in_side = unpack_basis(me, in_own, flip(in_own, "c"))

    own, in_high, in_low = lax.optimization_barrier((own, in_high, in_low))
    v, out_high, out_low = front(got, own, words)
    v = lax.all_to_all(v, PAIR, 0, 0, tiled=True)
    u = middle(v, in_high, in_low, in_side, piece)
    u = lax.all_to_all(u, PAIR, 0, 0, tiled=True)
    return back(u, out_high, out_low)


def along(block, axis, shift):
    if shift == 0:
        return block
    return lax.ppermute(block, axis, [(i, (i + shift) % 4) for i in range(4)])


def flip(block, axis):
    return lax.ppermute(block, axis, [(0, 1), (1, 0)])


def solution(mesh):
    fine = Mesh(mesh.devices.reshape(4, 2, 4, 2, 2), ("y", "h", "z", "l", "c"))
    dp, mp = ("y", "h", "z"), ("l", "c")
    in_specs = (
        P(dp + mp, None, None),
        P(dp, None, mp),
        P(),
        P(),
        P(),
        P(dp, None),
        P(dp),
        P(dp, mp, None),
        P(dp, mp),
    )
    return jax.shard_map(body, mesh=fine, in_specs=in_specs, out_specs=P(dp, mp), check_vma=False)
```

```python
import jax
import jax.numpy as jnp
from jax import lax
from jax.experimental import pallas as pl
from jax.experimental.pallas import tpu as pltpu
from jax.sharding import Mesh, PartitionSpec as P

DIN = 4096
BLK = 1024
LANES = 128
GROUP = 256
ROWS = 136
DAMPING = 0.1
TOP = 32767.0
LOG_UNIT = 65536.0
VALUE_UNIT = 134217728.0
PAIR = ("h", "z")
ALL_DP = ("y", "h", "z")
VMEM = 48 * 1024 * 1024
f32, bf16, i32 = jnp.float32, jnp.bfloat16, jnp.int32


def params(*semantics):
    return pltpu.CompilerParams(vmem_limit_bytes=VMEM, dimension_semantics=semantics or None)


def mul(a, b, ca=1, cb=0):
    return lax.dot_general(a, b, (((ca,), (cb,)), ((), ())), preferred_element_type=f32)


def halves(a):
    high = a.astype(bf16)
    return high, (a - high.astype(f32)).astype(bf16)


def gather_kernel(me_ref, order_ref, x_ref, out_ref):
    x = [x_ref[:, k * LANES:(k + 1) * LANES].astype(f32) for k in range(DIN // LANES)]
    for n in range(4):
        pair = sum(jnp.where(me_ref[4 + j] == pl.program_id(0) * 2 + n // 2, j, 0) for j in range(4))
        start = pair * BLK + n % 2 * 512
        for b in range(4):
            idx = order_ref[:, pl.ds(pl.multiple_of(start + b * LANES, LANES), LANES)]
            lane = jnp.broadcast_to(jnp.bitwise_and(idx, LANES - 1), (32, LANES))
            src = jnp.broadcast_to(jnp.right_shift(idx, 7), (32, LANES))
            acc = jnp.zeros((32, LANES), f32)
            for k in range(DIN // LANES):
                acc = jnp.where(src == k, jnp.take_along_axis(x[k], lane, axis=1), acc)
            out_ref[n, :, b * LANES:(b + 1) * LANES] = acc.astype(bf16)


def gather_columns(me, order, x):
    return pl.pallas_call(
        gather_kernel,
        grid=(2,),
        in_specs=[
            pl.BlockSpec(memory_space=pltpu.SMEM),
            pl.BlockSpec((1, DIN), lambda i: (0, 0)),
            pl.BlockSpec((32, DIN), lambda i: (0, 0)),
        ],
        out_specs=pl.BlockSpec((4, 32, 512), lambda i: (i, 0, 0)),
        out_shape=jax.ShapeDtypeStruct((8, 32, 512), bf16),
        compiler_params=params("arbitrary"),
        cost_estimate=pl.CostEstimate(flops=10**6, bytes_accessed=10**6, transcendentals=0),
    )(me, order, x)


def diagonal():
    return lax.broadcasted_iota(i32, (LANES, LANES), 0) == lax.broadcasted_iota(i32, (LANES, LANES), 1)


def encode(part):
    most = jnp.maximum(jnp.max(jnp.abs(part), axis=1, keepdims=True), 1e-30)
    code = jnp.ceil(jnp.log2(most) * LOG_UNIT) + 4.0
    q = jnp.round(part * (TOP * jnp.exp2(-code / LOG_UNIT))).astype(i32)
    word = jnp.bitwise_or(jnp.left_shift(q[:, LANES:], 16), jnp.bitwise_and(q[:, :LANES], 65535))
    return word, code.astype(i32)


def decode(word, unit):
    first = jnp.right_shift(jnp.left_shift(word, 16), 16).astype(f32) * unit
    return first, jnp.right_shift(word, 16).astype(f32) * unit


def to_row(column, eye):
    return jnp.sum(jnp.where(eye, column, 0), axis=0, keepdims=True)


def to_unit(row, eye):
    return jnp.exp2(jnp.sum(jnp.where(eye, row, 0), axis=1, keepdims=True).astype(f32) / LOG_UNIT) / TOP


def pack_kernel(basis_ref, values_ref, out_ref):
    eye = diagonal()
    blocks = values_ref.shape[1] // LANES
    count = out_ref.shape[0]
    for n in range(count // 4):
        codes = [[] for _ in range(4)]
        for g in range(4):
            word, code = encode(basis_ref[n * LANES:(n + 1) * LANES, g * GROUP:(g + 1) * GROUP])
            for d in range(4):
                out_ref[n * 4 + d, g * 32:(g + 1) * 32, :] = word[d * 32:(d + 1) * 32]
                codes[d].append(code[d * 32:(d + 1) * 32])
        for d in range(4):
            row = to_row(jnp.concatenate(codes[d], axis=0), eye)
            block = (n * 4 + d) % blocks
            coded = (values_ref[:, block * LANES:(block + 1) * LANES] * VALUE_UNIT).astype(i32)
            out_ref[n * 4 + d, LANES:ROWS, :] = jnp.concatenate([row, coded, jnp.zeros((6, LANES), i32)], axis=0)


def pack_basis(basis, values):
    rows = basis.shape[0]
    size = min(rows, 512)
    return pl.pallas_call(
        pack_kernel,
        grid=(rows // size,),
        in_specs=[pl.BlockSpec((size, BLK), lambda i: (i, 0)), pl.BlockSpec(values.shape, lambda i: (0, 0))],
        out_specs=pl.BlockSpec((size // 32, ROWS, LANES), lambda i: (i, 0, 0)),
        out_shape=jax.ShapeDtypeStruct((rows // 32, ROWS, LANES), i32),
        compiler_params=params("arbitrary"),
        cost_estimate=pl.CostEstimate(flops=rows * 10**4, bytes_accessed=rows * 6000, transcendentals=0),
    )(basis, values)


def decode_chunks(get, first, count, high_ref, low_ref, eye):
    for d in range(count):
        unit = to_unit(get(d, LANES, 1), eye)
        for g in range(4):
            pair = decode(get(d, g * 32, 32), unit[g * 32:(g + 1) * 32])
            for k in range(2):
                high, low = halves(pair[k])
                start = (first + d) * 32
                where = (slice(start, start + 32), slice(g * GROUP + k * LANES, g * GROUP + (k + 1) * LANES))
                high_ref[where] = high
                low_ref[where] = low


def unpack_kernel(me_ref, own_ref, other_ref, high_ref, low_ref, side_ref):
    core = lax.rem(me_ref[3], 2)
    eye = diagonal()
    for z in range(4):
        def get(d, start, size):
            rows = slice(start, start + size)
            return jnp.where(core == d // 2, own_ref[z, 0, d % 2, rows, :], other_ref[z, 0, d % 2, rows, :])
        decode_chunks(get, z * 4, 4, high_ref, low_ref, eye)
        side_ref[z] = get(0, LANES, 8)


def unpack_basis(me, own, other):
    rows = lambda i, m: (i, 0)
    half = pl.BlockSpec((4, 1, 2, ROWS, LANES), lambda i, m: (0, lax.rem(i + m[1], 2), 0, 0, 0))
    return pl.pallas_call(
        unpack_kernel,
        grid_spec=pltpu.PrefetchScalarGridSpec(
            num_scalar_prefetch=1,
            grid=(2,),
            in_specs=[half, half],
            out_specs=[pl.BlockSpec((512, BLK), rows)] * 2 + [pl.BlockSpec((4, 8, LANES), lambda i, m: (i, 0, 0))],
        ),
        out_shape=[jax.ShapeDtypeStruct((BLK, BLK), bf16)] * 2 + [jax.ShapeDtypeStruct((8, 8, LANES), i32)],
        compiler_params=params("arbitrary"),
        cost_estimate=pl.CostEstimate(flops=10**7, bytes_accessed=6 * 10**6, transcendentals=0),
    )(me, own, other)


def partial_kernel(me_ref, x0_ref, x1_ref, x2_ref, x3_ref, grads_ref, *refs):
    own_ref, word_refs, tokens, total = refs[0], refs[1:4], refs[4], refs[5]
    for j, x_ref in enumerate((x0_ref, x2_ref, x1_ref, x3_ref)):
        place = jnp.bitwise_xor(me_ref[3], j)
        for r in range(8):
            tokens[pl.ds(pl.multiple_of(r * LANES + place * 32, 32), 32), :] = x_ref[r]
    for r in range(4):
        grads = jnp.concatenate([grads_ref[r, me_ref[1]], grads_ref[r, 1 - me_ref[1]]], axis=0)
        part = mul(tokens[r * GROUP:(r + 1) * GROUP, :], grads, 0, 0)
        total[...] = part if r == 0 else total[...] + part
    eye = diagonal()
    for k in range(4):
        start = pl.multiple_of(lax.rem(me_ref[2] + k, 4) * LANES, LANES)
        if k == 0:
            own_ref[...] = total[pl.ds(start, LANES), :]
            continue
        rows = []
        for g in range(4):
            word, code = encode(total[pl.ds(start, LANES), g * GROUP:(g + 1) * GROUP])
            word_refs[k - 1][g * LANES:(g + 1) * LANES, :] = word
            rows.append(to_row(code, eye))
        word_refs[k - 1][4 * LANES:, :] = jnp.concatenate(rows + [jnp.zeros((4, LANES), i32)], axis=0)


def partial_rows(me, tokens, grads):
    vmem = pl.BlockSpec(memory_space=pltpu.VMEM)
    return pl.pallas_call(
        partial_kernel,
        in_specs=[pl.BlockSpec(memory_space=pltpu.SMEM)] + [vmem] * 5,
        out_specs=[vmem] * 4,
        out_shape=[jax.ShapeDtypeStruct((LANES, BLK), f32)] + [jax.ShapeDtypeStruct((520, LANES), i32)] * 3,
        scratch_shapes=[pltpu.VMEM((BLK, 512), bf16), pltpu.VMEM((512, BLK), f32)],
        compiler_params=params(),
        cost_estimate=pl.CostEstimate(flops=10**9, bytes_accessed=5 * 10**6, transcendentals=0),
    )(me, *tokens, grads)


def front_kernel(got_ref, own_ref, w1_ref, w2_ref, w3_ref, v_ref, high_ref, low_ref, grad):
    step = pl.program_id(0)
    eye = diagonal()
    decode_chunks(lambda d, start, size: got_ref[d, start:start + size, :], 0, 16, high_ref, low_ref, eye)

    @pl.when(step == 0)
    def _():
        for g in range(4):
            sums = [own_ref[:, g * GROUP:g * GROUP + LANES], own_ref[:, g * GROUP + LANES:(g + 1) * GROUP]]
            for ref in (w1_ref, w2_ref, w3_ref):
                unit = to_unit(ref[4 * LANES + g:4 * LANES + g + 1, :], eye)
                pair = decode(ref[g * LANES:(g + 1) * LANES, :], unit)
                sums = [sums[0] + pair[0], sums[1] + pair[1]]
            grad[g // 2, :, g % 2 * GROUP:(g % 2 + 1) * GROUP] = jnp.concatenate(sums, axis=1)

    grad_high, grad_low = halves(grad[step])
    both = mul(jnp.concatenate([grad_high, grad_low], axis=0), high_ref[...])
    v = both[:LANES] + both[LANES:] + mul(grad_high, low_ref[...])
    for c in range(8):
        part = v[:, c * LANES:(c + 1) * LANES]
        v_ref[c] = jnp.where(step == 0, part, v_ref[c] + part)


def front(got, own, words):
    whole = lambda i: (0, 0)
    return pl.pallas_call(
        front_kernel,
        grid=(2,),
        in_specs=[pl.BlockSpec((16, ROWS, LANES), lambda i: (i, 0, 0)), pl.BlockSpec((LANES, BLK), whole)]
        + [pl.BlockSpec((520, LANES), whole)] * 3,
        out_specs=[pl.BlockSpec((8, LANES, LANES), lambda i: (0, 0, 0))]
        + [pl.BlockSpec((512, BLK), lambda i: (i, 0))] * 2,
        out_shape=[jax.ShapeDtypeStruct((8, LANES, LANES), f32)] + [jax.ShapeDtypeStruct((BLK, BLK), bf16)] * 2,
        scratch_shapes=[pltpu.VMEM((2, LANES, 512), f32)],
        compiler_params=params("arbitrary"),
        cost_estimate=pl.CostEstimate(flops=8 * 10**8, bytes_accessed=8 * 10**6, transcendentals=0),
    )(got, own, *words)


def middle_kernel(v_ref, high_ref, low_ref, in_side_ref, out_side_ref, u_ref):
    v = v_ref[...].reshape(BLK, LANES)
    v_high, v_low = halves(v)
    qh, ql = high_ref[...], low_ref[...]
    both = mul(jnp.concatenate([v_high, v_low], axis=1), qh, 0, 0)
    rt = both[:LANES] + both[LANES:] + mul(v_high, ql, 0, 0)
    la = jnp.concatenate([in_side_ref[c, 1:2, :] for c in range(8)], axis=1).astype(f32) / VALUE_UNIT
    lb = jnp.sum(jnp.where(diagonal(), out_side_ref[0, 1:2, :], 0), axis=1, keepdims=True).astype(f32) / VALUE_UNIT
    st = rt / (lb * la + DAMPING)
    s_high, s_low = halves(st)
    both = mul(jnp.concatenate([s_high, s_low], axis=0), qh, 1, 1)
    ut = both[:LANES] + both[LANES:] + mul(s_high, ql, 1, 1)
    for c in range(8):
        u_ref[c] = ut[:, c * LANES:(c + 1) * LANES]


def middle(v, high, low, in_side, piece):
    whole = lambda i: (0, 0)
    return pl.pallas_call(
        middle_kernel,
        grid=(1,),
        in_specs=[
            pl.BlockSpec((8, LANES, LANES), lambda i: (0, 0, 0)),
            pl.BlockSpec((BLK, BLK), whole),
            pl.BlockSpec((BLK, BLK), whole),
            pl.BlockSpec((8, 8, LANES), lambda i: (0, 0, 0)),
            pl.BlockSpec((1, 8, LANES), lambda i: (0, 16, 0)),
        ],
        out_specs=pl.BlockSpec((8, LANES, LANES), lambda i: (0, 0, 0)),
        out_shape=jax.ShapeDtypeStruct((8, LANES, LANES), f32),
        compiler_params=params("arbitrary"),
        cost_estimate=pl.CostEstimate(flops=16 * 10**8, bytes_accessed=6 * 10**6, transcendentals=0),
    )(v, high, low, in_side, piece)


def back_kernel(u_ref, high_ref, low_ref, out_ref):
    u_high, u_low = halves(u_ref[...].reshape(BLK, LANES).T)
    both = mul(jnp.concatenate([u_high, u_low], axis=0), high_ref[...], 1, 1)
    out_ref[...] = both[:LANES] + both[LANES:] + mul(u_high, low_ref[...], 1, 1)


def back(u, high, low):
    return pl.pallas_call(
        back_kernel,
        grid=(2,),
        in_specs=[
            pl.BlockSpec((8, LANES, LANES), lambda i: (0, 0, 0)),
            pl.BlockSpec((512, BLK), lambda i: (i, 0)),
            pl.BlockSpec((512, BLK), lambda i: (i, 0)),
        ],
        out_specs=pl.BlockSpec((LANES, 512), lambda i: (0, i)),
        out_shape=jax.ShapeDtypeStruct((LANES, BLK), f32),
        compiler_params=params("arbitrary"),
        cost_estimate=pl.CostEstimate(flops=8 * 10**8, bytes_accessed=5 * 10**6, transcendentals=0),
    )(u, high, low)


def body(
    layer_inputs,
    output_grads,
    feature_order,
    block_slot,
    layer_owner,
    in_basis,
    in_values,
    out_basis,
    out_values,
):
    me = jnp.stack([lax.axis_index("y"), lax.axis_index("h"), lax.axis_index("z"), lax.axis_index(("l", "c"))])
    me = jnp.concatenate([me.astype(i32), block_slot])

    chunks = gather_columns(me, feature_order, layer_inputs.reshape(32, DIN))
    chunks, out_part = lax.optimization_barrier((chunks, out_basis[0]))
    moved = lax.all_to_all(chunks, ("y", "h"), 0, 0, tiled=True)

    packed = pack_basis(out_part, out_values)
    grads = output_grads.reshape(LANES, BLK)
    grads = jnp.stack([grads, flip(grads, "h")])
    packed, moved, grads, in_part = lax.optimization_barrier((packed, moved, grads, in_basis))
    spread = lax.all_to_all(packed, ALL_DP, 0, 0, tiled=True)
    piece = lax.dynamic_index_in_dim(spread, layer_owner[0], 0, keepdims=True)

    tokens = [moved, flip(moved, "l")]
    tokens += [flip(t, "c") for t in tokens]

    grads = lax.all_gather(grads, "y")

    in_part = pack_basis(in_part, in_values.reshape(1, LANES))
    in_part = lax.dynamic_slice_in_dim(in_part, lax.axis_index("c") * 2, 2, 0)
    in_cross = lax.ppermute(in_part, ("h", "l"), [(i, 3 - i) for i in range(4)])

    piece, *tokens, in_part, in_cross = lax.optimization_barrier((piece, *tokens, in_part, in_cross))
    got = lax.all_to_all(jnp.broadcast_to(piece, spread.shape), ALL_DP, 0, 0, tiled=True)

    own, *words = partial_rows(me, tokens, grads)
    words = [along(w, "z", k + 1) for k, w in enumerate(words)]

    in_own = lax.all_gather(jnp.stack([in_part, in_cross]), "z")
    in_high, in_low, in_side = unpack_basis(me, in_own, flip(in_own, "c"))

    own, in_high, in_low = lax.optimization_barrier((own, in_high, in_low))
    v, out_high, out_low = front(got, own, words)
    v = lax.all_to_all(v, PAIR, 0, 0, tiled=True)
    u = middle(v, in_high, in_low, in_side, piece)
    u = lax.all_to_all(u, PAIR, 0, 0, tiled=True)
    return back(u, out_high, out_low)


def along(block, axis, shift):
    if shift == 0:
        return block
    return lax.ppermute(block, axis, [(i, (i + shift) % 4) for i in range(4)])


def flip(block, axis):
    return lax.ppermute(block, axis, [(0, 1), (1, 0)])


def solution(mesh):
    fine = Mesh(mesh.devices.reshape(4, 2, 4, 2, 2), ("y", "h", "z", "l", "c"))
    dp, mp = ("y", "h", "z"), ("l", "c")
    in_specs = (
        P(dp + mp, None, None),
        P(dp, None, mp),
        P(),
        P(),
        P(),
        P(dp, None),
        P(dp),
        P(dp, mp, None),
        P(dp, mp),
    )
    return jax.shard_map(body, mesh=fine, in_specs=in_specs, out_specs=P(dp, mp), check_vma=False)
```

```python
import jax
import jax.numpy as jnp
from jax import lax
from jax.experimental import pallas as pl
from jax.experimental.pallas import tpu as pltpu
from jax.sharding import Mesh, PartitionSpec as P

DIN = 4096
BLK = 1024
LANES = 128
GROUP = 256
ROWS = 136
DAMPING = 0.1
TOP = 32767.0
LOG_UNIT = 65536.0
VALUE_UNIT = 134217728.0
PAIR = ("h", "z")
ALL_DP = ("y", "h", "z")
VMEM = 48 * 1024 * 1024
f32, bf16, i32 = jnp.float32, jnp.bfloat16, jnp.int32


def params(*semantics):
    return pltpu.CompilerParams(vmem_limit_bytes=VMEM, dimension_semantics=semantics or None)


def mul(a, b, ca=1, cb=0):
    return lax.dot_general(a, b, (((ca,), (cb,)), ((), ())), preferred_element_type=f32)


def halves(a):
    high = a.astype(bf16)
    return high, (a - high.astype(f32)).astype(bf16)


def gather_kernel(me_ref, order_ref, x_ref, out_ref):
    x = [x_ref[:, k * LANES:(k + 1) * LANES].astype(f32) for k in range(DIN // LANES)]
    for n in range(4):
        pair = sum(jnp.where(me_ref[4 + j] == pl.program_id(0) * 2 + n // 2, j, 0) for j in range(4))
        start = pair * BLK + n % 2 * 512
        for b in range(4):
            idx = order_ref[:, pl.ds(pl.multiple_of(start + b * LANES, LANES), LANES)]
            lane = jnp.broadcast_to(jnp.bitwise_and(idx, LANES - 1), (32, LANES))
            src = jnp.broadcast_to(jnp.right_shift(idx, 7), (32, LANES))
            acc = jnp.zeros((32, LANES), f32)
            for k in range(DIN // LANES):
                acc = jnp.where(src == k, jnp.take_along_axis(x[k], lane, axis=1), acc)
            out_ref[n, :, b * LANES:(b + 1) * LANES] = acc.astype(bf16)


def gather_columns(me, order, x):
    return pl.pallas_call(
        gather_kernel,
        grid=(2,),
        in_specs=[
            pl.BlockSpec(memory_space=pltpu.SMEM),
            pl.BlockSpec((1, DIN), lambda i: (0, 0)),
            pl.BlockSpec((32, DIN), lambda i: (0, 0)),
        ],
        out_specs=pl.BlockSpec((4, 32, 512), lambda i: (i, 0, 0)),
        out_shape=jax.ShapeDtypeStruct((8, 32, 512), bf16),
        compiler_params=params("arbitrary"),
        cost_estimate=pl.CostEstimate(flops=10**6, bytes_accessed=10**6, transcendentals=0),
    )(me, order, x)


def diagonal():
    return lax.broadcasted_iota(i32, (LANES, LANES), 0) == lax.broadcasted_iota(i32, (LANES, LANES), 1)


def encode(part):
    most = jnp.maximum(jnp.max(jnp.abs(part), axis=1, keepdims=True), 1e-30)
    code = jnp.ceil(jnp.log2(most) * LOG_UNIT) + 4.0
    q = jnp.round(part * (TOP * jnp.exp2(-code / LOG_UNIT))).astype(i32)
    word = jnp.bitwise_or(jnp.left_shift(q[:, LANES:], 16), jnp.bitwise_and(q[:, :LANES], 65535))
    return word, code.astype(i32)


def decode(word, unit):
    first = jnp.right_shift(jnp.left_shift(word, 16), 16).astype(f32) * unit
    return first, jnp.right_shift(word, 16).astype(f32) * unit


def to_row(column, eye):
    return jnp.sum(jnp.where(eye, column, 0), axis=0, keepdims=True)


def to_unit(row, eye):
    return jnp.exp2(jnp.sum(jnp.where(eye, row, 0), axis=1, keepdims=True).astype(f32) / LOG_UNIT) / TOP


def pack_kernel(basis_ref, values_ref, out_ref):
    eye = diagonal()
    blocks = values_ref.shape[1] // LANES
    count = out_ref.shape[0]
    for n in range(count // 4):
        codes = [[] for _ in range(4)]
        for g in range(4):
            word, code = encode(basis_ref[n * LANES:(n + 1) * LANES, g * GROUP:(g + 1) * GROUP])
            for d in range(4):
                out_ref[n * 4 + d, g * 32:(g + 1) * 32, :] = word[d * 32:(d + 1) * 32]
                codes[d].append(code[d * 32:(d + 1) * 32])
        for d in range(4):
            row = to_row(jnp.concatenate(codes[d], axis=0), eye)
            block = (n * 4 + d) % blocks
            coded = (values_ref[:, block * LANES:(block + 1) * LANES] * VALUE_UNIT).astype(i32)
            out_ref[n * 4 + d, LANES:ROWS, :] = jnp.concatenate([row, coded, jnp.zeros((6, LANES), i32)], axis=0)


def pack_basis(basis, values):
    rows = basis.shape[0]
    size = min(rows, 512)
    return pl.pallas_call(
        pack_kernel,
        grid=(rows // size,),
        in_specs=[pl.BlockSpec((size, BLK), lambda i: (i, 0)), pl.BlockSpec(values.shape, lambda i: (0, 0))],
        out_specs=pl.BlockSpec((size // 32, ROWS, LANES), lambda i: (i, 0, 0)),
        out_shape=jax.ShapeDtypeStruct((rows // 32, ROWS, LANES), i32),
        compiler_params=params("arbitrary"),
        cost_estimate=pl.CostEstimate(flops=rows * 10**4, bytes_accessed=rows * 6000, transcendentals=0),
    )(basis, values)


def decode_chunks(get, first, count, high_ref, low_ref, eye):
    for d in range(count):
        unit = to_unit(get(d, LANES, 1), eye)
        for g in range(4):
            pair = decode(get(d, g * 32, 32), unit[g * 32:(g + 1) * 32])
            for k in range(2):
                high, low = halves(pair[k])
                start = (first + d) * 32
                where = (slice(start, start + 32), slice(g * GROUP + k * LANES, g * GROUP + (k + 1) * LANES))
                high_ref[where] = high
                low_ref[where] = low


def unpack_kernel(me_ref, own_ref, other_ref, high_ref, low_ref, side_ref):
    core = lax.rem(me_ref[3], 2)
    eye = diagonal()
    for z in range(4):
        def get(d, start, size):
            rows = slice(start, start + size)
            return jnp.where(core == d // 2, own_ref[z, 0, d % 2, rows, :], other_ref[z, 0, d % 2, rows, :])
        decode_chunks(get, z * 4, 4, high_ref, low_ref, eye)
        side_ref[z] = get(0, LANES, 8)


def unpack_basis(me, own, other):
    rows = lambda i, m: (i, 0)
    half = pl.BlockSpec((4, 1, 2, ROWS, LANES), lambda i, m: (0, lax.rem(i + m[1], 2), 0, 0, 0))
    return pl.pallas_call(
        unpack_kernel,
        grid_spec=pltpu.PrefetchScalarGridSpec(
            num_scalar_prefetch=1,
            grid=(2,),
            in_specs=[half, half],
            out_specs=[pl.BlockSpec((512, BLK), rows)] * 2 + [pl.BlockSpec((4, 8, LANES), lambda i, m: (i, 0, 0))],
        ),
        out_shape=[jax.ShapeDtypeStruct((BLK, BLK), bf16)] * 2 + [jax.ShapeDtypeStruct((8, 8, LANES), i32)],
        compiler_params=params("arbitrary"),
        cost_estimate=pl.CostEstimate(flops=10**7, bytes_accessed=6 * 10**6, transcendentals=0),
    )(me, own, other)


def partial_kernel(me_ref, x0_ref, x1_ref, x2_ref, x3_ref, grads_ref, *refs):
    own_ref, word_refs, tokens, total = refs[0], refs[1:4], refs[4], refs[5]
    for j, x_ref in enumerate((x0_ref, x2_ref, x1_ref, x3_ref)):
        place = jnp.bitwise_xor(me_ref[3], j)
        for r in range(8):
            tokens[pl.ds(pl.multiple_of(r * LANES + place * 32, 32), 32), :] = x_ref[r]
    for r in range(4):
        grads = jnp.concatenate([grads_ref[r, me_ref[1]], grads_ref[r, 1 - me_ref[1]]], axis=0)
        part = mul(tokens[r * GROUP:(r + 1) * GROUP, :], grads, 0, 0)
        total[...] = part if r == 0 else total[...] + part
    eye = diagonal()
    for k in range(4):
        start = pl.multiple_of(lax.rem(me_ref[2] + k, 4) * LANES, LANES)
        if k == 0:
            own_ref[...] = total[pl.ds(start, LANES), :]
            continue
        rows = []
        for g in range(4):
            word, code = encode(total[pl.ds(start, LANES), g * GROUP:(g + 1) * GROUP])
            word_refs[k - 1][g * LANES:(g + 1) * LANES, :] = word
            rows.append(to_row(code, eye))
        word_refs[k - 1][4 * LANES:, :] = jnp.concatenate(rows + [jnp.zeros((4, LANES), i32)], axis=0)


def partial_rows(me, tokens, grads):
    vmem = pl.BlockSpec(memory_space=pltpu.VMEM)
    return pl.pallas_call(
        partial_kernel,
        in_specs=[pl.BlockSpec(memory_space=pltpu.SMEM)] + [vmem] * 5,
        out_specs=[vmem] * 4,
        out_shape=[jax.ShapeDtypeStruct((LANES, BLK), f32)] + [jax.ShapeDtypeStruct((520, LANES), i32)] * 3,
        scratch_shapes=[pltpu.VMEM((BLK, 512), bf16), pltpu.VMEM((512, BLK), f32)],
        compiler_params=params(),
        cost_estimate=pl.CostEstimate(flops=10**9, bytes_accessed=5 * 10**6, transcendentals=0),
    )(me, *tokens, grads)


def front_kernel(got_ref, own_ref, w1_ref, w2_ref, w3_ref, v_ref, high_ref, low_ref, grad):
    step = pl.program_id(0)
    eye = diagonal()
    decode_chunks(lambda d, start, size: got_ref[d, start:start + size, :], 0, 16, high_ref, low_ref, eye)

    @pl.when(step == 0)
    def _():
        for g in range(4):
            sums = [own_ref[:, g * GROUP:g * GROUP + LANES], own_ref[:, g * GROUP + LANES:(g + 1) * GROUP]]
            for ref in (w1_ref, w2_ref, w3_ref):
                unit = to_unit(ref[4 * LANES + g:4 * LANES + g + 1, :], eye)
                pair = decode(ref[g * LANES:(g + 1) * LANES, :], unit)
                sums = [sums[0] + pair[0], sums[1] + pair[1]]
            grad[g // 2, :, g % 2 * GROUP:(g % 2 + 1) * GROUP] = jnp.concatenate(sums, axis=1)

    grad_high, grad_low = halves(grad[step])
    both = mul(jnp.concatenate([grad_high, grad_low], axis=0), high_ref[...])
    v = both[:LANES] + both[LANES:] + mul(grad_high, low_ref[...])
    for c in range(8):
        part = v[:, c * LANES:(c + 1) * LANES]
        v_ref[c] = jnp.where(step == 0, part, v_ref[c] + part)


def front(got, own, words):
    whole = lambda i: (0, 0)
    return pl.pallas_call(
        front_kernel,
        grid=(2,),
        in_specs=[pl.BlockSpec((16, ROWS, LANES), lambda i: (i, 0, 0)), pl.BlockSpec((LANES, BLK), whole)]
        + [pl.BlockSpec((520, LANES), whole)] * 3,
        out_specs=[pl.BlockSpec((8, LANES, LANES), lambda i: (0, 0, 0))]
        + [pl.BlockSpec((512, BLK), lambda i: (i, 0))] * 2,
        out_shape=[jax.ShapeDtypeStruct((8, LANES, LANES), f32)] + [jax.ShapeDtypeStruct((BLK, BLK), bf16)] * 2,
        scratch_shapes=[pltpu.VMEM((2, LANES, 512), f32)],
        compiler_params=params("arbitrary"),
        cost_estimate=pl.CostEstimate(flops=8 * 10**8, bytes_accessed=8 * 10**6, transcendentals=0),
    )(got, own, *words)


def middle_kernel(v_ref, high_ref, low_ref, in_side_ref, out_side_ref, u_ref):
    v = v_ref[...].reshape(BLK, LANES)
    v_high, v_low = halves(v)
    qh, ql = high_ref[...], low_ref[...]
    both = mul(jnp.concatenate([v_high, v_low], axis=1), qh, 0, 0)
    rt = both[:LANES] + both[LANES:] + mul(v_high, ql, 0, 0)
    la = jnp.concatenate([in_side_ref[c, 1:2, :] for c in range(8)], axis=1).astype(f32) / VALUE_UNIT
    lb = jnp.sum(jnp.where(diagonal(), out_side_ref[0, 1:2, :], 0), axis=1, keepdims=True).astype(f32) / VALUE_UNIT
    st = rt / (lb * la + DAMPING)
    s_high, s_low = halves(st)
    both = mul(jnp.concatenate([s_high, s_low], axis=0), qh, 1, 1)
    ut = both[:LANES] + both[LANES:] + mul(s_high, ql, 1, 1)
    for c in range(8):
        u_ref[c] = ut[:, c * LANES:(c + 1) * LANES]


def middle(v, high, low, in_side, piece):
    whole = lambda i: (0, 0)
    return pl.pallas_call(
        middle_kernel,
        grid=(1,),
        in_specs=[
            pl.BlockSpec((8, LANES, LANES), lambda i: (0, 0, 0)),
            pl.BlockSpec((BLK, BLK), whole),
            pl.BlockSpec((BLK, BLK), whole),
            pl.BlockSpec((8, 8, LANES), lambda i: (0, 0, 0)),
            pl.BlockSpec((1, 8, LANES), lambda i: (0, 16, 0)),
        ],
        out_specs=pl.BlockSpec((8, LANES, LANES), lambda i: (0, 0, 0)),
        out_shape=jax.ShapeDtypeStruct((8, LANES, LANES), f32),
        compiler_params=params("arbitrary"),
        cost_estimate=pl.CostEstimate(flops=16 * 10**8, bytes_accessed=6 * 10**6, transcendentals=0),
    )(v, high, low, in_side, piece)


def back_kernel(u_ref, high_ref, low_ref, out_ref):
    u_high, u_low = halves(u_ref[...].reshape(BLK, LANES).T)
    both = mul(jnp.concatenate([u_high, u_low], axis=0), high_ref[...], 1, 1)
    out_ref[...] = both[:LANES] + both[LANES:] + mul(u_high, low_ref[...], 1, 1)


def back(u, high, low):
    return pl.pallas_call(
        back_kernel,
        grid=(2,),
        in_specs=[
            pl.BlockSpec((8, LANES, LANES), lambda i: (0, 0, 0)),
            pl.BlockSpec((512, BLK), lambda i: (i, 0)),
            pl.BlockSpec((512, BLK), lambda i: (i, 0)),
        ],
        out_specs=pl.BlockSpec((LANES, 512), lambda i: (0, i)),
        out_shape=jax.ShapeDtypeStruct((LANES, BLK), f32),
        compiler_params=params("arbitrary"),
        cost_estimate=pl.CostEstimate(flops=8 * 10**8, bytes_accessed=5 * 10**6, transcendentals=0),
    )(u, high, low)


def body(
    layer_inputs,
    output_grads,
    feature_order,
    block_slot,
    layer_owner,
    in_basis,
    in_values,
    out_basis,
    out_values,
):
    me = jnp.stack([lax.axis_index("y"), lax.axis_index("h"), lax.axis_index("z"), lax.axis_index(("l", "c"))])
    me = jnp.concatenate([me.astype(i32), block_slot])

    chunks = gather_columns(me, feature_order, layer_inputs.reshape(32, DIN))
    chunks, out_part = lax.optimization_barrier((chunks, out_basis[0]))
    moved = lax.all_to_all(chunks, ("y", "h"), 0, 0, tiled=True)

    packed = pack_basis(out_part, out_values)
    grads = output_grads.reshape(LANES, BLK)
    grads = jnp.stack([grads, flip(grads, "h")])
    packed, moved, grads, in_part = lax.optimization_barrier((packed, moved, grads, in_basis))
    spread = lax.all_to_all(packed, ALL_DP, 0, 0, tiled=True)
    piece = lax.dynamic_index_in_dim(spread, layer_owner[0], 0, keepdims=True)

    tokens = [moved, flip(moved, "l")]
    tokens += [flip(t, "c") for t in tokens]

    grads = lax.all_gather(grads, "y")

    in_part = pack_basis(in_part, in_values.reshape(1, LANES))
    in_part = lax.dynamic_slice_in_dim(in_part, lax.axis_index("c") * 2, 2, 0)
    in_cross = lax.ppermute(in_part, ("h", "l"), [(i, 3 - i) for i in range(4)])

    piece, grads, in_part, in_cross, *tokens = lax.optimization_barrier((piece, grads, in_part, in_cross, *tokens))
    got = lax.all_to_all(jnp.broadcast_to(piece, spread.shape), ALL_DP, 0, 0, tiled=True)

    own, *words = partial_rows(me, tokens, grads)
    words = [along(w, "z", k + 1) for k, w in enumerate(words)]

    in_own = lax.all_gather(jnp.stack([in_part, in_cross]), "z")
    in_high, in_low, in_side = unpack_basis(me, in_own, flip(in_own, "c"))

    own, in_high, in_low = lax.optimization_barrier((own, in_high, in_low))
    v, out_high, out_low = front(got, own, words)
    v = lax.all_to_all(v, PAIR, 0, 0, tiled=True)
    u = middle(v, in_high, in_low, in_side, piece)
    u = lax.all_to_all(u, PAIR, 0, 0, tiled=True)
    return back(u, out_high, out_low)


def along(block, axis, shift):
    if shift == 0:
        return block
    return lax.ppermute(block, axis, [(i, (i + shift) % 4) for i in range(4)])


def flip(block, axis):
    return lax.ppermute(block, axis, [(0, 1), (1, 0)])


def solution(mesh):
    fine = Mesh(mesh.devices.reshape(4, 2, 4, 2, 2), ("y", "h", "z", "l", "c"))
    dp, mp = ("y", "h", "z"), ("l", "c")
    in_specs = (
        P(dp + mp, None, None),
        P(dp, None, mp),
        P(),
        P(),
        P(),
        P(dp, None),
        P(dp),
        P(dp, mp, None),
        P(dp, mp),
    )
    return jax.shard_map(body, mesh=fine, in_specs=in_specs, out_specs=P(dp, mp), check_vma=False)
```

```python
import jax
import jax.numpy as jnp
from jax import lax
from jax.experimental import pallas as pl
from jax.experimental.pallas import tpu as pltpu
from jax.sharding import Mesh, PartitionSpec as P

DIN = 4096
BLK = 1024
LANES = 128
GROUP = 256
ROWS = 136
DAMPING = 0.1
TOP = 32767.0
LOG_UNIT = 65536.0
VALUE_UNIT = 134217728.0
PAIR = ("h", "z")
ALL_DP = ("y", "h", "z")
VMEM = 48 * 1024 * 1024
f32, bf16, i32 = jnp.float32, jnp.bfloat16, jnp.int32


def params(*semantics):
    return pltpu.CompilerParams(vmem_limit_bytes=VMEM, dimension_semantics=semantics or None)


def mul(a, b, ca=1, cb=0):
    return lax.dot_general(a, b, (((ca,), (cb,)), ((), ())), preferred_element_type=f32)


def halves(a):
    high = a.astype(bf16)
    return high, (a - high.astype(f32)).astype(bf16)


def gather_kernel(me_ref, order_ref, x_ref, out_ref):
    x = [x_ref[:, k * LANES:(k + 1) * LANES].astype(f32) for k in range(DIN // LANES)]
    for n in range(4):
        pair = sum(jnp.where(me_ref[4 + j] == pl.program_id(0) * 2 + n // 2, j, 0) for j in range(4))
        start = pair * BLK + n % 2 * 512
        for b in range(4):
            idx = order_ref[:, pl.ds(pl.multiple_of(start + b * LANES, LANES), LANES)]
            lane = jnp.broadcast_to(jnp.bitwise_and(idx, LANES - 1), (32, LANES))
            src = jnp.broadcast_to(jnp.right_shift(idx, 7), (32, LANES))
            acc = jnp.zeros((32, LANES), f32)
            for k in range(DIN // LANES):
                acc = jnp.where(src == k, jnp.take_along_axis(x[k], lane, axis=1), acc)
            out_ref[n, :, b * LANES:(b + 1) * LANES] = acc.astype(bf16)


def gather_columns(me, order, x):
    return pl.pallas_call(
        gather_kernel,
        grid=(2,),
        in_specs=[
            pl.BlockSpec(memory_space=pltpu.SMEM),
            pl.BlockSpec((1, DIN), lambda i: (0, 0)),
            pl.BlockSpec((32, DIN), lambda i: (0, 0)),
        ],
        out_specs=pl.BlockSpec((4, 32, 512), lambda i: (i, 0, 0)),
        out_shape=jax.ShapeDtypeStruct((8, 32, 512), bf16),
        compiler_params=params("arbitrary"),
        cost_estimate=pl.CostEstimate(flops=10**6, bytes_accessed=10**6, transcendentals=0),
    )(me, order, x)


def diagonal():
    return lax.broadcasted_iota(i32, (LANES, LANES), 0) == lax.broadcasted_iota(i32, (LANES, LANES), 1)


def encode(part):
    most = jnp.maximum(jnp.max(jnp.abs(part), axis=1, keepdims=True), 1e-30)
    code = jnp.ceil(jnp.log2(most) * LOG_UNIT) + 4.0
    q = jnp.round(part * (TOP * jnp.exp2(-code / LOG_UNIT))).astype(i32)
    word = jnp.bitwise_or(jnp.left_shift(q[:, LANES:], 16), jnp.bitwise_and(q[:, :LANES], 65535))
    return word, code.astype(i32)


def decode(word, unit):
    first = jnp.right_shift(jnp.left_shift(word, 16), 16).astype(f32) * unit
    return first, jnp.right_shift(word, 16).astype(f32) * unit


def to_row(column, eye):
    return jnp.sum(jnp.where(eye, column, 0), axis=0, keepdims=True)


def to_unit(row, eye):
    return jnp.exp2(jnp.sum(jnp.where(eye, row, 0), axis=1, keepdims=True).astype(f32) / LOG_UNIT) / TOP


def pack_kernel(basis_ref, values_ref, out_ref):
    eye = diagonal()
    blocks = values_ref.shape[1] // LANES
    count = out_ref.shape[0]
    for n in range(count // 4):
        codes = [[] for _ in range(4)]
        for g in range(4):
            word, code = encode(basis_ref[n * LANES:(n + 1) * LANES, g * GROUP:(g + 1) * GROUP])
            for d in range(4):
                out_ref[n * 4 + d, g * 32:(g + 1) * 32, :] = word[d * 32:(d + 1) * 32]
                codes[d].append(code[d * 32:(d + 1) * 32])
        for d in range(4):
            row = to_row(jnp.concatenate(codes[d], axis=0), eye)
            block = (n * 4 + d) % blocks
            coded = (values_ref[:, block * LANES:(block + 1) * LANES] * VALUE_UNIT).astype(i32)
            out_ref[n * 4 + d, LANES:ROWS, :] = jnp.concatenate([row, coded, jnp.zeros((6, LANES), i32)], axis=0)


def pack_basis(basis, values):
    rows = basis.shape[0]
    size = min(rows, 512)
    return pl.pallas_call(
        pack_kernel,
        grid=(rows // size,),
        in_specs=[pl.BlockSpec((size, BLK), lambda i: (i, 0)), pl.BlockSpec(values.shape, lambda i: (0, 0))],
        out_specs=pl.BlockSpec((size // 32, ROWS, LANES), lambda i: (i, 0, 0)),
        out_shape=jax.ShapeDtypeStruct((rows // 32, ROWS, LANES), i32),
        compiler_params=params("arbitrary"),
        cost_estimate=pl.CostEstimate(flops=rows * 10**4, bytes_accessed=rows * 6000, transcendentals=0),
    )(basis, values)


def decode_chunks(get, first, count, high_ref, low_ref, eye):
    for d in range(count):
        unit = to_unit(get(d, LANES, 1), eye)
        for g in range(4):
            pair = decode(get(d, g * 32, 32), unit[g * 32:(g + 1) * 32])
            for k in range(2):
                high, low = halves(pair[k])
                start = (first + d) * 32
                where = (slice(start, start + 32), slice(g * GROUP + k * LANES, g * GROUP + (k + 1) * LANES))
                high_ref[where] = high
                low_ref[where] = low


def unpack_kernel(me_ref, own_ref, other_ref, high_ref, low_ref, side_ref):
    core = lax.rem(me_ref[3], 2)
    eye = diagonal()
    for z in range(4):
        def get(d, start, size):
            rows = slice(start, start + size)
            return jnp.where(core == d // 2, own_ref[z, 0, d % 2, rows, :], other_ref[z, 0, d % 2, rows, :])
        decode_chunks(get, z * 4, 4, high_ref, low_ref, eye)
        side_ref[z] = get(0, LANES, 8)


def unpack_basis(me, own, other):
    rows = lambda i, m: (i, 0)
    half = pl.BlockSpec((4, 1, 2, ROWS, LANES), lambda i, m: (0, lax.rem(i + m[1], 2), 0, 0, 0))
    return pl.pallas_call(
        unpack_kernel,
        grid_spec=pltpu.PrefetchScalarGridSpec(
            num_scalar_prefetch=1,
            grid=(2,),
            in_specs=[half, half],
            out_specs=[pl.BlockSpec((512, BLK), rows)] * 2 + [pl.BlockSpec((4, 8, LANES), lambda i, m: (i, 0, 0))],
        ),
        out_shape=[jax.ShapeDtypeStruct((BLK, BLK), bf16)] * 2 + [jax.ShapeDtypeStruct((8, 8, LANES), i32)],
        compiler_params=params("arbitrary"),
        cost_estimate=pl.CostEstimate(flops=10**7, bytes_accessed=6 * 10**6, transcendentals=0),
    )(me, own, other)


def partial_kernel(me_ref, x0_ref, x1_ref, x2_ref, x3_ref, grads_ref, *refs):
    own_ref, word_refs, tokens, total = refs[0], refs[1:4], refs[4], refs[5]
    for j, x_ref in enumerate((x0_ref, x2_ref, x1_ref, x3_ref)):
        place = jnp.bitwise_xor(me_ref[3], j)
        for r in range(8):
            tokens[pl.ds(pl.multiple_of(r * LANES + place * 32, 32), 32), :] = x_ref[r]
    for r in range(4):
        grads = jnp.concatenate([grads_ref[r, me_ref[1]], grads_ref[r, 1 - me_ref[1]]], axis=0)
        part = mul(tokens[r * GROUP:(r + 1) * GROUP, :], grads, 0, 0)
        total[...] = part if r == 0 else total[...] + part
    eye = diagonal()
    for k in range(4):
        start = pl.multiple_of(lax.rem(me_ref[2] + k, 4) * LANES, LANES)
        if k == 0:
            own_ref[...] = total[pl.ds(start, LANES), :]
            continue
        rows = []
        for g in range(4):
            word, code = encode(total[pl.ds(start, LANES), g * GROUP:(g + 1) * GROUP])
            word_refs[k - 1][g * LANES:(g + 1) * LANES, :] = word
            rows.append(to_row(code, eye))
        word_refs[k - 1][4 * LANES:, :] = jnp.concatenate(rows + [jnp.zeros((4, LANES), i32)], axis=0)


def partial_rows(me, tokens, grads):
    vmem = pl.BlockSpec(memory_space=pltpu.VMEM)
    return pl.pallas_call(
        partial_kernel,
        in_specs=[pl.BlockSpec(memory_space=pltpu.SMEM)] + [vmem] * 5,
        out_specs=[vmem] * 4,
        out_shape=[jax.ShapeDtypeStruct((LANES, BLK), f32)] + [jax.ShapeDtypeStruct((520, LANES), i32)] * 3,
        scratch_shapes=[pltpu.VMEM((BLK, 512), bf16), pltpu.VMEM((512, BLK), f32)],
        compiler_params=params(),
        cost_estimate=pl.CostEstimate(flops=10**9, bytes_accessed=5 * 10**6, transcendentals=0),
    )(me, *tokens, grads)


def front_kernel(got_ref, own_ref, w1_ref, w2_ref, w3_ref, v_ref, high_ref, low_ref, grad):
    step = pl.program_id(0)
    eye = diagonal()
    decode_chunks(lambda d, start, size: got_ref[d, start:start + size, :], 0, 16, high_ref, low_ref, eye)

    @pl.when(step == 0)
    def _():
        for g in range(4):
            sums = [own_ref[:, g * GROUP:g * GROUP + LANES], own_ref[:, g * GROUP + LANES:(g + 1) * GROUP]]
            for ref in (w1_ref, w2_ref, w3_ref):
                unit = to_unit(ref[4 * LANES + g:4 * LANES + g + 1, :], eye)
                pair = decode(ref[g * LANES:(g + 1) * LANES, :], unit)
                sums = [sums[0] + pair[0], sums[1] + pair[1]]
            grad[g // 2, :, g % 2 * GROUP:(g % 2 + 1) * GROUP] = jnp.concatenate(sums, axis=1)

    grad_high, grad_low = halves(grad[step])
    both = mul(jnp.concatenate([grad_high, grad_low], axis=0), high_ref[...])
    v = both[:LANES] + both[LANES:] + mul(grad_high, low_ref[...])
    for c in range(8):
        part = v[:, c * LANES:(c + 1) * LANES]
        v_ref[c] = jnp.where(step == 0, part, v_ref[c] + part)


def front(got, own, words):
    whole = lambda i: (0, 0)
    return pl.pallas_call(
        front_kernel,
        grid=(2,),
        in_specs=[pl.BlockSpec((16, ROWS, LANES), lambda i: (i, 0, 0)), pl.BlockSpec((LANES, BLK), whole)]
        + [pl.BlockSpec((520, LANES), whole)] * 3,
        out_specs=[pl.BlockSpec((8, LANES, LANES), lambda i: (0, 0, 0))]
        + [pl.BlockSpec((512, BLK), lambda i: (i, 0))] * 2,
        out_shape=[jax.ShapeDtypeStruct((8, LANES, LANES), f32)] + [jax.ShapeDtypeStruct((BLK, BLK), bf16)] * 2,
        scratch_shapes=[pltpu.VMEM((2, LANES, 512), f32)],
        compiler_params=params("arbitrary"),
        cost_estimate=pl.CostEstimate(flops=8 * 10**8, bytes_accessed=8 * 10**6, transcendentals=0),
    )(got, own, *words)


def middle_kernel(v_ref, high_ref, low_ref, in_side_ref, out_side_ref, u_ref):
    v = v_ref[...].reshape(BLK, LANES)
    v_high, v_low = halves(v)
    qh, ql = high_ref[...], low_ref[...]
    both = mul(jnp.concatenate([v_high, v_low], axis=1), qh, 0, 0)
    rt = both[:LANES] + both[LANES:] + mul(v_high, ql, 0, 0)
    la = jnp.concatenate([in_side_ref[c, 1:2, :] for c in range(8)], axis=1).astype(f32) / VALUE_UNIT
    lb = jnp.sum(jnp.where(diagonal(), out_side_ref[0, 1:2, :], 0), axis=1, keepdims=True).astype(f32) / VALUE_UNIT
    st = rt / (lb * la + DAMPING)
    s_high, s_low = halves(st)
    both = mul(jnp.concatenate([s_high, s_low], axis=0), qh, 1, 1)
    ut = both[:LANES] + both[LANES:] + mul(s_high, ql, 1, 1)
    for c in range(8):
        u_ref[c] = ut[:, c * LANES:(c + 1) * LANES]


def middle(v, high, low, in_side, piece):
    whole = lambda i: (0, 0)
    return pl.pallas_call(
        middle_kernel,
        grid=(1,),
        in_specs=[
            pl.BlockSpec((8, LANES, LANES), lambda i: (0, 0, 0)),
            pl.BlockSpec((BLK, BLK), whole),
            pl.BlockSpec((BLK, BLK), whole),
            pl.BlockSpec((8, 8, LANES), lambda i: (0, 0, 0)),
            pl.BlockSpec((1, 8, LANES), lambda i: (0, 16, 0)),
        ],
        out_specs=pl.BlockSpec((8, LANES, LANES), lambda i: (0, 0, 0)),
        out_shape=jax.ShapeDtypeStruct((8, LANES, LANES), f32),
        compiler_params=params("arbitrary"),
        cost_estimate=pl.CostEstimate(flops=16 * 10**8, bytes_accessed=6 * 10**6, transcendentals=0),
    )(v, high, low, in_side, piece)


def back_kernel(u_ref, high_ref, low_ref, out_ref):
    u_high, u_low = halves(u_ref[...].reshape(BLK, LANES).T)
    both = mul(jnp.concatenate([u_high, u_low], axis=0), high_ref[...], 1, 1)
    out_ref[...] = both[:LANES] + both[LANES:] + mul(u_high, low_ref[...], 1, 1)


def back(u, high, low):
    return pl.pallas_call(
        back_kernel,
        grid=(2,),
        in_specs=[
            pl.BlockSpec((8, LANES, LANES), lambda i: (0, 0, 0)),
            pl.BlockSpec((512, BLK), lambda i: (i, 0)),
            pl.BlockSpec((512, BLK), lambda i: (i, 0)),
        ],
        out_specs=pl.BlockSpec((LANES, 512), lambda i: (0, i)),
        out_shape=jax.ShapeDtypeStruct((LANES, BLK), f32),
        compiler_params=params("arbitrary"),
        cost_estimate=pl.CostEstimate(flops=8 * 10**8, bytes_accessed=5 * 10**6, transcendentals=0),
    )(u, high, low)


def body(
    layer_inputs,
    output_grads,
    feature_order,
    block_slot,
    layer_owner,
    in_basis,
    in_values,
    out_basis,
    out_values,
):
    me = jnp.stack([lax.axis_index("y"), lax.axis_index("h"), lax.axis_index("z"), lax.axis_index(("l", "c"))])
    me = jnp.concatenate([me.astype(i32), block_slot])

    chunks = gather_columns(me, feature_order, layer_inputs.reshape(32, DIN))
    grads = output_grads.reshape(LANES, BLK)
    grads = jnp.stack([grads, flip(grads, "h")])
    chunks, grads, out_part = lax.optimization_barrier((chunks, grads, out_basis[0]))
    moved = lax.all_to_all(chunks, ("y", "h"), 0, 0, tiled=True)

    packed = pack_basis(out_part, out_values)
    packed, moved, in_part = lax.optimization_barrier((packed, moved, in_basis))
    spread = lax.all_to_all(packed, ALL_DP, 0, 0, tiled=True)
    piece = lax.dynamic_index_in_dim(spread, layer_owner[0], 0, keepdims=True)

    tokens = [moved, flip(moved, "l")]
    tokens += [flip(t, "c") for t in tokens]

    grads = lax.all_gather(grads, "y")

    in_part = pack_basis(in_part, in_values.reshape(1, LANES))
    in_part = lax.dynamic_slice_in_dim(in_part, lax.axis_index("c") * 2, 2, 0)
    in_cross = lax.ppermute(in_part, ("h", "l"), [(i, 3 - i) for i in range(4)])

    piece, grads, in_part, in_cross, *tokens = lax.optimization_barrier((piece, grads, in_part, in_cross, *tokens))
    got = lax.all_to_all(jnp.broadcast_to(piece, spread.shape), ALL_DP, 0, 0, tiled=True)

    own, *words = partial_rows(me, tokens, grads)
    words = [along(w, "z", k + 1) for k, w in enumerate(words)]

    in_own = lax.all_gather(jnp.stack([in_part, in_cross]), "z")
    in_own, *_ = lax.optimization_barrier((in_own, *words))
    in_high, in_low, in_side = unpack_basis(me, in_own, flip(in_own, "c"))

    v, out_high, out_low = front(got, own, words)
    v = lax.all_to_all(v, PAIR, 0, 0, tiled=True)
    u = middle(v, in_high, in_low, in_side, piece)
    u = lax.all_to_all(u, PAIR, 0, 0, tiled=True)
    return back(u, out_high, out_low)


def along(block, axis, shift):
    if shift == 0:
        return block
    return lax.ppermute(block, axis, [(i, (i + shift) % 4) for i in range(4)])


def flip(block, axis):
    return lax.ppermute(block, axis, [(0, 1), (1, 0)])


def solution(mesh):
    fine = Mesh(mesh.devices.reshape(4, 2, 4, 2, 2), ("y", "h", "z", "l", "c"))
    dp, mp = ("y", "h", "z"), ("l", "c")
    in_specs = (
        P(dp + mp, None, None),
        P(dp, None, mp),
        P(),
        P(),
        P(),
        P(dp, None),
        P(dp),
        P(dp, mp, None),
        P(dp, mp),
    )
    return jax.shard_map(body, mesh=fine, in_specs=in_specs, out_specs=P(dp, mp), check_vma=False)
```

```python
import jax
import jax.numpy as jnp
from jax import lax
from jax.experimental import pallas as pl
from jax.experimental.pallas import tpu as pltpu
from jax.sharding import Mesh, PartitionSpec as P

DIN = 4096
BLK = 1024
LANES = 128
GROUP = 256
ROWS = 136
DAMPING = 0.1
TOP = 32767.0
LOG_UNIT = 65536.0
VALUE_UNIT = 134217728.0
PAIR = ("h", "z")
ALL_DP = ("y", "h", "z")
VMEM = 48 * 1024 * 1024
f32, bf16, i32 = jnp.float32, jnp.bfloat16, jnp.int32


def params(*semantics):
    return pltpu.CompilerParams(vmem_limit_bytes=VMEM, dimension_semantics=semantics or None)


def mul(a, b, ca=1, cb=0):
    return lax.dot_general(a, b, (((ca,), (cb,)), ((), ())), preferred_element_type=f32)


def halves(a):
    high = a.astype(bf16)
    return high, (a - high.astype(f32)).astype(bf16)


def gather_kernel(me_ref, order_ref, x_ref, out_ref):
    x = [x_ref[:, k * LANES:(k + 1) * LANES].astype(f32) for k in range(DIN // LANES)]
    for n in range(4):
        pair = sum(jnp.where(me_ref[4 + j] == pl.program_id(0) * 2 + n // 2, j, 0) for j in range(4))
        start = pair * BLK + n % 2 * 512
        for b in range(4):
            idx = order_ref[:, pl.ds(pl.multiple_of(start + b * LANES, LANES), LANES)]
            lane = jnp.broadcast_to(jnp.bitwise_and(idx, LANES - 1), (32, LANES))
            src = jnp.broadcast_to(jnp.right_shift(idx, 7), (32, LANES))
            acc = jnp.zeros((32, LANES), f32)
            for k in range(DIN // LANES):
                acc = jnp.where(src == k, jnp.take_along_axis(x[k], lane, axis=1), acc)
            for m in range(4):
                out_ref[n * 4 + m, :, b * LANES:(b + 1) * LANES] = acc.astype(bf16)


def gather_columns(me, order, x):
    return pl.pallas_call(
        gather_kernel,
        grid=(2,),
        in_specs=[
            pl.BlockSpec(memory_space=pltpu.SMEM),
            pl.BlockSpec((1, DIN), lambda i: (0, 0)),
            pl.BlockSpec((32, DIN), lambda i: (0, 0)),
        ],
        out_specs=pl.BlockSpec((16, 32, 512), lambda i: (i, 0, 0)),
        out_shape=jax.ShapeDtypeStruct((32, 32, 512), bf16),
        compiler_params=params("arbitrary"),
        cost_estimate=pl.CostEstimate(flops=10**6, bytes_accessed=10**6, transcendentals=0),
    )(me, order, x)


def diagonal():
    return lax.broadcasted_iota(i32, (LANES, LANES), 0) == lax.broadcasted_iota(i32, (LANES, LANES), 1)


def encode(part):
    most = jnp.maximum(jnp.max(jnp.abs(part), axis=1, keepdims=True), 1e-30)
    code = jnp.ceil(jnp.log2(most) * LOG_UNIT) + 4.0
    q = jnp.round(part * (TOP * jnp.exp2(-code / LOG_UNIT))).astype(i32)
    word = jnp.bitwise_or(jnp.left_shift(q[:, LANES:], 16), jnp.bitwise_and(q[:, :LANES], 65535))
    return word, code.astype(i32)


def decode(word, unit):
    first = jnp.right_shift(jnp.left_shift(word, 16), 16).astype(f32) * unit
    return first, jnp.right_shift(word, 16).astype(f32) * unit


def to_row(column, eye):
    return jnp.sum(jnp.where(eye, column, 0), axis=0, keepdims=True)


def to_unit(row, eye):
    return jnp.exp2(jnp.sum(jnp.where(eye, row, 0), axis=1, keepdims=True).astype(f32) / LOG_UNIT) / TOP


def pack_kernel(basis_ref, values_ref, out_ref):
    eye = diagonal()
    blocks = values_ref.shape[1] // LANES
    count = out_ref.shape[0]
    for n in range(count // 4):
        codes = [[] for _ in range(4)]
        for g in range(4):
            word, code = encode(basis_ref[n * LANES:(n + 1) * LANES, g * GROUP:(g + 1) * GROUP])
            for d in range(4):
                out_ref[n * 4 + d, g * 32:(g + 1) * 32, :] = word[d * 32:(d + 1) * 32]
                codes[d].append(code[d * 32:(d + 1) * 32])
        for d in range(4):
            row = to_row(jnp.concatenate(codes[d], axis=0), eye)
            block = (n * 4 + d) % blocks
            coded = (values_ref[:, block * LANES:(block + 1) * LANES] * VALUE_UNIT).astype(i32)
            out_ref[n * 4 + d, LANES:ROWS, :] = jnp.concatenate([row, coded, jnp.zeros((6, LANES), i32)], axis=0)


def pack_basis(basis, values):
    rows = basis.shape[0]
    size = min(rows, 512)
    return pl.pallas_call(
        pack_kernel,
        grid=(rows // size,),
        in_specs=[pl.BlockSpec((size, BLK), lambda i: (i, 0)), pl.BlockSpec(values.shape, lambda i: (0, 0))],
        out_specs=pl.BlockSpec((size // 32, ROWS, LANES), lambda i: (i, 0, 0)),
        out_shape=jax.ShapeDtypeStruct((rows // 32, ROWS, LANES), i32),
        compiler_params=params("arbitrary"),
        cost_estimate=pl.CostEstimate(flops=rows * 10**4, bytes_accessed=rows * 6000, transcendentals=0),
    )(basis, values)


def decode_chunks(get, first, count, high_ref, low_ref, eye):
    for d in range(count):
        unit = to_unit(get(d, LANES, 1), eye)
        for g in range(4):
            pair = decode(get(d, g * 32, 32), unit[g * 32:(g + 1) * 32])
            for k in range(2):
                high, low = halves(pair[k])
                start = (first + d) * 32
                where = (slice(start, start + 32), slice(g * GROUP + k * LANES, g * GROUP + (k + 1) * LANES))
                high_ref[where] = high
                low_ref[where] = low


def unpack_kernel(me_ref, own_ref, other_ref, high_ref, low_ref, side_ref):
    core = lax.rem(me_ref[3], 2)
    eye = diagonal()
    for z in range(4):
        def get(d, start, size):
            rows = slice(start, start + size)
            return jnp.where(core == d // 2, own_ref[z, 0, d % 2, rows, :], other_ref[z, 0, d % 2, rows, :])
        decode_chunks(get, z * 4, 4, high_ref, low_ref, eye)
        side_ref[z] = get(0, LANES, 8)


def unpack_basis(me, own, other):
    rows = lambda i, m: (i, 0)
    half = pl.BlockSpec((4, 1, 2, ROWS, LANES), lambda i, m: (0, lax.rem(i + m[1], 2), 0, 0, 0))
    return pl.pallas_call(
        unpack_kernel,
        grid_spec=pltpu.PrefetchScalarGridSpec(
            num_scalar_prefetch=1,
            grid=(2,),
            in_specs=[half, half],
            out_specs=[pl.BlockSpec((512, BLK), rows)] * 2 + [pl.BlockSpec((4, 8, LANES), lambda i, m: (i, 0, 0))],
        ),
        out_shape=[jax.ShapeDtypeStruct((BLK, BLK), bf16)] * 2 + [jax.ShapeDtypeStruct((8, 8, LANES), i32)],
        compiler_params=params("arbitrary"),
        cost_estimate=pl.CostEstimate(flops=10**7, bytes_accessed=6 * 10**6, transcendentals=0),
    )(me, own, other)


def partial_kernel(me_ref, tokens, grads_ref, *refs):
    own_ref, word_refs, total = refs[0], refs[1:4], refs[4]
    for r in range(4):
        grads = jnp.concatenate([grads_ref[r, me_ref[1]], grads_ref[r, 1 - me_ref[1]]], axis=0)
        part = mul(tokens[r * GROUP:(r + 1) * GROUP, :], grads, 0, 0)
        total[...] = part if r == 0 else total[...] + part
    eye = diagonal()
    for k in range(4):
        start = pl.multiple_of(lax.rem(me_ref[2] + k, 4) * LANES, LANES)
        if k == 0:
            own_ref[...] = total[pl.ds(start, LANES), :]
            continue
        rows = []
        for g in range(4):
            word, code = encode(total[pl.ds(start, LANES), g * GROUP:(g + 1) * GROUP])
            word_refs[k - 1][g * LANES:(g + 1) * LANES, :] = word
            rows.append(to_row(code, eye))
        word_refs[k - 1][4 * LANES:, :] = jnp.concatenate(rows + [jnp.zeros((4, LANES), i32)], axis=0)


def partial_rows(me, tokens, grads):
    vmem = pl.BlockSpec(memory_space=pltpu.VMEM)
    return pl.pallas_call(
        partial_kernel,
        in_specs=[pl.BlockSpec(memory_space=pltpu.SMEM)] + [vmem] * 2,
        out_specs=[vmem] * 4,
        out_shape=[jax.ShapeDtypeStruct((LANES, BLK), f32)] + [jax.ShapeDtypeStruct((520, LANES), i32)] * 3,
        scratch_shapes=[pltpu.VMEM((512, BLK), f32)],
        compiler_params=params(),
        cost_estimate=pl.CostEstimate(flops=10**9, bytes_accessed=5 * 10**6, transcendentals=0),
    )(me, tokens, grads)


def front_kernel(got_ref, own_ref, w1_ref, w2_ref, w3_ref, v_ref, high_ref, low_ref, grad):
    step = pl.program_id(0)
    eye = diagonal()
    decode_chunks(lambda d, start, size: got_ref[d, start:start + size, :], 0, 16, high_ref, low_ref, eye)

    @pl.when(step == 0)
    def _():
        for g in range(4):
            sums = [own_ref[:, g * GROUP:g * GROUP + LANES], own_ref[:, g * GROUP + LANES:(g + 1) * GROUP]]
            for ref in (w1_ref, w2_ref, w3_ref):
                unit = to_unit(ref[4 * LANES + g:4 * LANES + g + 1, :], eye)
                pair = decode(ref[g * LANES:(g + 1) * LANES, :], unit)
                sums = [sums[0] + pair[0], sums[1] + pair[1]]
            grad[g // 2, :, g % 2 * GROUP:(g % 2 + 1) * GROUP] = jnp.concatenate(sums, axis=1)

    grad_high, grad_low = halves(grad[step])
    both = mul(jnp.concatenate([grad_high, grad_low], axis=0), high_ref[...])
    v = both[:LANES] + both[LANES:] + mul(grad_high, low_ref[...])
    for c in range(8):
        part = v[:, c * LANES:(c + 1) * LANES]
        v_ref[c] = jnp.where(step == 0, part, v_ref[c] + part)


def front(got, own, words):
    whole = lambda i: (0, 0)
    return pl.pallas_call(
        front_kernel,
        grid=(2,),
        in_specs=[pl.BlockSpec((16, ROWS, LANES), lambda i: (i, 0, 0)), pl.BlockSpec((LANES, BLK), whole)]
        + [pl.BlockSpec((520, LANES), whole)] * 3,
        out_specs=[pl.BlockSpec((8, LANES, LANES), lambda i: (0, 0, 0))]
        + [pl.BlockSpec((512, BLK), lambda i: (i, 0))] * 2,
        out_shape=[jax.ShapeDtypeStruct((8, LANES, LANES), f32)] + [jax.ShapeDtypeStruct((BLK, BLK), bf16)] * 2,
        scratch_shapes=[pltpu.VMEM((2, LANES, 512), f32)],
        compiler_params=params("arbitrary"),
        cost_estimate=pl.CostEstimate(flops=8 * 10**8, bytes_accessed=8 * 10**6, transcendentals=0),
    )(got, own, *words)


def middle_kernel(v_ref, high_ref, low_ref, in_side_ref, out_side_ref, u_ref):
    v = v_ref[...].reshape(BLK, LANES)
    v_high, v_low = halves(v)
    qh, ql = high_ref[...], low_ref[...]
    both = mul(jnp.concatenate([v_high, v_low], axis=1), qh, 0, 0)
    rt = both[:LANES] + both[LANES:] + mul(v_high, ql, 0, 0)
    la = jnp.concatenate([in_side_ref[c, 1:2, :] for c in range(8)], axis=1).astype(f32) / VALUE_UNIT
    lb = jnp.sum(jnp.where(diagonal(), out_side_ref[0, 1:2, :], 0), axis=1, keepdims=True).astype(f32) / VALUE_UNIT
    st = rt / (lb * la + DAMPING)
    s_high, s_low = halves(st)
    both = mul(jnp.concatenate([s_high, s_low], axis=0), qh, 1, 1)
    ut = both[:LANES] + both[LANES:] + mul(s_high, ql, 1, 1)
    for c in range(8):
        u_ref[c] = ut[:, c * LANES:(c + 1) * LANES]


def middle(v, high, low, in_side, piece):
    whole = lambda i: (0, 0)
    return pl.pallas_call(
        middle_kernel,
        grid=(1,),
        in_specs=[
            pl.BlockSpec((8, LANES, LANES), lambda i: (0, 0, 0)),
            pl.BlockSpec((BLK, BLK), whole),
            pl.BlockSpec((BLK, BLK), whole),
            pl.BlockSpec((8, 8, LANES), lambda i: (0, 0, 0)),
            pl.BlockSpec((1, 8, LANES), lambda i: (0, 16, 0)),
        ],
        out_specs=pl.BlockSpec((8, LANES, LANES), lambda i: (0, 0, 0)),
        out_shape=jax.ShapeDtypeStruct((8, LANES, LANES), f32),
        compiler_params=params("arbitrary"),
        cost_estimate=pl.CostEstimate(flops=16 * 10**8, bytes_accessed=6 * 10**6, transcendentals=0),
    )(v, high, low, in_side, piece)


def back_kernel(u_ref, high_ref, low_ref, out_ref):
    u_high, u_low = halves(u_ref[...].reshape(BLK, LANES).T)
    both = mul(jnp.concatenate([u_high, u_low], axis=0), high_ref[...], 1, 1)
    out_ref[...] = both[:LANES] + both[LANES:] + mul(u_high, low_ref[...], 1, 1)


def back(u, high, low):
    return pl.pallas_call(
        back_kernel,
        grid=(2,),
        in_specs=[
            pl.BlockSpec((8, LANES, LANES), lambda i: (0, 0, 0)),
            pl.BlockSpec((512, BLK), lambda i: (i, 0)),
            pl.BlockSpec((512, BLK), lambda i: (i, 0)),
        ],
        out_specs=pl.BlockSpec((LANES, 512), lambda i: (0, i)),
        out_shape=jax.ShapeDtypeStruct((LANES, BLK), f32),
        compiler_params=params("arbitrary"),
        cost_estimate=pl.CostEstimate(flops=8 * 10**8, bytes_accessed=5 * 10**6, transcendentals=0),
    )(u, high, low)


def body(
    layer_inputs,
    output_grads,
    feature_order,
    block_slot,
    layer_owner,
    in_basis,
    in_values,
    out_basis,
    out_values,
):
    me = jnp.stack([lax.axis_index("y"), lax.axis_index("h"), lax.axis_index("z"), lax.axis_index(("l", "c"))])
    me = jnp.concatenate([me.astype(i32), block_slot])

    chunks = gather_columns(me, feature_order, layer_inputs.reshape(32, DIN))
    grads = output_grads.reshape(LANES, BLK)
    grads = jnp.stack([grads, flip(grads, "h")])
    chunks, grads, out_part = lax.optimization_barrier((chunks, grads, out_basis[0]))
    tokens = lax.all_to_all(chunks, ("y", "h", "l", "c"), 0, 0, tiled=True).reshape(BLK, 512)

    packed = pack_basis(out_part, out_values)
    packed, tokens, in_part = lax.optimization_barrier((packed, tokens, in_basis))
    spread = lax.all_to_all(packed, ALL_DP, 0, 0, tiled=True)
    piece = lax.dynamic_index_in_dim(spread, layer_owner[0], 0, keepdims=True)

    in_part = pack_basis(in_part, in_values.reshape(1, LANES))
    in_part = lax.dynamic_slice_in_dim(in_part, lax.axis_index("c") * 2, 2, 0)
    in_part = jnp.stack([in_part, lax.ppermute(in_part, ("h", "l"), [(i, 3 - i) for i in range(4)])])

    grads, in_part = lax.optimization_barrier((lax.all_gather(grads, "y"), in_part))
    in_own = lax.all_gather(in_part, "z")
    own, *words = partial_rows(me, tokens, grads)
    piece, own, *words = lax.optimization_barrier((piece, own, *words))
    words = [along(w, "z", k + 1) for k, w in enumerate(words)]

    got = lax.all_to_all(jnp.broadcast_to(piece, spread.shape), ALL_DP, 0, 0, tiled=True)
    in_own, *_ = lax.optimization_barrier((in_own, *words))
    in_high, in_low, in_side = unpack_basis(me, in_own, flip(in_own, "c"))

    v, out_high, out_low = front(got, own, words)
    v = lax.all_to_all(v, PAIR, 0, 0, tiled=True)
    u = middle(v, in_high, in_low, in_side, piece)
    u = lax.all_to_all(u, PAIR, 0, 0, tiled=True)
    return back(u, out_high, out_low)


def along(block, axis, shift):
    if shift == 0:
        return block
    return lax.ppermute(block, axis, [(i, (i + shift) % 4) for i in range(4)])


def flip(block, axis):
    return lax.ppermute(block, axis, [(0, 1), (1, 0)])


def solution(mesh):
    fine = Mesh(mesh.devices.reshape(4, 2, 4, 2, 2), ("y", "h", "z", "l", "c"))
    dp, mp = ("y", "h", "z"), ("l", "c")
    in_specs = (
        P(dp + mp, None, None),
        P(dp, None, mp),
        P(),
        P(),
        P(),
        P(dp, None),
        P(dp),
        P(dp, mp, None),
        P(dp, mp),
    )
    return jax.shard_map(body, mesh=fine, in_specs=in_specs, out_specs=P(dp, mp), check_vma=False)
```

```python
import jax
import jax.numpy as jnp
from jax import lax
from jax.experimental import pallas as pl
from jax.experimental.pallas import tpu as pltpu
from jax.sharding import Mesh, PartitionSpec as P

DIN = 4096
BLK = 1024
LANES = 128
GROUP = 256
ROWS = 136
DAMPING = 0.1
TOP = 32767.0
LOG_UNIT = 65536.0
VALUE_UNIT = 134217728.0
PAIR = ("h", "z")
ALL_DP = ("y", "h", "z")
VMEM = 48 * 1024 * 1024
MOST = 60 * 1024 * 1024
f32, bf16, i32 = jnp.float32, jnp.bfloat16, jnp.int32


def params(*semantics, limit=VMEM):
    return pltpu.CompilerParams(vmem_limit_bytes=limit, dimension_semantics=semantics or None)


def mul(a, b, ca=1, cb=0):
    return lax.dot_general(a, b, (((ca,), (cb,)), ((), ())), preferred_element_type=f32)


def halves(a):
    high = a.astype(bf16)
    return high, (a - high.astype(f32)).astype(bf16)


def gather_kernel(me_ref, order_ref, x_ref, out_ref):
    x = [x_ref[:, k * LANES:(k + 1) * LANES].astype(f32) for k in range(DIN // LANES)]
    for n in range(4):
        pair = sum(jnp.where(me_ref[4 + j] == pl.program_id(0) * 2 + n // 2, j, 0) for j in range(4))
        start = pair * BLK + n % 2 * 512
        for b in range(4):
            idx = order_ref[:, pl.ds(pl.multiple_of(start + b * LANES, LANES), LANES)]
            lane = jnp.broadcast_to(jnp.bitwise_and(idx, LANES - 1), (32, LANES))
            src = jnp.broadcast_to(jnp.right_shift(idx, 7), (32, LANES))
            acc = jnp.zeros((32, LANES), f32)
            for k in range(DIN // LANES):
                acc = jnp.where(src == k, jnp.take_along_axis(x[k], lane, axis=1), acc)
            for m in range(4):
                out_ref[n * 4 + m, :, b * LANES:(b + 1) * LANES] = acc.astype(bf16)


def gather_columns(me, order, x):
    return pl.pallas_call(
        gather_kernel,
        grid=(2,),
        in_specs=[
            pl.BlockSpec(memory_space=pltpu.SMEM),
            pl.BlockSpec((1, DIN), lambda i: (0, 0)),
            pl.BlockSpec((32, DIN), lambda i: (0, 0)),
        ],
        out_specs=pl.BlockSpec((16, 32, 512), lambda i: (i, 0, 0)),
        out_shape=jax.ShapeDtypeStruct((32, 32, 512), bf16),
        compiler_params=params("arbitrary"),
        cost_estimate=pl.CostEstimate(flops=10**6, bytes_accessed=10**6, transcendentals=0),
    )(me, order, x)


def diagonal():
    return lax.broadcasted_iota(i32, (LANES, LANES), 0) == lax.broadcasted_iota(i32, (LANES, LANES), 1)


def encode(part):
    most = jnp.maximum(jnp.max(jnp.abs(part), axis=1, keepdims=True), 1e-30)
    code = jnp.ceil(jnp.log2(most) * LOG_UNIT) + 4.0
    q = jnp.round(part * (TOP * jnp.exp2(-code / LOG_UNIT))).astype(i32)
    word = jnp.bitwise_or(jnp.left_shift(q[:, LANES:], 16), jnp.bitwise_and(q[:, :LANES], 65535))
    return word, code.astype(i32)


def decode(word, unit):
    first = jnp.right_shift(jnp.left_shift(word, 16), 16).astype(f32) * unit
    return first, jnp.right_shift(word, 16).astype(f32) * unit


def to_row(column, eye):
    return jnp.sum(jnp.where(eye, column, 0), axis=0, keepdims=True)


def to_unit(row, eye):
    return jnp.exp2(jnp.sum(jnp.where(eye, row, 0), axis=1, keepdims=True).astype(f32) / LOG_UNIT) / TOP


def pack_kernel(basis_ref, values_ref, out_ref):
    eye = diagonal()
    blocks = values_ref.shape[1] // LANES
    count = out_ref.shape[0]
    for n in range(count // 4):
        codes = [[] for _ in range(4)]
        for g in range(4):
            word, code = encode(basis_ref[n * LANES:(n + 1) * LANES, g * GROUP:(g + 1) * GROUP])
            for d in range(4):
                out_ref[n * 4 + d, g * 32:(g + 1) * 32, :] = word[d * 32:(d + 1) * 32]
                codes[d].append(code[d * 32:(d + 1) * 32])
        for d in range(4):
            row = to_row(jnp.concatenate(codes[d], axis=0), eye)
            block = (n * 4 + d) % blocks
            coded = (values_ref[:, block * LANES:(block + 1) * LANES] * VALUE_UNIT).astype(i32)
            out_ref[n * 4 + d, LANES:ROWS, :] = jnp.concatenate([row, coded, jnp.zeros((6, LANES), i32)], axis=0)


def pack_basis(basis, values):
    rows = basis.shape[0]
    size = min(rows, 512)
    return pl.pallas_call(
        pack_kernel,
        grid=(rows // size,),
        in_specs=[pl.BlockSpec((size, BLK), lambda i: (i, 0)), pl.BlockSpec(values.shape, lambda i: (0, 0))],
        out_specs=pl.BlockSpec((size // 32, ROWS, LANES), lambda i: (i, 0, 0)),
        out_shape=jax.ShapeDtypeStruct((rows // 32, ROWS, LANES), i32),
        compiler_params=params("arbitrary"),
        cost_estimate=pl.CostEstimate(flops=rows * 10**4, bytes_accessed=rows * 6000, transcendentals=0),
    )(basis, values)


def decode_chunks(get, base, count, high_ref, low_ref, eye):
    for d in range(count):
        unit = to_unit(get(d, LANES, 1), eye)
        for g in range(4):
            pair = decode(get(d, g * 32, 32), unit[g * 32:(g + 1) * 32])
            for k in range(2):
                high, low = halves(pair[k])
                where = (pl.ds(base + d * 32, 32), slice(g * GROUP + k * LANES, g * GROUP + (k + 1) * LANES))
                high_ref[where] = high
                low_ref[where] = low


def unpack_kernel(me_ref, p0_ref, p1_ref, p2_ref, p3_ref, high_ref, low_ref, side_ref):
    eye = diagonal()
    for k, ref in enumerate((p0_ref, p1_ref, p2_ref, p3_ref)):
        z = lax.rem(me_ref[2] + 4 - k, 4)
        base = pl.multiple_of(z * LANES, LANES)
        decode_chunks(lambda d, start, size: ref[0, d, start:start + size, :], base, 4, high_ref, low_ref, eye)
        side_ref[z] = ref[0, 0, LANES:ROWS, :]


def unpack_basis(me, pieces):
    rows = lambda i, m: (i, 0)
    half = pl.BlockSpec((1, 4, ROWS, LANES), lambda i, m: (lax.rem(i + m[1], 2), 0, 0, 0))
    return pl.pallas_call(
        unpack_kernel,
        grid_spec=pltpu.PrefetchScalarGridSpec(
            num_scalar_prefetch=1,
            grid=(2,),
            in_specs=[half] * 4,
            out_specs=[pl.BlockSpec((512, BLK), rows)] * 2 + [pl.BlockSpec((4, 8, LANES), lambda i, m: (i, 0, 0))],
        ),
        out_shape=[jax.ShapeDtypeStruct((BLK, BLK), bf16)] * 2 + [jax.ShapeDtypeStruct((8, 8, LANES), i32)],
        compiler_params=params("arbitrary", limit=MOST),
        cost_estimate=pl.CostEstimate(flops=10**7, bytes_accessed=6 * 10**6, transcendentals=0),
    )(me, *pieces)


def partial_kernel(me_ref, tokens, grads_ref, *refs):
    own_ref, word_refs, total = refs[0], refs[1:4], refs[4]
    for r in range(4):
        grads = jnp.concatenate([grads_ref[r, me_ref[1]], grads_ref[r, 1 - me_ref[1]]], axis=0)
        part = mul(tokens[r * GROUP:(r + 1) * GROUP, :], grads, 0, 0)
        total[...] = part if r == 0 else total[...] + part
    eye = diagonal()
    for k in range(4):
        start = pl.multiple_of(lax.rem(me_ref[2] + k, 4) * LANES, LANES)
        if k == 0:
            own_ref[...] = total[pl.ds(start, LANES), :]
            continue
        rows = []
        for g in range(4):
            word, code = encode(total[pl.ds(start, LANES), g * GROUP:(g + 1) * GROUP])
            word_refs[k - 1][g * LANES:(g + 1) * LANES, :] = word
            rows.append(to_row(code, eye))
        word_refs[k - 1][4 * LANES:, :] = jnp.concatenate(rows + [jnp.zeros((4, LANES), i32)], axis=0)


def partial_rows(me, tokens, grads):
    vmem = pl.BlockSpec(memory_space=pltpu.VMEM)
    return pl.pallas_call(
        partial_kernel,
        in_specs=[pl.BlockSpec(memory_space=pltpu.SMEM)] + [vmem] * 2,
        out_specs=[vmem] * 4,
        out_shape=[jax.ShapeDtypeStruct((LANES, BLK), f32)] + [jax.ShapeDtypeStruct((520, LANES), i32)] * 3,
        scratch_shapes=[pltpu.VMEM((512, BLK), f32)],
        compiler_params=params(limit=MOST),
        cost_estimate=pl.CostEstimate(flops=10**9, bytes_accessed=5 * 10**6, transcendentals=0),
    )(me, tokens, grads)


def front_kernel(got_ref, own_ref, w1_ref, w2_ref, w3_ref, v_ref, high_ref, low_ref, grad):
    step = pl.program_id(0)
    eye = diagonal()
    decode_chunks(lambda d, start, size: got_ref[d, start:start + size, :], 0, 16, high_ref, low_ref, eye)

    @pl.when(step == 0)
    def _():
        for g in range(4):
            sums = [own_ref[:, g * GROUP:g * GROUP + LANES], own_ref[:, g * GROUP + LANES:(g + 1) * GROUP]]
            for ref in (w1_ref, w2_ref, w3_ref):
                unit = to_unit(ref[4 * LANES + g:4 * LANES + g + 1, :], eye)
                pair = decode(ref[g * LANES:(g + 1) * LANES, :], unit)
                sums = [sums[0] + pair[0], sums[1] + pair[1]]
            grad[g // 2, :, g % 2 * GROUP:(g % 2 + 1) * GROUP] = jnp.concatenate(sums, axis=1)

    grad_high, grad_low = halves(grad[step])
    both = mul(jnp.concatenate([grad_high, grad_low], axis=0), high_ref[...])
    v = both[:LANES] + both[LANES:] + mul(grad_high, low_ref[...])
    for c in range(8):
        part = v[:, c * LANES:(c + 1) * LANES]
        v_ref[c] = jnp.where(step == 0, part, v_ref[c] + part)


def front(got, own, words):
    whole = lambda i: (0, 0)
    return pl.pallas_call(
        front_kernel,
        grid=(2,),
        in_specs=[pl.BlockSpec((16, ROWS, LANES), lambda i: (i, 0, 0)), pl.BlockSpec((LANES, BLK), whole)]
        + [pl.BlockSpec((520, LANES), whole)] * 3,
        out_specs=[pl.BlockSpec((8, LANES, LANES), lambda i: (0, 0, 0))]
        + [pl.BlockSpec((512, BLK), lambda i: (i, 0))] * 2,
        out_shape=[jax.ShapeDtypeStruct((8, LANES, LANES), f32)] + [jax.ShapeDtypeStruct((BLK, BLK), bf16)] * 2,
        scratch_shapes=[pltpu.VMEM((2, LANES, 512), f32)],
        compiler_params=params("arbitrary", limit=MOST),
        cost_estimate=pl.CostEstimate(flops=8 * 10**8, bytes_accessed=8 * 10**6, transcendentals=0),
    )(got, own, *words)


def middle_kernel(v_ref, high_ref, low_ref, in_side_ref, out_side_ref, u_ref):
    v_high, v_low = halves(v_ref[...].reshape(BLK, LANES))
    qh, ql = high_ref[...], low_ref[...]
    both = mul(jnp.concatenate([v_high, v_low], axis=1), qh, 0, 0)
    rt = both[:LANES] + both[LANES:] + mul(v_high, ql, 0, 0)
    la = jnp.concatenate([in_side_ref[c, 1:2, :] for c in range(4)], axis=1).astype(f32) / VALUE_UNIT
    lb = jnp.sum(jnp.where(diagonal(), out_side_ref[0, 1:2, :], 0), axis=1, keepdims=True).astype(f32) / VALUE_UNIT
    st = rt / (lb * la + DAMPING)
    s_high, s_low = halves(st)
    both = mul(jnp.concatenate([s_high, s_low], axis=0), qh, 1, 1)
    ut = both[:LANES] + both[LANES:] + mul(s_high, ql, 1, 1)
    for c in range(8):
        part = ut[:, c * LANES:(c + 1) * LANES]
        u_ref[c] = jnp.where(pl.program_id(0) == 0, part, u_ref[c] + part)


def middle(v, high, low, in_side, piece):
    return pl.pallas_call(
        middle_kernel,
        grid=(2,),
        in_specs=[
            pl.BlockSpec((8, LANES, LANES), lambda i: (0, 0, 0)),
            pl.BlockSpec((BLK, 512), lambda i: (0, i)),
            pl.BlockSpec((BLK, 512), lambda i: (0, i)),
            pl.BlockSpec((4, 8, LANES), lambda i: (i, 0, 0)),
            pl.BlockSpec((1, 8, LANES), lambda i: (0, 16, 0)),
        ],
        out_specs=pl.BlockSpec((8, LANES, LANES), lambda i: (0, 0, 0)),
        out_shape=jax.ShapeDtypeStruct((8, LANES, LANES), f32),
        compiler_params=params("arbitrary", limit=MOST),
        cost_estimate=pl.CostEstimate(flops=16 * 10**8, bytes_accessed=6 * 10**6, transcendentals=0),
    )(v, high, low, in_side, piece)


def back_kernel(u_ref, high_ref, low_ref, out_ref):
    u_high, u_low = halves(u_ref[...].reshape(BLK, LANES).T)
    both = mul(jnp.concatenate([u_high, u_low], axis=0), high_ref[...], 1, 1)
    out_ref[...] = both[:LANES] + both[LANES:] + mul(u_high, low_ref[...], 1, 1)


def back(u, high, low):
    return pl.pallas_call(
        back_kernel,
        grid=(2,),
        in_specs=[
            pl.BlockSpec((8, LANES, LANES), lambda i: (0, 0, 0)),
            pl.BlockSpec((512, BLK), lambda i: (i, 0)),
            pl.BlockSpec((512, BLK), lambda i: (i, 0)),
        ],
        out_specs=pl.BlockSpec((LANES, 512), lambda i: (0, i)),
        out_shape=jax.ShapeDtypeStruct((LANES, BLK), f32),
        compiler_params=params("arbitrary"),
        cost_estimate=pl.CostEstimate(flops=8 * 10**8, bytes_accessed=5 * 10**6, transcendentals=0),
    )(u, high, low)


def body(
    layer_inputs,
    output_grads,
    feature_order,
    block_slot,
    layer_owner,
    in_basis,
    in_values,
    out_basis,
    out_values,
):
    me = jnp.stack([lax.axis_index("y"), lax.axis_index("h"), lax.axis_index("z"), lax.axis_index(("l", "c"))])
    me = jnp.concatenate([me.astype(i32), block_slot])

    in_part = pack_basis(in_basis, in_values.reshape(1, LANES))
    in_cross = lax.ppermute(in_part, ("h", "l"), [(i, 3 - i) for i in range(4)])

    chunks = gather_columns(me, feature_order, layer_inputs.reshape(32, DIN))
    grads = output_grads.reshape(LANES, BLK)
    grads = jnp.stack([grads, flip(grads, "h")])
    chunks, grads, in_part, in_cross, out_part = lax.optimization_barrier((chunks, grads, in_part, in_cross, out_basis[0]))
    tokens = lax.all_to_all(chunks, ("y", "h", "l", "c"), 0, 0, tiled=True).reshape(BLK, 512)

    packed = pack_basis(out_part, out_values)
    packed, tokens = lax.optimization_barrier((packed, tokens))
    spread = lax.all_to_all(packed, ALL_DP, 0, 0, tiled=True)
    piece = lax.dynamic_index_in_dim(spread, layer_owner[0], 0, keepdims=True)

    grads = lax.all_gather(grads, "y")
    own, *words = partial_rows(me, tokens, grads)
    piece, own, *words = lax.optimization_barrier((piece, own, *words))
    words = [along(w, "z", k + 1) for k, w in enumerate(words)]

    piece, in_part, in_cross = lax.optimization_barrier((piece, in_part, in_cross))
    got = lax.all_to_all(jnp.broadcast_to(piece, spread.shape), ALL_DP, 0, 0, tiled=True)
    v, out_high, out_low = front(got, own, words)

    in_pieces = [jnp.stack([along(in_part, "z", k), along(in_cross, "z", k)]) for k in range(4)]
    v, *in_pieces = lax.optimization_barrier((v, *in_pieces))
    v = lax.all_to_all(v, PAIR, 0, 0, tiled=True)
    in_high, in_low, in_side = unpack_basis(me, in_pieces)
    u = middle(v, in_high, in_low, in_side, piece)
    u = lax.all_to_all(u, PAIR, 0, 0, tiled=True)
    return back(u, out_high, out_low)


def along(block, axis, shift):
    if shift == 0:
        return block
    return lax.ppermute(block, axis, [(i, (i + shift) % 4) for i in range(4)])


def flip(block, axis):
    return lax.ppermute(block, axis, [(0, 1), (1, 0)])


def solution(mesh):
    fine = Mesh(mesh.devices.reshape(4, 2, 4, 2, 2), ("y", "h", "z", "l", "c"))
    dp, mp = ("y", "h", "z"), ("l", "c")
    in_specs = (
        P(dp + mp, None, None),
        P(dp, None, mp),
        P(),
        P(),
        P(),
        P(dp, None),
        P(dp),
        P(dp, mp, None),
        P(dp, mp),
    )
    return jax.shard_map(body, mesh=fine, in_specs=in_specs, out_specs=P(dp, mp), check_vma=False)
```

```python
import jax
import jax.numpy as jnp
from jax import lax
from jax.experimental import pallas as pl
from jax.experimental.pallas import tpu as pltpu
from jax.sharding import Mesh, PartitionSpec as P

DIN = 4096
BLK = 1024
LANES = 128
GROUP = 256
ROWS = 136
DAMPING = 0.1
TOP = 32767.0
LOG_UNIT = 65536.0
VALUE_UNIT = 134217728.0
PAIR = ("h", "z")
ALL_DP = ("y", "h", "z")
VMEM = 48 * 1024 * 1024
MOST = 60 * 1024 * 1024
f32, bf16, i32 = jnp.float32, jnp.bfloat16, jnp.int32


def params(*semantics, limit=VMEM):
    return pltpu.CompilerParams(vmem_limit_bytes=limit, dimension_semantics=semantics or None)


def mul(a, b, ca=1, cb=0):
    return lax.dot_general(a, b, (((ca,), (cb,)), ((), ())), preferred_element_type=f32)


def halves(a):
    high = a.astype(bf16)
    return high, (a - high.astype(f32)).astype(bf16)


def gather_kernel(me_ref, order_ref, x_ref, out_ref):
    x = [x_ref[:, k * LANES:(k + 1) * LANES].astype(f32) for k in range(DIN // LANES)]
    for n in range(4):
        pair = sum(jnp.where(me_ref[4 + j] == pl.program_id(0) * 2 + n // 2, j, 0) for j in range(4))
        start = pair * BLK + n % 2 * 512
        for b in range(4):
            idx = order_ref[:, pl.ds(pl.multiple_of(start + b * LANES, LANES), LANES)]
            lane = jnp.broadcast_to(jnp.bitwise_and(idx, LANES - 1), (32, LANES))
            src = jnp.broadcast_to(jnp.right_shift(idx, 7), (32, LANES))
            acc = jnp.zeros((32, LANES), f32)
            for k in range(DIN // LANES):
                acc = jnp.where(src == k, jnp.take_along_axis(x[k], lane, axis=1), acc)
            out_ref[n, :, b * LANES:(b + 1) * LANES] = acc.astype(bf16)


def gather_columns(me, order, x):
    return pl.pallas_call(
        gather_kernel,
        grid=(2,),
        in_specs=[
            pl.BlockSpec(memory_space=pltpu.SMEM),
            pl.BlockSpec((1, DIN), lambda i: (0, 0)),
            pl.BlockSpec((32, DIN), lambda i: (0, 0)),
        ],
        out_specs=pl.BlockSpec((4, 32, 512), lambda i: (i, 0, 0)),
        out_shape=jax.ShapeDtypeStruct((8, 32, 512), bf16),
        compiler_params=params("arbitrary"),
        cost_estimate=pl.CostEstimate(flops=10**6, bytes_accessed=10**6, transcendentals=0),
    )(me, order, x)


def diagonal():
    return lax.broadcasted_iota(i32, (LANES, LANES), 0) == lax.broadcasted_iota(i32, (LANES, LANES), 1)


def encode(part):
    most = jnp.maximum(jnp.max(jnp.abs(part), axis=1, keepdims=True), 1e-30)
    code = jnp.ceil(jnp.log2(most) * LOG_UNIT) + 4.0
    q = jnp.round(part * (TOP * jnp.exp2(-code / LOG_UNIT))).astype(i32)
    word = jnp.bitwise_or(jnp.left_shift(q[:, LANES:], 16), jnp.bitwise_and(q[:, :LANES], 65535))
    return word, code.astype(i32)


def decode(word, unit):
    first = jnp.right_shift(jnp.left_shift(word, 16), 16).astype(f32) * unit
    return first, jnp.right_shift(word, 16).astype(f32) * unit


def to_row(column, eye):
    return jnp.sum(jnp.where(eye, column, 0), axis=0, keepdims=True)


def to_unit(row, eye):
    return jnp.exp2(jnp.sum(jnp.where(eye, row, 0), axis=1, keepdims=True).astype(f32) / LOG_UNIT) / TOP


def pack_kernel(basis_ref, values_ref, out_ref):
    eye = diagonal()
    blocks = values_ref.shape[1] // LANES
    count = out_ref.shape[0]
    for n in range(count // 4):
        codes = [[] for _ in range(4)]
        for g in range(4):
            word, code = encode(basis_ref[n * LANES:(n + 1) * LANES, g * GROUP:(g + 1) * GROUP])
            for d in range(4):
                out_ref[n * 4 + d, g * 32:(g + 1) * 32, :] = word[d * 32:(d + 1) * 32]
                codes[d].append(code[d * 32:(d + 1) * 32])
        for d in range(4):
            row = to_row(jnp.concatenate(codes[d], axis=0), eye)
            block = (n * 4 + d) % blocks
            coded = (values_ref[:, block * LANES:(block + 1) * LANES] * VALUE_UNIT).astype(i32)
            out_ref[n * 4 + d, LANES:ROWS, :] = jnp.concatenate([row, coded, jnp.zeros((6, LANES), i32)], axis=0)


def pack_basis(basis, values):
    rows = basis.shape[0]
    size = min(rows, 512)
    return pl.pallas_call(
        pack_kernel,
        grid=(rows // size,),
        in_specs=[pl.BlockSpec((size, BLK), lambda i: (i, 0)), pl.BlockSpec(values.shape, lambda i: (0, 0))],
        out_specs=pl.BlockSpec((size // 32, ROWS, LANES), lambda i: (i, 0, 0)),
        out_shape=jax.ShapeDtypeStruct((rows // 32, ROWS, LANES), i32),
        compiler_params=params("arbitrary"),
        cost_estimate=pl.CostEstimate(flops=rows * 10**4, bytes_accessed=rows * 6000, transcendentals=0),
    )(basis, values)


def decode_chunks(get, base, count, high_ref, low_ref, eye):
    for d in range(count):
        unit = to_unit(get(d, LANES, 1), eye)
        for g in range(4):
            pair = decode(get(d, g * 32, 32), unit[g * 32:(g + 1) * 32])
            for k in range(2):
                high, low = halves(pair[k])
                where = (pl.ds(base + d * 32, 32), slice(g * GROUP + k * LANES, g * GROUP + (k + 1) * LANES))
                high_ref[where] = high
                low_ref[where] = low


def unpack_kernel(me_ref, p0_ref, p1_ref, p2_ref, p3_ref, high_ref, low_ref, side_ref):
    eye = diagonal()
    for k, ref in enumerate((p0_ref, p1_ref, p2_ref, p3_ref)):
        z = lax.rem(me_ref[2] + 4 - k, 4)
        base = pl.multiple_of(z * LANES, LANES)
        decode_chunks(lambda d, start, size: ref[0, d, start:start + size, :], base, 4, high_ref, low_ref, eye)
        side_ref[z] = ref[0, 0, LANES:ROWS, :]


def unpack_basis(me, pieces):
    rows = lambda i, m: (i, 0)
    half = pl.BlockSpec((1, 4, ROWS, LANES), lambda i, m: (lax.rem(i + m[1], 2), 0, 0, 0))
    return pl.pallas_call(
        unpack_kernel,
        grid_spec=pltpu.PrefetchScalarGridSpec(
            num_scalar_prefetch=1,
            grid=(2,),
            in_specs=[half] * 4,
            out_specs=[pl.BlockSpec((512, BLK), rows)] * 2 + [pl.BlockSpec((4, 8, LANES), lambda i, m: (i, 0, 0))],
        ),
        out_shape=[jax.ShapeDtypeStruct((BLK, BLK), bf16)] * 2 + [jax.ShapeDtypeStruct((8, 8, LANES), i32)],
        compiler_params=params("arbitrary", limit=MOST),
        cost_estimate=pl.CostEstimate(flops=10**7, bytes_accessed=6 * 10**6, transcendentals=0),
    )(me, *pieces)


def partial_kernel(me_ref, x0_ref, x1_ref, x2_ref, x3_ref, grads_ref, *refs):
    own_ref, word_refs, tokens, total = refs[0], refs[1:4], refs[4], refs[5]
    for j, x_ref in enumerate((x0_ref, x1_ref, x2_ref, x3_ref)):
        place = jnp.bitwise_xor(me_ref[3], j)
        for r in range(8):
            tokens[pl.ds(pl.multiple_of(r * LANES + place * 32, 32), 32), :] = x_ref[r]
    for r in range(4):
        grads = jnp.concatenate([grads_ref[r, me_ref[1]], grads_ref[r, 1 - me_ref[1]]], axis=0)
        part = mul(tokens[r * GROUP:(r + 1) * GROUP, :], grads, 0, 0)
        total[...] = part if r == 0 else total[...] + part
    eye = diagonal()
    for k in range(4):
        start = pl.multiple_of(lax.rem(me_ref[2] + k, 4) * LANES, LANES)
        if k == 0:
            own_ref[...] = total[pl.ds(start, LANES), :]
            continue
        rows = []
        for g in range(4):
            word, code = encode(total[pl.ds(start, LANES), g * GROUP:(g + 1) * GROUP])
            word_refs[k - 1][g * LANES:(g + 1) * LANES, :] = word
            rows.append(to_row(code, eye))
        word_refs[k - 1][4 * LANES:, :] = jnp.concatenate(rows + [jnp.zeros((4, LANES), i32)], axis=0)


def partial_rows(me, tokens, grads):
    vmem = pl.BlockSpec(memory_space=pltpu.VMEM)
    return pl.pallas_call(
        partial_kernel,
        in_specs=[pl.BlockSpec(memory_space=pltpu.SMEM)] + [vmem] * 5,
        out_specs=[vmem] * 4,
        out_shape=[jax.ShapeDtypeStruct((LANES, BLK), f32)] + [jax.ShapeDtypeStruct((520, LANES), i32)] * 3,
        scratch_shapes=[pltpu.VMEM((BLK, 512), bf16), pltpu.VMEM((512, BLK), f32)],
        compiler_params=params(limit=MOST),
        cost_estimate=pl.CostEstimate(flops=10**9, bytes_accessed=5 * 10**6, transcendentals=0),
    )(me, *tokens, grads)


def front_kernel(got_ref, own_ref, w1_ref, w2_ref, w3_ref, v_ref, high_ref, low_ref, grad):
    step = pl.program_id(0)
    eye = diagonal()
    decode_chunks(lambda d, start, size: got_ref[d, start:start + size, :], 0, 16, high_ref, low_ref, eye)

    @pl.when(step == 0)
    def _():
        for g in range(4):
            sums = [own_ref[:, g * GROUP:g * GROUP + LANES], own_ref[:, g * GROUP + LANES:(g + 1) * GROUP]]
            for ref in (w1_ref, w2_ref, w3_ref):
                unit = to_unit(ref[4 * LANES + g:4 * LANES + g + 1, :], eye)
                pair = decode(ref[g * LANES:(g + 1) * LANES, :], unit)
                sums = [sums[0] + pair[0], sums[1] + pair[1]]
            grad[g // 2, :, g % 2 * GROUP:(g % 2 + 1) * GROUP] = jnp.concatenate(sums, axis=1)

    grad_high, grad_low = halves(grad[step])
    both = mul(jnp.concatenate([grad_high, grad_low], axis=0), high_ref[...])
    v = both[:LANES] + both[LANES:] + mul(grad_high, low_ref[...])
    for c in range(8):
        part = v[:, c * LANES:(c + 1) * LANES]
        v_ref[c] = jnp.where(step == 0, part, v_ref[c] + part)


def front(got, own, words):
    whole = lambda i: (0, 0)
    return pl.pallas_call(
        front_kernel,
        grid=(2,),
        in_specs=[pl.BlockSpec((16, ROWS, LANES), lambda i: (i, 0, 0)), pl.BlockSpec((LANES, BLK), whole)]
        + [pl.BlockSpec((520, LANES), whole)] * 3,
        out_specs=[pl.BlockSpec((8, LANES, LANES), lambda i: (0, 0, 0))]
        + [pl.BlockSpec((512, BLK), lambda i: (i, 0))] * 2,
        out_shape=[jax.ShapeDtypeStruct((8, LANES, LANES), f32)] + [jax.ShapeDtypeStruct((BLK, BLK), bf16)] * 2,
        scratch_shapes=[pltpu.VMEM((2, LANES, 512), f32)],
        compiler_params=params("arbitrary", limit=MOST),
        cost_estimate=pl.CostEstimate(flops=8 * 10**8, bytes_accessed=8 * 10**6, transcendentals=0),
    )(got, own, *words)


def middle_kernel(v_ref, high_ref, low_ref, in_side_ref, out_side_ref, u_ref):
    v_high, v_low = halves(v_ref[...].reshape(BLK, LANES))
    qh, ql = high_ref[...], low_ref[...]
    both = mul(jnp.concatenate([v_high, v_low], axis=1), qh, 0, 0)
    rt = both[:LANES] + both[LANES:] + mul(v_high, ql, 0, 0)
    la = jnp.concatenate([in_side_ref[c, 1:2, :] for c in range(4)], axis=1).astype(f32) / VALUE_UNIT
    lb = jnp.sum(jnp.where(diagonal(), out_side_ref[0, 1:2, :], 0), axis=1, keepdims=True).astype(f32) / VALUE_UNIT
    st = rt / (lb * la + DAMPING)
    s_high, s_low = halves(st)
    both = mul(jnp.concatenate([s_high, s_low], axis=0), qh, 1, 1)
    ut = both[:LANES] + both[LANES:] + mul(s_high, ql, 1, 1)
    for c in range(8):
        part = ut[:, c * LANES:(c + 1) * LANES]
        u_ref[c] = jnp.where(pl.program_id(0) == 0, part, u_ref[c] + part)


def middle(v, high, low, in_side, piece):
    return pl.pallas_call(
        middle_kernel,
        grid=(2,),
        in_specs=[
            pl.BlockSpec((8, LANES, LANES), lambda i: (0, 0, 0)),
            pl.BlockSpec((BLK, 512), lambda i: (0, i)),
            pl.BlockSpec((BLK, 512), lambda i: (0, i)),
            pl.BlockSpec((4, 8, LANES), lambda i: (i, 0, 0)),
            pl.BlockSpec((1, 8, LANES), lambda i: (0, 16, 0)),
        ],
        out_specs=pl.BlockSpec((8, LANES, LANES), lambda i: (0, 0, 0)),
        out_shape=jax.ShapeDtypeStruct((8, LANES, LANES), f32),
        compiler_params=params("arbitrary", limit=MOST),
        cost_estimate=pl.CostEstimate(flops=16 * 10**8, bytes_accessed=6 * 10**6, transcendentals=0),
    )(v, high, low, in_side, piece)


def back_kernel(u_ref, high_ref, low_ref, out_ref):
    u_high, u_low = halves(u_ref[...].reshape(BLK, LANES).T)
    both = mul(jnp.concatenate([u_high, u_low], axis=0), high_ref[...], 1, 1)
    out_ref[...] = both[:LANES] + both[LANES:] + mul(u_high, low_ref[...], 1, 1)


def back(u, high, low):
    return pl.pallas_call(
        back_kernel,
        grid=(2,),
        in_specs=[
            pl.BlockSpec((8, LANES, LANES), lambda i: (0, 0, 0)),
            pl.BlockSpec((512, BLK), lambda i: (i, 0)),
            pl.BlockSpec((512, BLK), lambda i: (i, 0)),
        ],
        out_specs=pl.BlockSpec((LANES, 512), lambda i: (0, i)),
        out_shape=jax.ShapeDtypeStruct((LANES, BLK), f32),
        compiler_params=params("arbitrary"),
        cost_estimate=pl.CostEstimate(flops=8 * 10**8, bytes_accessed=5 * 10**6, transcendentals=0),
    )(u, high, low)


def body(
    layer_inputs,
    output_grads,
    feature_order,
    block_slot,
    layer_owner,
    in_basis,
    in_values,
    out_basis,
    out_values,
):
    me = jnp.stack([lax.axis_index("y"), lax.axis_index("h"), lax.axis_index("z"), lax.axis_index(("l", "c"))])
    me = jnp.concatenate([me.astype(i32), block_slot])

    in_part = pack_basis(in_basis, in_values.reshape(1, LANES))
    in_cross = lax.ppermute(in_part, ("h", "l"), [(i, 3 - i) for i in range(4)])

    chunks = gather_columns(me, feature_order, layer_inputs.reshape(32, DIN))
    grads = output_grads.reshape(LANES, BLK)
    grads = jnp.stack([grads, flip(grads, "h")])
    chunks, grads, out_part = lax.optimization_barrier((chunks, grads, out_basis[0]))
    moved = lax.all_to_all(chunks, ("y", "h"), 0, 0, tiled=True)
    tokens = [moved] + [lax.ppermute(moved, ("l", "c"), [(m, m ^ j) for m in range(4)]) for j in range(1, 4)]

    packed = pack_basis(out_part, out_values)
    packed, *tokens = lax.optimization_barrier((packed, *tokens))
    spread = lax.all_to_all(packed, ALL_DP, 0, 0, tiled=True)
    piece = lax.dynamic_index_in_dim(spread, layer_owner[0], 0, keepdims=True)

    grads = lax.all_gather(grads, "y")
    own, *words = partial_rows(me, tokens, grads)
    words = [along(w, "z", k + 1) for k, w in enumerate(words)]

    piece, in_part, in_cross, *words = lax.optimization_barrier((piece, in_part, in_cross, *words))
    got = lax.all_to_all(jnp.broadcast_to(piece, spread.shape), ALL_DP, 0, 0, tiled=True)
    v, out_high, out_low = front(got, own, words)

    in_pieces = [jnp.stack([along(in_part, "z", k), along(in_cross, "z", k)]) for k in range(4)]
    _, *in_pieces = lax.optimization_barrier((v, *in_pieces))
    v = lax.all_to_all(v, PAIR, 0, 0, tiled=True)
    in_high, in_low, in_side = unpack_basis(me, in_pieces)
    u = middle(v, in_high, in_low, in_side, piece)
    u = lax.all_to_all(u, PAIR, 0, 0, tiled=True)
    return back(u, out_high, out_low)


def along(block, axis, shift):
    if shift == 0:
        return block
    return lax.ppermute(block, axis, [(i, (i + shift) % 4) for i in range(4)])


def flip(block, axis):
    return lax.ppermute(block, axis, [(0, 1), (1, 0)])


def solution(mesh):
    fine = Mesh(mesh.devices.reshape(4, 2, 4, 2, 2), ("y", "h", "z", "l", "c"))
    dp, mp = ("y", "h", "z"), ("l", "c")
    in_specs = (
        P(dp + mp, None, None),
        P(dp, None, mp),
        P(),
        P(),
        P(),
        P(dp, None),
        P(dp),
        P(dp, mp, None),
        P(dp, mp),
    )
    return jax.shard_map(body, mesh=fine, in_specs=in_specs, out_specs=P(dp, mp), check_vma=False)
```

```python
import jax
import jax.numpy as jnp
from jax import lax
from jax.experimental import pallas as pl
from jax.experimental.pallas import tpu as pltpu
from jax.sharding import Mesh, PartitionSpec as P

DIN = 4096
BLK = 1024
LANES = 128
GROUP = 256
ROWS = 136
DAMPING = 0.1
TOP = 32767.0
LOG_UNIT = 65536.0
VALUE_UNIT = 134217728.0
PAIR = ("h", "z")
ALL_DP = ("y", "h", "z")
VMEM = 48 * 1024 * 1024
MOST = 60 * 1024 * 1024
f32, bf16, i32 = jnp.float32, jnp.bfloat16, jnp.int32


def params(*semantics, limit=VMEM):
    return pltpu.CompilerParams(vmem_limit_bytes=limit, dimension_semantics=semantics or None)


def mul(a, b, ca=1, cb=0):
    return lax.dot_general(a, b, (((ca,), (cb,)), ((), ())), preferred_element_type=f32)


def halves(a):
    high = a.astype(bf16)
    return high, (a - high.astype(f32)).astype(bf16)


def gather_kernel(me_ref, order_ref, x_ref, out_ref):
    x = [x_ref[:, k * LANES:(k + 1) * LANES].astype(f32) for k in range(DIN // LANES)]
    for n in range(4):
        pair = sum(jnp.where(me_ref[4 + j] == pl.program_id(0) * 2 + n // 2, j, 0) for j in range(4))
        start = pair * BLK + n % 2 * 512
        for b in range(4):
            idx = order_ref[:, pl.ds(pl.multiple_of(start + b * LANES, LANES), LANES)]
            lane = jnp.broadcast_to(jnp.bitwise_and(idx, LANES - 1), (32, LANES))
            src = jnp.broadcast_to(jnp.right_shift(idx, 7), (32, LANES))
            acc = jnp.zeros((32, LANES), f32)
            for k in range(DIN // LANES):
                acc = jnp.where(src == k, jnp.take_along_axis(x[k], lane, axis=1), acc)
            out_ref[n, :, b * LANES:(b + 1) * LANES] = acc.astype(bf16)


def gather_columns(me, order, x):
    return pl.pallas_call(
        gather_kernel,
        grid=(2,),
        in_specs=[
            pl.BlockSpec(memory_space=pltpu.SMEM),
            pl.BlockSpec((1, DIN), lambda i: (0, 0)),
            pl.BlockSpec((32, DIN), lambda i: (0, 0)),
        ],
        out_specs=pl.BlockSpec((4, 32, 512), lambda i: (i, 0, 0)),
        out_shape=jax.ShapeDtypeStruct((8, 32, 512), bf16),
        compiler_params=params("arbitrary"),
        cost_estimate=pl.CostEstimate(flops=10**6, bytes_accessed=10**6, transcendentals=0),
    )(me, order, x)


def diagonal():
    return lax.broadcasted_iota(i32, (LANES, LANES), 0) == lax.broadcasted_iota(i32, (LANES, LANES), 1)


def encode(part):
    most = jnp.maximum(jnp.max(jnp.abs(part), axis=1, keepdims=True), 1e-30)
    code = jnp.ceil(jnp.log2(most) * LOG_UNIT) + 4.0
    q = jnp.round(part * (TOP * jnp.exp2(-code / LOG_UNIT))).astype(i32)
    word = jnp.bitwise_or(jnp.left_shift(q[:, LANES:], 16), jnp.bitwise_and(q[:, :LANES], 65535))
    return word, code.astype(i32)


def decode(word, unit):
    first = jnp.right_shift(jnp.left_shift(word, 16), 16).astype(f32) * unit
    return first, jnp.right_shift(word, 16).astype(f32) * unit


def to_row(column, eye):
    return jnp.sum(jnp.where(eye, column, 0), axis=0, keepdims=True)


def to_unit(row, eye):
    return jnp.exp2(jnp.sum(jnp.where(eye, row, 0), axis=1, keepdims=True).astype(f32) / LOG_UNIT) / TOP


def pack_kernel(basis_ref, values_ref, out_ref):
    eye = diagonal()
    blocks = values_ref.shape[1] // LANES
    count = out_ref.shape[0]
    for n in range(count // 4):
        codes = [[] for _ in range(4)]
        for g in range(4):
            word, code = encode(basis_ref[n * LANES:(n + 1) * LANES, g * GROUP:(g + 1) * GROUP])
            for d in range(4):
                out_ref[n * 4 + d, g * 32:(g + 1) * 32, :] = word[d * 32:(d + 1) * 32]
                codes[d].append(code[d * 32:(d + 1) * 32])
        for d in range(4):
            row = to_row(jnp.concatenate(codes[d], axis=0), eye)
            block = (n * 4 + d) % blocks
            coded = (values_ref[:, block * LANES:(block + 1) * LANES] * VALUE_UNIT).astype(i32)
            out_ref[n * 4 + d, LANES:ROWS, :] = jnp.concatenate([row, coded, jnp.zeros((6, LANES), i32)], axis=0)


def pack_basis(basis, values):
    rows = basis.shape[0]
    size = min(rows, 512)
    return pl.pallas_call(
        pack_kernel,
        grid=(rows // size,),
        in_specs=[pl.BlockSpec((size, BLK), lambda i: (i, 0)), pl.BlockSpec(values.shape, lambda i: (0, 0))],
        out_specs=pl.BlockSpec((size // 32, ROWS, LANES), lambda i: (i, 0, 0)),
        out_shape=jax.ShapeDtypeStruct((rows // 32, ROWS, LANES), i32),
        compiler_params=params("arbitrary"),
        cost_estimate=pl.CostEstimate(flops=rows * 10**4, bytes_accessed=rows * 6000, transcendentals=0),
    )(basis, values)


def decode_chunks(get, base, count, high_ref, low_ref, eye):
    for d in range(count):
        unit = to_unit(get(d, LANES, 1), eye)
        for g in range(4):
            pair = decode(get(d, g * 32, 32), unit[g * 32:(g + 1) * 32])
            for k in range(2):
                high, low = halves(pair[k])
                where = (pl.ds(base + d * 32, 32), slice(g * GROUP + k * LANES, g * GROUP + (k + 1) * LANES))
                high_ref[where] = high
                low_ref[where] = low


def unpack_kernel(me_ref, got_ref, high_ref, low_ref, side_ref):
    eye = diagonal()
    for z in range(4):
        decode_chunks(lambda d, start, size: got_ref[z, 0, d, start:start + size, :], z * LANES, 4, high_ref, low_ref, eye)
        side_ref[z] = got_ref[z, 0, 0, LANES:ROWS, :]


def unpack_basis(me, got):
    rows = lambda i, m: (i, 0)
    return pl.pallas_call(
        unpack_kernel,
        grid_spec=pltpu.PrefetchScalarGridSpec(
            num_scalar_prefetch=1,
            grid=(2,),
            in_specs=[pl.BlockSpec((4, 1, 4, ROWS, LANES), lambda i, m: (0, lax.rem(i + m[1], 2), 0, 0, 0))],
            out_specs=[pl.BlockSpec((512, BLK), rows)] * 2 + [pl.BlockSpec((4, 8, LANES), lambda i, m: (i, 0, 0))],
        ),
        out_shape=[jax.ShapeDtypeStruct((BLK, BLK), bf16)] * 2 + [jax.ShapeDtypeStruct((8, 8, LANES), i32)],
        compiler_params=params("arbitrary", limit=MOST),
        cost_estimate=pl.CostEstimate(flops=10**7, bytes_accessed=6 * 10**6, transcendentals=0),
    )(me, got)


def partial_kernel(me_ref, x0_ref, x1_ref, x2_ref, x3_ref, grads_ref, *refs):
    own_ref, word_refs, tokens, total = refs[0], refs[1:4], refs[4], refs[5]
    for j, x_ref in enumerate((x0_ref, x1_ref, x2_ref, x3_ref)):
        place = jnp.bitwise_xor(me_ref[3], j)
        for r in range(8):
            tokens[pl.ds(pl.multiple_of(r * LANES + place * 32, 32), 32), :] = x_ref[r]
    for r in range(4):
        grads = jnp.concatenate([grads_ref[r, me_ref[1]], grads_ref[r, 1 - me_ref[1]]], axis=0)
        part = mul(tokens[r * GROUP:(r + 1) * GROUP, :], grads, 0, 0)
        total[...] = part if r == 0 else total[...] + part
    eye = diagonal()
    for k in range(4):
        start = pl.multiple_of(lax.rem(me_ref[2] + k, 4) * LANES, LANES)
        if k == 0:
            own_ref[...] = total[pl.ds(start, LANES), :]
            continue
        rows = []
        for g in range(4):
            word, code = encode(total[pl.ds(start, LANES), g * GROUP:(g + 1) * GROUP])
            word_refs[k - 1][g * LANES:(g + 1) * LANES, :] = word
            rows.append(to_row(code, eye))
        word_refs[k - 1][4 * LANES:, :] = jnp.concatenate(rows + [jnp.zeros((4, LANES), i32)], axis=0)


def partial_rows(me, tokens, grads):
    vmem = pl.BlockSpec(memory_space=pltpu.VMEM)
    return pl.pallas_call(
        partial_kernel,
        in_specs=[pl.BlockSpec(memory_space=pltpu.SMEM)] + [vmem] * 5,
        out_specs=[vmem] * 4,
        out_shape=[jax.ShapeDtypeStruct((LANES, BLK), f32)] + [jax.ShapeDtypeStruct((520, LANES), i32)] * 3,
        scratch_shapes=[pltpu.VMEM((BLK, 512), bf16), pltpu.VMEM((512, BLK), f32)],
        compiler_params=params(limit=MOST),
        cost_estimate=pl.CostEstimate(flops=10**9, bytes_accessed=5 * 10**6, transcendentals=0),
    )(me, *tokens, grads)


def front_kernel(got_ref, own_ref, w1_ref, w2_ref, w3_ref, v_ref, high_ref, low_ref, grad):
    step = pl.program_id(0)
    eye = diagonal()
    decode_chunks(lambda d, start, size: got_ref[d, start:start + size, :], 0, 16, high_ref, low_ref, eye)

    @pl.when(step == 0)
    def _():
        for g in range(4):
            sums = [own_ref[:, g * GROUP:g * GROUP + LANES], own_ref[:, g * GROUP + LANES:(g + 1) * GROUP]]
            for ref in (w1_ref, w2_ref, w3_ref):
                unit = to_unit(ref[4 * LANES + g:4 * LANES + g + 1, :], eye)
                pair = decode(ref[g * LANES:(g + 1) * LANES, :], unit)
                sums = [sums[0] + pair[0], sums[1] + pair[1]]
            grad[g // 2, :, g % 2 * GROUP:(g % 2 + 1) * GROUP] = jnp.concatenate(sums, axis=1)

    grad_high, grad_low = halves(grad[step])
    both = mul(jnp.concatenate([grad_high, grad_low], axis=0), high_ref[...])
    v = both[:LANES] + both[LANES:] + mul(grad_high, low_ref[...])
    for c in range(8):
        part = v[:, c * LANES:(c + 1) * LANES]
        v_ref[c] = jnp.where(step == 0, part, v_ref[c] + part)


def front(got, own, words):
    whole = lambda i: (0, 0)
    return pl.pallas_call(
        front_kernel,
        grid=(2,),
        in_specs=[pl.BlockSpec((16, ROWS, LANES), lambda i: (i, 0, 0)), pl.BlockSpec((LANES, BLK), whole)]
        + [pl.BlockSpec((520, LANES), whole)] * 3,
        out_specs=[pl.BlockSpec((8, LANES, LANES), lambda i: (0, 0, 0))]
        + [pl.BlockSpec((512, BLK), lambda i: (i, 0))] * 2,
        out_shape=[jax.ShapeDtypeStruct((8, LANES, LANES), f32)] + [jax.ShapeDtypeStruct((BLK, BLK), bf16)] * 2,
        scratch_shapes=[pltpu.VMEM((2, LANES, 512), f32)],
        compiler_params=params("arbitrary", limit=MOST),
        cost_estimate=pl.CostEstimate(flops=8 * 10**8, bytes_accessed=8 * 10**6, transcendentals=0),
    )(got, own, *words)


def middle_kernel(v_ref, high_ref, low_ref, in_side_ref, out_side_ref, u_ref):
    v_high, v_low = halves(v_ref[...].reshape(BLK, LANES))
    qh, ql = high_ref[...], low_ref[...]
    both = mul(jnp.concatenate([v_high, v_low], axis=1), qh, 0, 0)
    rt = both[:LANES] + both[LANES:] + mul(v_high, ql, 0, 0)
    la = jnp.concatenate([in_side_ref[c, 1:2, :] for c in range(4)], axis=1).astype(f32) / VALUE_UNIT
    lb = jnp.sum(jnp.where(diagonal(), out_side_ref[0, 1:2, :], 0), axis=1, keepdims=True).astype(f32) / VALUE_UNIT
    st = rt / (lb * la + DAMPING)
    s_high, s_low = halves(st)
    both = mul(jnp.concatenate([s_high, s_low], axis=0), qh, 1, 1)
    ut = both[:LANES] + both[LANES:] + mul(s_high, ql, 1, 1)
    for c in range(8):
        part = ut[:, c * LANES:(c + 1) * LANES]
        u_ref[c] = jnp.where(pl.program_id(0) == 0, part, u_ref[c] + part)


def middle(v, high, low, in_side, piece):
    return pl.pallas_call(
        middle_kernel,
        grid=(2,),
        in_specs=[
            pl.BlockSpec((8, LANES, LANES), lambda i: (0, 0, 0)),
            pl.BlockSpec((BLK, 512), lambda i: (0, i)),
            pl.BlockSpec((BLK, 512), lambda i: (0, i)),
            pl.BlockSpec((4, 8, LANES), lambda i: (i, 0, 0)),
            pl.BlockSpec((1, 8, LANES), lambda i: (0, 16, 0)),
        ],
        out_specs=pl.BlockSpec((8, LANES, LANES), lambda i: (0, 0, 0)),
        out_shape=jax.ShapeDtypeStruct((8, LANES, LANES), f32),
        compiler_params=params("arbitrary", limit=MOST),
        cost_estimate=pl.CostEstimate(flops=16 * 10**8, bytes_accessed=6 * 10**6, transcendentals=0),
    )(v, high, low, in_side, piece)


def back_kernel(u_ref, high_ref, low_ref, out_ref):
    u_high, u_low = halves(u_ref[...].reshape(BLK, LANES).T)
    both = mul(jnp.concatenate([u_high, u_low], axis=0), high_ref[...], 1, 1)
    out_ref[...] = both[:LANES] + both[LANES:] + mul(u_high, low_ref[...], 1, 1)


def back(u, high, low):
    return pl.pallas_call(
        back_kernel,
        grid=(2,),
        in_specs=[
            pl.BlockSpec((8, LANES, LANES), lambda i: (0, 0, 0)),
            pl.BlockSpec((512, BLK), lambda i: (i, 0)),
            pl.BlockSpec((512, BLK), lambda i: (i, 0)),
        ],
        out_specs=pl.BlockSpec((LANES, 512), lambda i: (0, i)),
        out_shape=jax.ShapeDtypeStruct((LANES, BLK), f32),
        compiler_params=params("arbitrary"),
        cost_estimate=pl.CostEstimate(flops=8 * 10**8, bytes_accessed=5 * 10**6, transcendentals=0),
    )(u, high, low)


def body(
    layer_inputs,
    output_grads,
    feature_order,
    block_slot,
    layer_owner,
    in_basis,
    in_values,
    out_basis,
    out_values,
):
    me = jnp.stack([lax.axis_index("y"), lax.axis_index("h"), lax.axis_index("z"), lax.axis_index(("l", "c"))])
    me = jnp.concatenate([me.astype(i32), block_slot])

    in_part = pack_basis(in_basis, in_values.reshape(1, LANES))
    in_pair = jnp.stack([in_part, lax.ppermute(in_part, ("h", "l"), [(i, 3 - i) for i in range(4)])])

    chunks = gather_columns(me, feature_order, layer_inputs.reshape(32, DIN))
    grads = output_grads.reshape(LANES, BLK)
    grads = jnp.stack([grads, flip(grads, "h")])
    chunks, grads, out_part = lax.optimization_barrier((chunks, grads, out_basis[0]))
    moved = lax.all_to_all(chunks, ("y", "h"), 0, 0, tiled=True)
    tokens = [moved] + [lax.ppermute(moved, ("l", "c"), [(m, m ^ j) for m in range(4)]) for j in range(1, 4)]

    packed = pack_basis(out_part, out_values)
    packed, in_pair, *tokens = lax.optimization_barrier((packed, in_pair, *tokens))
    spread = lax.all_to_all(packed, ALL_DP, 0, 0, tiled=True)
    piece = lax.dynamic_index_in_dim(spread, layer_owner[0], 0, keepdims=True)

    grads = lax.all_gather(grads, "y")
    _, in_pair = lax.optimization_barrier((grads, in_pair))
    in_all = lax.all_gather(in_pair, "z")
    own, *words = partial_rows(me, tokens, grads)
    piece, _ = lax.optimization_barrier((piece, own))
    words = [along(w, "z", k + 1) for k, w in enumerate(words)]

    got = lax.all_to_all(jnp.broadcast_to(piece, spread.shape), ALL_DP, 0, 0, tiled=True)
    v, out_high, out_low = front(got, own, words)

    v = lax.all_to_all(v, PAIR, 0, 0, tiled=True)
    in_high, in_low, in_side = unpack_basis(me, in_all)
    u = middle(v, in_high, in_low, in_side, piece)
    u = lax.all_to_all(u, PAIR, 0, 0, tiled=True)
    return back(u, out_high, out_low)


def along(block, axis, shift):
    if shift == 0:
        return block
    return lax.ppermute(block, axis, [(i, (i + shift) % 4) for i in range(4)])


def flip(block, axis):
    return lax.ppermute(block, axis, [(0, 1), (1, 0)])


def solution(mesh):
    fine = Mesh(mesh.devices.reshape(4, 2, 4, 2, 2), ("y", "h", "z", "l", "c"))
    dp, mp = ("y", "h", "z"), ("l", "c")
    in_specs = (
        P(dp + mp, None, None),
        P(dp, None, mp),
        P(),
        P(),
        P(),
        P(dp, None),
        P(dp),
        P(dp, mp, None),
        P(dp, mp),
    )
    return jax.shard_map(body, mesh=fine, in_specs=in_specs, out_specs=P(dp, mp), check_vma=False)
```

```python
import jax
import jax.numpy as jnp
from jax import lax
from jax.experimental import pallas as pl
from jax.experimental.pallas import tpu as pltpu
from jax.sharding import Mesh, PartitionSpec as P

DIN = 4096
BLK = 1024
LANES = 128
GROUP = 256
ROWS = 136
DAMPING = 0.1
TOP = 32767.0
LOG_UNIT = 65536.0
VALUE_UNIT = 134217728.0
PAIR = ("h", "z")
ALL_DP = ("y", "h", "z")
VMEM = 48 * 1024 * 1024
MOST = 60 * 1024 * 1024
f32, bf16, i32 = jnp.float32, jnp.bfloat16, jnp.int32


def params(*semantics, limit=VMEM):
    return pltpu.CompilerParams(vmem_limit_bytes=limit, dimension_semantics=semantics or None)


def mul(a, b, ca=1, cb=0):
    return lax.dot_general(a, b, (((ca,), (cb,)), ((), ())), preferred_element_type=f32)


def halves(a):
    high = a.astype(bf16)
    return high, (a - high.astype(f32)).astype(bf16)


def gather_kernel(me_ref, order_ref, x_ref, out_ref):
    x = [x_ref[:, k * LANES:(k + 1) * LANES].astype(f32) for k in range(DIN // LANES)]
    for n in range(4):
        pair = sum(jnp.where(me_ref[4 + j] == pl.program_id(0) * 2 + n // 2, j, 0) for j in range(4))
        start = pair * BLK + n % 2 * 512
        for b in range(4):
            idx = order_ref[:, pl.ds(pl.multiple_of(start + b * LANES, LANES), LANES)]
            lane = jnp.broadcast_to(jnp.bitwise_and(idx, LANES - 1), (32, LANES))
            src = jnp.broadcast_to(jnp.right_shift(idx, 7), (32, LANES))
            acc = jnp.zeros((32, LANES), f32)
            for k in range(DIN // LANES):
                acc = jnp.where(src == k, jnp.take_along_axis(x[k], lane, axis=1), acc)
            out_ref[n, :, b * LANES:(b + 1) * LANES] = acc.astype(bf16)


def gather_columns(me, order, x):
    return pl.pallas_call(
        gather_kernel,
        grid=(2,),
        in_specs=[
            pl.BlockSpec(memory_space=pltpu.SMEM),
            pl.BlockSpec((1, DIN), lambda i: (0, 0)),
            pl.BlockSpec((32, DIN), lambda i: (0, 0)),
        ],
        out_specs=pl.BlockSpec((4, 32, 512), lambda i: (i, 0, 0)),
        out_shape=jax.ShapeDtypeStruct((8, 32, 512), bf16),
        compiler_params=params("arbitrary"),
        cost_estimate=pl.CostEstimate(flops=10**6, bytes_accessed=10**6, transcendentals=0),
    )(me, order, x)


def diagonal():
    return lax.broadcasted_iota(i32, (LANES, LANES), 0) == lax.broadcasted_iota(i32, (LANES, LANES), 1)


def encode(part):
    most = jnp.maximum(jnp.max(jnp.abs(part), axis=1, keepdims=True), 1e-30)
    code = jnp.ceil(jnp.log2(most) * LOG_UNIT) + 4.0
    q = jnp.round(part * (TOP * jnp.exp2(-code / LOG_UNIT))).astype(i32)
    word = jnp.bitwise_or(jnp.left_shift(q[:, LANES:], 16), jnp.bitwise_and(q[:, :LANES], 65535))
    return word, code.astype(i32)


def decode(word, unit):
    first = jnp.right_shift(jnp.left_shift(word, 16), 16).astype(f32) * unit
    return first, jnp.right_shift(word, 16).astype(f32) * unit


def to_row(column, eye):
    return jnp.sum(jnp.where(eye, column, 0), axis=0, keepdims=True)


def to_unit(row, eye):
    return jnp.exp2(jnp.sum(jnp.where(eye, row, 0), axis=1, keepdims=True).astype(f32) / LOG_UNIT) / TOP


def pack_kernel(basis_ref, values_ref, out_ref):
    eye = diagonal()
    blocks = values_ref.shape[1] // LANES
    count = out_ref.shape[0]
    for n in range(count // 4):
        codes = [[] for _ in range(4)]
        for g in range(4):
            word, code = encode(basis_ref[n * LANES:(n + 1) * LANES, g * GROUP:(g + 1) * GROUP])
            for d in range(4):
                out_ref[n * 4 + d, g * 32:(g + 1) * 32, :] = word[d * 32:(d + 1) * 32]
                codes[d].append(code[d * 32:(d + 1) * 32])
        for d in range(4):
            row = to_row(jnp.concatenate(codes[d], axis=0), eye)
            block = (n * 4 + d) % blocks
            coded = (values_ref[:, block * LANES:(block + 1) * LANES] * VALUE_UNIT).astype(i32)
            out_ref[n * 4 + d, LANES:ROWS, :] = jnp.concatenate([row, coded, jnp.zeros((6, LANES), i32)], axis=0)


def pack_basis(basis, values):
    rows = basis.shape[0]
    size = min(rows, 512)
    return pl.pallas_call(
        pack_kernel,
        grid=(rows // size,),
        in_specs=[pl.BlockSpec((size, BLK), lambda i: (i, 0)), pl.BlockSpec(values.shape, lambda i: (0, 0))],
        out_specs=pl.BlockSpec((size // 32, ROWS, LANES), lambda i: (i, 0, 0)),
        out_shape=jax.ShapeDtypeStruct((rows // 32, ROWS, LANES), i32),
        compiler_params=params("arbitrary"),
        cost_estimate=pl.CostEstimate(flops=rows * 10**4, bytes_accessed=rows * 6000, transcendentals=0),
    )(basis, values)


def decode_chunks(get, base, count, high_ref, low_ref, eye):
    for d in range(count):
        unit = to_unit(get(d, LANES, 1), eye)
        for g in range(4):
            pair = decode(get(d, g * 32, 32), unit[g * 32:(g + 1) * 32])
            for k in range(2):
                high, low = halves(pair[k])
                where = (pl.ds(base + d * 32, 32), slice(g * GROUP + k * LANES, g * GROUP + (k + 1) * LANES))
                high_ref[where] = high
                low_ref[where] = low


def unpack_kernel(me_ref, got_ref, high_ref, low_ref, side_ref):
    eye = diagonal()
    for z in range(4):
        decode_chunks(lambda d, start, size: got_ref[z, 0, d, start:start + size, :], z * LANES, 4, high_ref, low_ref, eye)
        side_ref[z] = got_ref[z, 0, 0, LANES:ROWS, :]


def unpack_basis(me, got):
    rows = lambda i, m: (i, 0)
    return pl.pallas_call(
        unpack_kernel,
        grid_spec=pltpu.PrefetchScalarGridSpec(
            num_scalar_prefetch=1,
            grid=(2,),
            in_specs=[pl.BlockSpec((4, 1, 4, ROWS, LANES), lambda i, m: (0, lax.rem(i + m[1], 2), 0, 0, 0))],
            out_specs=[pl.BlockSpec((512, BLK), rows)] * 2 + [pl.BlockSpec((4, 8, LANES), lambda i, m: (i, 0, 0))],
        ),
        out_shape=[jax.ShapeDtypeStruct((BLK, BLK), bf16)] * 2 + [jax.ShapeDtypeStruct((8, 8, LANES), i32)],
        compiler_params=params("arbitrary", limit=MOST),
        cost_estimate=pl.CostEstimate(flops=10**7, bytes_accessed=6 * 10**6, transcendentals=0),
    )(me, got)


def partial_kernel(me_ref, x0_ref, x1_ref, x2_ref, x3_ref, grads_ref, *refs):
    own_ref, word_refs, tokens, total = refs[0], refs[1:4], refs[4], refs[5]
    for j, x_ref in enumerate((x0_ref, x1_ref, x2_ref, x3_ref)):
        place = jnp.bitwise_xor(me_ref[3], j)
        for r in range(8):
            tokens[pl.ds(pl.multiple_of(r * LANES + place * 32, 32), 32), :] = x_ref[r]
    for r in range(4):
        grads = jnp.concatenate([grads_ref[r, me_ref[1]], grads_ref[r, 1 - me_ref[1]]], axis=0)
        part = mul(tokens[r * GROUP:(r + 1) * GROUP, :], grads, 0, 0)
        total[...] = part if r == 0 else total[...] + part
    eye = diagonal()
    for k in range(4):
        start = pl.multiple_of(lax.rem(me_ref[2] + k, 4) * LANES, LANES)
        if k == 0:
            own_ref[...] = total[pl.ds(start, LANES), :]
            continue
        rows = []
        for g in range(4):
            word, code = encode(total[pl.ds(start, LANES), g * GROUP:(g + 1) * GROUP])
            word_refs[k - 1][g * LANES:(g + 1) * LANES, :] = word
            rows.append(to_row(code, eye))
        word_refs[k - 1][4 * LANES:, :] = jnp.concatenate(rows + [jnp.zeros((4, LANES), i32)], axis=0)


def partial_rows(me, tokens, grads):
    vmem = pl.BlockSpec(memory_space=pltpu.VMEM)
    return pl.pallas_call(
        partial_kernel,
        in_specs=[pl.BlockSpec(memory_space=pltpu.SMEM)] + [vmem] * 5,
        out_specs=[vmem] * 4,
        out_shape=[jax.ShapeDtypeStruct((LANES, BLK), f32)] + [jax.ShapeDtypeStruct((520, LANES), i32)] * 3,
        scratch_shapes=[pltpu.VMEM((BLK, 512), bf16), pltpu.VMEM((512, BLK), f32)],
        compiler_params=params(limit=MOST),
        cost_estimate=pl.CostEstimate(flops=10**9, bytes_accessed=5 * 10**6, transcendentals=0),
    )(me, *tokens, grads)


def front_kernel(got_ref, own_ref, w1_ref, w2_ref, w3_ref, v_ref, high_ref, low_ref, grad):
    step = pl.program_id(0)
    eye = diagonal()
    decode_chunks(lambda d, start, size: got_ref[d, start:start + size, :], 0, 16, high_ref, low_ref, eye)

    @pl.when(step == 0)
    def _():
        for g in range(4):
            sums = [own_ref[:, g * GROUP:g * GROUP + LANES], own_ref[:, g * GROUP + LANES:(g + 1) * GROUP]]
            for ref in (w1_ref, w2_ref, w3_ref):
                unit = to_unit(ref[4 * LANES + g:4 * LANES + g + 1, :], eye)
                pair = decode(ref[g * LANES:(g + 1) * LANES, :], unit)
                sums = [sums[0] + pair[0], sums[1] + pair[1]]
            grad[g // 2, :, g % 2 * GROUP:(g % 2 + 1) * GROUP] = jnp.concatenate(sums, axis=1)

    grad_high, grad_low = halves(grad[step])
    both = mul(jnp.concatenate([grad_high, grad_low], axis=0), high_ref[...])
    v = both[:LANES] + both[LANES:] + mul(grad_high, low_ref[...])
    for c in range(8):
        part = v[:, c * LANES:(c + 1) * LANES]
        v_ref[c] = jnp.where(step == 0, part, v_ref[c] + part)


def front(got, own, words):
    whole = lambda i: (0, 0)
    return pl.pallas_call(
        front_kernel,
        grid=(2,),
        in_specs=[pl.BlockSpec((16, ROWS, LANES), lambda i: (i, 0, 0)), pl.BlockSpec((LANES, BLK), whole)]
        + [pl.BlockSpec((520, LANES), whole)] * 3,
        out_specs=[pl.BlockSpec((8, LANES, LANES), lambda i: (0, 0, 0))]
        + [pl.BlockSpec((512, BLK), lambda i: (i, 0))] * 2,
        out_shape=[jax.ShapeDtypeStruct((8, LANES, LANES), f32)] + [jax.ShapeDtypeStruct((BLK, BLK), bf16)] * 2,
        scratch_shapes=[pltpu.VMEM((2, LANES, 512), f32)],
        compiler_params=params("arbitrary", limit=MOST),
        cost_estimate=pl.CostEstimate(flops=8 * 10**8, bytes_accessed=8 * 10**6, transcendentals=0),
    )(got, own, *words)


def middle_kernel(v_ref, high_ref, low_ref, in_side_ref, out_side_ref, u_ref):
    v_high, v_low = halves(v_ref[...].reshape(BLK, LANES))
    qh, ql = high_ref[...], low_ref[...]
    both = mul(jnp.concatenate([v_high, v_low], axis=1), qh, 0, 0)
    rt = both[:LANES] + both[LANES:] + mul(v_high, ql, 0, 0)
    la = jnp.concatenate([in_side_ref[c, 1:2, :] for c in range(4)], axis=1).astype(f32) / VALUE_UNIT
    lb = jnp.sum(jnp.where(diagonal(), out_side_ref[0, 1:2, :], 0), axis=1, keepdims=True).astype(f32) / VALUE_UNIT
    st = rt / (lb * la + DAMPING)
    s_high, s_low = halves(st)
    both = mul(jnp.concatenate([s_high, s_low], axis=0), qh, 1, 1)
    ut = both[:LANES] + both[LANES:] + mul(s_high, ql, 1, 1)
    for c in range(8):
        part = ut[:, c * LANES:(c + 1) * LANES]
        u_ref[c] = jnp.where(pl.program_id(0) == 0, part, u_ref[c] + part)


def middle(v, high, low, in_side, piece):
    return pl.pallas_call(
        middle_kernel,
        grid=(2,),
        in_specs=[
            pl.BlockSpec((8, LANES, LANES), lambda i: (0, 0, 0)),
            pl.BlockSpec((BLK, 512), lambda i: (0, i)),
            pl.BlockSpec((BLK, 512), lambda i: (0, i)),
            pl.BlockSpec((4, 8, LANES), lambda i: (i, 0, 0)),
            pl.BlockSpec((1, 8, LANES), lambda i: (0, 16, 0)),
        ],
        out_specs=pl.BlockSpec((8, LANES, LANES), lambda i: (0, 0, 0)),
        out_shape=jax.ShapeDtypeStruct((8, LANES, LANES), f32),
        compiler_params=params("arbitrary", limit=MOST),
        cost_estimate=pl.CostEstimate(flops=16 * 10**8, bytes_accessed=6 * 10**6, transcendentals=0),
    )(v, high, low, in_side, piece)


def back_kernel(u_ref, high_ref, low_ref, out_ref):
    u_high, u_low = halves(u_ref[...].reshape(BLK, LANES).T)
    both = mul(jnp.concatenate([u_high, u_low], axis=0), high_ref[...], 1, 1)
    out_ref[...] = both[:LANES] + both[LANES:] + mul(u_high, low_ref[...], 1, 1)


def back(u, high, low):
    return pl.pallas_call(
        back_kernel,
        grid=(2,),
        in_specs=[
            pl.BlockSpec((8, LANES, LANES), lambda i: (0, 0, 0)),
            pl.BlockSpec((512, BLK), lambda i: (i, 0)),
            pl.BlockSpec((512, BLK), lambda i: (i, 0)),
        ],
        out_specs=pl.BlockSpec((LANES, 512), lambda i: (0, i)),
        out_shape=jax.ShapeDtypeStruct((LANES, BLK), f32),
        compiler_params=params("arbitrary"),
        cost_estimate=pl.CostEstimate(flops=8 * 10**8, bytes_accessed=5 * 10**6, transcendentals=0),
    )(u, high, low)


def body(
    layer_inputs,
    output_grads,
    feature_order,
    block_slot,
    layer_owner,
    in_basis,
    in_values,
    out_basis,
    out_values,
):
    me = jnp.stack([lax.axis_index("y"), lax.axis_index("h"), lax.axis_index("z"), lax.axis_index(("l", "c"))])
    me = jnp.concatenate([me.astype(i32), block_slot])

    packed = pack_basis(out_basis[0], out_values)
    grads = output_grads.reshape(LANES, BLK)
    grads = jnp.stack([grads, flip(grads, "h")])
    packed, grads = lax.optimization_barrier((packed, grads))
    spread = lax.all_to_all(packed, ALL_DP, 0, 0, tiled=True)
    piece = lax.dynamic_index_in_dim(spread, layer_owner[0], 0, keepdims=True)
    grads = lax.all_gather(grads, "y")

    in_part = pack_basis(in_basis, in_values.reshape(1, LANES))
    in_pair = jnp.stack([in_part, lax.ppermute(in_part, ("h", "l"), [(i, 3 - i) for i in range(4)])])

    chunks = gather_columns(me, feature_order, layer_inputs.reshape(32, DIN))
    chunks, piece = lax.optimization_barrier((chunks, piece))
    moved = lax.all_to_all(chunks, ("y", "h"), 0, 0, tiled=True)
    tokens = [moved] + [lax.ppermute(moved, ("l", "c"), [(m, m ^ j) for m in range(4)]) for j in range(1, 4)]

    piece, in_pair, *tokens = lax.optimization_barrier((piece, in_pair, *tokens))
    got = lax.all_to_all(jnp.broadcast_to(piece, spread.shape), ALL_DP, 0, 0, tiled=True)
    _, in_pair = lax.optimization_barrier((grads, in_pair))
    in_all = lax.all_gather(in_pair, "z")
    own, *words = partial_rows(me, tokens, grads)
    words = [along(w, "z", k + 1) for k, w in enumerate(words)]
    v, out_high, out_low = front(got, own, words)

    v = lax.all_to_all(v, PAIR, 0, 0, tiled=True)
    in_high, in_low, in_side = unpack_basis(me, in_all)
    u = middle(v, in_high, in_low, in_side, piece)
    u = lax.all_to_all(u, PAIR, 0, 0, tiled=True)
    return back(u, out_high, out_low)


def along(block, axis, shift):
    if shift == 0:
        return block
    return lax.ppermute(block, axis, [(i, (i + shift) % 4) for i in range(4)])


def flip(block, axis):
    return lax.ppermute(block, axis, [(0, 1), (1, 0)])


def solution(mesh):
    fine = Mesh(mesh.devices.reshape(4, 2, 4, 2, 2), ("y", "h", "z", "l", "c"))
    dp, mp = ("y", "h", "z"), ("l", "c")
    in_specs = (
        P(dp + mp, None, None),
        P(dp, None, mp),
        P(),
        P(),
        P(),
        P(dp, None),
        P(dp),
        P(dp, mp, None),
        P(dp, mp),
    )
    return jax.shard_map(body, mesh=fine, in_specs=in_specs, out_specs=P(dp, mp), check_vma=False)
```

```python
import jax
import jax.numpy as jnp
from jax import lax
from jax.experimental import pallas as pl
from jax.experimental.pallas import tpu as pltpu
from jax.sharding import Mesh, PartitionSpec as P

DIN = 4096
BLK = 1024
LANES = 128
GROUP = 256
ROWS = 136
DAMPING = 0.1
TOP = 32767.0
LOG_UNIT = 65536.0
VALUE_UNIT = 134217728.0
PAIR = ("h", "z")
ALL_DP = ("y", "h", "z")
VMEM = 48 * 1024 * 1024
MOST = 60 * 1024 * 1024
f32, bf16, i32 = jnp.float32, jnp.bfloat16, jnp.int32


def params(*semantics, limit=VMEM):
    return pltpu.CompilerParams(vmem_limit_bytes=limit, dimension_semantics=semantics or None)


def mul(a, b, ca=1, cb=0):
    return lax.dot_general(a, b, (((ca,), (cb,)), ((), ())), preferred_element_type=f32)


def halves(a):
    high = a.astype(bf16)
    return high, (a - high.astype(f32)).astype(bf16)


def gather_kernel(me_ref, order_ref, x_ref, out_ref):
    x = [x_ref[:, k * LANES:(k + 1) * LANES].astype(f32) for k in range(DIN // LANES)]
    for n in range(4):
        pair = sum(jnp.where(me_ref[4 + j] == pl.program_id(0) * 2 + n // 2, j, 0) for j in range(4))
        start = pair * BLK + n % 2 * 512
        for b in range(4):
            idx = order_ref[:, pl.ds(pl.multiple_of(start + b * LANES, LANES), LANES)]
            lane = jnp.broadcast_to(jnp.bitwise_and(idx, LANES - 1), (32, LANES))
            src = jnp.broadcast_to(jnp.right_shift(idx, 7), (32, LANES))
            acc = jnp.zeros((32, LANES), f32)
            for k in range(DIN // LANES):
                acc = jnp.where(src == k, jnp.take_along_axis(x[k], lane, axis=1), acc)
            for m in range(4):
                out_ref[n * 4 + m, :, b * LANES:(b + 1) * LANES] = acc.astype(bf16)


def gather_columns(me, order, x):
    return pl.pallas_call(
        gather_kernel,
        grid=(2,),
        in_specs=[
            pl.BlockSpec(memory_space=pltpu.SMEM),
            pl.BlockSpec((1, DIN), lambda i: (0, 0)),
            pl.BlockSpec((32, DIN), lambda i: (0, 0)),
        ],
        out_specs=pl.BlockSpec((16, 32, 512), lambda i: (i, 0, 0)),
        out_shape=jax.ShapeDtypeStruct((32, 32, 512), bf16),
        compiler_params=params("arbitrary"),
        cost_estimate=pl.CostEstimate(flops=10**6, bytes_accessed=10**6, transcendentals=0),
    )(me, order, x)


def diagonal():
    return lax.broadcasted_iota(i32, (LANES, LANES), 0) == lax.broadcasted_iota(i32, (LANES, LANES), 1)


def encode(part):
    most = jnp.maximum(jnp.max(jnp.abs(part), axis=1, keepdims=True), 1e-30)
    code = jnp.ceil(jnp.log2(most) * LOG_UNIT) + 4.0
    q = jnp.round(part * (TOP * jnp.exp2(-code / LOG_UNIT))).astype(i32)
    word = jnp.bitwise_or(jnp.left_shift(q[:, LANES:], 16), jnp.bitwise_and(q[:, :LANES], 65535))
    return word, code.astype(i32)


def decode(word, unit):
    first = jnp.right_shift(jnp.left_shift(word, 16), 16).astype(f32) * unit
    return first, jnp.right_shift(word, 16).astype(f32) * unit


def to_row(column, eye):
    return jnp.sum(jnp.where(eye, column, 0), axis=0, keepdims=True)


def to_unit(row, eye):
    return jnp.exp2(jnp.sum(jnp.where(eye, row, 0), axis=1, keepdims=True).astype(f32) / LOG_UNIT) / TOP


def pack_kernel(basis_ref, values_ref, out_ref):
    eye = diagonal()
    blocks = values_ref.shape[1] // LANES
    count = out_ref.shape[0]
    for n in range(count // 4):
        codes = [[] for _ in range(4)]
        for g in range(4):
            word, code = encode(basis_ref[n * LANES:(n + 1) * LANES, g * GROUP:(g + 1) * GROUP])
            for d in range(4):
                out_ref[n * 4 + d, g * 32:(g + 1) * 32, :] = word[d * 32:(d + 1) * 32]
                codes[d].append(code[d * 32:(d + 1) * 32])
        for d in range(4):
            row = to_row(jnp.concatenate(codes[d], axis=0), eye)
            block = (n * 4 + d) % blocks
            coded = (values_ref[:, block * LANES:(block + 1) * LANES] * VALUE_UNIT).astype(i32)
            out_ref[n * 4 + d, LANES:ROWS, :] = jnp.concatenate([row, coded, jnp.zeros((6, LANES), i32)], axis=0)


def pack_basis(basis, values):
    rows = basis.shape[0]
    size = min(rows, 512)
    return pl.pallas_call(
        pack_kernel,
        grid=(rows // size,),
        in_specs=[pl.BlockSpec((size, BLK), lambda i: (i, 0)), pl.BlockSpec(values.shape, lambda i: (0, 0))],
        out_specs=pl.BlockSpec((size // 32, ROWS, LANES), lambda i: (i, 0, 0)),
        out_shape=jax.ShapeDtypeStruct((rows // 32, ROWS, LANES), i32),
        compiler_params=params("arbitrary"),
        cost_estimate=pl.CostEstimate(flops=rows * 10**4, bytes_accessed=rows * 6000, transcendentals=0),
    )(basis, values)


def decode_chunks(get, base, count, high_ref, low_ref, eye):
    for d in range(count):
        unit = to_unit(get(d, LANES, 1), eye)
        for g in range(4):
            pair = decode(get(d, g * 32, 32), unit[g * 32:(g + 1) * 32])
            for k in range(2):
                high, low = halves(pair[k])
                where = (pl.ds(base + d * 32, 32), slice(g * GROUP + k * LANES, g * GROUP + (k + 1) * LANES))
                high_ref[where] = high
                low_ref[where] = low


def unpack_kernel(me_ref, got_ref, high_ref, low_ref, side_ref):
    eye = diagonal()
    for z in range(4):
        decode_chunks(lambda d, start, size: got_ref[z, 0, d, start:start + size, :], z * LANES, 4, high_ref, low_ref, eye)
        side_ref[z] = got_ref[z, 0, 0, LANES:ROWS, :]


def unpack_basis(me, got):
    rows = lambda i, m: (i, 0)
    return pl.pallas_call(
        unpack_kernel,
        grid_spec=pltpu.PrefetchScalarGridSpec(
            num_scalar_prefetch=1,
            grid=(2,),
            in_specs=[pl.BlockSpec((4, 1, 4, ROWS, LANES), lambda i, m: (0, lax.rem(i + m[1], 2), 0, 0, 0))],
            out_specs=[pl.BlockSpec((512, BLK), rows)] * 2 + [pl.BlockSpec((4, 8, LANES), lambda i, m: (i, 0, 0))],
        ),
        out_shape=[jax.ShapeDtypeStruct((BLK, BLK), bf16)] * 2 + [jax.ShapeDtypeStruct((8, 8, LANES), i32)],
        compiler_params=params("arbitrary", limit=MOST),
        cost_estimate=pl.CostEstimate(flops=10**7, bytes_accessed=6 * 10**6, transcendentals=0),
    )(me, got)


def partial_kernel(me_ref, tokens, grads_ref, *refs):
    own_ref, word_refs, total = refs[0], refs[1:4], refs[4]
    for r in range(4):
        grads = jnp.concatenate([grads_ref[r, me_ref[1]], grads_ref[r, 1 - me_ref[1]]], axis=0)
        part = mul(tokens[r * GROUP:(r + 1) * GROUP, :], grads, 0, 0)
        total[...] = part if r == 0 else total[...] + part
    eye = diagonal()
    for k in range(4):
        start = pl.multiple_of(lax.rem(me_ref[2] + k, 4) * LANES, LANES)
        if k == 0:
            own_ref[...] = total[pl.ds(start, LANES), :]
            continue
        rows = []
        for g in range(4):
            word, code = encode(total[pl.ds(start, LANES), g * GROUP:(g + 1) * GROUP])
            word_refs[k - 1][g * LANES:(g + 1) * LANES, :] = word
            rows.append(to_row(code, eye))
        word_refs[k - 1][4 * LANES:, :] = jnp.concatenate(rows + [jnp.zeros((4, LANES), i32)], axis=0)


def partial_rows(me, tokens, grads):
    vmem = pl.BlockSpec(memory_space=pltpu.VMEM)
    return pl.pallas_call(
        partial_kernel,
        in_specs=[pl.BlockSpec(memory_space=pltpu.SMEM)] + [vmem] * 2,
        out_specs=[vmem] * 4,
        out_shape=[jax.ShapeDtypeStruct((LANES, BLK), f32)] + [jax.ShapeDtypeStruct((520, LANES), i32)] * 3,
        scratch_shapes=[pltpu.VMEM((512, BLK), f32)],
        compiler_params=params(limit=MOST),
        cost_estimate=pl.CostEstimate(flops=10**9, bytes_accessed=5 * 10**6, transcendentals=0),
    )(me, tokens, grads)


def front_kernel(got_ref, own_ref, w1_ref, w2_ref, w3_ref, v_ref, high_ref, low_ref, grad):
    step = pl.program_id(0)
    eye = diagonal()
    decode_chunks(lambda d, start, size: got_ref[d, start:start + size, :], 0, 16, high_ref, low_ref, eye)

    @pl.when(step == 0)
    def _():
        for g in range(4):
            sums = [own_ref[:, g * GROUP:g * GROUP + LANES], own_ref[:, g * GROUP + LANES:(g + 1) * GROUP]]
            for ref in (w1_ref, w2_ref, w3_ref):
                unit = to_unit(ref[4 * LANES + g:4 * LANES + g + 1, :], eye)
                pair = decode(ref[g * LANES:(g + 1) * LANES, :], unit)
                sums = [sums[0] + pair[0], sums[1] + pair[1]]
            grad[g // 2, :, g % 2 * GROUP:(g % 2 + 1) * GROUP] = jnp.concatenate(sums, axis=1)

    grad_high, grad_low = halves(grad[step])
    both = mul(jnp.concatenate([grad_high, grad_low], axis=0), high_ref[...])
    v = both[:LANES] + both[LANES:] + mul(grad_high, low_ref[...])
    for c in range(8):
        part = v[:, c * LANES:(c + 1) * LANES]
        v_ref[c] = jnp.where(step == 0, part, v_ref[c] + part)


def front(got, own, words):
    whole = lambda i: (0, 0)
    return pl.pallas_call(
        front_kernel,
        grid=(2,),
        in_specs=[pl.BlockSpec((16, ROWS, LANES), lambda i: (i, 0, 0)), pl.BlockSpec((LANES, BLK), whole)]
        + [pl.BlockSpec((520, LANES), whole)] * 3,
        out_specs=[pl.BlockSpec((8, LANES, LANES), lambda i: (0, 0, 0))]
        + [pl.BlockSpec((512, BLK), lambda i: (i, 0))] * 2,
        out_shape=[jax.ShapeDtypeStruct((8, LANES, LANES), f32)] + [jax.ShapeDtypeStruct((BLK, BLK), bf16)] * 2,
        scratch_shapes=[pltpu.VMEM((2, LANES, 512), f32)],
        compiler_params=params("arbitrary", limit=MOST),
        cost_estimate=pl.CostEstimate(flops=8 * 10**8, bytes_accessed=8 * 10**6, transcendentals=0),
    )(got, own, *words)


def middle_kernel(v_ref, high_ref, low_ref, in_side_ref, out_side_ref, u_ref):
    v_high, v_low = halves(v_ref[...].reshape(BLK, LANES))
    qh, ql = high_ref[...], low_ref[...]
    both = mul(jnp.concatenate([v_high, v_low], axis=1), qh, 0, 0)
    rt = both[:LANES] + both[LANES:] + mul(v_high, ql, 0, 0)
    la = jnp.concatenate([in_side_ref[c, 1:2, :] for c in range(4)], axis=1).astype(f32) / VALUE_UNIT
    lb = jnp.sum(jnp.where(diagonal(), out_side_ref[0, 1:2, :], 0), axis=1, keepdims=True).astype(f32) / VALUE_UNIT
    st = rt / (lb * la + DAMPING)
    s_high, s_low = halves(st)
    both = mul(jnp.concatenate([s_high, s_low], axis=0), qh, 1, 1)
    ut = both[:LANES] + both[LANES:] + mul(s_high, ql, 1, 1)
    for c in range(8):
        part = ut[:, c * LANES:(c + 1) * LANES]
        u_ref[c] = jnp.where(pl.program_id(0) == 0, part, u_ref[c] + part)


def middle(v, high, low, in_side, piece):
    return pl.pallas_call(
        middle_kernel,
        grid=(2,),
        in_specs=[
            pl.BlockSpec((8, LANES, LANES), lambda i: (0, 0, 0)),
            pl.BlockSpec((BLK, 512), lambda i: (0, i)),
            pl.BlockSpec((BLK, 512), lambda i: (0, i)),
            pl.BlockSpec((4, 8, LANES), lambda i: (i, 0, 0)),
            pl.BlockSpec((1, 8, LANES), lambda i: (0, 16, 0)),
        ],
        out_specs=pl.BlockSpec((8, LANES, LANES), lambda i: (0, 0, 0)),
        out_shape=jax.ShapeDtypeStruct((8, LANES, LANES), f32),
        compiler_params=params("arbitrary", limit=MOST),
        cost_estimate=pl.CostEstimate(flops=16 * 10**8, bytes_accessed=6 * 10**6, transcendentals=0),
    )(v, high, low, in_side, piece)


def back_kernel(u_ref, high_ref, low_ref, out_ref):
    u_high, u_low = halves(u_ref[...].reshape(BLK, LANES).T)
    both = mul(jnp.concatenate([u_high, u_low], axis=0), high_ref[...], 1, 1)
    out_ref[...] = both[:LANES] + both[LANES:] + mul(u_high, low_ref[...], 1, 1)


def back(u, high, low):
    return pl.pallas_call(
        back_kernel,
        grid=(2,),
        in_specs=[
            pl.BlockSpec((8, LANES, LANES), lambda i: (0, 0, 0)),
            pl.BlockSpec((512, BLK), lambda i: (i, 0)),
            pl.BlockSpec((512, BLK), lambda i: (i, 0)),
        ],
        out_specs=pl.BlockSpec((LANES, 512), lambda i: (0, i)),
        out_shape=jax.ShapeDtypeStruct((LANES, BLK), f32),
        compiler_params=params("arbitrary"),
        cost_estimate=pl.CostEstimate(flops=8 * 10**8, bytes_accessed=5 * 10**6, transcendentals=0),
    )(u, high, low)


def body(
    layer_inputs,
    output_grads,
    feature_order,
    block_slot,
    layer_owner,
    in_basis,
    in_values,
    out_basis,
    out_values,
):
    me = jnp.stack([lax.axis_index("y"), lax.axis_index("h"), lax.axis_index("z"), lax.axis_index(("l", "c"))])
    me = jnp.concatenate([me.astype(i32), block_slot])

    in_part = pack_basis(in_basis, in_values.reshape(1, LANES))
    in_pair = jnp.stack([in_part, lax.ppermute(in_part, ("h", "l"), [(i, 3 - i) for i in range(4)])])

    chunks = gather_columns(me, feature_order, layer_inputs.reshape(32, DIN))
    grads = output_grads.reshape(LANES, BLK)
    grads = jnp.stack([grads, flip(grads, "h")])
    chunks, grads, out_part = lax.optimization_barrier((chunks, grads, out_basis[0]))
    tokens = lax.all_to_all(chunks, ("y", "h", "l", "c"), 0, 0, tiled=True).reshape(BLK, 512)

    packed = pack_basis(out_part, out_values)
    packed, in_pair, tokens = lax.optimization_barrier((packed, in_pair, tokens))
    spread = lax.all_to_all(packed, ALL_DP, 0, 0, tiled=True)
    piece = lax.dynamic_index_in_dim(spread, layer_owner[0], 0, keepdims=True)

    grads = lax.all_gather(grads, "y")
    _, in_pair = lax.optimization_barrier((grads, in_pair))
    in_all = lax.all_gather(in_pair, "z")
    own, *words = partial_rows(me, tokens, grads)
    piece, _ = lax.optimization_barrier((piece, along(words[0][512:], "z", 1)))
    words = [along(w, "z", k + 1) for k, w in enumerate(words)]

    got = lax.all_to_all(jnp.broadcast_to(piece, spread.shape), ALL_DP, 0, 0, tiled=True)
    v, out_high, out_low = front(got, own, words)

    v = lax.all_to_all(v, PAIR, 0, 0, tiled=True)
    in_high, in_low, in_side = unpack_basis(me, in_all)
    u = middle(v, in_high, in_low, in_side, piece)
    u = lax.all_to_all(u, PAIR, 0, 0, tiled=True)
    return back(u, out_high, out_low)


def along(block, axis, shift):
    if shift == 0:
        return block
    return lax.ppermute(block, axis, [(i, (i + shift) % 4) for i in range(4)])


def flip(block, axis):
    return lax.ppermute(block, axis, [(0, 1), (1, 0)])


def solution(mesh):
    fine = Mesh(mesh.devices.reshape(4, 2, 4, 2, 2), ("y", "h", "z", "l", "c"))
    dp, mp = ("y", "h", "z"), ("l", "c")
    in_specs = (
        P(dp + mp, None, None),
        P(dp, None, mp),
        P(),
        P(),
        P(),
        P(dp, None),
        P(dp),
        P(dp, mp, None),
        P(dp, mp),
    )
    return jax.shard_map(body, mesh=fine, in_specs=in_specs, out_specs=P(dp, mp), check_vma=False)
```

```python
import jax
import jax.numpy as jnp
from jax import lax
from jax.experimental import pallas as pl
from jax.experimental.pallas import tpu as pltpu
from jax.sharding import Mesh, PartitionSpec as P

DIN = 4096
BLK = 1024
LANES = 128
GROUP = 256
ROWS = 136
DAMPING = 0.1
TOP = 32767.0
LOG_UNIT = 65536.0
VALUE_UNIT = 134217728.0
PAIR = ("h", "z")
ALL_DP = ("y", "h", "z")
VMEM = 48 * 1024 * 1024
MOST = 60 * 1024 * 1024
f32, bf16, i32 = jnp.float32, jnp.bfloat16, jnp.int32


def params(*semantics, limit=VMEM):
    return pltpu.CompilerParams(vmem_limit_bytes=limit, dimension_semantics=semantics or None)


def mul(a, b, ca=1, cb=0):
    return lax.dot_general(a, b, (((ca,), (cb,)), ((), ())), preferred_element_type=f32)


def halves(a):
    high = a.astype(bf16)
    return high, (a - high.astype(f32)).astype(bf16)


def gather_kernel(me_ref, order_ref, x_ref, out_ref):
    x = [x_ref[:, k * LANES:(k + 1) * LANES].astype(f32) for k in range(DIN // LANES)]
    for n in range(4):
        pair = sum(jnp.where(me_ref[4 + j] == pl.program_id(0) * 2 + n // 2, j, 0) for j in range(4))
        start = pair * BLK + n % 2 * 512
        for b in range(4):
            idx = order_ref[:, pl.ds(pl.multiple_of(start + b * LANES, LANES), LANES)]
            lane = jnp.broadcast_to(jnp.bitwise_and(idx, LANES - 1), (32, LANES))
            src = jnp.broadcast_to(jnp.right_shift(idx, 7), (32, LANES))
            acc = jnp.zeros((32, LANES), f32)
            for k in range(DIN // LANES):
                acc = jnp.where(src == k, jnp.take_along_axis(x[k], lane, axis=1), acc)
            for m in range(4):
                out_ref[n * 4 + m, :, b * LANES:(b + 1) * LANES] = acc.astype(bf16)


def gather_columns(me, order, x):
    return pl.pallas_call(
        gather_kernel,
        grid=(2,),
        in_specs=[
            pl.BlockSpec(memory_space=pltpu.SMEM),
            pl.BlockSpec((1, DIN), lambda i: (0, 0)),
            pl.BlockSpec((32, DIN), lambda i: (0, 0)),
        ],
        out_specs=pl.BlockSpec((16, 32, 512), lambda i: (i, 0, 0)),
        out_shape=jax.ShapeDtypeStruct((32, 32, 512), bf16),
        compiler_params=params("arbitrary"),
        cost_estimate=pl.CostEstimate(flops=10**6, bytes_accessed=10**6, transcendentals=0),
    )(me, order, x)


def diagonal():
    return lax.broadcasted_iota(i32, (LANES, LANES), 0) == lax.broadcasted_iota(i32, (LANES, LANES), 1)


def encode(part):
    most = jnp.maximum(jnp.max(jnp.abs(part), axis=1, keepdims=True), 1e-30)
    code = jnp.ceil(jnp.log2(most) * LOG_UNIT) + 4.0
    q = jnp.round(part * (TOP * jnp.exp2(-code / LOG_UNIT))).astype(i32)
    word = jnp.bitwise_or(jnp.left_shift(q[:, LANES:], 16), jnp.bitwise_and(q[:, :LANES], 65535))
    return word, code.astype(i32)


def decode(word, unit):
    first = jnp.right_shift(jnp.left_shift(word, 16), 16).astype(f32) * unit
    return first, jnp.right_shift(word, 16).astype(f32) * unit


def to_row(column, eye):
    return jnp.sum(jnp.where(eye, column, 0), axis=0, keepdims=True)


def to_unit(row, eye):
    return jnp.exp2(jnp.sum(jnp.where(eye, row, 0), axis=1, keepdims=True).astype(f32) / LOG_UNIT) / TOP


def pack_kernel(basis_ref, values_ref, out_ref):
    eye = diagonal()
    blocks = values_ref.shape[1] // LANES
    count = out_ref.shape[0]
    for n in range(count // 4):
        codes = [[] for _ in range(4)]
        for g in range(4):
            word, code = encode(basis_ref[n * LANES:(n + 1) * LANES, g * GROUP:(g + 1) * GROUP])
            for d in range(4):
                out_ref[n * 4 + d, g * 32:(g + 1) * 32, :] = word[d * 32:(d + 1) * 32]
                codes[d].append(code[d * 32:(d + 1) * 32])
        for d in range(4):
            row = to_row(jnp.concatenate(codes[d], axis=0), eye)
            block = (n * 4 + d) % blocks
            coded = (values_ref[:, block * LANES:(block + 1) * LANES] * VALUE_UNIT).astype(i32)
            out_ref[n * 4 + d, LANES:ROWS, :] = jnp.concatenate([row, coded, jnp.zeros((6, LANES), i32)], axis=0)


def pack_basis(basis, values):
    rows = basis.shape[0]
    size = min(rows, 512)
    return pl.pallas_call(
        pack_kernel,
        grid=(rows // size,),
        in_specs=[pl.BlockSpec((size, BLK), lambda i: (i, 0)), pl.BlockSpec(values.shape, lambda i: (0, 0))],
        out_specs=pl.BlockSpec((size // 32, ROWS, LANES), lambda i: (i, 0, 0)),
        out_shape=jax.ShapeDtypeStruct((rows // 32, ROWS, LANES), i32),
        compiler_params=params("arbitrary"),
        cost_estimate=pl.CostEstimate(flops=rows * 10**4, bytes_accessed=rows * 6000, transcendentals=0),
    )(basis, values)


def decode_chunks(get, base, count, high_ref, low_ref, eye):
    for d in range(count):
        unit = to_unit(get(d, LANES, 1), eye)
        for g in range(4):
            pair = decode(get(d, g * 32, 32), unit[g * 32:(g + 1) * 32])
            for k in range(2):
                high, low = halves(pair[k])
                where = (pl.ds(base + d * 32, 32), slice(g * GROUP + k * LANES, g * GROUP + (k + 1) * LANES))
                high_ref[where] = high
                low_ref[where] = low


def unpack_kernel(me_ref, got_ref, high_ref, low_ref, side_ref):
    eye = diagonal()
    for z in range(4):
        decode_chunks(lambda d, start, size: got_ref[z, 0, d, start:start + size, :], z * LANES, 4, high_ref, low_ref, eye)
        side_ref[z] = got_ref[z, 0, 0, LANES:ROWS, :]


def unpack_basis(me, got):
    rows = lambda i, m: (i, 0)
    return pl.pallas_call(
        unpack_kernel,
        grid_spec=pltpu.PrefetchScalarGridSpec(
            num_scalar_prefetch=1,
            grid=(2,),
            in_specs=[pl.BlockSpec((4, 1, 4, ROWS, LANES), lambda i, m: (0, lax.rem(i + m[1], 2), 0, 0, 0))],
            out_specs=[pl.BlockSpec((512, BLK), rows)] * 2 + [pl.BlockSpec((4, 8, LANES), lambda i, m: (i, 0, 0))],
        ),
        out_shape=[jax.ShapeDtypeStruct((BLK, BLK), bf16)] * 2 + [jax.ShapeDtypeStruct((8, 8, LANES), i32)],
        compiler_params=params("arbitrary", limit=MOST),
        cost_estimate=pl.CostEstimate(flops=10**7, bytes_accessed=6 * 10**6, transcendentals=0),
    )(me, got)


def partial_kernel(me_ref, tokens, grads_ref, *refs):
    own_ref, word_refs, total = refs[0], refs[1:4], refs[4]
    for r in range(4):
        grads = jnp.concatenate([grads_ref[r, me_ref[1]], grads_ref[r, 1 - me_ref[1]]], axis=0)
        part = mul(tokens[r * GROUP:(r + 1) * GROUP, :], grads, 0, 0)
        total[...] = part if r == 0 else total[...] + part
    eye = diagonal()
    for k in range(4):
        start = pl.multiple_of(lax.rem(me_ref[2] + k, 4) * LANES, LANES)
        if k == 0:
            own_ref[...] = total[pl.ds(start, LANES), :]
            continue
        rows = []
        for g in range(4):
            word, code = encode(total[pl.ds(start, LANES), g * GROUP:(g + 1) * GROUP])
            word_refs[k - 1][g * LANES:(g + 1) * LANES, :] = word
            rows.append(to_row(code, eye))
        word_refs[k - 1][4 * LANES:, :] = jnp.concatenate(rows + [jnp.zeros((4, LANES), i32)], axis=0)


def partial_rows(me, tokens, grads):
    vmem = pl.BlockSpec(memory_space=pltpu.VMEM)
    return pl.pallas_call(
        partial_kernel,
        in_specs=[pl.BlockSpec(memory_space=pltpu.SMEM)] + [vmem] * 2,
        out_specs=[vmem] * 4,
        out_shape=[jax.ShapeDtypeStruct((LANES, BLK), f32)] + [jax.ShapeDtypeStruct((520, LANES), i32)] * 3,
        scratch_shapes=[pltpu.VMEM((512, BLK), f32)],
        compiler_params=params(limit=MOST),
        cost_estimate=pl.CostEstimate(flops=10**9, bytes_accessed=5 * 10**6, transcendentals=0),
    )(me, tokens, grads)


def front_kernel(got_ref, own_ref, w1_ref, w2_ref, w3_ref, v_ref, high_ref, low_ref, grad):
    step = pl.program_id(0)
    eye = diagonal()
    decode_chunks(lambda d, start, size: got_ref[d, start:start + size, :], 0, 16, high_ref, low_ref, eye)

    @pl.when(step == 0)
    def _():
        for g in range(4):
            sums = [own_ref[:, g * GROUP:g * GROUP + LANES], own_ref[:, g * GROUP + LANES:(g + 1) * GROUP]]
            for ref in (w1_ref, w2_ref, w3_ref):
                unit = to_unit(ref[4 * LANES + g:4 * LANES + g + 1, :], eye)
                pair = decode(ref[g * LANES:(g + 1) * LANES, :], unit)
                sums = [sums[0] + pair[0], sums[1] + pair[1]]
            grad[g // 2, :, g % 2 * GROUP:(g % 2 + 1) * GROUP] = jnp.concatenate(sums, axis=1)

    grad_high, grad_low = halves(grad[step])
    both = mul(jnp.concatenate([grad_high, grad_low], axis=0), high_ref[...])
    v = both[:LANES] + both[LANES:] + mul(grad_high, low_ref[...])
    for c in range(8):
        part = v[:, c * LANES:(c + 1) * LANES]
        v_ref[c] = jnp.where(step == 0, part, v_ref[c] + part)


def front(got, own, words):
    whole = lambda i: (0, 0)
    return pl.pallas_call(
        front_kernel,
        grid=(2,),
        in_specs=[pl.BlockSpec((16, ROWS, LANES), lambda i: (i, 0, 0)), pl.BlockSpec((LANES, BLK), whole)]
        + [pl.BlockSpec((520, LANES), whole)] * 3,
        out_specs=[pl.BlockSpec((8, LANES, LANES), lambda i: (0, 0, 0))]
        + [pl.BlockSpec((512, BLK), lambda i: (i, 0))] * 2,
        out_shape=[jax.ShapeDtypeStruct((8, LANES, LANES), f32)] + [jax.ShapeDtypeStruct((BLK, BLK), bf16)] * 2,
        scratch_shapes=[pltpu.VMEM((2, LANES, 512), f32)],
        compiler_params=params("arbitrary", limit=MOST),
        cost_estimate=pl.CostEstimate(flops=8 * 10**8, bytes_accessed=8 * 10**6, transcendentals=0),
    )(got, own, *words)


def middle_kernel(v_ref, high_ref, low_ref, in_side_ref, out_side_ref, u_ref):
    v_high, v_low = halves(v_ref[...].reshape(BLK, LANES))
    qh, ql = high_ref[...], low_ref[...]
    both = mul(jnp.concatenate([v_high, v_low], axis=1), qh, 0, 0)
    rt = both[:LANES] + both[LANES:] + mul(v_high, ql, 0, 0)
    la = jnp.concatenate([in_side_ref[c, 1:2, :] for c in range(4)], axis=1).astype(f32) / VALUE_UNIT
    lb = jnp.sum(jnp.where(diagonal(), out_side_ref[0, 1:2, :], 0), axis=1, keepdims=True).astype(f32) / VALUE_UNIT
    st = rt / (lb * la + DAMPING)
    s_high, s_low = halves(st)
    both = mul(jnp.concatenate([s_high, s_low], axis=0), qh, 1, 1)
    ut = both[:LANES] + both[LANES:] + mul(s_high, ql, 1, 1)
    for c in range(8):
        part = ut[:, c * LANES:(c + 1) * LANES]
        u_ref[c] = jnp.where(pl.program_id(0) == 0, part, u_ref[c] + part)


def middle(v, high, low, in_side, piece):
    return pl.pallas_call(
        middle_kernel,
        grid=(2,),
        in_specs=[
            pl.BlockSpec((8, LANES, LANES), lambda i: (0, 0, 0)),
            pl.BlockSpec((BLK, 512), lambda i: (0, i)),
            pl.BlockSpec((BLK, 512), lambda i: (0, i)),
            pl.BlockSpec((4, 8, LANES), lambda i: (i, 0, 0)),
            pl.BlockSpec((1, 8, LANES), lambda i: (0, 16, 0)),
        ],
        out_specs=pl.BlockSpec((8, LANES, LANES), lambda i: (0, 0, 0)),
        out_shape=jax.ShapeDtypeStruct((8, LANES, LANES), f32),
        compiler_params=params("arbitrary", limit=MOST),
        cost_estimate=pl.CostEstimate(flops=16 * 10**8, bytes_accessed=6 * 10**6, transcendentals=0),
    )(v, high, low, in_side, piece)


def back_kernel(u_ref, high_ref, low_ref, out_ref):
    u_high, u_low = halves(u_ref[...].reshape(BLK, LANES).T)
    both = mul(jnp.concatenate([u_high, u_low], axis=0), high_ref[...], 1, 1)
    out_ref[...] = both[:LANES] + both[LANES:] + mul(u_high, low_ref[...], 1, 1)


def back(u, high, low):
    return pl.pallas_call(
        back_kernel,
        grid=(2,),
        in_specs=[
            pl.BlockSpec((8, LANES, LANES), lambda i: (0, 0, 0)),
            pl.BlockSpec((512, BLK), lambda i: (i, 0)),
            pl.BlockSpec((512, BLK), lambda i: (i, 0)),
        ],
        out_specs=pl.BlockSpec((LANES, 512), lambda i: (0, i)),
        out_shape=jax.ShapeDtypeStruct((LANES, BLK), f32),
        compiler_params=params("arbitrary"),
        cost_estimate=pl.CostEstimate(flops=8 * 10**8, bytes_accessed=5 * 10**6, transcendentals=0),
    )(u, high, low)


def body(
    layer_inputs,
    output_grads,
    feature_order,
    block_slot,
    layer_owner,
    in_basis,
    in_values,
    out_basis,
    out_values,
):
    me = jnp.stack([lax.axis_index("y"), lax.axis_index("h"), lax.axis_index("z"), lax.axis_index(("l", "c"))])
    me = jnp.concatenate([me.astype(i32), block_slot])

    in_part = pack_basis(in_basis, in_values.reshape(1, LANES))
    in_pair = jnp.stack([in_part, lax.ppermute(in_part, ("h", "l"), [(i, 3 - i) for i in range(4)])])

    chunks = gather_columns(me, feature_order, layer_inputs.reshape(32, DIN))
    grads = output_grads.reshape(LANES, BLK)
    grads = jnp.stack([grads, flip(grads, "h")])
    chunks, out_part = lax.optimization_barrier((chunks, out_basis[0]))
    tokens = lax.all_to_all(chunks, ("y", "h", "l", "c"), 0, 0, tiled=True).reshape(BLK, 512)

    grads, out_part = lax.optimization_barrier((grads, out_part))
    packed = pack_basis(out_part, out_values)
    packed, in_pair, tokens = lax.optimization_barrier((packed, in_pair, tokens))
    spread = lax.all_to_all(packed, ALL_DP, 0, 0, tiled=True)
    piece = lax.dynamic_index_in_dim(spread, layer_owner[0], 0, keepdims=True)

    grads = lax.all_gather(grads, "y")
    _, in_pair = lax.optimization_barrier((grads, in_pair))
    in_all = lax.all_gather(in_pair, "z")
    own, *words = partial_rows(me, tokens, grads)
    words = [along(w, "z", k + 1) for k, w in enumerate(words)]
    piece, *words = lax.optimization_barrier((piece, *words))

    got = lax.all_to_all(jnp.broadcast_to(piece, spread.shape), ALL_DP, 0, 0, tiled=True)
    v, out_high, out_low = front(got, own, words)

    v = lax.all_to_all(v, PAIR, 0, 0, tiled=True)
    in_high, in_low, in_side = unpack_basis(me, in_all)
    u = middle(v, in_high, in_low, in_side, piece)
    u = lax.all_to_all(u, PAIR, 0, 0, tiled=True)
    return back(u, out_high, out_low)


def along(block, axis, shift):
    if shift == 0:
        return block
    return lax.ppermute(block, axis, [(i, (i + shift) % 4) for i in range(4)])


def flip(block, axis):
    return lax.ppermute(block, axis, [(0, 1), (1, 0)])


def solution(mesh):
    fine = Mesh(mesh.devices.reshape(4, 2, 4, 2, 2), ("y", "h", "z", "l", "c"))
    dp, mp = ("y", "h", "z"), ("l", "c")
    in_specs = (
        P(dp + mp, None, None),
        P(dp, None, mp),
        P(),
        P(),
        P(),
        P(dp, None),
        P(dp),
        P(dp, mp, None),
        P(dp, mp),
    )
    return jax.shard_map(body, mesh=fine, in_specs=in_specs, out_specs=P(dp, mp), check_vma=False)
```

```python
import jax
import jax.numpy as jnp
from jax import lax
from jax.experimental import pallas as pl
from jax.experimental.pallas import tpu as pltpu
from jax.sharding import Mesh, PartitionSpec as P

DIN = 4096
BLK = 1024
LANES = 128
GROUP = 256
ROWS = 136
DAMPING = 0.1
TOP = 32767.0
LOG_UNIT = 65536.0
VALUE_UNIT = 134217728.0
PAIR = ("h", "z")
ALL_DP = ("y", "h", "z")
VMEM = 48 * 1024 * 1024
f32, bf16, i32 = jnp.float32, jnp.bfloat16, jnp.int32


def params(*semantics):
    return pltpu.CompilerParams(vmem_limit_bytes=VMEM, dimension_semantics=semantics or None)


def mul(a, b, ca=1, cb=0):
    return lax.dot_general(a, b, (((ca,), (cb,)), ((), ())), preferred_element_type=f32)


def halves(a):
    high = a.astype(bf16)
    return high, (a - high.astype(f32)).astype(bf16)


def gather_kernel(me_ref, order_ref, x_ref, out_ref):
    x = [x_ref[:, k * LANES:(k + 1) * LANES].astype(f32) for k in range(DIN // LANES)]
    for n in range(4):
        pair = sum(jnp.where(me_ref[4 + j] == pl.program_id(0) * 2 + n // 2, j, 0) for j in range(4))
        start = pair * BLK + n % 2 * 512
        for b in range(4):
            idx = order_ref[:, pl.ds(pl.multiple_of(start + b * LANES, LANES), LANES)]
            lane = jnp.broadcast_to(jnp.bitwise_and(idx, LANES - 1), (32, LANES))
            src = jnp.broadcast_to(jnp.right_shift(idx, 7), (32, LANES))
            acc = jnp.zeros((32, LANES), f32)
            for k in range(DIN // LANES):
                acc = jnp.where(src == k, jnp.take_along_axis(x[k], lane, axis=1), acc)
            out_ref[n, :, b * LANES:(b + 1) * LANES] = acc.astype(bf16)


def gather_columns(me, order, x):
    return pl.pallas_call(
        gather_kernel,
        grid=(2,),
        in_specs=[
            pl.BlockSpec(memory_space=pltpu.SMEM),
            pl.BlockSpec((1, DIN), lambda i: (0, 0)),
            pl.BlockSpec((32, DIN), lambda i: (0, 0)),
        ],
        out_specs=pl.BlockSpec((4, 32, 512), lambda i: (i, 0, 0)),
        out_shape=jax.ShapeDtypeStruct((8, 32, 512), bf16),
        compiler_params=params("arbitrary"),
        cost_estimate=pl.CostEstimate(flops=10**6, bytes_accessed=10**6, transcendentals=0),
    )(me, order, x)


def diagonal():
    return lax.broadcasted_iota(i32, (LANES, LANES), 0) == lax.broadcasted_iota(i32, (LANES, LANES), 1)


def encode(part):
    most = jnp.maximum(jnp.max(jnp.abs(part), axis=1, keepdims=True), 1e-30)
    code = jnp.ceil(jnp.log2(most) * LOG_UNIT) + 4.0
    q = jnp.round(part * (TOP * jnp.exp2(-code / LOG_UNIT))).astype(i32)
    word = jnp.bitwise_or(jnp.left_shift(q[:, LANES:], 16), jnp.bitwise_and(q[:, :LANES], 65535))
    return word, code.astype(i32)


def decode(word, unit):
    first = jnp.right_shift(jnp.left_shift(word, 16), 16).astype(f32) * unit
    return first, jnp.right_shift(word, 16).astype(f32) * unit


def to_row(column, eye):
    return jnp.sum(jnp.where(eye, column, 0), axis=0, keepdims=True)


def to_unit(row, eye):
    return jnp.exp2(jnp.sum(jnp.where(eye, row, 0), axis=1, keepdims=True).astype(f32) / LOG_UNIT) / TOP


def pack_kernel(basis_ref, values_ref, out_ref):
    eye = diagonal()
    blocks = values_ref.shape[1] // LANES
    count = out_ref.shape[0]
    for n in range(count // 4):
        codes = [[] for _ in range(4)]
        for g in range(4):
            word, code = encode(basis_ref[n * LANES:(n + 1) * LANES, g * GROUP:(g + 1) * GROUP])
            for d in range(4):
                out_ref[n * 4 + d, g * 32:(g + 1) * 32, :] = word[d * 32:(d + 1) * 32]
                codes[d].append(code[d * 32:(d + 1) * 32])
        for d in range(4):
            row = to_row(jnp.concatenate(codes[d], axis=0), eye)
            block = (n * 4 + d) % blocks
            coded = (values_ref[:, block * LANES:(block + 1) * LANES] * VALUE_UNIT).astype(i32)
            out_ref[n * 4 + d, LANES:ROWS, :] = jnp.concatenate([row, coded, jnp.zeros((6, LANES), i32)], axis=0)


def pack_basis(basis, values):
    rows = basis.shape[0]
    size = min(rows, 512)
    return pl.pallas_call(
        pack_kernel,
        grid=(rows // size,),
        in_specs=[pl.BlockSpec((size, BLK), lambda i: (i, 0)), pl.BlockSpec(values.shape, lambda i: (0, 0))],
        out_specs=pl.BlockSpec((size // 32, ROWS, LANES), lambda i: (i, 0, 0)),
        out_shape=jax.ShapeDtypeStruct((rows // 32, ROWS, LANES), i32),
        compiler_params=params("arbitrary"),
        cost_estimate=pl.CostEstimate(flops=rows * 10**4, bytes_accessed=rows * 6000, transcendentals=0),
    )(basis, values)


def decode_chunks(get, base, count, high_ref, low_ref, eye):
    for d in range(count):
        unit = to_unit(get(d, LANES, 1), eye)
        for g in range(4):
            pair = decode(get(d, g * 32, 32), unit[g * 32:(g + 1) * 32])
            for k in range(2):
                high, low = halves(pair[k])
                where = (pl.ds(base + d * 32, 32), slice(g * GROUP + k * LANES, g * GROUP + (k + 1) * LANES))
                high_ref[where] = high
                low_ref[where] = low


def unpack_kernel(me_ref, got_ref, high_ref, low_ref, side_ref):
    eye = diagonal()
    for z in range(4):
        decode_chunks(lambda d, start, size: got_ref[z, 0, d, start:start + size, :], z * LANES, 4, high_ref, low_ref, eye)
        side_ref[z] = got_ref[z, 0, 0, LANES:ROWS, :]


def unpack_basis(me, got):
    rows = lambda i, m: (i, 0)
    return pl.pallas_call(
        unpack_kernel,
        grid_spec=pltpu.PrefetchScalarGridSpec(
            num_scalar_prefetch=1,
            grid=(2,),
            in_specs=[pl.BlockSpec((4, 1, 4, ROWS, LANES), lambda i, m: (0, lax.rem(i + m[1], 2), 0, 0, 0))],
            out_specs=[pl.BlockSpec((512, BLK), rows)] * 2 + [pl.BlockSpec((4, 8, LANES), lambda i, m: (i, 0, 0))],
        ),
        out_shape=[jax.ShapeDtypeStruct((BLK, BLK), bf16)] * 2 + [jax.ShapeDtypeStruct((8, 8, LANES), i32)],
        compiler_params=params("arbitrary"),
        cost_estimate=pl.CostEstimate(flops=10**7, bytes_accessed=6 * 10**6, transcendentals=0),
    )(me, got)


def partial_kernel(me_ref, x0_ref, x1_ref, x2_ref, x3_ref, grads_ref, *refs):
    own_ref, word_refs, tokens, total = refs[0], refs[1:4], refs[4], refs[5]
    for j, x_ref in enumerate((x0_ref, x1_ref, x2_ref, x3_ref)):
        place = jnp.bitwise_xor(me_ref[3], j)
        for r in range(8):
            tokens[pl.ds(pl.multiple_of(r * LANES + place * 32, 32), 32), :] = x_ref[r]
    for r in range(4):
        grads = jnp.concatenate([grads_ref[r, me_ref[1]], grads_ref[r, 1 - me_ref[1]]], axis=0)
        part = mul(tokens[r * GROUP:(r + 1) * GROUP, :], grads, 0, 0)
        total[...] = part if r == 0 else total[...] + part
    eye = diagonal()
    for k in range(4):
        start = pl.multiple_of(lax.rem(me_ref[2] + k, 4) * LANES, LANES)
        if k == 0:
            own_ref[...] = total[pl.ds(start, LANES), :]
            continue
        rows = []
        for g in range(4):
            word, code = encode(total[pl.ds(start, LANES), g * GROUP:(g + 1) * GROUP])
            word_refs[k - 1][g * LANES:(g + 1) * LANES, :] = word
            rows.append(to_row(code, eye))
        word_refs[k - 1][4 * LANES:, :] = jnp.concatenate(rows + [jnp.zeros((4, LANES), i32)], axis=0)


def partial_rows(me, tokens, grads):
    vmem = pl.BlockSpec(memory_space=pltpu.VMEM)
    return pl.pallas_call(
        partial_kernel,
        in_specs=[pl.BlockSpec(memory_space=pltpu.SMEM)] + [vmem] * 5,
        out_specs=[vmem] * 4,
        out_shape=[jax.ShapeDtypeStruct((LANES, BLK), f32)] + [jax.ShapeDtypeStruct((520, LANES), i32)] * 3,
        scratch_shapes=[pltpu.VMEM((BLK, 512), bf16), pltpu.VMEM((512, BLK), f32)],
        compiler_params=params(),
        cost_estimate=pl.CostEstimate(flops=10**9, bytes_accessed=5 * 10**6, transcendentals=0),
    )(me, *tokens, grads)


def front_kernel(got_ref, own_ref, w1_ref, w2_ref, w3_ref, v_ref, high_ref, low_ref, grad):
    step = pl.program_id(0)
    eye = diagonal()
    decode_chunks(lambda d, start, size: got_ref[d, start:start + size, :], 0, 16, high_ref, low_ref, eye)

    @pl.when(step == 0)
    def _():
        for g in range(4):
            sums = [own_ref[:, g * GROUP:g * GROUP + LANES], own_ref[:, g * GROUP + LANES:(g + 1) * GROUP]]
            for ref in (w1_ref, w2_ref, w3_ref):
                unit = to_unit(ref[4 * LANES + g:4 * LANES + g + 1, :], eye)
                pair = decode(ref[g * LANES:(g + 1) * LANES, :], unit)
                sums = [sums[0] + pair[0], sums[1] + pair[1]]
            grad[g // 2, :, g % 2 * GROUP:(g % 2 + 1) * GROUP] = jnp.concatenate(sums, axis=1)

    grad_high, grad_low = halves(grad[step])
    both = mul(jnp.concatenate([grad_high, grad_low], axis=0), high_ref[...])
    v = both[:LANES] + both[LANES:] + mul(grad_high, low_ref[...])
    for c in range(8):
        part = v[:, c * LANES:(c + 1) * LANES]
        v_ref[c] = jnp.where(step == 0, part, v_ref[c] + part)


def front(got, own, words):
    whole = lambda i: (0, 0)
    return pl.pallas_call(
        front_kernel,
        grid=(2,),
        in_specs=[pl.BlockSpec((16, ROWS, LANES), lambda i: (i, 0, 0)), pl.BlockSpec((LANES, BLK), whole)]
        + [pl.BlockSpec((520, LANES), whole)] * 3,
        out_specs=[pl.BlockSpec((8, LANES, LANES), lambda i: (0, 0, 0))]
        + [pl.BlockSpec((512, BLK), lambda i: (i, 0))] * 2,
        out_shape=[jax.ShapeDtypeStruct((8, LANES, LANES), f32)] + [jax.ShapeDtypeStruct((BLK, BLK), bf16)] * 2,
        scratch_shapes=[pltpu.VMEM((2, LANES, 512), f32)],
        compiler_params=params("arbitrary"),
        cost_estimate=pl.CostEstimate(flops=8 * 10**8, bytes_accessed=8 * 10**6, transcendentals=0),
    )(got, own, *words)


def middle_kernel(v_ref, high_ref, low_ref, in_side_ref, out_side_ref, u_ref):
    v = v_ref[...].reshape(BLK, LANES)
    v_high, v_low = halves(v)
    qh, ql = high_ref[...], low_ref[...]
    both = mul(jnp.concatenate([v_high, v_low], axis=1), qh, 0, 0)
    rt = both[:LANES] + both[LANES:] + mul(v_high, ql, 0, 0)
    la = jnp.concatenate([in_side_ref[c, 1:2, :] for c in range(8)], axis=1).astype(f32) / VALUE_UNIT
    lb = jnp.sum(jnp.where(diagonal(), out_side_ref[0, 1:2, :], 0), axis=1, keepdims=True).astype(f32) / VALUE_UNIT
    st = rt / (lb * la + DAMPING)
    s_high, s_low = halves(st)
    both = mul(jnp.concatenate([s_high, s_low], axis=0), qh, 1, 1)
    ut = both[:LANES] + both[LANES:] + mul(s_high, ql, 1, 1)
    for c in range(8):
        u_ref[c] = ut[:, c * LANES:(c + 1) * LANES]


def middle(v, high, low, in_side, piece):
    whole = lambda i: (0, 0)
    return pl.pallas_call(
        middle_kernel,
        grid=(1,),
        in_specs=[
            pl.BlockSpec((8, LANES, LANES), lambda i: (0, 0, 0)),
            pl.BlockSpec((BLK, BLK), whole),
            pl.BlockSpec((BLK, BLK), whole),
            pl.BlockSpec((8, 8, LANES), lambda i: (0, 0, 0)),
            pl.BlockSpec((1, 8, LANES), lambda i: (0, 16, 0)),
        ],
        out_specs=pl.BlockSpec((8, LANES, LANES), lambda i: (0, 0, 0)),
        out_shape=jax.ShapeDtypeStruct((8, LANES, LANES), f32),
        compiler_params=params("arbitrary"),
        cost_estimate=pl.CostEstimate(flops=16 * 10**8, bytes_accessed=6 * 10**6, transcendentals=0),
    )(v, high, low, in_side, piece)


def back_kernel(u_ref, high_ref, low_ref, out_ref):
    u_high, u_low = halves(u_ref[...].reshape(BLK, LANES).T)
    both = mul(jnp.concatenate([u_high, u_low], axis=0), high_ref[...], 1, 1)
    out_ref[...] = both[:LANES] + both[LANES:] + mul(u_high, low_ref[...], 1, 1)


def back(u, high, low):
    return pl.pallas_call(
        back_kernel,
        grid=(2,),
        in_specs=[
            pl.BlockSpec((8, LANES, LANES), lambda i: (0, 0, 0)),
            pl.BlockSpec((512, BLK), lambda i: (i, 0)),
            pl.BlockSpec((512, BLK), lambda i: (i, 0)),
        ],
        out_specs=pl.BlockSpec((LANES, 512), lambda i: (0, i)),
        out_shape=jax.ShapeDtypeStruct((LANES, BLK), f32),
        compiler_params=params("arbitrary"),
        cost_estimate=pl.CostEstimate(flops=8 * 10**8, bytes_accessed=5 * 10**6, transcendentals=0),
    )(u, high, low)


def body(
    layer_inputs,
    output_grads,
    feature_order,
    block_slot,
    layer_owner,
    in_basis,
    in_values,
    out_basis,
    out_values,
):
    me = jnp.stack([lax.axis_index("y"), lax.axis_index("h"), lax.axis_index("z"), lax.axis_index(("l", "c"))])
    me = jnp.concatenate([me.astype(i32), block_slot])

    in_part = pack_basis(in_basis, in_values.reshape(1, LANES))
    in_pair = jnp.stack([in_part, lax.ppermute(in_part, ("h", "l"), [(i, 3 - i) for i in range(4)])])

    chunks = gather_columns(me, feature_order, layer_inputs.reshape(32, DIN))
    grads = output_grads.reshape(LANES, BLK)
    grads = jnp.stack([grads, flip(grads, "h")])
    chunks, grads, out_part = lax.optimization_barrier((chunks, grads, out_basis[0]))
    moved = lax.all_to_all(chunks, ("y", "h"), 0, 0, tiled=True)
    tokens = [moved] + [lax.ppermute(moved, ("l", "c"), [(m, m ^ j) for m in range(4)]) for j in range(1, 4)]

    packed = pack_basis(out_part, out_values)
    packed, in_pair, *tokens = lax.optimization_barrier((packed, in_pair, *tokens))
    spread = lax.all_to_all(packed, ALL_DP, 0, 0, tiled=True)
    piece = lax.dynamic_index_in_dim(spread, layer_owner[0], 0, keepdims=True)

    grads = lax.all_gather(grads, "y")
    _, in_pair = lax.optimization_barrier((grads, in_pair))
    in_all = lax.all_gather(in_pair, "z")
    own, *words = partial_rows(me, tokens, grads)
    words = [along(w, "z", k + 1) for k, w in enumerate(words)]

    got = lax.all_to_all(jnp.broadcast_to(piece, spread.shape), ALL_DP, 0, 0, tiled=True)
    in_high, in_low, in_side = unpack_basis(me, in_all)
    own, in_high, in_low = lax.optimization_barrier((own, in_high, in_low))
    v, out_high, out_low = front(got, own, words)

    v = lax.all_to_all(v, PAIR, 0, 0, tiled=True)
    u = middle(v, in_high, in_low, in_side, piece)
    u = lax.all_to_all(u, PAIR, 0, 0, tiled=True)
    return back(u, out_high, out_low)


def along(block, axis, shift):
    if shift == 0:
        return block
    return lax.ppermute(block, axis, [(i, (i + shift) % 4) for i in range(4)])


def flip(block, axis):
    return lax.ppermute(block, axis, [(0, 1), (1, 0)])


def solution(mesh):
    fine = Mesh(mesh.devices.reshape(4, 2, 4, 2, 2), ("y", "h", "z", "l", "c"))
    dp, mp = ("y", "h", "z"), ("l", "c")
    in_specs = (
        P(dp + mp, None, None),
        P(dp, None, mp),
        P(),
        P(),
        P(),
        P(dp, None),
        P(dp),
        P(dp, mp, None),
        P(dp, mp),
    )
    return jax.shard_map(body, mesh=fine, in_specs=in_specs, out_specs=P(dp, mp), check_vma=False)
```

```python
import jax
import jax.numpy as jnp
from jax import lax
from jax.experimental import pallas as pl
from jax.experimental.pallas import tpu as pltpu
from jax.sharding import Mesh, PartitionSpec as P

DIN = 4096
BLK = 1024
LANES = 128
GROUP = 256
ROWS = 136
DAMPING = 0.1
TOP = 32767.0
LOG_UNIT = 65536.0
VALUE_UNIT = 134217728.0
PAIR = ("h", "z")
ALL_DP = ("y", "h", "z")
VMEM = 48 * 1024 * 1024
f32, bf16, i32 = jnp.float32, jnp.bfloat16, jnp.int32


def params(*semantics):
    return pltpu.CompilerParams(vmem_limit_bytes=VMEM, dimension_semantics=semantics or None)


def mul(a, b, ca=1, cb=0):
    return lax.dot_general(a, b, (((ca,), (cb,)), ((), ())), preferred_element_type=f32)


def halves(a):
    high = a.astype(bf16)
    return high, (a - high.astype(f32)).astype(bf16)


def gather_kernel(me_ref, order_ref, x_ref, out_ref):
    x = [x_ref[:, k * LANES:(k + 1) * LANES].astype(f32) for k in range(DIN // LANES)]
    for n in range(4):
        pair = sum(jnp.where(me_ref[4 + j] == pl.program_id(0) * 2 + n // 2, j, 0) for j in range(4))
        start = pair * BLK + n % 2 * 512
        for b in range(4):
            idx = order_ref[:, pl.ds(pl.multiple_of(start + b * LANES, LANES), LANES)]
            lane = jnp.broadcast_to(jnp.bitwise_and(idx, LANES - 1), (32, LANES))
            src = jnp.broadcast_to(jnp.right_shift(idx, 7), (32, LANES))
            acc = jnp.zeros((32, LANES), f32)
            for k in range(DIN // LANES):
                acc = jnp.where(src == k, jnp.take_along_axis(x[k], lane, axis=1), acc)
            out_ref[n, :, b * LANES:(b + 1) * LANES] = acc.astype(bf16)


def gather_columns(me, order, x):
    return pl.pallas_call(
        gather_kernel,
        grid=(2,),
        in_specs=[
            pl.BlockSpec(memory_space=pltpu.SMEM),
            pl.BlockSpec((1, DIN), lambda i: (0, 0)),
            pl.BlockSpec((32, DIN), lambda i: (0, 0)),
        ],
        out_specs=pl.BlockSpec((4, 32, 512), lambda i: (i, 0, 0)),
        out_shape=jax.ShapeDtypeStruct((8, 32, 512), bf16),
        compiler_params=params("arbitrary"),
        cost_estimate=pl.CostEstimate(flops=10**6, bytes_accessed=10**6, transcendentals=0),
    )(me, order, x)


def diagonal():
    return lax.broadcasted_iota(i32, (LANES, LANES), 0) == lax.broadcasted_iota(i32, (LANES, LANES), 1)


def encode(part):
    most = jnp.maximum(jnp.max(jnp.abs(part), axis=1, keepdims=True), 1e-30)
    code = jnp.ceil(jnp.log2(most) * LOG_UNIT) + 4.0
    q = jnp.round(part * (TOP * jnp.exp2(-code / LOG_UNIT))).astype(i32)
    word = jnp.bitwise_or(jnp.left_shift(q[:, LANES:], 16), jnp.bitwise_and(q[:, :LANES], 65535))
    return word, code.astype(i32)


def decode(word, unit):
    first = jnp.right_shift(jnp.left_shift(word, 16), 16).astype(f32) * unit
    return first, jnp.right_shift(word, 16).astype(f32) * unit


def to_row(column, eye):
    return jnp.sum(jnp.where(eye, column, 0), axis=0, keepdims=True)


def to_unit(row, eye):
    return jnp.exp2(jnp.sum(jnp.where(eye, row, 0), axis=1, keepdims=True).astype(f32) / LOG_UNIT) / TOP


def pack_kernel(basis_ref, values_ref, out_ref):
    eye = diagonal()
    blocks = values_ref.shape[1] // LANES
    count = out_ref.shape[0]
    for n in range(count // 4):
        codes = [[] for _ in range(4)]
        for g in range(4):
            word, code = encode(basis_ref[n * LANES:(n + 1) * LANES, g * GROUP:(g + 1) * GROUP])
            for d in range(4):
                out_ref[n * 4 + d, g * 32:(g + 1) * 32, :] = word[d * 32:(d + 1) * 32]
                codes[d].append(code[d * 32:(d + 1) * 32])
        for d in range(4):
            row = to_row(jnp.concatenate(codes[d], axis=0), eye)
            block = (n * 4 + d) % blocks
            coded = (values_ref[:, block * LANES:(block + 1) * LANES] * VALUE_UNIT).astype(i32)
            out_ref[n * 4 + d, LANES:ROWS, :] = jnp.concatenate([row, coded, jnp.zeros((6, LANES), i32)], axis=0)


def pack_basis(basis, values):
    rows = basis.shape[0]
    size = min(rows, 512)
    return pl.pallas_call(
        pack_kernel,
        grid=(rows // size,),
        in_specs=[pl.BlockSpec((size, BLK), lambda i: (i, 0)), pl.BlockSpec(values.shape, lambda i: (0, 0))],
        out_specs=pl.BlockSpec((size // 32, ROWS, LANES), lambda i: (i, 0, 0)),
        out_shape=jax.ShapeDtypeStruct((rows // 32, ROWS, LANES), i32),
        compiler_params=params("arbitrary"),
        cost_estimate=pl.CostEstimate(flops=rows * 10**4, bytes_accessed=rows * 6000, transcendentals=0),
    )(basis, values)


def decode_chunks(get, base, count, high_ref, low_ref, eye):
    for d in range(count):
        unit = to_unit(get(d, LANES, 1), eye)
        for g in range(4):
            pair = decode(get(d, g * 32, 32), unit[g * 32:(g + 1) * 32])
            for k in range(2):
                high, low = halves(pair[k])
                where = (pl.ds(base + d * 32, 32), slice(g * GROUP + k * LANES, g * GROUP + (k + 1) * LANES))
                high_ref[where] = high
                low_ref[where] = low


def unpack_kernel(me_ref, own_ref, other_ref, high_ref, low_ref, side_ref):
    core = lax.rem(me_ref[3], 2)
    eye = diagonal()
    for z in range(4):
        def get(d, start, size):
            rows = slice(start, start + size)
            return jnp.where(core == d // 2, own_ref[z, 0, d % 2, rows, :], other_ref[z, 0, d % 2, rows, :])
        decode_chunks(get, z * LANES, 4, high_ref, low_ref, eye)
        side_ref[z] = get(0, LANES, 8)


def unpack_basis(me, own, other):
    rows = lambda i, m: (i, 0)
    half = pl.BlockSpec((4, 1, 2, ROWS, LANES), lambda i, m: (0, lax.rem(i + m[1], 2), 0, 0, 0))
    return pl.pallas_call(
        unpack_kernel,
        grid_spec=pltpu.PrefetchScalarGridSpec(
            num_scalar_prefetch=1,
            grid=(2,),
            in_specs=[half, half],
            out_specs=[pl.BlockSpec((512, BLK), rows)] * 2 + [pl.BlockSpec((4, 8, LANES), lambda i, m: (i, 0, 0))],
        ),
        out_shape=[jax.ShapeDtypeStruct((BLK, BLK), bf16)] * 2 + [jax.ShapeDtypeStruct((8, 8, LANES), i32)],
        compiler_params=params("arbitrary"),
        cost_estimate=pl.CostEstimate(flops=10**7, bytes_accessed=6 * 10**6, transcendentals=0),
    )(me, own, other)


def partial_kernel(me_ref, x0_ref, x1_ref, x2_ref, x3_ref, grads_ref, *refs):
    own_ref, word_refs, tokens, total = refs[0], refs[1:4], refs[4], refs[5]
    for j, x_ref in enumerate((x0_ref, x1_ref, x2_ref, x3_ref)):
        place = jnp.bitwise_xor(me_ref[3], j)
        for r in range(8):
            tokens[pl.ds(pl.multiple_of(r * LANES + place * 32, 32), 32), :] = x_ref[r]
    for r in range(4):
        grads = jnp.concatenate([grads_ref[r, me_ref[1]], grads_ref[r, 1 - me_ref[1]]], axis=0)
        part = mul(tokens[r * GROUP:(r + 1) * GROUP, :], grads, 0, 0)
        total[...] = part if r == 0 else total[...] + part
    eye = diagonal()
    for k in range(4):
        start = pl.multiple_of(lax.rem(me_ref[2] + k, 4) * LANES, LANES)
        if k == 0:
            own_ref[...] = total[pl.ds(start, LANES), :]
            continue
        rows = []
        for g in range(4):
            word, code = encode(total[pl.ds(start, LANES), g * GROUP:(g + 1) * GROUP])
            word_refs[k - 1][g * LANES:(g + 1) * LANES, :] = word
            rows.append(to_row(code, eye))
        word_refs[k - 1][4 * LANES:, :] = jnp.concatenate(rows + [jnp.zeros((4, LANES), i32)], axis=0)


def partial_rows(me, tokens, grads):
    vmem = pl.BlockSpec(memory_space=pltpu.VMEM)
    return pl.pallas_call(
        partial_kernel,
        in_specs=[pl.BlockSpec(memory_space=pltpu.SMEM)] + [vmem] * 5,
        out_specs=[vmem] * 4,
        out_shape=[jax.ShapeDtypeStruct((LANES, BLK), f32)] + [jax.ShapeDtypeStruct((520, LANES), i32)] * 3,
        scratch_shapes=[pltpu.VMEM((BLK, 512), bf16), pltpu.VMEM((512, BLK), f32)],
        compiler_params=params(),
        cost_estimate=pl.CostEstimate(flops=10**9, bytes_accessed=5 * 10**6, transcendentals=0),
    )(me, *tokens, grads)


def front_kernel(got_ref, own_ref, w1_ref, w2_ref, w3_ref, v_ref, high_ref, low_ref, grad):
    step = pl.program_id(0)
    eye = diagonal()
    decode_chunks(lambda d, start, size: got_ref[d, start:start + size, :], 0, 16, high_ref, low_ref, eye)

    @pl.when(step == 0)
    def _():
        for g in range(4):
            sums = [own_ref[:, g * GROUP:g * GROUP + LANES], own_ref[:, g * GROUP + LANES:(g + 1) * GROUP]]
            for ref in (w1_ref, w2_ref, w3_ref):
                unit = to_unit(ref[4 * LANES + g:4 * LANES + g + 1, :], eye)
                pair = decode(ref[g * LANES:(g + 1) * LANES, :], unit)
                sums = [sums[0] + pair[0], sums[1] + pair[1]]
            grad[g // 2, :, g % 2 * GROUP:(g % 2 + 1) * GROUP] = jnp.concatenate(sums, axis=1)

    grad_high, grad_low = halves(grad[step])
    both = mul(jnp.concatenate([grad_high, grad_low], axis=0), high_ref[...])
    v = both[:LANES] + both[LANES:] + mul(grad_high, low_ref[...])
    for c in range(8):
        part = v[:, c * LANES:(c + 1) * LANES]
        v_ref[c] = jnp.where(step == 0, part, v_ref[c] + part)


def front(got, own, words):
    whole = lambda i: (0, 0)
    return pl.pallas_call(
        front_kernel,
        grid=(2,),
        in_specs=[pl.BlockSpec((16, ROWS, LANES), lambda i: (i, 0, 0)), pl.BlockSpec((LANES, BLK), whole)]
        + [pl.BlockSpec((520, LANES), whole)] * 3,
        out_specs=[pl.BlockSpec((8, LANES, LANES), lambda i: (0, 0, 0))]
        + [pl.BlockSpec((512, BLK), lambda i: (i, 0))] * 2,
        out_shape=[jax.ShapeDtypeStruct((8, LANES, LANES), f32)] + [jax.ShapeDtypeStruct((BLK, BLK), bf16)] * 2,
        scratch_shapes=[pltpu.VMEM((2, LANES, 512), f32)],
        compiler_params=params("arbitrary"),
        cost_estimate=pl.CostEstimate(flops=8 * 10**8, bytes_accessed=8 * 10**6, transcendentals=0),
    )(got, own, *words)


def middle_kernel(v_ref, high_ref, low_ref, in_side_ref, out_side_ref, u_ref):
    v = v_ref[...].reshape(BLK, LANES)
    v_high, v_low = halves(v)
    qh, ql = high_ref[...], low_ref[...]
    both = mul(jnp.concatenate([v_high, v_low], axis=1), qh, 0, 0)
    rt = both[:LANES] + both[LANES:] + mul(v_high, ql, 0, 0)
    la = jnp.concatenate([in_side_ref[c, 1:2, :] for c in range(8)], axis=1).astype(f32) / VALUE_UNIT
    lb = jnp.sum(jnp.where(diagonal(), out_side_ref[0, 1:2, :], 0), axis=1, keepdims=True).astype(f32) / VALUE_UNIT
    st = rt / (lb * la + DAMPING)
    s_high, s_low = halves(st)
    both = mul(jnp.concatenate([s_high, s_low], axis=0), qh, 1, 1)
    ut = both[:LANES] + both[LANES:] + mul(s_high, ql, 1, 1)
    for c in range(8):
        u_ref[c] = ut[:, c * LANES:(c + 1) * LANES]


def middle(v, high, low, in_side, piece):
    whole = lambda i: (0, 0)
    return pl.pallas_call(
        middle_kernel,
        grid=(1,),
        in_specs=[
            pl.BlockSpec((8, LANES, LANES), lambda i: (0, 0, 0)),
            pl.BlockSpec((BLK, BLK), whole),
            pl.BlockSpec((BLK, BLK), whole),
            pl.BlockSpec((8, 8, LANES), lambda i: (0, 0, 0)),
            pl.BlockSpec((1, 8, LANES), lambda i: (0, 16, 0)),
        ],
        out_specs=pl.BlockSpec((8, LANES, LANES), lambda i: (0, 0, 0)),
        out_shape=jax.ShapeDtypeStruct((8, LANES, LANES), f32),
        compiler_params=params("arbitrary"),
        cost_estimate=pl.CostEstimate(flops=16 * 10**8, bytes_accessed=6 * 10**6, transcendentals=0),
    )(v, high, low, in_side, piece)


def back_kernel(u_ref, high_ref, low_ref, out_ref):
    u_high, u_low = halves(u_ref[...].reshape(BLK, LANES).T)
    both = mul(jnp.concatenate([u_high, u_low], axis=0), high_ref[...], 1, 1)
    out_ref[...] = both[:LANES] + both[LANES:] + mul(u_high, low_ref[...], 1, 1)


def back(u, high, low):
    return pl.pallas_call(
        back_kernel,
        grid=(2,),
        in_specs=[
            pl.BlockSpec((8, LANES, LANES), lambda i: (0, 0, 0)),
            pl.BlockSpec((512, BLK), lambda i: (i, 0)),
            pl.BlockSpec((512, BLK), lambda i: (i, 0)),
        ],
        out_specs=pl.BlockSpec((LANES, 512), lambda i: (0, i)),
        out_shape=jax.ShapeDtypeStruct((LANES, BLK), f32),
        compiler_params=params("arbitrary"),
        cost_estimate=pl.CostEstimate(flops=8 * 10**8, bytes_accessed=5 * 10**6, transcendentals=0),
    )(u, high, low)


def body(
    layer_inputs,
    output_grads,
    feature_order,
    block_slot,
    layer_owner,
    in_basis,
    in_values,
    out_basis,
    out_values,
):
    me = jnp.stack([lax.axis_index("y"), lax.axis_index("h"), lax.axis_index("z"), lax.axis_index(("l", "c"))])
    me = jnp.concatenate([me.astype(i32), block_slot])

    in_part = pack_basis(in_basis, in_values.reshape(1, LANES))
    in_part = lax.dynamic_slice_in_dim(in_part, lax.axis_index("c") * 2, 2, 0)
    in_pair = jnp.stack([in_part, lax.ppermute(in_part, ("h", "l"), [(i, 3 - i) for i in range(4)])])

    chunks = gather_columns(me, feature_order, layer_inputs.reshape(32, DIN))
    grads = output_grads.reshape(LANES, BLK)
    grads = jnp.stack([grads, flip(grads, "h")])
    chunks, grads, out_part = lax.optimization_barrier((chunks, grads, out_basis[0]))
    moved = lax.all_to_all(chunks, ("y", "h"), 0, 0, tiled=True)
    tokens = [moved] + [lax.ppermute(moved, ("l", "c"), [(m, m ^ j) for m in range(4)]) for j in range(1, 4)]

    packed = pack_basis(out_part, out_values)
    packed, in_pair, *tokens = lax.optimization_barrier((packed, in_pair, *tokens))
    spread = lax.all_to_all(packed, ALL_DP, 0, 0, tiled=True)
    piece = lax.dynamic_index_in_dim(spread, layer_owner[0], 0, keepdims=True)

    grads = lax.all_gather(grads, "y")
    _, in_pair = lax.optimization_barrier((grads, in_pair))
    in_all = lax.all_gather(in_pair, "z")
    own, *words = partial_rows(me, tokens, grads)
    codes = along(words[0][512:], "z", 1)
    words = [along(words[0][:512], "z", 1)] + [along(words[k], "z", k + 1) for k in (1, 2)]
    piece, codes = lax.optimization_barrier((piece, codes))
    words[0] = jnp.concatenate([words[0], codes], 0)

    got = lax.all_to_all(jnp.broadcast_to(piece, spread.shape), ALL_DP, 0, 0, tiled=True)
    v, out_high, out_low = front(got, own, words)

    v = lax.all_to_all(v, PAIR, 0, 0, tiled=True)
    in_high, in_low, in_side = unpack_basis(me, in_all, jnp.stack([flip(in_all[z], "c") for z in range(4)]))
    u = middle(v, in_high, in_low, in_side, piece)
    u = lax.all_to_all(u, PAIR, 0, 0, tiled=True)
    return back(u, out_high, out_low)


def along(block, axis, shift):
    if shift == 0:
        return block
    return lax.ppermute(block, axis, [(i, (i + shift) % 4) for i in range(4)])


def flip(block, axis):
    return lax.ppermute(block, axis, [(0, 1), (1, 0)])


def solution(mesh):
    fine = Mesh(mesh.devices.reshape(4, 2, 4, 2, 2), ("y", "h", "z", "l", "c"))
    dp, mp = ("y", "h", "z"), ("l", "c")
    in_specs = (
        P(dp + mp, None, None),
        P(dp, None, mp),
        P(),
        P(),
        P(),
        P(dp, None),
        P(dp),
        P(dp, mp, None),
        P(dp, mp),
    )
    return jax.shard_map(body, mesh=fine, in_specs=in_specs, out_specs=P(dp, mp), check_vma=False)
```

```python
import jax
import jax.numpy as jnp
from jax import lax
from jax.experimental import pallas as pl
from jax.experimental.pallas import tpu as pltpu
from jax.sharding import Mesh, PartitionSpec as P

DIN = 4096
BLK = 1024
LANES = 128
GROUP = 256
ROWS = 136
DAMPING = 0.1
TOP = 32767.0
LOG_UNIT = 65536.0
VALUE_UNIT = 134217728.0
PAIR = ("h", "z")
ALL_DP = ("y", "h", "z")
VMEM = 48 * 1024 * 1024
f32, bf16, i32 = jnp.float32, jnp.bfloat16, jnp.int32


def params(*semantics):
    return pltpu.CompilerParams(vmem_limit_bytes=VMEM, dimension_semantics=semantics or None)


def mul(a, b, ca=1, cb=0):
    return lax.dot_general(a, b, (((ca,), (cb,)), ((), ())), preferred_element_type=f32)


def halves(a):
    high = a.astype(bf16)
    return high, (a - high.astype(f32)).astype(bf16)


def gather_kernel(me_ref, order_ref, x_ref, out_ref):
    x = [x_ref[:, k * LANES:(k + 1) * LANES].astype(f32) for k in range(DIN // LANES)]
    for n in range(4):
        pair = sum(jnp.where(me_ref[4 + j] == pl.program_id(0) * 2 + n // 2, j, 0) for j in range(4))
        start = pair * BLK + n % 2 * 512
        for b in range(4):
            idx = order_ref[:, pl.ds(pl.multiple_of(start + b * LANES, LANES), LANES)]
            lane = jnp.broadcast_to(jnp.bitwise_and(idx, LANES - 1), (32, LANES))
            src = jnp.broadcast_to(jnp.right_shift(idx, 7), (32, LANES))
            acc = jnp.zeros((32, LANES), f32)
            for k in range(DIN // LANES):
                acc = jnp.where(src == k, jnp.take_along_axis(x[k], lane, axis=1), acc)
            out_ref[n, :, b * LANES:(b + 1) * LANES] = acc.astype(bf16)


def gather_columns(me, order, x):
    return pl.pallas_call(
        gather_kernel,
        grid=(2,),
        in_specs=[
            pl.BlockSpec(memory_space=pltpu.SMEM),
            pl.BlockSpec((1, DIN), lambda i: (0, 0)),
            pl.BlockSpec((32, DIN), lambda i: (0, 0)),
        ],
        out_specs=pl.BlockSpec((4, 32, 512), lambda i: (i, 0, 0)),
        out_shape=jax.ShapeDtypeStruct((8, 32, 512), bf16),
        compiler_params=params("arbitrary"),
        cost_estimate=pl.CostEstimate(flops=10**6, bytes_accessed=10**6, transcendentals=0),
    )(me, order, x)


def diagonal():
    return lax.broadcasted_iota(i32, (LANES, LANES), 0) == lax.broadcasted_iota(i32, (LANES, LANES), 1)


def encode(part):
    most = jnp.maximum(jnp.max(jnp.abs(part), axis=1, keepdims=True), 1e-30)
    code = jnp.ceil(jnp.log2(most) * LOG_UNIT) + 4.0
    q = jnp.round(part * (TOP * jnp.exp2(-code / LOG_UNIT))).astype(i32)
    word = jnp.bitwise_or(jnp.left_shift(q[:, LANES:], 16), jnp.bitwise_and(q[:, :LANES], 65535))
    return word, code.astype(i32)


def decode(word, unit):
    first = jnp.right_shift(jnp.left_shift(word, 16), 16).astype(f32) * unit
    return first, jnp.right_shift(word, 16).astype(f32) * unit


def to_row(column, eye):
    return jnp.sum(jnp.where(eye, column, 0), axis=0, keepdims=True)


def to_unit(row, eye):
    return jnp.exp2(jnp.sum(jnp.where(eye, row, 0), axis=1, keepdims=True).astype(f32) / LOG_UNIT) / TOP


def pack_kernel(basis_ref, values_ref, out_ref):
    eye = diagonal()
    blocks = values_ref.shape[1] // LANES
    count = out_ref.shape[0]
    for n in range(count // 4):
        codes = [[] for _ in range(4)]
        for g in range(4):
            word, code = encode(basis_ref[n * LANES:(n + 1) * LANES, g * GROUP:(g + 1) * GROUP])
            for d in range(4):
                out_ref[n * 4 + d, g * 32:(g + 1) * 32, :] = word[d * 32:(d + 1) * 32]
                codes[d].append(code[d * 32:(d + 1) * 32])
        for d in range(4):
            row = to_row(jnp.concatenate(codes[d], axis=0), eye)
            block = (n * 4 + d) % blocks
            coded = (values_ref[:, block * LANES:(block + 1) * LANES] * VALUE_UNIT).astype(i32)
            out_ref[n * 4 + d, LANES:ROWS, :] = jnp.concatenate([row, coded, jnp.zeros((6, LANES), i32)], axis=0)


def pack_basis(basis, values):
    rows = basis.shape[0]
    size = min(rows, 512)
    return pl.pallas_call(
        pack_kernel,
        grid=(rows // size,),
        in_specs=[pl.BlockSpec((size, BLK), lambda i: (i, 0)), pl.BlockSpec(values.shape, lambda i: (0, 0))],
        out_specs=pl.BlockSpec((size // 32, ROWS, LANES), lambda i: (i, 0, 0)),
        out_shape=jax.ShapeDtypeStruct((rows // 32, ROWS, LANES), i32),
        compiler_params=params("arbitrary"),
        cost_estimate=pl.CostEstimate(flops=rows * 10**4, bytes_accessed=rows * 6000, transcendentals=0),
    )(basis, values)


def decode_chunks(get, base, count, high_ref, low_ref, eye):
    for d in range(count):
        unit = to_unit(get(d, LANES, 1), eye)
        for g in range(4):
            pair = decode(get(d, g * 32, 32), unit[g * 32:(g + 1) * 32])
            for k in range(2):
                high, low = halves(pair[k])
                where = (pl.ds(base + d * 32, 32), slice(g * GROUP + k * LANES, g * GROUP + (k + 1) * LANES))
                high_ref[where] = high
                low_ref[where] = low


def unpack_kernel(me_ref, own_ref, other_ref, high_ref, low_ref, side_ref):
    core = lax.rem(me_ref[3], 2)
    eye = diagonal()
    for z in range(4):
        def get(d, start, size):
            rows = slice(start, start + size)
            return jnp.where(core == d // 2, own_ref[z, 0, d % 2, rows, :], other_ref[z, 0, d % 2, rows, :])
        decode_chunks(get, z * LANES, 4, high_ref, low_ref, eye)
        side_ref[z] = get(0, LANES, 8)


def unpack_basis(me, own, other):
    rows = lambda i, m: (i, 0)
    half = pl.BlockSpec((4, 1, 2, ROWS, LANES), lambda i, m: (0, lax.rem(i + m[1], 2), 0, 0, 0))
    return pl.pallas_call(
        unpack_kernel,
        grid_spec=pltpu.PrefetchScalarGridSpec(
            num_scalar_prefetch=1,
            grid=(2,),
            in_specs=[half, half],
            out_specs=[pl.BlockSpec((512, BLK), rows)] * 2 + [pl.BlockSpec((4, 8, LANES), lambda i, m: (i, 0, 0))],
        ),
        out_shape=[jax.ShapeDtypeStruct((BLK, BLK), bf16)] * 2 + [jax.ShapeDtypeStruct((8, 8, LANES), i32)],
        compiler_params=params("arbitrary"),
        cost_estimate=pl.CostEstimate(flops=10**7, bytes_accessed=6 * 10**6, transcendentals=0),
    )(me, own, other)


def partial_kernel(me_ref, x0_ref, x1_ref, x2_ref, x3_ref, grads_ref, *refs):
    own_ref, word_refs, tokens, total = refs[0], refs[1:4], refs[4], refs[5]
    for j, x_ref in enumerate((x0_ref, x1_ref, x2_ref, x3_ref)):
        place = jnp.bitwise_xor(me_ref[3], j)
        for r in range(8):
            tokens[pl.ds(pl.multiple_of(r * LANES + place * 32, 32), 32), :] = x_ref[r]
    for r in range(4):
        grads = jnp.concatenate([grads_ref[r, me_ref[1]], grads_ref[r, 1 - me_ref[1]]], axis=0)
        part = mul(tokens[r * GROUP:(r + 1) * GROUP, :], grads, 0, 0)
        total[...] = part if r == 0 else total[...] + part
    eye = diagonal()
    for k in range(4):
        start = pl.multiple_of(lax.rem(me_ref[2] + k, 4) * LANES, LANES)
        if k == 0:
            own_ref[...] = total[pl.ds(start, LANES), :]
            continue
        rows = []
        for g in range(4):
            word, code = encode(total[pl.ds(start, LANES), g * GROUP:(g + 1) * GROUP])
            word_refs[k - 1][g * LANES:(g + 1) * LANES, :] = word
            rows.append(to_row(code, eye))
        word_refs[k - 1][4 * LANES:, :] = jnp.concatenate(rows + [jnp.zeros((4, LANES), i32)], axis=0)


def partial_rows(me, tokens, grads):
    vmem = pl.BlockSpec(memory_space=pltpu.VMEM)
    return pl.pallas_call(
        partial_kernel,
        in_specs=[pl.BlockSpec(memory_space=pltpu.SMEM)] + [vmem] * 5,
        out_specs=[vmem] * 4,
        out_shape=[jax.ShapeDtypeStruct((LANES, BLK), f32)] + [jax.ShapeDtypeStruct((520, LANES), i32)] * 3,
        scratch_shapes=[pltpu.VMEM((BLK, 512), bf16), pltpu.VMEM((512, BLK), f32)],
        compiler_params=params(),
        cost_estimate=pl.CostEstimate(flops=10**9, bytes_accessed=5 * 10**6, transcendentals=0),
    )(me, *tokens, grads)


def front_kernel(got_ref, own_ref, w1_ref, w2_ref, w3_ref, v_ref, high_ref, low_ref, grad):
    step = pl.program_id(0)
    eye = diagonal()
    decode_chunks(lambda d, start, size: got_ref[d, start:start + size, :], 0, 16, high_ref, low_ref, eye)

    @pl.when(step == 0)
    def _():
        for g in range(4):
            sums = [own_ref[:, g * GROUP:g * GROUP + LANES], own_ref[:, g * GROUP + LANES:(g + 1) * GROUP]]
            for ref in (w1_ref, w2_ref, w3_ref):
                unit = to_unit(ref[4 * LANES + g:4 * LANES + g + 1, :], eye)
                pair = decode(ref[g * LANES:(g + 1) * LANES, :], unit)
                sums = [sums[0] + pair[0], sums[1] + pair[1]]
            grad[g // 2, :, g % 2 * GROUP:(g % 2 + 1) * GROUP] = jnp.concatenate(sums, axis=1)

    grad_high, grad_low = halves(grad[step])
    both = mul(jnp.concatenate([grad_high, grad_low], axis=0), high_ref[...])
    v = both[:LANES] + both[LANES:] + mul(grad_high, low_ref[...])
    for c in range(8):
        part = v[:, c * LANES:(c + 1) * LANES]
        v_ref[c] = jnp.where(step == 0, part, v_ref[c] + part)


def front(got, own, words):
    whole = lambda i: (0, 0)
    return pl.pallas_call(
        front_kernel,
        grid=(2,),
        in_specs=[pl.BlockSpec((16, ROWS, LANES), lambda i: (i, 0, 0)), pl.BlockSpec((LANES, BLK), whole)]
        + [pl.BlockSpec((520, LANES), whole)] * 3,
        out_specs=[pl.BlockSpec((8, LANES, LANES), lambda i: (0, 0, 0))]
        + [pl.BlockSpec((512, BLK), lambda i: (i, 0))] * 2,
        out_shape=[jax.ShapeDtypeStruct((8, LANES, LANES), f32)] + [jax.ShapeDtypeStruct((BLK, BLK), bf16)] * 2,
        scratch_shapes=[pltpu.VMEM((2, LANES, 512), f32)],
        compiler_params=params("arbitrary"),
        cost_estimate=pl.CostEstimate(flops=8 * 10**8, bytes_accessed=8 * 10**6, transcendentals=0),
    )(got, own, *words)


def middle_kernel(v_ref, high_ref, low_ref, in_side_ref, out_side_ref, u_ref):
    v = v_ref[...].reshape(BLK, LANES)
    v_high, v_low = halves(v)
    qh, ql = high_ref[...], low_ref[...]
    both = mul(jnp.concatenate([v_high, v_low], axis=1), qh, 0, 0)
    rt = both[:LANES] + both[LANES:] + mul(v_high, ql, 0, 0)
    la = jnp.concatenate([in_side_ref[c, 1:2, :] for c in range(8)], axis=1).astype(f32) / VALUE_UNIT
    lb = jnp.sum(jnp.where(diagonal(), out_side_ref[0, 1:2, :], 0), axis=1, keepdims=True).astype(f32) / VALUE_UNIT
    st = rt / (lb * la + DAMPING)
    s_high, s_low = halves(st)
    both = mul(jnp.concatenate([s_high, s_low], axis=0), qh, 1, 1)
    ut = both[:LANES] + both[LANES:] + mul(s_high, ql, 1, 1)
    for c in range(8):
        u_ref[c] = ut[:, c * LANES:(c + 1) * LANES]


def middle(v, high, low, in_side, piece):
    whole = lambda i: (0, 0)
    return pl.pallas_call(
        middle_kernel,
        grid=(1,),
        in_specs=[
            pl.BlockSpec((8, LANES, LANES), lambda i: (0, 0, 0)),
            pl.BlockSpec((BLK, BLK), whole),
            pl.BlockSpec((BLK, BLK), whole),
            pl.BlockSpec((8, 8, LANES), lambda i: (0, 0, 0)),
            pl.BlockSpec((1, 8, LANES), lambda i: (0, 16, 0)),
        ],
        out_specs=pl.BlockSpec((8, LANES, LANES), lambda i: (0, 0, 0)),
        out_shape=jax.ShapeDtypeStruct((8, LANES, LANES), f32),
        compiler_params=params("arbitrary"),
        cost_estimate=pl.CostEstimate(flops=16 * 10**8, bytes_accessed=6 * 10**6, transcendentals=0),
    )(v, high, low, in_side, piece)


def back_kernel(u_ref, high_ref, low_ref, out_ref):
    u_high, u_low = halves(u_ref[...].reshape(BLK, LANES).T)
    both = mul(jnp.concatenate([u_high, u_low], axis=0), high_ref[...], 1, 1)
    out_ref[...] = both[:LANES] + both[LANES:] + mul(u_high, low_ref[...], 1, 1)


def back(u, high, low):
    return pl.pallas_call(
        back_kernel,
        grid=(2,),
        in_specs=[
            pl.BlockSpec((8, LANES, LANES), lambda i: (0, 0, 0)),
            pl.BlockSpec((512, BLK), lambda i: (i, 0)),
            pl.BlockSpec((512, BLK), lambda i: (i, 0)),
        ],
        out_specs=pl.BlockSpec((LANES, 512), lambda i: (0, i)),
        out_shape=jax.ShapeDtypeStruct((LANES, BLK), f32),
        compiler_params=params("arbitrary"),
        cost_estimate=pl.CostEstimate(flops=8 * 10**8, bytes_accessed=5 * 10**6, transcendentals=0),
    )(u, high, low)


def body(
    layer_inputs,
    output_grads,
    feature_order,
    block_slot,
    layer_owner,
    in_basis,
    in_values,
    out_basis,
    out_values,
):
    me = jnp.stack([lax.axis_index("y"), lax.axis_index("h"), lax.axis_index("z"), lax.axis_index(("l", "c"))])
    me = jnp.concatenate([me.astype(i32), block_slot])

    in_part = pack_basis(in_basis, in_values.reshape(1, LANES))
    in_part = lax.dynamic_slice_in_dim(in_part, lax.axis_index("c") * 2, 2, 0)
    in_pair = jnp.stack([in_part, lax.ppermute(in_part, ("h", "l"), [(i, 3 - i) for i in range(4)])])

    chunks = gather_columns(me, feature_order, layer_inputs.reshape(32, DIN))
    grads = output_grads.reshape(LANES, BLK)
    grads = jnp.stack([grads, flip(grads, "h")])
    chunks, grads, out_part = lax.optimization_barrier((chunks, grads, out_basis[0]))
    moved = lax.all_to_all(chunks, ("y", "h"), 0, 0, tiled=True)
    tokens = [moved] + [lax.ppermute(moved, ("l", "c"), [(m, m ^ j) for m in range(4)]) for j in range(1, 4)]

    packed = pack_basis(out_part, out_values)
    packed, in_pair, *tokens = lax.optimization_barrier((packed, in_pair, *tokens))
    spread = lax.all_to_all(packed, ALL_DP, 0, 0, tiled=True)
    piece = lax.dynamic_index_in_dim(spread, layer_owner[0], 0, keepdims=True)

    grads = lax.all_gather(grads, "y")
    _, in_pair = lax.optimization_barrier((grads, in_pair))
    in_all = lax.all_gather(in_pair, "z")
    own, *words = partial_rows(me, tokens, grads)
    words = [along(w, "z", k + 1) for k, w in enumerate(words)]
    in_other = [flip(in_all[z], "c") for z in range(4)]
    piece, in_all, in_other, words = lax.optimization_barrier((piece, in_all, in_other, words))

    got = lax.all_to_all(jnp.broadcast_to(piece, spread.shape), ALL_DP, 0, 0, tiled=True)
    in_high, in_low, in_side = unpack_basis(me, in_all, jnp.stack(in_other))
    own, in_high, in_low = lax.optimization_barrier((own, in_high, in_low))
    v, out_high, out_low = front(got, own, words)

    v = lax.all_to_all(v, PAIR, 0, 0, tiled=True)
    u = middle(v, in_high, in_low, in_side, piece)
    u = lax.all_to_all(u, PAIR, 0, 0, tiled=True)
    return back(u, out_high, out_low)


def along(block, axis, shift):
    if shift == 0:
        return block
    return lax.ppermute(block, axis, [(i, (i + shift) % 4) for i in range(4)])


def flip(block, axis):
    return lax.ppermute(block, axis, [(0, 1), (1, 0)])


def solution(mesh):
    fine = Mesh(mesh.devices.reshape(4, 2, 4, 2, 2), ("y", "h", "z", "l", "c"))
    dp, mp = ("y", "h", "z"), ("l", "c")
    in_specs = (
        P(dp + mp, None, None),
        P(dp, None, mp),
        P(),
        P(),
        P(),
        P(dp, None),
        P(dp),
        P(dp, mp, None),
        P(dp, mp),
    )
    return jax.shard_map(body, mesh=fine, in_specs=in_specs, out_specs=P(dp, mp), check_vma=False)
```

```python
import jax
import jax.numpy as jnp
from jax import lax
from jax.experimental import pallas as pl
from jax.experimental.pallas import tpu as pltpu
from jax.sharding import Mesh, PartitionSpec as P

DIN = 4096
BLK = 1024
LANES = 128
GROUP = 256
ROWS = 136
DAMPING = 0.1
TOP = 32767.0
LOG_UNIT = 65536.0
VALUE_UNIT = 134217728.0
PAIR = ("h", "z")
ALL_DP = ("y", "h", "z")
VMEM = 48 * 1024 * 1024
f32, bf16, i32 = jnp.float32, jnp.bfloat16, jnp.int32


def params(*semantics):
    return pltpu.CompilerParams(vmem_limit_bytes=VMEM, dimension_semantics=semantics or None)


def mul(a, b, ca=1, cb=0):
    return lax.dot_general(a, b, (((ca,), (cb,)), ((), ())), preferred_element_type=f32)


def halves(a):
    high = a.astype(bf16)
    return high, (a - high.astype(f32)).astype(bf16)


def gather_kernel(me_ref, order_ref, x_ref, out_ref):
    x = [x_ref[:, k * LANES:(k + 1) * LANES].astype(f32) for k in range(DIN // LANES)]
    for n in range(4):
        pair = sum(jnp.where(me_ref[4 + j] == pl.program_id(0) * 2 + n // 2, j, 0) for j in range(4))
        start = pair * BLK + n % 2 * 512
        for b in range(4):
            idx = order_ref[:, pl.ds(pl.multiple_of(start + b * LANES, LANES), LANES)]
            lane = jnp.broadcast_to(jnp.bitwise_and(idx, LANES - 1), (32, LANES))
            src = jnp.broadcast_to(jnp.right_shift(idx, 7), (32, LANES))
            acc = jnp.zeros((32, LANES), f32)
            for k in range(DIN // LANES):
                acc = jnp.where(src == k, jnp.take_along_axis(x[k], lane, axis=1), acc)
            out_ref[n, :, b * LANES:(b + 1) * LANES] = acc.astype(bf16)


def gather_columns(me, order, x):
    return pl.pallas_call(
        gather_kernel,
        grid=(2,),
        in_specs=[
            pl.BlockSpec(memory_space=pltpu.SMEM),
            pl.BlockSpec((1, DIN), lambda i: (0, 0)),
            pl.BlockSpec((32, DIN), lambda i: (0, 0)),
        ],
        out_specs=pl.BlockSpec((4, 32, 512), lambda i: (i, 0, 0)),
        out_shape=jax.ShapeDtypeStruct((8, 32, 512), bf16),
        compiler_params=params("arbitrary"),
        cost_estimate=pl.CostEstimate(flops=10**6, bytes_accessed=10**6, transcendentals=0),
    )(me, order, x)


def diagonal():
    return lax.broadcasted_iota(i32, (LANES, LANES), 0) == lax.broadcasted_iota(i32, (LANES, LANES), 1)


def encode(part):
    most = jnp.maximum(jnp.max(jnp.abs(part), axis=1, keepdims=True), 1e-30)
    code = jnp.ceil(jnp.log2(most) * LOG_UNIT) + 4.0
    q = jnp.round(part * (TOP * jnp.exp2(-code / LOG_UNIT))).astype(i32)
    word = jnp.bitwise_or(jnp.left_shift(q[:, LANES:], 16), jnp.bitwise_and(q[:, :LANES], 65535))
    return word, code.astype(i32)


def decode(word, unit):
    first = jnp.right_shift(jnp.left_shift(word, 16), 16).astype(f32) * unit
    return first, jnp.right_shift(word, 16).astype(f32) * unit


def to_row(column, eye):
    return jnp.sum(jnp.where(eye, column, 0), axis=0, keepdims=True)


def to_unit(row, eye):
    return jnp.exp2(jnp.sum(jnp.where(eye, row, 0), axis=1, keepdims=True).astype(f32) / LOG_UNIT) / TOP


def pack_kernel(basis_ref, values_ref, out_ref):
    eye = diagonal()
    blocks = values_ref.shape[1] // LANES
    count = out_ref.shape[0]
    for n in range(count // 4):
        codes = [[] for _ in range(4)]
        for g in range(4):
            word, code = encode(basis_ref[n * LANES:(n + 1) * LANES, g * GROUP:(g + 1) * GROUP])
            for d in range(4):
                out_ref[n * 4 + d, g * 32:(g + 1) * 32, :] = word[d * 32:(d + 1) * 32]
                codes[d].append(code[d * 32:(d + 1) * 32])
        for d in range(4):
            row = to_row(jnp.concatenate(codes[d], axis=0), eye)
            block = (n * 4 + d) % blocks
            coded = (values_ref[:, block * LANES:(block + 1) * LANES] * VALUE_UNIT).astype(i32)
            out_ref[n * 4 + d, LANES:ROWS, :] = jnp.concatenate([row, coded, jnp.zeros((6, LANES), i32)], axis=0)


def pack_basis(basis, values):
    rows = basis.shape[0]
    size = min(rows, 512)
    return pl.pallas_call(
        pack_kernel,
        grid=(rows // size,),
        in_specs=[pl.BlockSpec((size, BLK), lambda i: (i, 0)), pl.BlockSpec(values.shape, lambda i: (0, 0))],
        out_specs=pl.BlockSpec((size // 32, ROWS, LANES), lambda i: (i, 0, 0)),
        out_shape=jax.ShapeDtypeStruct((rows // 32, ROWS, LANES), i32),
        compiler_params=params("arbitrary"),
        cost_estimate=pl.CostEstimate(flops=rows * 10**4, bytes_accessed=rows * 6000, transcendentals=0),
    )(basis, values)


def decode_chunks(get, base, count, high_ref, low_ref, eye):
    for d in range(count):
        unit = to_unit(get(d, LANES, 1), eye)
        for g in range(4):
            pair = decode(get(d, g * 32, 32), unit[g * 32:(g + 1) * 32])
            for k in range(2):
                high, low = halves(pair[k])
                where = (pl.ds(base + d * 32, 32), slice(g * GROUP + k * LANES, g * GROUP + (k + 1) * LANES))
                high_ref[where] = high
                low_ref[where] = low


def unpack_kernel(me_ref, own_ref, other_ref, high_ref, low_ref, side_ref):
    core = lax.rem(me_ref[3], 2)
    eye = diagonal()
    for z in range(4):
        def get(d, start, size):
            rows = slice(start, start + size)
            return jnp.where(core == d // 2, own_ref[z, 0, d % 2, rows, :], other_ref[z, 0, d % 2, rows, :])
        decode_chunks(get, z * LANES, 4, high_ref, low_ref, eye)
        side_ref[z] = get(0, LANES, 8)


def unpack_basis(me, own, other):
    rows = lambda i, m: (i, 0)
    half = pl.BlockSpec((4, 1, 2, ROWS, LANES), lambda i, m: (0, lax.rem(i + m[1], 2), 0, 0, 0))
    return pl.pallas_call(
        unpack_kernel,
        grid_spec=pltpu.PrefetchScalarGridSpec(
            num_scalar_prefetch=1,
            grid=(2,),
            in_specs=[half, half],
            out_specs=[pl.BlockSpec((512, BLK), rows)] * 2 + [pl.BlockSpec((4, 8, LANES), lambda i, m: (i, 0, 0))],
        ),
        out_shape=[jax.ShapeDtypeStruct((BLK, BLK), bf16)] * 2 + [jax.ShapeDtypeStruct((8, 8, LANES), i32)],
        compiler_params=params("arbitrary"),
        cost_estimate=pl.CostEstimate(flops=10**7, bytes_accessed=6 * 10**6, transcendentals=0),
    )(me, own, other)


def partial_kernel(me_ref, x0_ref, x1_ref, x2_ref, x3_ref, grads_ref, *refs):
    own_ref, word_refs, tokens, total = refs[0], refs[1:4], refs[4], refs[5]
    for j, x_ref in enumerate((x0_ref, x1_ref, x2_ref, x3_ref)):
        place = jnp.bitwise_xor(me_ref[3], j)
        for r in range(8):
            tokens[pl.ds(pl.multiple_of(r * LANES + place * 32, 32), 32), :] = x_ref[r]
    for r in range(4):
        grads = jnp.concatenate([grads_ref[r, me_ref[1]], grads_ref[r, 1 - me_ref[1]]], axis=0)
        part = mul(tokens[r * GROUP:(r + 1) * GROUP, :], grads, 0, 0)
        total[...] = part if r == 0 else total[...] + part
    eye = diagonal()
    for k in range(4):
        start = pl.multiple_of(lax.rem(me_ref[2] + k, 4) * LANES, LANES)
        if k == 0:
            own_ref[...] = total[pl.ds(start, LANES), :]
            continue
        rows = []
        for g in range(4):
            word, code = encode(total[pl.ds(start, LANES), g * GROUP:(g + 1) * GROUP])
            word_refs[k - 1][g * LANES:(g + 1) * LANES, :] = word
            rows.append(to_row(code, eye))
        word_refs[k - 1][4 * LANES:, :] = jnp.concatenate(rows + [jnp.zeros((4, LANES), i32)], axis=0)


def partial_rows(me, tokens, grads):
    vmem = pl.BlockSpec(memory_space=pltpu.VMEM)
    return pl.pallas_call(
        partial_kernel,
        in_specs=[pl.BlockSpec(memory_space=pltpu.SMEM)] + [vmem] * 5,
        out_specs=[vmem] * 4,
        out_shape=[jax.ShapeDtypeStruct((LANES, BLK), f32)] + [jax.ShapeDtypeStruct((520, LANES), i32)] * 3,
        scratch_shapes=[pltpu.VMEM((BLK, 512), bf16), pltpu.VMEM((512, BLK), f32)],
        compiler_params=params(),
        cost_estimate=pl.CostEstimate(flops=10**9, bytes_accessed=5 * 10**6, transcendentals=0),
    )(me, *tokens, grads)


def front_kernel(got_ref, own_ref, w1_ref, w2_ref, w3_ref, v_ref, high_ref, low_ref, grad):
    step = pl.program_id(0)
    eye = diagonal()
    decode_chunks(lambda d, start, size: got_ref[d, start:start + size, :], 0, 16, high_ref, low_ref, eye)

    @pl.when(step == 0)
    def _():
        for g in range(4):
            sums = [own_ref[:, g * GROUP:g * GROUP + LANES], own_ref[:, g * GROUP + LANES:(g + 1) * GROUP]]
            for ref in (w1_ref, w2_ref, w3_ref):
                unit = to_unit(ref[4 * LANES + g:4 * LANES + g + 1, :], eye)
                pair = decode(ref[g * LANES:(g + 1) * LANES, :], unit)
                sums = [sums[0] + pair[0], sums[1] + pair[1]]
            grad[g // 2, :, g % 2 * GROUP:(g % 2 + 1) * GROUP] = jnp.concatenate(sums, axis=1)

    grad_high, grad_low = halves(grad[step])
    both = mul(jnp.concatenate([grad_high, grad_low], axis=0), high_ref[...])
    v = both[:LANES] + both[LANES:] + mul(grad_high, low_ref[...])
    for c in range(8):
        part = v[:, c * LANES:(c + 1) * LANES]
        v_ref[c] = jnp.where(step == 0, part, v_ref[c] + part)


def front(got, own, words):
    whole = lambda i: (0, 0)
    return pl.pallas_call(
        front_kernel,
        grid=(2,),
        in_specs=[pl.BlockSpec((16, ROWS, LANES), lambda i: (i, 0, 0)), pl.BlockSpec((LANES, BLK), whole)]
        + [pl.BlockSpec((520, LANES), whole)] * 3,
        out_specs=[pl.BlockSpec((8, LANES, LANES), lambda i: (0, 0, 0))]
        + [pl.BlockSpec((512, BLK), lambda i: (i, 0))] * 2,
        out_shape=[jax.ShapeDtypeStruct((8, LANES, LANES), f32)] + [jax.ShapeDtypeStruct((BLK, BLK), bf16)] * 2,
        scratch_shapes=[pltpu.VMEM((2, LANES, 512), f32)],
        compiler_params=params("arbitrary"),
        cost_estimate=pl.CostEstimate(flops=8 * 10**8, bytes_accessed=8 * 10**6, transcendentals=0),
    )(got, own, *words)


def middle_kernel(v_ref, high_ref, low_ref, in_side_ref, out_side_ref, u_ref):
    v = v_ref[...].reshape(BLK, LANES)
    v_high, v_low = halves(v)
    qh, ql = high_ref[...], low_ref[...]
    both = mul(jnp.concatenate([v_high, v_low], axis=1), qh, 0, 0)
    rt = both[:LANES] + both[LANES:] + mul(v_high, ql, 0, 0)
    la = jnp.concatenate([in_side_ref[c, 1:2, :] for c in range(8)], axis=1).astype(f32) / VALUE_UNIT
    lb = jnp.sum(jnp.where(diagonal(), out_side_ref[0, 1:2, :], 0), axis=1, keepdims=True).astype(f32) / VALUE_UNIT
    st = rt / (lb * la + DAMPING)
    s_high, s_low = halves(st)
    both = mul(jnp.concatenate([s_high, s_low], axis=0), qh, 1, 1)
    ut = both[:LANES] + both[LANES:] + mul(s_high, ql, 1, 1)
    for c in range(8):
        u_ref[c] = ut[:, c * LANES:(c + 1) * LANES]


def middle(v, high, low, in_side, piece):
    whole = lambda i: (0, 0)
    return pl.pallas_call(
        middle_kernel,
        grid=(1,),
        in_specs=[
            pl.BlockSpec((8, LANES, LANES), lambda i: (0, 0, 0)),
            pl.BlockSpec((BLK, BLK), whole),
            pl.BlockSpec((BLK, BLK), whole),
            pl.BlockSpec((8, 8, LANES), lambda i: (0, 0, 0)),
            pl.BlockSpec((1, 8, LANES), lambda i: (0, 16, 0)),
        ],
        out_specs=pl.BlockSpec((8, LANES, LANES), lambda i: (0, 0, 0)),
        out_shape=jax.ShapeDtypeStruct((8, LANES, LANES), f32),
        compiler_params=params("arbitrary"),
        cost_estimate=pl.CostEstimate(flops=16 * 10**8, bytes_accessed=6 * 10**6, transcendentals=0),
    )(v, high, low, in_side, piece)


def back_kernel(u_ref, high_ref, low_ref, out_ref):
    u_high, u_low = halves(u_ref[...].reshape(BLK, LANES).T)
    both = mul(jnp.concatenate([u_high, u_low], axis=0), high_ref[...], 1, 1)
    out_ref[...] = both[:LANES] + both[LANES:] + mul(u_high, low_ref[...], 1, 1)


def back(u, high, low):
    return pl.pallas_call(
        back_kernel,
        grid=(2,),
        in_specs=[
            pl.BlockSpec((8, LANES, LANES), lambda i: (0, 0, 0)),
            pl.BlockSpec((512, BLK), lambda i: (i, 0)),
            pl.BlockSpec((512, BLK), lambda i: (i, 0)),
        ],
        out_specs=pl.BlockSpec((LANES, 512), lambda i: (0, i)),
        out_shape=jax.ShapeDtypeStruct((LANES, BLK), f32),
        compiler_params=params("arbitrary"),
        cost_estimate=pl.CostEstimate(flops=8 * 10**8, bytes_accessed=5 * 10**6, transcendentals=0),
    )(u, high, low)


def body(
    layer_inputs,
    output_grads,
    feature_order,
    block_slot,
    layer_owner,
    in_basis,
    in_values,
    out_basis,
    out_values,
):
    me = jnp.stack([lax.axis_index("y"), lax.axis_index("h"), lax.axis_index("z"), lax.axis_index(("l", "c"))])
    me = jnp.concatenate([me.astype(i32), block_slot])

    in_part = pack_basis(in_basis, in_values.reshape(1, LANES))
    in_part = lax.dynamic_slice_in_dim(in_part, lax.axis_index("c") * 2, 2, 0)
    in_pair = jnp.stack([in_part, lax.ppermute(in_part, ("h", "l"), [(i, 3 - i) for i in range(4)])])

    chunks = gather_columns(me, feature_order, layer_inputs.reshape(32, DIN))
    grads = output_grads.reshape(LANES, BLK)
    grads = jnp.stack([grads, flip(grads, "h")])
    chunks, grads, out_part = lax.optimization_barrier((chunks, grads, out_basis[0]))
    moved = lax.all_to_all(chunks, ("y", "h"), 0, 0, tiled=True)
    tokens = [moved] + [lax.ppermute(moved, ("l", "c"), [(m, m ^ j) for m in range(4)]) for j in range(1, 4)]

    packed = pack_basis(out_part, out_values)
    packed, in_pair, *tokens = lax.optimization_barrier((packed, in_pair, *tokens))
    spread = lax.all_to_all(packed, ALL_DP, 0, 0, tiled=True)
    piece = lax.dynamic_index_in_dim(spread, layer_owner[0], 0, keepdims=True)

    grads = lax.all_gather(grads, "y")
    _, in_pair = lax.optimization_barrier((grads, in_pair))
    in_all = lax.all_gather(in_pair, "z")
    own, *words = partial_rows(me, tokens, grads)
    words = [along(w, "z", k + 1) for k, w in enumerate(words)]
    piece, words = lax.optimization_barrier((piece, words))

    got = lax.all_to_all(jnp.broadcast_to(piece, spread.shape), ALL_DP, 0, 0, tiled=True)
    v, out_high, out_low = front(got, own, words)

    v = lax.all_to_all(v, PAIR, 0, 0, tiled=True)
    in_high, in_low, in_side = unpack_basis(me, in_all, jnp.stack([flip(in_all[z], "c") for z in range(4)]))
    u = middle(v, in_high, in_low, in_side, piece)
    u = lax.all_to_all(u, PAIR, 0, 0, tiled=True)
    return back(u, out_high, out_low)


def along(block, axis, shift):
    if shift == 0:
        return block
    return lax.ppermute(block, axis, [(i, (i + shift) % 4) for i in range(4)])


def flip(block, axis):
    return lax.ppermute(block, axis, [(0, 1), (1, 0)])


def solution(mesh):
    fine = Mesh(mesh.devices.reshape(4, 2, 4, 2, 2), ("y", "h", "z", "l", "c"))
    dp, mp = ("y", "h", "z"), ("l", "c")
    in_specs = (
        P(dp + mp, None, None),
        P(dp, None, mp),
        P(),
        P(),
        P(),
        P(dp, None),
        P(dp),
        P(dp, mp, None),
        P(dp, mp),
    )
    return jax.shard_map(body, mesh=fine, in_specs=in_specs, out_specs=P(dp, mp), check_vma=False)
```

```python
import jax
import jax.numpy as jnp
from jax import lax
from jax.experimental import pallas as pl
from jax.experimental.pallas import tpu as pltpu
from jax.sharding import Mesh, PartitionSpec as P

DIN = 4096
BLK = 1024
LANES = 128
GROUP = 256
ROWS = 136
DAMPING = 0.1
TOP = 32767.0
LOG_UNIT = 65536.0
VALUE_UNIT = 134217728.0
PAIR = ("h", "z")
ALL_DP = ("y", "h", "z")
VMEM = 48 * 1024 * 1024
f32, bf16, i32 = jnp.float32, jnp.bfloat16, jnp.int32


def params(*semantics):
    return pltpu.CompilerParams(vmem_limit_bytes=VMEM, dimension_semantics=semantics or None)


def mul(a, b, ca=1, cb=0):
    return lax.dot_general(a, b, (((ca,), (cb,)), ((), ())), preferred_element_type=f32)


def halves(a):
    high = a.astype(bf16)
    return high, (a - high.astype(f32)).astype(bf16)


def gather_kernel(me_ref, order_ref, x_ref, out_ref):
    x = [x_ref[:, k * LANES:(k + 1) * LANES].astype(f32) for k in range(DIN // LANES)]
    for n in range(4):
        pair = sum(jnp.where(me_ref[4 + j] == pl.program_id(0) * 2 + n // 2, j, 0) for j in range(4))
        start = pair * BLK + n % 2 * 512
        for b in range(4):
            idx = order_ref[:, pl.ds(pl.multiple_of(start + b * LANES, LANES), LANES)]
            lane = jnp.broadcast_to(jnp.bitwise_and(idx, LANES - 1), (32, LANES))
            src = jnp.broadcast_to(jnp.right_shift(idx, 7), (32, LANES))
            acc = jnp.zeros((32, LANES), f32)
            for k in range(DIN // LANES):
                acc = jnp.where(src == k, jnp.take_along_axis(x[k], lane, axis=1), acc)
            out_ref[n, :, b * LANES:(b + 1) * LANES] = acc.astype(bf16)


def gather_columns(me, order, x):
    return pl.pallas_call(
        gather_kernel,
        grid=(2,),
        in_specs=[
            pl.BlockSpec(memory_space=pltpu.SMEM),
            pl.BlockSpec((1, DIN), lambda i: (0, 0)),
            pl.BlockSpec((32, DIN), lambda i: (0, 0)),
        ],
        out_specs=pl.BlockSpec((4, 32, 512), lambda i: (i, 0, 0)),
        out_shape=jax.ShapeDtypeStruct((8, 32, 512), bf16),
        compiler_params=params("arbitrary"),
        cost_estimate=pl.CostEstimate(flops=10**6, bytes_accessed=10**6, transcendentals=0),
    )(me, order, x)


def diagonal():
    return lax.broadcasted_iota(i32, (LANES, LANES), 0) == lax.broadcasted_iota(i32, (LANES, LANES), 1)


def encode(part):
    most = jnp.maximum(jnp.max(jnp.abs(part), axis=1, keepdims=True), 1e-30)
    code = jnp.ceil(jnp.log2(most) * LOG_UNIT) + 4.0
    q = jnp.round(part * (TOP * jnp.exp2(-code / LOG_UNIT))).astype(i32)
    word = jnp.bitwise_or(jnp.left_shift(q[:, LANES:], 16), jnp.bitwise_and(q[:, :LANES], 65535))
    return word, code.astype(i32)


def decode(word, unit):
    first = jnp.right_shift(jnp.left_shift(word, 16), 16).astype(f32) * unit
    return first, jnp.right_shift(word, 16).astype(f32) * unit


def to_row(column, eye):
    return jnp.sum(jnp.where(eye, column, 0), axis=0, keepdims=True)


def to_unit(row, eye):
    return jnp.exp2(jnp.sum(jnp.where(eye, row, 0), axis=1, keepdims=True).astype(f32) / LOG_UNIT) / TOP


def pack_kernel(basis_ref, values_ref, out_ref):
    eye = diagonal()
    blocks = values_ref.shape[1] // LANES
    count = out_ref.shape[0]
    for n in range(count // 4):
        codes = [[] for _ in range(4)]
        for g in range(4):
            word, code = encode(basis_ref[n * LANES:(n + 1) * LANES, g * GROUP:(g + 1) * GROUP])
            for d in range(4):
                out_ref[n * 4 + d, g * 32:(g + 1) * 32, :] = word[d * 32:(d + 1) * 32]
                codes[d].append(code[d * 32:(d + 1) * 32])
        for d in range(4):
            row = to_row(jnp.concatenate(codes[d], axis=0), eye)
            block = (n * 4 + d) % blocks
            coded = (values_ref[:, block * LANES:(block + 1) * LANES] * VALUE_UNIT).astype(i32)
            out_ref[n * 4 + d, LANES:ROWS, :] = jnp.concatenate([row, coded, jnp.zeros((6, LANES), i32)], axis=0)


def pack_basis(basis, values):
    rows = basis.shape[0]
    size = min(rows, 512)
    return pl.pallas_call(
        pack_kernel,
        grid=(rows // size,),
        in_specs=[pl.BlockSpec((size, BLK), lambda i: (i, 0)), pl.BlockSpec(values.shape, lambda i: (0, 0))],
        out_specs=pl.BlockSpec((size // 32, ROWS, LANES), lambda i: (i, 0, 0)),
        out_shape=jax.ShapeDtypeStruct((rows // 32, ROWS, LANES), i32),
        compiler_params=params("arbitrary"),
        cost_estimate=pl.CostEstimate(flops=rows * 10**4, bytes_accessed=rows * 6000, transcendentals=0),
    )(basis, values)


def decode_chunks(get, base, count, high_ref, low_ref, eye):
    for d in range(count):
        unit = to_unit(get(d, LANES, 1), eye)
        for g in range(4):
            pair = decode(get(d, g * 32, 32), unit[g * 32:(g + 1) * 32])
            for k in range(2):
                high, low = halves(pair[k])
                where = (pl.ds(base + d * 32, 32), slice(g * GROUP + k * LANES, g * GROUP + (k + 1) * LANES))
                high_ref[where] = high
                low_ref[where] = low


def unpack_kernel(me_ref, own_ref, other_ref, high_ref, low_ref, side_ref):
    core = lax.rem(me_ref[3], 2)
    eye = diagonal()
    for z in range(4):
        def get(d, start, size):
            rows = slice(start, start + size)
            return jnp.where(core == d // 2, own_ref[z, 0, d % 2, rows, :], other_ref[z, 0, d % 2, rows, :])
        decode_chunks(get, z * LANES, 4, high_ref, low_ref, eye)
        side_ref[z] = get(0, LANES, 8)


def unpack_basis(me, own, other):
    rows = lambda i, m: (i, 0)
    half = pl.BlockSpec((4, 1, 2, ROWS, LANES), lambda i, m: (0, lax.rem(i + m[1], 2), 0, 0, 0))
    return pl.pallas_call(
        unpack_kernel,
        grid_spec=pltpu.PrefetchScalarGridSpec(
            num_scalar_prefetch=1,
            grid=(2,),
            in_specs=[half, half],
            out_specs=[pl.BlockSpec((512, BLK), rows)] * 2 + [pl.BlockSpec((4, 8, LANES), lambda i, m: (i, 0, 0))],
        ),
        out_shape=[jax.ShapeDtypeStruct((BLK, BLK), bf16)] * 2 + [jax.ShapeDtypeStruct((8, 8, LANES), i32)],
        compiler_params=params("arbitrary"),
        cost_estimate=pl.CostEstimate(flops=10**7, bytes_accessed=6 * 10**6, transcendentals=0),
    )(me, own, other)


def partial_kernel(me_ref, x0_ref, x1_ref, x2_ref, x3_ref, grads_ref, *refs):
    own_ref, word_refs, tokens, total = refs[0], refs[1:4], refs[4], refs[5]
    for j, x_ref in enumerate((x0_ref, x1_ref, x2_ref, x3_ref)):
        place = jnp.bitwise_xor(me_ref[3], j)
        for r in range(8):
            tokens[pl.ds(pl.multiple_of(r * LANES + place * 32, 32), 32), :] = x_ref[r]
    for r in range(4):
        grads = jnp.concatenate([grads_ref[r, me_ref[1]], grads_ref[r, 1 - me_ref[1]]], axis=0)
        part = mul(tokens[r * GROUP:(r + 1) * GROUP, :], grads, 0, 0)
        total[...] = part if r == 0 else total[...] + part
    eye = diagonal()
    for k in range(4):
        start = pl.multiple_of(lax.rem(me_ref[2] + k, 4) * LANES, LANES)
        if k == 0:
            own_ref[...] = total[pl.ds(start, LANES), :]
            continue
        rows = []
        for g in range(4):
            word, code = encode(total[pl.ds(start, LANES), g * GROUP:(g + 1) * GROUP])
            word_refs[k - 1][g * LANES:(g + 1) * LANES, :] = word
            rows.append(to_row(code, eye))
        word_refs[k - 1][4 * LANES:, :] = jnp.concatenate(rows + [jnp.zeros((4, LANES), i32)], axis=0)


def partial_rows(me, tokens, grads):
    vmem = pl.BlockSpec(memory_space=pltpu.VMEM)
    return pl.pallas_call(
        partial_kernel,
        in_specs=[pl.BlockSpec(memory_space=pltpu.SMEM)] + [vmem] * 5,
        out_specs=[vmem] * 4,
        out_shape=[jax.ShapeDtypeStruct((LANES, BLK), f32)] + [jax.ShapeDtypeStruct((520, LANES), i32)] * 3,
        scratch_shapes=[pltpu.VMEM((BLK, 512), bf16), pltpu.VMEM((512, BLK), f32)],
        compiler_params=params(),
        cost_estimate=pl.CostEstimate(flops=10**9, bytes_accessed=5 * 10**6, transcendentals=0),
    )(me, *tokens, grads)


def front_kernel(got_ref, own_ref, w1_ref, w2_ref, w3_ref, v_ref, high_ref, low_ref, grad):
    step = pl.program_id(0)
    eye = diagonal()
    decode_chunks(lambda d, start, size: got_ref[d, start:start + size, :], 0, 16, high_ref, low_ref, eye)

    @pl.when(step == 0)
    def _():
        for g in range(4):
            sums = [own_ref[:, g * GROUP:g * GROUP + LANES], own_ref[:, g * GROUP + LANES:(g + 1) * GROUP]]
            for ref in (w1_ref, w2_ref, w3_ref):
                unit = to_unit(ref[4 * LANES + g:4 * LANES + g + 1, :], eye)
                pair = decode(ref[g * LANES:(g + 1) * LANES, :], unit)
                sums = [sums[0] + pair[0], sums[1] + pair[1]]
            grad[g // 2, :, g % 2 * GROUP:(g % 2 + 1) * GROUP] = jnp.concatenate(sums, axis=1)

    grad_high, grad_low = halves(grad[step])
    both = mul(jnp.concatenate([grad_high, grad_low], axis=0), high_ref[...])
    v = both[:LANES] + both[LANES:] + mul(grad_high, low_ref[...])
    for c in range(8):
        part = v[:, c * LANES:(c + 1) * LANES]
        v_ref[c] = jnp.where(step == 0, part, v_ref[c] + part)


def front(got, own, words):
    whole = lambda i: (0, 0)
    return pl.pallas_call(
        front_kernel,
        grid=(2,),
        in_specs=[pl.BlockSpec((16, ROWS, LANES), lambda i: (i, 0, 0)), pl.BlockSpec((LANES, BLK), whole)]
        + [pl.BlockSpec((520, LANES), whole)] * 3,
        out_specs=[pl.BlockSpec((8, LANES, LANES), lambda i: (0, 0, 0))]
        + [pl.BlockSpec((512, BLK), lambda i: (i, 0))] * 2,
        out_shape=[jax.ShapeDtypeStruct((8, LANES, LANES), f32)] + [jax.ShapeDtypeStruct((BLK, BLK), bf16)] * 2,
        scratch_shapes=[pltpu.VMEM((2, LANES, 512), f32)],
        compiler_params=params("arbitrary"),
        cost_estimate=pl.CostEstimate(flops=8 * 10**8, bytes_accessed=8 * 10**6, transcendentals=0),
    )(got, own, *words)


def middle_kernel(v_ref, high_ref, low_ref, in_side_ref, out_side_ref, u_ref):
    v = v_ref[...].reshape(BLK, LANES)
    v_high, v_low = halves(v)
    qh, ql = high_ref[...], low_ref[...]
    both = mul(jnp.concatenate([v_high, v_low], axis=1), qh, 0, 0)
    rt = both[:LANES] + both[LANES:] + mul(v_high, ql, 0, 0)
    la = jnp.concatenate([in_side_ref[c, 1:2, :] for c in range(8)], axis=1).astype(f32) / VALUE_UNIT
    lb = jnp.sum(jnp.where(diagonal(), out_side_ref[0, 1:2, :], 0), axis=1, keepdims=True).astype(f32) / VALUE_UNIT
    st = rt / (lb * la + DAMPING)
    s_high, s_low = halves(st)
    both = mul(jnp.concatenate([s_high, s_low], axis=0), qh, 1, 1)
    ut = both[:LANES] + both[LANES:] + mul(s_high, ql, 1, 1)
    for c in range(8):
        u_ref[c] = ut[:, c * LANES:(c + 1) * LANES]


def middle(v, high, low, in_side, piece):
    whole = lambda i: (0, 0)
    return pl.pallas_call(
        middle_kernel,
        grid=(1,),
        in_specs=[
            pl.BlockSpec((8, LANES, LANES), lambda i: (0, 0, 0)),
            pl.BlockSpec((BLK, BLK), whole),
            pl.BlockSpec((BLK, BLK), whole),
            pl.BlockSpec((8, 8, LANES), lambda i: (0, 0, 0)),
            pl.BlockSpec((1, 8, LANES), lambda i: (0, 16, 0)),
        ],
        out_specs=pl.BlockSpec((8, LANES, LANES), lambda i: (0, 0, 0)),
        out_shape=jax.ShapeDtypeStruct((8, LANES, LANES), f32),
        compiler_params=params("arbitrary"),
        cost_estimate=pl.CostEstimate(flops=16 * 10**8, bytes_accessed=6 * 10**6, transcendentals=0),
    )(v, high, low, in_side, piece)


def back_kernel(u_ref, high_ref, low_ref, out_ref):
    u_high, u_low = halves(u_ref[...].reshape(BLK, LANES).T)
    both = mul(jnp.concatenate([u_high, u_low], axis=0), high_ref[...], 1, 1)
    out_ref[...] = both[:LANES] + both[LANES:] + mul(u_high, low_ref[...], 1, 1)


def back(u, high, low):
    return pl.pallas_call(
        back_kernel,
        grid=(2,),
        in_specs=[
            pl.BlockSpec((8, LANES, LANES), lambda i: (0, 0, 0)),
            pl.BlockSpec((512, BLK), lambda i: (i, 0)),
            pl.BlockSpec((512, BLK), lambda i: (i, 0)),
        ],
        out_specs=pl.BlockSpec((LANES, 512), lambda i: (0, i)),
        out_shape=jax.ShapeDtypeStruct((LANES, BLK), f32),
        compiler_params=params("arbitrary"),
        cost_estimate=pl.CostEstimate(flops=8 * 10**8, bytes_accessed=5 * 10**6, transcendentals=0),
    )(u, high, low)


def body(
    layer_inputs,
    output_grads,
    feature_order,
    block_slot,
    layer_owner,
    in_basis,
    in_values,
    out_basis,
    out_values,
):
    me = jnp.stack([lax.axis_index("y"), lax.axis_index("h"), lax.axis_index("z"), lax.axis_index(("l", "c"))])
    me = jnp.concatenate([me.astype(i32), block_slot])

    in_part = pack_basis(in_basis, in_values.reshape(1, LANES))
    in_part = lax.dynamic_slice_in_dim(in_part, lax.axis_index("c") * 2, 2, 0)
    in_pair = jnp.stack([in_part, lax.ppermute(in_part, ("h", "l"), [(i, 3 - i) for i in range(4)])])

    chunks = gather_columns(me, feature_order, layer_inputs.reshape(32, DIN))
    grads = output_grads.reshape(LANES, BLK)
    grads = jnp.stack([grads, flip(grads, "h")])
    chunks, grads, out_part = lax.optimization_barrier((chunks, grads, out_basis[0]))
    moved = lax.all_to_all(chunks, ("y", "h"), 0, 0, tiled=True)
    tokens = [moved] + [lax.ppermute(moved, ("l", "c"), [(m, m ^ j) for m in range(4)]) for j in range(1, 4)]

    packed = pack_basis(out_part, out_values)
    packed, in_pair, *tokens = lax.optimization_barrier((packed, in_pair, *tokens))
    spread = lax.all_to_all(packed, ALL_DP, 0, 0, tiled=True)
    piece = lax.dynamic_index_in_dim(spread, layer_owner[0], 0, keepdims=True)

    grads = lax.all_gather(grads, "y")
    _, in_pair = lax.optimization_barrier((grads, in_pair))
    in_all = lax.all_gather(in_pair, "z")
    own, *words = partial_rows(me, tokens, grads)
    words = [along(w, "z", k + 1) for k, w in enumerate(words)]
    piece, words = lax.optimization_barrier((piece, words))

    got = lax.all_to_all(jnp.broadcast_to(piece, spread.shape), ALL_DP, 0, 0, tiled=True)
    in_high, in_low, in_side = unpack_basis(me, in_all, jnp.stack([flip(in_all[z], "c") for z in range(4)]))
    own, in_high, in_low = lax.optimization_barrier((own, in_high, in_low))
    v, out_high, out_low = front(got, own, words)

    v = lax.all_to_all(v, PAIR, 0, 0, tiled=True)
    u = middle(v, in_high, in_low, in_side, piece)
    u = lax.all_to_all(u, PAIR, 0, 0, tiled=True)
    return back(u, out_high, out_low)


def along(block, axis, shift):
    if shift == 0:
        return block
    return lax.ppermute(block, axis, [(i, (i + shift) % 4) for i in range(4)])


def flip(block, axis):
    return lax.ppermute(block, axis, [(0, 1), (1, 0)])


def solution(mesh):
    fine = Mesh(mesh.devices.reshape(4, 2, 4, 2, 2), ("y", "h", "z", "l", "c"))
    dp, mp = ("y", "h", "z"), ("l", "c")
    in_specs = (
        P(dp + mp, None, None),
        P(dp, None, mp),
        P(),
        P(),
        P(),
        P(dp, None),
        P(dp),
        P(dp, mp, None),
        P(dp, mp),
    )
    return jax.shard_map(body, mesh=fine, in_specs=in_specs, out_specs=P(dp, mp), check_vma=False)
```

```python
import jax
import jax.numpy as jnp
from jax import lax
from jax.experimental import pallas as pl
from jax.experimental.pallas import tpu as pltpu
from jax.sharding import Mesh, PartitionSpec as P

DIN = 4096
BLK = 1024
LANES = 128
GROUP = 256
ROWS = 136
DAMPING = 0.1
TOP = 32767.0
LOG_UNIT = 65536.0
VALUE_UNIT = 134217728.0
PAIR = ("h", "z")
ALL_DP = ("y", "h", "z")
VMEM = 48 * 1024 * 1024
f32, bf16, i32 = jnp.float32, jnp.bfloat16, jnp.int32


def params(*semantics):
    return pltpu.CompilerParams(vmem_limit_bytes=VMEM, dimension_semantics=semantics or None)


def mul(a, b, ca=1, cb=0):
    return lax.dot_general(a, b, (((ca,), (cb,)), ((), ())), preferred_element_type=f32)


def halves(a):
    high = a.astype(bf16)
    return high, (a - high.astype(f32)).astype(bf16)


def gather_kernel(me_ref, order_ref, x_ref, out_ref):
    x = [x_ref[:, k * LANES:(k + 1) * LANES].astype(f32) for k in range(DIN // LANES)]
    for n in range(4):
        pair = sum(jnp.where(me_ref[4 + j] == pl.program_id(0) * 2 + n // 2, j, 0) for j in range(4))
        start = pair * BLK + n % 2 * 512
        for b in range(4):
            idx = order_ref[:, pl.ds(pl.multiple_of(start + b * LANES, LANES), LANES)]
            lane = jnp.broadcast_to(jnp.bitwise_and(idx, LANES - 1), (32, LANES))
            src = jnp.broadcast_to(jnp.right_shift(idx, 7), (32, LANES))
            acc = jnp.zeros((32, LANES), f32)
            for k in range(DIN // LANES):
                acc = jnp.where(src == k, jnp.take_along_axis(x[k], lane, axis=1), acc)
            out_ref[n, :, b * LANES:(b + 1) * LANES] = acc.astype(bf16)


def gather_columns(me, order, x):
    return pl.pallas_call(
        gather_kernel,
        grid=(2,),
        in_specs=[
            pl.BlockSpec(memory_space=pltpu.SMEM),
            pl.BlockSpec((1, DIN), lambda i: (0, 0)),
            pl.BlockSpec((32, DIN), lambda i: (0, 0)),
        ],
        out_specs=pl.BlockSpec((4, 32, 512), lambda i: (i, 0, 0)),
        out_shape=jax.ShapeDtypeStruct((8, 32, 512), bf16),
        compiler_params=params("arbitrary"),
        cost_estimate=pl.CostEstimate(flops=10**6, bytes_accessed=10**6, transcendentals=0),
    )(me, order, x)


def diagonal():
    return lax.broadcasted_iota(i32, (LANES, LANES), 0) == lax.broadcasted_iota(i32, (LANES, LANES), 1)


def encode(part):
    most = jnp.maximum(jnp.max(jnp.abs(part), axis=1, keepdims=True), 1e-30)
    code = jnp.ceil(jnp.log2(most) * LOG_UNIT) + 4.0
    q = jnp.round(part * (TOP * jnp.exp2(-code / LOG_UNIT))).astype(i32)
    word = jnp.bitwise_or(jnp.left_shift(q[:, LANES:], 16), jnp.bitwise_and(q[:, :LANES], 65535))
    return word, code.astype(i32)


def decode(word, unit):
    first = jnp.right_shift(jnp.left_shift(word, 16), 16).astype(f32) * unit
    return first, jnp.right_shift(word, 16).astype(f32) * unit


def to_row(column, eye):
    return jnp.sum(jnp.where(eye, column, 0), axis=0, keepdims=True)


def to_unit(row, eye):
    return jnp.exp2(jnp.sum(jnp.where(eye, row, 0), axis=1, keepdims=True).astype(f32) / LOG_UNIT) / TOP


def pack_kernel(basis_ref, values_ref, out_ref):
    eye = diagonal()
    blocks = values_ref.shape[1] // LANES
    count = out_ref.shape[0]
    for n in range(count // 4):
        codes = [[] for _ in range(4)]
        for g in range(4):
            word, code = encode(basis_ref[n * LANES:(n + 1) * LANES, g * GROUP:(g + 1) * GROUP])
            for d in range(4):
                out_ref[n * 4 + d, g * 32:(g + 1) * 32, :] = word[d * 32:(d + 1) * 32]
                codes[d].append(code[d * 32:(d + 1) * 32])
        for d in range(4):
            row = to_row(jnp.concatenate(codes[d], axis=0), eye)
            block = (n * 4 + d) % blocks
            coded = (values_ref[:, block * LANES:(block + 1) * LANES] * VALUE_UNIT).astype(i32)
            out_ref[n * 4 + d, LANES:ROWS, :] = jnp.concatenate([row, coded, jnp.zeros((6, LANES), i32)], axis=0)


def pack_basis(basis, values):
    rows = basis.shape[0]
    size = min(rows, 512)
    return pl.pallas_call(
        pack_kernel,
        grid=(rows // size,),
        in_specs=[pl.BlockSpec((size, BLK), lambda i: (i, 0)), pl.BlockSpec(values.shape, lambda i: (0, 0))],
        out_specs=pl.BlockSpec((size // 32, ROWS, LANES), lambda i: (i, 0, 0)),
        out_shape=jax.ShapeDtypeStruct((rows // 32, ROWS, LANES), i32),
        compiler_params=params("arbitrary"),
        cost_estimate=pl.CostEstimate(flops=rows * 10**4, bytes_accessed=rows * 6000, transcendentals=0),
    )(basis, values)


def decode_chunks(get, base, count, high_ref, low_ref, eye):
    for d in range(count):
        unit = to_unit(get(d, LANES, 1), eye)
        for g in range(4):
            pair = decode(get(d, g * 32, 32), unit[g * 32:(g + 1) * 32])
            for k in range(2):
                high, low = halves(pair[k])
                where = (pl.ds(base + d * 32, 32), slice(g * GROUP + k * LANES, g * GROUP + (k + 1) * LANES))
                high_ref[where] = high
                low_ref[where] = low


def unpack_kernel(me_ref, own_ref, other_ref, high_ref, low_ref, side_ref):
    core = lax.rem(me_ref[3], 2)
    eye = diagonal()
    for z in range(4):
        def get(d, start, size):
            rows = slice(start, start + size)
            return jnp.where(core == d // 2, own_ref[z, 0, d % 2, rows, :], other_ref[z, 0, d % 2, rows, :])
        decode_chunks(get, z * LANES, 4, high_ref, low_ref, eye)
        side_ref[z] = get(0, LANES, 8)


def unpack_basis(me, own, other):
    rows = lambda i, m: (i, 0)
    half = pl.BlockSpec((4, 1, 2, ROWS, LANES), lambda i, m: (0, lax.rem(i + m[1], 2), 0, 0, 0))
    return pl.pallas_call(
        unpack_kernel,
        grid_spec=pltpu.PrefetchScalarGridSpec(
            num_scalar_prefetch=1,
            grid=(2,),
            in_specs=[half, half],
            out_specs=[pl.BlockSpec((512, BLK), rows)] * 2 + [pl.BlockSpec((4, 8, LANES), lambda i, m: (i, 0, 0))],
        ),
        out_shape=[jax.ShapeDtypeStruct((BLK, BLK), bf16)] * 2 + [jax.ShapeDtypeStruct((8, 8, LANES), i32)],
        compiler_params=params("arbitrary"),
        cost_estimate=pl.CostEstimate(flops=10**7, bytes_accessed=6 * 10**6, transcendentals=0),
    )(me, own, other)


def partial_kernel(me_ref, x0_ref, x1_ref, x2_ref, x3_ref, grads_ref, *refs):
    own_ref, word_refs, tokens, total = refs[0], refs[1:4], refs[4], refs[5]
    for j, x_ref in enumerate((x0_ref, x1_ref, x2_ref, x3_ref)):
        place = jnp.bitwise_xor(me_ref[3], j)
        for r in range(8):
            tokens[pl.ds(pl.multiple_of(r * LANES + place * 32, 32), 32), :] = x_ref[r]
    for r in range(4):
        grads = jnp.concatenate([grads_ref[r, me_ref[1]], grads_ref[r, 1 - me_ref[1]]], axis=0)
        part = mul(tokens[r * GROUP:(r + 1) * GROUP, :], grads, 0, 0)
        total[...] = part if r == 0 else total[...] + part
    eye = diagonal()
    for k in range(4):
        start = pl.multiple_of(lax.rem(me_ref[2] + k, 4) * LANES, LANES)
        if k == 0:
            own_ref[...] = total[pl.ds(start, LANES), :]
            continue
        rows = []
        for g in range(4):
            word, code = encode(total[pl.ds(start, LANES), g * GROUP:(g + 1) * GROUP])
            word_refs[k - 1][g * LANES:(g + 1) * LANES, :] = word
            rows.append(to_row(code, eye))
        word_refs[k - 1][4 * LANES:, :] = jnp.concatenate(rows + [jnp.zeros((4, LANES), i32)], axis=0)


def partial_rows(me, tokens, grads):
    vmem = pl.BlockSpec(memory_space=pltpu.VMEM)
    return pl.pallas_call(
        partial_kernel,
        in_specs=[pl.BlockSpec(memory_space=pltpu.SMEM)] + [vmem] * 5,
        out_specs=[vmem] * 4,
        out_shape=[jax.ShapeDtypeStruct((LANES, BLK), f32)] + [jax.ShapeDtypeStruct((520, LANES), i32)] * 3,
        scratch_shapes=[pltpu.VMEM((BLK, 512), bf16), pltpu.VMEM((512, BLK), f32)],
        compiler_params=params(),
        cost_estimate=pl.CostEstimate(flops=10**9, bytes_accessed=5 * 10**6, transcendentals=0),
    )(me, *tokens, grads)


def front_kernel(got_ref, own_ref, w1_ref, w2_ref, w3_ref, v_ref, high_ref, low_ref, grad):
    step = pl.program_id(0)
    eye = diagonal()
    decode_chunks(lambda d, start, size: got_ref[d, start:start + size, :], 0, 16, high_ref, low_ref, eye)

    @pl.when(step == 0)
    def _():
        for g in range(4):
            sums = [own_ref[:, g * GROUP:g * GROUP + LANES], own_ref[:, g * GROUP + LANES:(g + 1) * GROUP]]
            for ref in (w1_ref, w2_ref, w3_ref):
                unit = to_unit(ref[4 * LANES + g:4 * LANES + g + 1, :], eye)
                pair = decode(ref[g * LANES:(g + 1) * LANES, :], unit)
                sums = [sums[0] + pair[0], sums[1] + pair[1]]
            grad[g // 2, :, g % 2 * GROUP:(g % 2 + 1) * GROUP] = jnp.concatenate(sums, axis=1)

    grad_high, grad_low = halves(grad[step])
    both = mul(jnp.concatenate([grad_high, grad_low], axis=0), high_ref[...])
    v = both[:LANES] + both[LANES:] + mul(grad_high, low_ref[...])
    for c in range(8):
        part = v[:, c * LANES:(c + 1) * LANES]
        v_ref[c] = jnp.where(step == 0, part, v_ref[c] + part)


def front(got, own, words):
    whole = lambda i: (0, 0)
    return pl.pallas_call(
        front_kernel,
        grid=(2,),
        in_specs=[pl.BlockSpec((16, ROWS, LANES), lambda i: (i, 0, 0)), pl.BlockSpec((LANES, BLK), whole)]
        + [pl.BlockSpec((520, LANES), whole)] * 3,
        out_specs=[pl.BlockSpec((8, LANES, LANES), lambda i: (0, 0, 0))]
        + [pl.BlockSpec((512, BLK), lambda i: (i, 0))] * 2,
        out_shape=[jax.ShapeDtypeStruct((8, LANES, LANES), f32)] + [jax.ShapeDtypeStruct((BLK, BLK), bf16)] * 2,
        scratch_shapes=[pltpu.VMEM((2, LANES, 512), f32)],
        compiler_params=params("arbitrary"),
        cost_estimate=pl.CostEstimate(flops=8 * 10**8, bytes_accessed=8 * 10**6, transcendentals=0),
    )(got, own, *words)


def middle_kernel(v_ref, high_ref, low_ref, in_side_ref, out_side_ref, u_ref):
    v = v_ref[...].reshape(BLK, LANES)
    v_high, v_low = halves(v)
    qh, ql = high_ref[...], low_ref[...]
    both = mul(jnp.concatenate([v_high, v_low], axis=1), qh, 0, 0)
    rt = both[:LANES] + both[LANES:] + mul(v_high, ql, 0, 0)
    la = jnp.concatenate([in_side_ref[c, 1:2, :] for c in range(8)], axis=1).astype(f32) / VALUE_UNIT
    lb = jnp.sum(jnp.where(diagonal(), out_side_ref[0, 1:2, :], 0), axis=1, keepdims=True).astype(f32) / VALUE_UNIT
    st = rt / (lb * la + DAMPING)
    s_high, s_low = halves(st)
    both = mul(jnp.concatenate([s_high, s_low], axis=0), qh, 1, 1)
    ut = both[:LANES] + both[LANES:] + mul(s_high, ql, 1, 1)
    for c in range(8):
        u_ref[c] = ut[:, c * LANES:(c + 1) * LANES]


def middle(v, high, low, in_side, piece):
    whole = lambda i: (0, 0)
    return pl.pallas_call(
        middle_kernel,
        grid=(1,),
        in_specs=[
            pl.BlockSpec((8, LANES, LANES), lambda i: (0, 0, 0)),
            pl.BlockSpec((BLK, BLK), whole),
            pl.BlockSpec((BLK, BLK), whole),
            pl.BlockSpec((8, 8, LANES), lambda i: (0, 0, 0)),
            pl.BlockSpec((1, 8, LANES), lambda i: (0, 16, 0)),
        ],
        out_specs=pl.BlockSpec((8, LANES, LANES), lambda i: (0, 0, 0)),
        out_shape=jax.ShapeDtypeStruct((8, LANES, LANES), f32),
        compiler_params=params("arbitrary"),
        cost_estimate=pl.CostEstimate(flops=16 * 10**8, bytes_accessed=6 * 10**6, transcendentals=0),
    )(v, high, low, in_side, piece)


def back_kernel(u_ref, high_ref, low_ref, out_ref):
    u_high, u_low = halves(u_ref[...].reshape(BLK, LANES).T)
    both = mul(jnp.concatenate([u_high, u_low], axis=0), high_ref[...], 1, 1)
    out_ref[...] = both[:LANES] + both[LANES:] + mul(u_high, low_ref[...], 1, 1)


def back(u, high, low):
    return pl.pallas_call(
        back_kernel,
        grid=(2,),
        in_specs=[
            pl.BlockSpec((8, LANES, LANES), lambda i: (0, 0, 0)),
            pl.BlockSpec((512, BLK), lambda i: (i, 0)),
            pl.BlockSpec((512, BLK), lambda i: (i, 0)),
        ],
        out_specs=pl.BlockSpec((LANES, 512), lambda i: (0, i)),
        out_shape=jax.ShapeDtypeStruct((LANES, BLK), f32),
        compiler_params=params("arbitrary"),
        cost_estimate=pl.CostEstimate(flops=8 * 10**8, bytes_accessed=5 * 10**6, transcendentals=0),
    )(u, high, low)


def body(
    layer_inputs,
    output_grads,
    feature_order,
    block_slot,
    layer_owner,
    in_basis,
    in_values,
    out_basis,
    out_values,
):
    me = jnp.stack([lax.axis_index("y"), lax.axis_index("h"), lax.axis_index("z"), lax.axis_index(("l", "c"))])
    me = jnp.concatenate([me.astype(i32), block_slot])

    in_part = pack_basis(in_basis, in_values.reshape(1, LANES))
    in_part = lax.dynamic_slice_in_dim(in_part, lax.axis_index("c") * 2, 2, 0)
    in_pair = jnp.stack([in_part, lax.ppermute(in_part, ("h", "l"), [(i, 3 - i) for i in range(4)])])

    chunks = gather_columns(me, feature_order, layer_inputs.reshape(32, DIN))
    grads = output_grads.reshape(LANES, BLK)
    grads = jnp.stack([grads, flip(grads, "h")])
    chunks, grads, out_part = lax.optimization_barrier((chunks, grads, out_basis[0]))
    moved = lax.all_to_all(chunks, ("y", "h"), 0, 0, tiled=True)
    tokens = [moved] + [lax.ppermute(moved, ("l", "c"), [(m, m ^ j) for m in range(4)]) for j in range(1, 4)]

    packed = pack_basis(out_part, out_values)
    packed, in_pair, *tokens = lax.optimization_barrier((packed, in_pair, *tokens))
    spread = lax.all_to_all(packed, ALL_DP, 0, 0, tiled=True)
    piece = lax.dynamic_index_in_dim(spread, layer_owner[0], 0, keepdims=True)

    grads = lax.all_gather(grads, "y")
    own, *words = partial_rows(me, tokens, grads)
    words = [along(w, "z", k + 1) for k, w in enumerate(words)]
    piece, in_pair, words = lax.optimization_barrier((piece, in_pair, words))
    in_all = lax.all_gather(in_pair, "z")

    got = lax.all_to_all(jnp.broadcast_to(piece, spread.shape), ALL_DP, 0, 0, tiled=True)
    in_high, in_low, in_side = unpack_basis(me, in_all, jnp.stack([flip(in_all[z], "c") for z in range(4)]))
    own, in_high, in_low = lax.optimization_barrier((own, in_high, in_low))
    v, out_high, out_low = front(got, own, words)

    v = lax.all_to_all(v, PAIR, 0, 0, tiled=True)
    u = middle(v, in_high, in_low, in_side, piece)
    u = lax.all_to_all(u, PAIR, 0, 0, tiled=True)
    return back(u, out_high, out_low)


def along(block, axis, shift):
    if shift == 0:
        return block
    return lax.ppermute(block, axis, [(i, (i + shift) % 4) for i in range(4)])


def flip(block, axis):
    return lax.ppermute(block, axis, [(0, 1), (1, 0)])


def solution(mesh):
    fine = Mesh(mesh.devices.reshape(4, 2, 4, 2, 2), ("y", "h", "z", "l", "c"))
    dp, mp = ("y", "h", "z"), ("l", "c")
    in_specs = (
        P(dp + mp, None, None),
        P(dp, None, mp),
        P(),
        P(),
        P(),
        P(dp, None),
        P(dp),
        P(dp, mp, None),
        P(dp, mp),
    )
    return jax.shard_map(body, mesh=fine, in_specs=in_specs, out_specs=P(dp, mp), check_vma=False)
```

```python
import jax
import jax.numpy as jnp
from jax import lax
from jax.experimental import pallas as pl
from jax.experimental.pallas import tpu as pltpu
from jax.sharding import Mesh, PartitionSpec as P

DIN = 4096
BLK = 1024
LANES = 128
GROUP = 256
ROWS = 136
DAMPING = 0.1
TOP = 32767.0
LOG_UNIT = 65536.0
VALUE_UNIT = 134217728.0
PAIR = ("h", "z")
ALL_DP = ("y", "h", "z")
VMEM = 48 * 1024 * 1024
f32, bf16, i32 = jnp.float32, jnp.bfloat16, jnp.int32


def params(*semantics):
    return pltpu.CompilerParams(vmem_limit_bytes=VMEM, dimension_semantics=semantics or None)


def mul(a, b, ca=1, cb=0):
    return lax.dot_general(a, b, (((ca,), (cb,)), ((), ())), preferred_element_type=f32)


def halves(a):
    high = a.astype(bf16)
    return high, (a - high.astype(f32)).astype(bf16)


def gather_kernel(me_ref, order_ref, x_ref, out_ref):
    x = [x_ref[:, k * LANES:(k + 1) * LANES].astype(f32) for k in range(DIN // LANES)]
    for n in range(4):
        pair = sum(jnp.where(me_ref[4 + j] == pl.program_id(0) * 2 + n // 2, j, 0) for j in range(4))
        start = pair * BLK + n % 2 * 512
        for b in range(4):
            idx = order_ref[:, pl.ds(pl.multiple_of(start + b * LANES, LANES), LANES)]
            lane = jnp.broadcast_to(jnp.bitwise_and(idx, LANES - 1), (32, LANES))
            src = jnp.broadcast_to(jnp.right_shift(idx, 7), (32, LANES))
            acc = jnp.zeros((32, LANES), f32)
            for k in range(DIN // LANES):
                acc = jnp.where(src == k, jnp.take_along_axis(x[k], lane, axis=1), acc)
            out_ref[n, :, b * LANES:(b + 1) * LANES] = acc.astype(bf16)


def gather_columns(me, order, x):
    return pl.pallas_call(
        gather_kernel,
        grid=(2,),
        in_specs=[
            pl.BlockSpec(memory_space=pltpu.SMEM),
            pl.BlockSpec((1, DIN), lambda i: (0, 0)),
            pl.BlockSpec((32, DIN), lambda i: (0, 0)),
        ],
        out_specs=pl.BlockSpec((4, 32, 512), lambda i: (i, 0, 0)),
        out_shape=jax.ShapeDtypeStruct((8, 32, 512), bf16),
        compiler_params=params("arbitrary"),
        cost_estimate=pl.CostEstimate(flops=10**6, bytes_accessed=10**6, transcendentals=0),
    )(me, order, x)


def diagonal():
    return lax.broadcasted_iota(i32, (LANES, LANES), 0) == lax.broadcasted_iota(i32, (LANES, LANES), 1)


def encode(part):
    most = jnp.maximum(jnp.max(jnp.abs(part), axis=1, keepdims=True), 1e-30)
    code = jnp.ceil(jnp.log2(most) * LOG_UNIT) + 4.0
    q = jnp.round(part * (TOP * jnp.exp2(-code / LOG_UNIT))).astype(i32)
    word = jnp.bitwise_or(jnp.left_shift(q[:, LANES:], 16), jnp.bitwise_and(q[:, :LANES], 65535))
    return word, code.astype(i32)


def decode(word, unit):
    first = jnp.right_shift(jnp.left_shift(word, 16), 16).astype(f32) * unit
    return first, jnp.right_shift(word, 16).astype(f32) * unit


def to_row(column, eye):
    return jnp.sum(jnp.where(eye, column, 0), axis=0, keepdims=True)


def to_unit(row, eye):
    return jnp.exp2(jnp.sum(jnp.where(eye, row, 0), axis=1, keepdims=True).astype(f32) / LOG_UNIT) / TOP


def pack_kernel(basis_ref, values_ref, out_ref):
    eye = diagonal()
    blocks = values_ref.shape[1] // LANES
    count = out_ref.shape[0]
    for n in range(count // 4):
        codes = [[] for _ in range(4)]
        for g in range(4):
            word, code = encode(basis_ref[n * LANES:(n + 1) * LANES, g * GROUP:(g + 1) * GROUP])
            for d in range(4):
                out_ref[n * 4 + d, g * 32:(g + 1) * 32, :] = word[d * 32:(d + 1) * 32]
                codes[d].append(code[d * 32:(d + 1) * 32])
        for d in range(4):
            row = to_row(jnp.concatenate(codes[d], axis=0), eye)
            block = (n * 4 + d) % blocks
            coded = (values_ref[:, block * LANES:(block + 1) * LANES] * VALUE_UNIT).astype(i32)
            out_ref[n * 4 + d, LANES:ROWS, :] = jnp.concatenate([row, coded, jnp.zeros((6, LANES), i32)], axis=0)


def pack_basis(basis, values):
    rows = basis.shape[0]
    size = min(rows, 512)
    return pl.pallas_call(
        pack_kernel,
        grid=(rows // size,),
        in_specs=[pl.BlockSpec((size, BLK), lambda i: (i, 0)), pl.BlockSpec(values.shape, lambda i: (0, 0))],
        out_specs=pl.BlockSpec((size // 32, ROWS, LANES), lambda i: (i, 0, 0)),
        out_shape=jax.ShapeDtypeStruct((rows // 32, ROWS, LANES), i32),
        compiler_params=params("arbitrary"),
        cost_estimate=pl.CostEstimate(flops=rows * 10**4, bytes_accessed=rows * 6000, transcendentals=0),
    )(basis, values)


def decode_chunks(get, base, count, high_ref, low_ref, eye):
    for d in range(count):
        unit = to_unit(get(d, LANES, 1), eye)
        for g in range(4):
            pair = decode(get(d, g * 32, 32), unit[g * 32:(g + 1) * 32])
            for k in range(2):
                high, low = halves(pair[k])
                where = (pl.ds(base + d * 32, 32), slice(g * GROUP + k * LANES, g * GROUP + (k + 1) * LANES))
                high_ref[where] = high
                low_ref[where] = low


def unpack_kernel(me_ref, own_ref, other_ref, high_ref, low_ref, side_ref):
    core = lax.rem(me_ref[3], 2)
    eye = diagonal()
    for z in range(4):
        def get(d, start, size):
            rows = slice(start, start + size)
            return jnp.where(core == d // 2, own_ref[z, 0, d % 2, rows, :], other_ref[z, 0, d % 2, rows, :])
        decode_chunks(get, z * LANES, 4, high_ref, low_ref, eye)
        side_ref[z] = get(0, LANES, 8)


def unpack_basis(me, own, other):
    rows = lambda i, m: (i, 0)
    half = pl.BlockSpec((4, 1, 2, ROWS, LANES), lambda i, m: (0, lax.rem(i + m[1], 2), 0, 0, 0))
    return pl.pallas_call(
        unpack_kernel,
        grid_spec=pltpu.PrefetchScalarGridSpec(
            num_scalar_prefetch=1,
            grid=(2,),
            in_specs=[half, half],
            out_specs=[pl.BlockSpec((512, BLK), rows)] * 2 + [pl.BlockSpec((4, 8, LANES), lambda i, m: (i, 0, 0))],
        ),
        out_shape=[jax.ShapeDtypeStruct((BLK, BLK), bf16)] * 2 + [jax.ShapeDtypeStruct((8, 8, LANES), i32)],
        compiler_params=params("arbitrary"),
        cost_estimate=pl.CostEstimate(flops=10**7, bytes_accessed=6 * 10**6, transcendentals=0),
    )(me, own, other)


def partial_kernel(me_ref, x0_ref, x1_ref, x2_ref, x3_ref, grads_ref, *refs):
    own_ref, word_refs, tokens, total = refs[0], refs[1:4], refs[4], refs[5]
    for j, x_ref in enumerate((x0_ref, x1_ref, x2_ref, x3_ref)):
        place = jnp.bitwise_xor(me_ref[3], j)
        for r in range(8):
            tokens[pl.ds(pl.multiple_of(r * LANES + place * 32, 32), 32), :] = x_ref[r]
    for r in range(4):
        grads = jnp.concatenate([grads_ref[r, me_ref[1]], grads_ref[r, 1 - me_ref[1]]], axis=0)
        part = mul(tokens[r * GROUP:(r + 1) * GROUP, :], grads, 0, 0)
        total[...] = part if r == 0 else total[...] + part
    eye = diagonal()
    for k in range(4):
        start = pl.multiple_of(lax.rem(me_ref[2] + k, 4) * LANES, LANES)
        if k == 0:
            own_ref[...] = total[pl.ds(start, LANES), :]
            continue
        rows = []
        for g in range(4):
            word, code = encode(total[pl.ds(start, LANES), g * GROUP:(g + 1) * GROUP])
            word_refs[k - 1][g * LANES:(g + 1) * LANES, :] = word
            rows.append(to_row(code, eye))
        word_refs[k - 1][4 * LANES:, :] = jnp.concatenate(rows + [jnp.zeros((4, LANES), i32)], axis=0)


def partial_rows(me, tokens, grads):
    vmem = pl.BlockSpec(memory_space=pltpu.VMEM)
    return pl.pallas_call(
        partial_kernel,
        in_specs=[pl.BlockSpec(memory_space=pltpu.SMEM)] + [vmem] * 5,
        out_specs=[vmem] * 4,
        out_shape=[jax.ShapeDtypeStruct((LANES, BLK), f32)] + [jax.ShapeDtypeStruct((520, LANES), i32)] * 3,
        scratch_shapes=[pltpu.VMEM((BLK, 512), bf16), pltpu.VMEM((512, BLK), f32)],
        compiler_params=params(),
        cost_estimate=pl.CostEstimate(flops=10**9, bytes_accessed=5 * 10**6, transcendentals=0),
    )(me, *tokens, grads)


def front_kernel(got_ref, own_ref, w1_ref, w2_ref, w3_ref, v_ref, high_ref, low_ref, grad):
    step = pl.program_id(0)
    eye = diagonal()
    decode_chunks(lambda d, start, size: got_ref[d, start:start + size, :], 0, 16, high_ref, low_ref, eye)

    @pl.when(step == 0)
    def _():
        for g in range(4):
            sums = [own_ref[:, g * GROUP:g * GROUP + LANES], own_ref[:, g * GROUP + LANES:(g + 1) * GROUP]]
            for ref in (w1_ref, w2_ref, w3_ref):
                unit = to_unit(ref[4 * LANES + g:4 * LANES + g + 1, :], eye)
                pair = decode(ref[g * LANES:(g + 1) * LANES, :], unit)
                sums = [sums[0] + pair[0], sums[1] + pair[1]]
            grad[g // 2, :, g % 2 * GROUP:(g % 2 + 1) * GROUP] = jnp.concatenate(sums, axis=1)

    grad_high, grad_low = halves(grad[step])
    both = mul(jnp.concatenate([grad_high, grad_low], axis=0), high_ref[...])
    v = both[:LANES] + both[LANES:] + mul(grad_high, low_ref[...])
    for c in range(8):
        part = v[:, c * LANES:(c + 1) * LANES]
        v_ref[c] = jnp.where(step == 0, part, v_ref[c] + part)


def front(got, own, words):
    whole = lambda i: (0, 0)
    return pl.pallas_call(
        front_kernel,
        grid=(2,),
        in_specs=[pl.BlockSpec((16, ROWS, LANES), lambda i: (i, 0, 0)), pl.BlockSpec((LANES, BLK), whole)]
        + [pl.BlockSpec((520, LANES), whole)] * 3,
        out_specs=[pl.BlockSpec((8, LANES, LANES), lambda i: (0, 0, 0))]
        + [pl.BlockSpec((512, BLK), lambda i: (i, 0))] * 2,
        out_shape=[jax.ShapeDtypeStruct((8, LANES, LANES), f32)] + [jax.ShapeDtypeStruct((BLK, BLK), bf16)] * 2,
        scratch_shapes=[pltpu.VMEM((2, LANES, 512), f32)],
        compiler_params=params("arbitrary"),
        cost_estimate=pl.CostEstimate(flops=8 * 10**8, bytes_accessed=8 * 10**6, transcendentals=0),
    )(got, own, *words)


def middle_kernel(v_ref, high_ref, low_ref, in_side_ref, out_side_ref, u_ref):
    v = v_ref[...].reshape(BLK, LANES)
    v_high, v_low = halves(v)
    qh, ql = high_ref[...], low_ref[...]
    both = mul(jnp.concatenate([v_high, v_low], axis=1), qh, 0, 0)
    rt = both[:LANES] + both[LANES:] + mul(v_high, ql, 0, 0)
    la = jnp.concatenate([in_side_ref[c, 1:2, :] for c in range(8)], axis=1).astype(f32) / VALUE_UNIT
    lb = jnp.sum(jnp.where(diagonal(), out_side_ref[0, 1:2, :], 0), axis=1, keepdims=True).astype(f32) / VALUE_UNIT
    st = rt / (lb * la + DAMPING)
    s_high, s_low = halves(st)
    both = mul(jnp.concatenate([s_high, s_low], axis=0), qh, 1, 1)
    ut = both[:LANES] + both[LANES:] + mul(s_high, ql, 1, 1)
    for c in range(8):
        u_ref[c] = ut[:, c * LANES:(c + 1) * LANES]


def middle(v, high, low, in_side, piece):
    whole = lambda i: (0, 0)
    return pl.pallas_call(
        middle_kernel,
        grid=(1,),
        in_specs=[
            pl.BlockSpec((8, LANES, LANES), lambda i: (0, 0, 0)),
            pl.BlockSpec((BLK, BLK), whole),
            pl.BlockSpec((BLK, BLK), whole),
            pl.BlockSpec((8, 8, LANES), lambda i: (0, 0, 0)),
            pl.BlockSpec((1, 8, LANES), lambda i: (0, 16, 0)),
        ],
        out_specs=pl.BlockSpec((8, LANES, LANES), lambda i: (0, 0, 0)),
        out_shape=jax.ShapeDtypeStruct((8, LANES, LANES), f32),
        compiler_params=params("arbitrary"),
        cost_estimate=pl.CostEstimate(flops=16 * 10**8, bytes_accessed=6 * 10**6, transcendentals=0),
    )(v, high, low, in_side, piece)


def back_kernel(u_ref, high_ref, low_ref, out_ref):
    u_high, u_low = halves(u_ref[...].reshape(BLK, LANES).T)
    both = mul(jnp.concatenate([u_high, u_low], axis=0), high_ref[...], 1, 1)
    out_ref[...] = both[:LANES] + both[LANES:] + mul(u_high, low_ref[...], 1, 1)


def back(u, high, low):
    return pl.pallas_call(
        back_kernel,
        grid=(2,),
        in_specs=[
            pl.BlockSpec((8, LANES, LANES), lambda i: (0, 0, 0)),
            pl.BlockSpec((512, BLK), lambda i: (i, 0)),
            pl.BlockSpec((512, BLK), lambda i: (i, 0)),
        ],
        out_specs=pl.BlockSpec((LANES, 512), lambda i: (0, i)),
        out_shape=jax.ShapeDtypeStruct((LANES, BLK), f32),
        compiler_params=params("arbitrary"),
        cost_estimate=pl.CostEstimate(flops=8 * 10**8, bytes_accessed=5 * 10**6, transcendentals=0),
    )(u, high, low)


def body(
    layer_inputs,
    output_grads,
    feature_order,
    block_slot,
    layer_owner,
    in_basis,
    in_values,
    out_basis,
    out_values,
):
    me = jnp.stack([lax.axis_index("y"), lax.axis_index("h"), lax.axis_index("z"), lax.axis_index(("l", "c"))])
    me = jnp.concatenate([me.astype(i32), block_slot])

    in_part = pack_basis(in_basis, in_values.reshape(1, LANES))
    in_part = lax.dynamic_slice_in_dim(in_part, lax.axis_index("c") * 2, 2, 0)
    in_pair = jnp.stack([in_part, lax.ppermute(in_part, ("h", "l"), [(i, 3 - i) for i in range(4)])])

    chunks = gather_columns(me, feature_order, layer_inputs.reshape(32, DIN))
    grads = output_grads.reshape(LANES, BLK)
    grads = jnp.stack([grads, flip(grads, "h")])
    chunks, grads, out_part = lax.optimization_barrier((chunks, grads, out_basis[0]))
    moved = lax.all_to_all(chunks, ("y", "h"), 0, 0, tiled=True)
    tokens = [moved] + [lax.ppermute(moved, ("l", "c"), [(m, m ^ j) for m in range(4)]) for j in range(1, 4)]

    packed = pack_basis(out_part, out_values)
    packed, in_pair, *tokens = lax.optimization_barrier((packed, in_pair, *tokens))
    spread = lax.all_to_all(packed, ALL_DP, 0, 0, tiled=True)
    piece = lax.dynamic_index_in_dim(spread, layer_owner[0], 0, keepdims=True)

    grads = lax.all_gather(grads, "y")
    _, in_pair = lax.optimization_barrier((grads, in_pair))
    in_all = lax.all_gather(in_pair, "z")
    own, *words = partial_rows(me, tokens, grads)
    words = [along(w, "z", k + 1) for k, w in enumerate(words)]
    piece, words[0], words[2] = lax.optimization_barrier((piece, words[0], words[2]))

    got = lax.all_to_all(jnp.broadcast_to(piece, spread.shape), ALL_DP, 0, 0, tiled=True)
    in_high, in_low, in_side = unpack_basis(me, in_all, jnp.stack([flip(in_all[z], "c") for z in range(4)]))
    own, in_high, in_low = lax.optimization_barrier((own, in_high, in_low))
    v, out_high, out_low = front(got, own, words)

    v = lax.all_to_all(v, PAIR, 0, 0, tiled=True)
    u = middle(v, in_high, in_low, in_side, piece)
    u = lax.all_to_all(u, PAIR, 0, 0, tiled=True)
    return back(u, out_high, out_low)


def along(block, axis, shift):
    if shift == 0:
        return block
    return lax.ppermute(block, axis, [(i, (i + shift) % 4) for i in range(4)])


def flip(block, axis):
    return lax.ppermute(block, axis, [(0, 1), (1, 0)])


def solution(mesh):
    fine = Mesh(mesh.devices.reshape(4, 2, 4, 2, 2), ("y", "h", "z", "l", "c"))
    dp, mp = ("y", "h", "z"), ("l", "c")
    in_specs = (
        P(dp + mp, None, None),
        P(dp, None, mp),
        P(),
        P(),
        P(),
        P(dp, None),
        P(dp),
        P(dp, mp, None),
        P(dp, mp),
    )
    return jax.shard_map(body, mesh=fine, in_specs=in_specs, out_specs=P(dp, mp), check_vma=False)
```
